32 devices in a mesh: seq: 8 (over z, y), band: 4 (over x, core).
Axes of the slice: x: 2, y: 2, z: 4, core: 2. Of those that a mesh axis runs over, the one named last changes fastest.
Arguments:
- tokens: bfloat16 [4, 2048, 1024], P('band', 'seq'), may hold values from -6 to 6
- ln_gain: float32 [1024], replicated, may hold values from 0.25 to 12
- w_qkv: bfloat16 [1024, 3072], P('band', 'seq'), may hold values from -0.1875 to 0.1875
- w_out: bfloat16 [1024, 1024], P('band', 'seq'), may hold values from -0.1875 to 0.1875
- dec_gain: float32 [1024], replicated, may hold values from 0.25 to 12
- w_kv: bfloat16 [1024, 2048], P('band', 'seq'), may hold values from -0.1875 to 0.1875
- w_final: bfloat16 [1024, 96], P('band', 'seq'), may hold values from -0.1875 to 0.1875
- reach: int32 [2048], P('seq'), may hold values from 1 to 128, as said below
- grid_query: bfloat16 [4, 2048, 1024], P('band', 'seq'), may hold values from -128 to 128
- neighbours: int32 [2048, 8], P('seq'), may hold values from 0 to 2047, as said below
- counts: int32 [2048], P('seq'), may hold values from 1 to 8, as said below
Outputs:
- fields: bfloat16 [4, 96, 2048], P('band', None, 'seq')
The draws below stay inside these ranges and needn't reach their ends.
Inputs may be any that keep to these rules, and one draw needn't show every extreme that they name: Every device's block of 256 tokens holds a token of reach 128. `neighbours`: grid points are in blocks of 256 rows, block s lying over mesh tokens s * 256 to (s + 1) * 256 - 1. Of one block's used slots (slot below counts), at most 12 name tokens of any one other block; one mesh block is named so by exactly 12 used slots of every other block. Unused slots name tokens of the point's own block. `counts`: every block of 256 grid points has a point with all 8 slots used.
All inputs are finite; a program needn't handle non-finite values.
Results may differ from the reference program's by a relative error of at most 0.025.
The reference program's roundings to bfloat16 on the way (of `normed`, `projected`, `attended`, `mixed`, `decoded`, `mesh_rows` and `gridded`) count: a program that leaves them out, or rounds other values in their place, can miss the bound.
Values may be sent and summed in bfloat16 or wider, within the bound.
No kernel may reach another device: no remote copies, remote signals or barrier semaphores. Data moves between devices by JAX's collectives and lax.ppermute only.
A program may use at most 64 MiB of HBM per device.

```python
import math
import jax
import jax.numpy as jnp
from jax import lax

D = 1024
HEADS = 16
OUT = 96
HALF = 128
K = 8
C = 12
TOK_DEV = 256
GPD = 256
MTOK = 2048
GRID_M = 2048
MEMBERS = 4


def edge_tables(key):
    keys = jax.random.split(key, 6)
    shards = GRID_M // GPD
    total = GPD * K
    counts = jax.random.randint(keys[0], (shards, GPD), 1, K + 1)
    counts = counts.at[:, 0].set(K)
    home = jnp.arange(shards, dtype=jnp.int32)
    hot = jax.random.randint(keys[1], (), 0, shards)
    hot_owner = jnp.where(home == hot, (hot + 1) % shards, hot)
    ranking = jax.random.randint(keys[2], (shards, GPD), 0, 1 << 20) * GPD + jnp.arange(GPD, dtype=jnp.int32)[None, :]
    places = jnp.argsort(jnp.argsort(ranking, axis=1), axis=1)
    picked = places < C
    slot_ids = jnp.arange(K, dtype=jnp.int32)[None, None, :]
    valid = slot_ids < counts[:, :, None]
    forced = picked[:, :, None] & (slot_ids == 0)
    coin = jax.random.randint(keys[3], (shards, GPD, K), 0, 16) == 0
    stride = jax.random.randint(keys[4], (shards, GPD, K), 1, shards)
    other = (home[:, None, None] + stride) % shards
    wanted = valid & jnp.logical_not(forced) & coin & (other != hot_owner[:, None, None])
    flat_owner = other.reshape(shards, total)
    flat_want = wanted.reshape(shards, total)
    hits = ((flat_owner[:, :, None] == home[None, None, :]) & flat_want[:, :, None]).astype(jnp.int32)
    running = jnp.sum(jnp.cumsum(hits, axis=1) * hits, axis=2)
    kept = flat_want & (running <= C)
    owner = jnp.where(forced.reshape(shards, total), hot_owner[:, None], jnp.where(kept, flat_owner, home[:, None]))
    offsets = jax.random.randint(keys[5], (shards, total), 0, TOK_DEV)
    ids = owner * TOK_DEV + offsets
    return (ids.reshape(GRID_M, K).astype(jnp.int32), counts.reshape(GRID_M).astype(jnp.int32))


def draw_neighbours(key, part):
    tables = edge_tables(key)
    return tables[0]


def draw_counts(key, part):
    tables = edge_tables(key)
    return tables[1]


def draw_reach(key, part):
    key = jax.random.fold_in(key, 11)
    reach = jax.random.randint(key, (MTOK,), 1, HALF + 1)
    position = jnp.arange(MTOK, dtype=jnp.int32)
    return jnp.where(position % TOK_DEV == 0, HALF, reach).astype(jnp.int32)


def log_spread(key, low, high):
    return jnp.exp(jax.random.uniform(key, (D,), jnp.float32, jnp.log(low), jnp.log(high)))


def draw_ln_gain(key, part):
    key = jax.random.fold_in(key, 21)
    return log_spread(key, 0.5, 2.0)


def draw_dec_gain(key, part):
    key = jax.random.fold_in(key, 22)
    return log_spread(key, 0.5, 2.0)


def draw_grid_query(key, part):
    key = jax.random.fold_in(key, 31)
    key_base = jax.random.fold_in(key, 0)
    shape = (MEMBERS, GRID_M, D)
    return jax.random.truncated_normal(key_base, -6.0, 6.0, shape, jnp.float32).astype(jnp.bfloat16)


def block_scale(rng, extent, cuts, least, high):
    level = 1.0
    for axis_at, parts in cuts:
        draws = jax.random.uniform(jax.random.fold_in(jax.random.fold_in(rng, 6), axis_at), (parts,), jnp.float32, least / len(cuts), high / len(cuts))
        level = level * jnp.repeat(jnp.exp(draws), extent[axis_at] // parts).reshape((-1,) + (1,) * (len(extent) - 1 - axis_at))
    return level


def noise(own_key, shape, scale, bound, cuts=(), kind=jnp.bfloat16):
    entries = scale * jax.random.normal(own_key, shape, jnp.float32)
    if cuts:
        entries = entries * block_scale(own_key, shape, cuts, -0.22, 0.18)
    return jnp.clip(entries, -bound, bound).astype(kind)


def setup_inputs(seed: int = 0) -> dict:
    streams_of = jax.random.split(jax.random.key(seed), 12)
    tokens = noise(streams_of[0], (MEMBERS, MTOK, D), 1.0, 6.0, ((0, 4), (1, 8)))
    ln_gain = draw_ln_gain(jax.random.fold_in(streams_of[11], 71), 0)
    w_qkv = noise(streams_of[2], (D, 3 * D), D ** -0.5, 0.1875, ((0, 4), (1, 8)))
    w_out = noise(streams_of[3], (D, D), D ** -0.5, 0.1875, ((0, 4), (1, 8)))
    dec_gain = draw_dec_gain(jax.random.fold_in(streams_of[11], 71), 0)
    w_kv = noise(streams_of[5], (D, 2 * D), D ** -0.5, 0.1875, ((0, 4), (1, 8)))
    w_final = noise(streams_of[6], (D, OUT), D ** -0.5, 0.1875, ((0, 4), (1, 8)))
    reach = draw_reach(jax.random.fold_in(streams_of[11], 71), 0)
    grid_query = draw_grid_query(jax.random.fold_in(streams_of[11], 71), 0)
    neighbours = draw_neighbours(jax.random.fold_in(streams_of[11], 71), 0)
    counts = draw_counts(jax.random.fold_in(streams_of[11], 71), 0)
    return {"tokens": tokens, "ln_gain": ln_gain, "w_qkv": w_qkv, "w_out": w_out, "dec_gain": dec_gain, "w_kv": w_kv, "w_final": w_final, "reach": reach, "grid_query": grid_query, "neighbours": neighbours, "counts": counts}


EPSILON = 1e-05
GROUP = 4

def layer_norm(values, gain):
    values = values.astype(jnp.float32)
    centred = values - lax.optimization_barrier(jnp.mean(values, axis=-1, keepdims=True))
    spread = lax.optimization_barrier(jnp.mean(centred * centred, axis=-1, keepdims=True))
    return (centred * lax.rsqrt(spread + EPSILON) * gain).astype(jnp.bfloat16)

def split_heads(values, count):
    length = values.shape[0]
    head_size = values.shape[1] // count
    return values.reshape(length, count, head_size).transpose(1, 0, 2).reshape(count // GROUP, GROUP, length, head_size)

def window_attend(queries, keys, values, allowed, scale):

    def one_group(operands):
        query_g, key_g, value_g = operands
        scores = jnp.einsum('gqd,gkd->gqk', query_g.astype(jnp.float32), key_g.astype(jnp.float32)) * scale
        scores = jnp.where(allowed[None], scores, -1e+30)
        top = lax.optimization_barrier(jnp.max(scores, axis=-1, keepdims=True))
        weights = jnp.exp(scores - top)
        weights = (weights / lax.optimization_barrier(jnp.sum(weights, axis=-1, keepdims=True))).astype(jnp.bfloat16)
        return jnp.einsum('gqk,gkd->gqd', weights.astype(jnp.float32), value_g.astype(jnp.float32)).astype(jnp.bfloat16)
    return lax.map(one_group, (queries, keys, values))

def decode(queries, table, where_rows, valid, w_final, scale):
    points = queries.shape[0]
    width = queries.shape[1]
    head_size = width // HEADS
    block = math.gcd(points, 128)
    slots = where_rows.shape[1]

    def one_block(block_index):
        first = block_index * block
        query_b = lax.dynamic_slice_in_dim(queries, first, block, 0).reshape(block, HEADS, head_size)
        index_b = lax.dynamic_slice_in_dim(where_rows, first, block, 0)
        valid_b = lax.dynamic_slice_in_dim(valid, first, block, 0)
        gathered = jnp.take(table, index_b, axis=0)
        keys = gathered[:, :, :width].reshape(block, slots, HEADS, head_size)
        values = gathered[:, :, width:].reshape(block, slots, HEADS, head_size)
        scores = jnp.einsum('phd,pkhd->phk', query_b.astype(jnp.float32), keys.astype(jnp.float32)) * scale
        scores = jnp.where(valid_b[:, None, :], scores, -1e+30)
        top = lax.optimization_barrier(jnp.max(scores, axis=-1, keepdims=True))
        weights = jnp.exp(scores - top)
        weights = (weights / lax.optimization_barrier(jnp.sum(weights, axis=-1, keepdims=True))).astype(jnp.bfloat16)
        gridded = jnp.einsum('phk,pkhd->phd', weights.astype(jnp.float32), values.astype(jnp.float32)).astype(jnp.bfloat16)
        return jnp.dot(gridded.reshape(block, width), w_final, preferred_element_type=jnp.float32)
    blocks = lax.map(one_block, jnp.arange(points // block, dtype=jnp.int32))
    return blocks.reshape(points, -1).T.astype(jnp.bfloat16)

def reference(tokens, ln_gain, w_qkv, w_out, dec_gain, w_kv, w_final, reach, grid_query, neighbours, counts):
    head_size = D // HEADS
    scale = 1.0 / math.sqrt(head_size)
    valid = jnp.arange(K, dtype=jnp.int32)[None, :] < counts[:, None]

    def member(operands):
        states, queries = operands
        normed = layer_norm(states, ln_gain)
        projected = jnp.dot(normed, w_qkv, preferred_element_type=jnp.float32).astype(jnp.bfloat16)
        query_all = projected[:, :D]
        padded = jnp.pad(projected[:, D:], ((HALF, HALF), (0, 0)))

        def one_span(block_index):
            start = block_index * TOK_DEV
            query_b = lax.dynamic_slice_in_dim(query_all, start, TOK_DEV, 0)
            window = lax.dynamic_slice_in_dim(padded, start, TOK_DEV + 2 * HALF, 0)
            reach_b = lax.dynamic_slice_in_dim(reach, start, TOK_DEV, 0)
            query_pos = start + jnp.arange(TOK_DEV, dtype=jnp.int32)
            key_pos = start - HALF + jnp.arange(TOK_DEV + 2 * HALF, dtype=jnp.int32)
            allowed = (jnp.abs(query_pos[:, None] - key_pos[None, :]) <= reach_b[:, None]) & (key_pos[None, :] >= 0) & (key_pos[None, :] < MTOK)
            heads_out = window_attend(split_heads(query_b, HEADS), split_heads(window[:, :D], HEADS), split_heads(window[:, D:], HEADS), allowed, scale)
            return heads_out.reshape(HEADS, TOK_DEV, head_size).transpose(1, 0, 2).reshape(TOK_DEV, D)
        attended = lax.map(one_span, jnp.arange(MTOK // TOK_DEV, dtype=jnp.int32)).reshape(MTOK, D)
        mixed = (states.astype(jnp.float32) + jnp.dot(attended, w_out, preferred_element_type=jnp.float32)).astype(jnp.bfloat16)
        decoded = layer_norm(mixed, dec_gain)
        mesh_rows = jnp.dot(decoded, w_kv, preferred_element_type=jnp.float32).astype(jnp.bfloat16)
        return decode(queries, mesh_rows, neighbours, valid, w_final, scale)
    return lax.map(member, (tokens, grid_query))
```

```python
import functools
import math

import jax
import jax.numpy as jnp
import numpy as np
from jax import lax
from jax.experimental import pallas as pl
from jax.experimental.pallas import tpu as pltpu
from jax.sharding import PartitionSpec as P

HEADS = 16
HALF = 128
C = 12
EPSILON = 1e-05
NEG = -1e30
LANES = 128
GROUPS = 8
BANDS = 4
VMEM = 56 * 1024 * 1024
F32 = jnp.float32
BF16 = jnp.bfloat16


def dot(a, b):
    return jnp.dot(a, b, preferred_element_type=F32)


def dot_nt(a, b):
    return lax.dot_general(a, b, (((1,), (1,)), ((), ())), preferred_element_type=F32)


def layer_norm(values, gain):
    values = values.astype(F32)
    centred = values - jnp.mean(values, axis=-1, keepdims=True)
    spread = jnp.mean(centred * centred, axis=-1, keepdims=True)
    return (centred * lax.rsqrt(spread + EPSILON) * gain).astype(BF16)


def params(**more):
    return pltpu.CompilerParams(vmem_limit_bytes=VMEM, **more)


def full_spec(shape):
    return pl.BlockSpec(shape, lambda *_: (0,) * len(shape))


def prepare_kernel(
    total, place, left, own, right, gain, reach, neighbours, counts, low, rank, tri,
    normed, bias, multiplicity, requested,
):
    tok = own.shape[0]
    normed[:HALF, :] = layer_norm(left[...], gain[...])
    normed[HALF : HALF + tok, :] = layer_norm(own[...], gain[...])
    normed[HALF + tok :, :] = layer_norm(right[...], gain[...])

    me = place[0]
    first = me * tok
    span = 3 * HALF
    row = lax.broadcasted_iota(jnp.int32, (HALF, span), 0)
    col = lax.broadcasted_iota(jnp.int32, (HALF, span), 1)
    away = jnp.abs(row + HALF - col)
    for block in range(tok // HALF):
        key = first + (block - 1) * HALF + col
        allowed = (away <= reach[block * HALF : (block + 1) * HALF, :]) & (key >= 0) & (key < total)
        bias[block] = jnp.where(allowed, 0.0, NEG)

    points, slots = neighbours.shape
    ids = neighbours[...]
    used = counts[...]
    mesh = lax.broadcasted_iota(jnp.int32, (points, tok), 1) + first
    here = jnp.zeros((points, tok), F32)
    for slot in range(slots):
        here += ((ids[:, slot : slot + 1] == mesh) & (slot < used)).astype(F32)
    multiplicity[:, :tok] = here

    start = low[...]
    elsewhere = start != first
    hits = []
    for slot in range(slots):
        which = ids[:, slot : slot + 1]
        hits.append(
            ((which >= start) & (which < start + tok) & (slot < used) & elsewhere).astype(F32)
        )
    running = dot(tri[...], sum(hits).astype(BF16))
    order = rank[...]
    asked = jnp.zeros(requested.shape, F32)
    there = jnp.zeros(hits[0].shape, F32)
    for slot in range(slots):
        mine = jnp.where(running == order, hits[slot], 0.0)
        there += mine
        offset = (ids[:, slot : slot + 1] - start).astype(F32)
        asked += jnp.sum(jnp.where(mine > 0, offset, 0.0), axis=0, keepdims=True)
        running += hits[slot]
    multiplicity[:, tok:] = there
    requested[...] = asked.astype(jnp.int32)


def prepare(total, place, left, own, right, gain, reach, neighbours, counts, shards):
    tok, width = own.shape
    points = neighbours.shape[0]
    remote = -(-shards * C // LANES) * LANES
    column = np.arange(remote)
    low = np.where(column < shards * C, column // C * tok, 1 << 30).astype(np.int32)[None]
    rank = (column % C).astype(np.float32)[None]
    tri = np.tril(np.ones((points, points), np.float32), -1).astype(BF16)
    operands = (left, own, right, gain, reach, neighbours, counts, low, rank, tri)
    outs = (
        jax.ShapeDtypeStruct((tok + 2 * HALF, width), BF16),
        jax.ShapeDtypeStruct((tok // HALF, HALF, 3 * HALF), F32),
        jax.ShapeDtypeStruct((points, tok + remote), F32),
        jax.ShapeDtypeStruct((1, remote), jnp.int32),
    )
    return pl.pallas_call(
        functools.partial(prepare_kernel, total),
        out_shape=outs,
        in_specs=[pl.BlockSpec(memory_space=pltpu.SMEM)]
        + [pl.BlockSpec(memory_space=pltpu.VMEM)] * len(operands),
        out_specs=[pl.BlockSpec(memory_space=pltpu.VMEM)] * len(outs),
        compiler_params=params(),
        cost_estimate=pl.CostEstimate(flops=20_000_000, bytes_accessed=4_000_000, transcendentals=0),
        name="prepare",
    )(place, *operands)


def pair_attend(queries, keys, values, bias, weights_of):
    rows = queries.shape[0]
    lane = lax.broadcasted_iota(jnp.int32, (rows, LANES), 1)
    first = lane < LANES // 2
    zero = jnp.zeros_like(queries)
    both = jnp.concatenate(
        [jnp.where(first, queries, zero), jnp.where(first, zero, queries)], axis=0
    )
    scores = dot_nt(both, keys)
    scores = scores + jnp.concatenate([bias, bias], axis=0)
    top = jnp.max(scores, axis=-1, keepdims=True)
    weights = weights_of(jnp.exp(scores - top)).astype(BF16)
    summed = dot(weights, jnp.concatenate([values, jnp.ones_like(values)], axis=1))
    share = summed[:, :LANES] / summed[:, LANES:]
    return jnp.where(first, share[:rows], share[rows:]).astype(BF16)


def attend_kernel(normed, weight, bias, attended, projected):
    step = pl.program_id(0)
    width = normed.shape[1]
    per = weight.shape[2] // LANES
    part = dot(normed[...], weight[0]).astype(BF16)
    for group in range(per):
        projected[step * per + group] = part[:, group * LANES : (group + 1) * LANES]

    @pl.when(step == pl.num_programs(0) - 1)
    def _():
        pairs = width // LANES
        scale = BF16(1.0 / math.sqrt(width // HEADS))
        for pair in range(pairs):
            for block in range(bias.shape[0]):
                at = block * HALF
                attended[at : at + HALF, pair * LANES : (pair + 1) * LANES] = pair_attend(
                    projected[pair, at + HALF : at + 2 * HALF, :] * scale,
                    projected[pairs + pair, at : at + 3 * HALF, :],
                    projected[2 * pairs + pair, at : at + 3 * HALF, :],
                    bias[block],
                    lambda weights: weights,
                )


def attend(normed, weight, bias):
    rows, width = normed.shape
    tok = rows - 2 * HALF
    groups, _, columns = weight.shape
    return pl.pallas_call(
        attend_kernel,
        grid=(groups,),
        out_shape=jax.ShapeDtypeStruct((tok, width), BF16),
        in_specs=[
            full_spec(normed.shape),
            pl.BlockSpec((1, width, columns), lambda s: (s, 0, 0)),
            full_spec(bias.shape),
        ],
        out_specs=full_spec((tok, width)),
        scratch_shapes=[pltpu.VMEM((groups * columns // LANES, rows, LANES), BF16)],
        compiler_params=params(),
        cost_estimate=pl.CostEstimate(
            flops=6_000_000_000, bytes_accessed=9_000_000, transcendentals=2_000_000
        ),
        name="attend",
    )(normed, weight, bias)


def mix_kernel(states, attended, weight, gain, ids, decoded, found, mixed):
    step = pl.program_id(0)
    columns = weight.shape[3]
    total = jnp.zeros((states.shape[0], columns), F32)
    depth = weight.shape[2]
    for band in range(weight.shape[1]):
        total += dot(attended[:, band * depth : (band + 1) * depth], weight[0, band])
    at = pl.multiple_of(step * columns, columns)
    mixed[:, pl.ds(at, columns)] = (
        states[:, pl.ds(at, columns)].astype(F32) + total
    ).astype(BF16)

    @pl.when(step == pl.num_programs(0) - 1)
    def _():
        rows = layer_norm(mixed[...], gain[...])
        decoded[...] = rows
        place = lax.broadcasted_iota(jnp.int32, (ids.shape[0], rows.shape[0]), 1)
        pick = (ids[...] == place).astype(BF16)
        found[...] = dot(pick, rows).astype(BF16)


def mix(states, attended, rest, gain, ids):
    tok, width = states.shape
    columns = width // GROUPS
    return pl.pallas_call(
        mix_kernel,
        grid=(GROUPS,),
        out_shape=(
            jax.ShapeDtypeStruct((tok, width), BF16),
            jax.ShapeDtypeStruct((ids.shape[0], width), BF16),
        ),
        in_specs=[
            full_spec(states.shape),
            full_spec(attended.shape),
            pl.BlockSpec((1, BANDS, width // BANDS, columns), lambda s: (s, 0, 0, 2)),
            full_spec(gain.shape),
            full_spec(ids.shape),
        ],
        out_specs=(full_spec((tok, width)), full_spec((ids.shape[0], width))),
        scratch_shapes=[pltpu.VMEM((tok, width), BF16)],
        compiler_params=params(),
        cost_estimate=pl.CostEstimate(
            flops=600_000_000, bytes_accessed=4_000_000, transcendentals=0
        ),
        name="mix",
    )(states, attended, rest, gain, ids)


def keys_values_kernel(decoded, weight, out):
    total = jnp.zeros(out.shape, F32)
    depth = weight.shape[2]
    for band in range(weight.shape[1]):
        total += dot(decoded[:, band * depth : (band + 1) * depth], weight[0, band])
    out[...] = total.astype(BF16)


def keys_values(decoded, rest):
    tok, width = decoded.shape
    columns = 2 * width // GROUPS
    return pl.pallas_call(
        keys_values_kernel,
        grid=(GROUPS,),
        out_shape=jax.ShapeDtypeStruct((tok, 2 * width), BF16),
        in_specs=[
            full_spec(decoded.shape),
            pl.BlockSpec((1, BANDS, width // BANDS, columns), lambda s: (s, 0, 0, 0)),
        ],
        out_specs=pl.BlockSpec((tok, columns), lambda s: (0, s)),
        compiler_params=params(),
        cost_estimate=pl.CostEstimate(
            flops=1_100_000_000, bytes_accessed=6_000_000, transcendentals=0
        ),
        name="keys_values",
    )(decoded, rest)


def decode_kernel(
    queries, local_rows, fetched, weight, final, multiplicity, fields, table, final_rows
):
    step = pl.program_id(0)
    tok = local_rows.shape[0]
    count = fetched.shape[0]
    columns = weight.shape[3]
    per = columns // LANES
    total = jnp.zeros((count, columns), F32)
    depth = weight.shape[2]
    for band in range(weight.shape[1]):
        total += dot(fetched[:, band * depth : (band + 1) * depth], weight[0, band])
        final_rows[step, :, band * depth : (band + 1) * depth] = final[0, band]
    total = total.astype(BF16)
    for group in range(per):
        table[step * per + group, :count, :] = total[:, group * LANES : (group + 1) * LANES]
        if table.shape[1] > count:
            table[step * per + group, count:, :] = jnp.zeros(
                (table.shape[1] - count, LANES), BF16
            )

    @pl.when(step == pl.num_programs(0) - 1)
    def _():
        points, width = queries.shape
        pairs = width // LANES
        scale = BF16(1.0 / math.sqrt(width // HEADS))
        times = multiplicity[...]
        bias = jnp.where(times > 0, 0.0, NEG)
        both = jnp.concatenate([times, times], axis=0)
        rows = []
        for pair in range(pairs):
            at = slice(pair * LANES, (pair + 1) * LANES)
            to = slice(width + pair * LANES, width + (pair + 1) * LANES)
            rows.append(
                pair_attend(
                    queries[:, at] * scale,
                    jnp.concatenate([local_rows[:, at], table[pair]], axis=0),
                    jnp.concatenate([local_rows[:, to], table[pairs + pair]], axis=0),
                    bias,
                    lambda weights: weights * both,
                )
            )
        gridded = jnp.concatenate(rows, axis=1)
        height = final_rows.shape[1]
        padded = dot_nt(final_rows[...].reshape(GROUPS * height, width), gridded)
        each = fields.shape[0] // GROUPS
        kept = [padded[group * height : group * height + each] for group in range(GROUPS)]
        fields[...] = jnp.concatenate(kept, axis=0).astype(BF16)


def decode(queries, local_rows, fetched, rest, multiplicity, outputs):
    points, width = queries.shape
    tok = local_rows.shape[0]
    depth = width // BANDS
    columns = 2 * width // GROUPS
    height = rest.shape[2] - depth
    remote = multiplicity.shape[1] - tok
    return pl.pallas_call(
        decode_kernel,
        grid=(GROUPS,),
        out_shape=jax.ShapeDtypeStruct((outputs, points), BF16),
        in_specs=[
            full_spec(queries.shape),
            full_spec(local_rows.shape),
            full_spec(fetched.shape),
            pl.BlockSpec((1, BANDS, depth, columns), lambda s: (s, 0, 0, 0)),
            pl.BlockSpec((1, BANDS, height, depth), lambda s: (s, 0, depth // height, 0)),
            full_spec(multiplicity.shape),
        ],
        out_specs=full_spec((outputs, points)),
        scratch_shapes=[
            pltpu.VMEM((2 * width // LANES, remote, LANES), BF16),
            pltpu.VMEM((GROUPS, height, width), BF16),
        ],
        compiler_params=params(),
        cost_estimate=pl.CostEstimate(
            flops=2_000_000_000, bytes_accessed=8_000_000, transcendentals=2_000_000
        ),
        name="decode",
    )(queries, local_rows, fetched, rest, rest, multiplicity)


def gather_weights(w_qkv, w_out, w_kv, w_final, axes):
    seq, band = axes
    count = (lax.axis_size(seq), lax.axis_size(band))
    each = w_final.shape[1] * count[0] // GROUPS
    height = -(-each // 16) * 16
    depth = w_qkv.shape[0] * count[1] // BANDS
    if count == (GROUPS, BANDS):
        final = jnp.pad(w_final.T, ((0, height - each), (0, w_kv.shape[1] + w_out.shape[1] - depth)))
        packed = jnp.concatenate([jnp.concatenate([w_kv, w_out], axis=1), final], axis=0)
        qkv = lax.all_gather(w_qkv, (seq, band), axis=0, tiled=False)
        rest = lax.all_gather(packed, (seq, band), axis=0, tiled=False)
        return (
            qkv.reshape(GROUPS, BANDS * depth, w_qkv.shape[1]),
            rest.reshape((GROUPS, BANDS) + packed.shape),
        )

    def whole(weight):
        columns = lax.all_gather(weight, seq, axis=1, tiled=True)
        return lax.all_gather(columns, band, axis=0, tiled=True)

    def blocks(weight):
        columns = weight.shape[1] // GROUPS
        return weight.reshape(BANDS, depth, GROUPS, columns).transpose(2, 0, 1, 3)

    qkv = blocks(whole(w_qkv))
    kv = blocks(whole(w_kv))
    out = blocks(whole(w_out))
    final = blocks(whole(w_final)).transpose(0, 1, 3, 2)
    final = jnp.pad(
        final, ((0, 0), (0, 0), (0, height - each), (0, kv.shape[3] + out.shape[3] - depth))
    )
    rest = jnp.concatenate([jnp.concatenate([kv, out], axis=3), final], axis=2)
    return qkv.reshape(GROUPS, BANDS * depth, qkv.shape[3]), rest


def local(
    tokens, ln_gain, w_qkv, w_out, dec_gain, w_kv, w_final, reach, grid_query, neighbours, counts
):
    states = tokens[0]
    tok, width = states.shape
    shards = lax.axis_size("seq")
    place = lax.axis_index("seq").astype(jnp.int32).reshape(1)
    outputs = w_final.shape[1] * shards
    up = [(i, i + 1) for i in range(shards - 1)]
    down = [(i + 1, i) for i in range(shards - 1)]
    left = lax.ppermute(states[tok - HALF :], "seq", up)
    right = lax.ppermute(states[:HALF], "seq", down)
    qkv, rest = gather_weights(w_qkv, w_out, w_kv, w_final, ("seq", "band"))
    normed, bias, multiplicity, requested = prepare(
        tok * shards, place, left, states, right, ln_gain.reshape(1, width),
        reach.reshape(tok, 1), neighbours, counts.reshape(-1, 1), shards,
    )
    requested = requested[:, : shards * C].reshape(shards, C)
    wanted = lax.all_to_all(requested, "seq", split_axis=0, concat_axis=0, tiled=True)
    attended = attend(normed, qkv, bias)
    decoded, found = mix(
        states, attended, rest, dec_gain.reshape(1, width), wanted.reshape(shards * C, 1)
    )
    fetched = lax.all_to_all(
        found.reshape(shards, C, width), "seq", split_axis=0, concat_axis=0, tiled=True
    )
    local_rows = keys_values(decoded, rest)
    fields = decode(
        grid_query[0], local_rows, fetched.reshape(shards * C, width), rest, multiplicity, outputs
    )
    return fields[None]


def solution(mesh):
    return jax.shard_map(
        local,
        mesh=mesh,
        in_specs=(
            P("band", "seq", None),
            P(),
            P("band", "seq"),
            P("band", "seq"),
            P(),
            P("band", "seq"),
            P("band", "seq"),
            P("seq"),
            P("band", "seq", None),
            P("seq", None),
            P("seq"),
        ),
        out_specs=P("band", None, "seq"),
        check_vma=False,
    )
```

```python
import functools
import math

import jax
import jax.numpy as jnp
import numpy as np
from jax import lax
from jax.experimental import pallas as pl
from jax.experimental.pallas import tpu as pltpu
from jax.sharding import PartitionSpec as P

HEADS = 16
HALF = 128
C = 12
EPSILON = 1e-05
NEG = -1e30
LANES = 128
GROUPS = 8
BANDS = 4
CHUNKS = (0, 2, 1, 3)
RING = (0, 2, 4, 6, 7, 5, 3, 1)
VMEM = 56 * 1024 * 1024
F32 = jnp.float32
BF16 = jnp.bfloat16


def dot(a, b):
    return jnp.dot(a, b, preferred_element_type=F32)


def dot_nt(a, b):
    return lax.dot_general(a, b, (((1,), (1,)), ((), ())), preferred_element_type=F32)


def layer_norm(values, gain):
    values = values.astype(F32)
    centred = values - jnp.mean(values, axis=-1, keepdims=True)
    spread = jnp.mean(centred * centred, axis=-1, keepdims=True)
    return (centred * lax.rsqrt(spread + EPSILON) * gain).astype(BF16)


def params(**more):
    return pltpu.CompilerParams(vmem_limit_bytes=VMEM, **more)


def full_spec(shape):
    return pl.BlockSpec(shape, lambda *_: (0,) * len(shape))


def prepare_kernel(
    total, place, left, own, right, gain, reach, neighbours, counts, low, rank, tri,
    normed, bias, multiplicity, requested,
):
    tok = own.shape[0]
    depth = own.shape[1] // BANDS
    for at, part in ((0, left), (HALF, own), (HALF + tok, right)):
        rows = layer_norm(part[...], gain[...])
        for chunk, band in enumerate(CHUNKS):
            normed[at : at + part.shape[0], chunk * depth : (chunk + 1) * depth] = rows[
                :, band * depth : (band + 1) * depth
            ]

    me = place[0]
    first = me * tok
    span = 3 * HALF
    row = lax.broadcasted_iota(jnp.int32, (HALF, span), 0)
    col = lax.broadcasted_iota(jnp.int32, (HALF, span), 1)
    away = jnp.abs(row + HALF - col)
    for block in range(tok // HALF):
        key = first + (block - 1) * HALF + col
        allowed = (away <= reach[block * HALF : (block + 1) * HALF, :]) & (key >= 0) & (key < total)
        bias[block] = jnp.where(allowed, 0.0, NEG)

    points, slots = neighbours.shape
    ids = neighbours[...]
    used = counts[...]
    mesh = lax.broadcasted_iota(jnp.int32, (points, tok), 1) + first
    here = jnp.zeros((points, tok), F32)
    for slot in range(slots):
        here += ((ids[:, slot : slot + 1] == mesh) & (slot < used)).astype(F32)
    multiplicity[:, :tok] = here

    start = low[...]
    elsewhere = start != first
    hits = []
    for slot in range(slots):
        which = ids[:, slot : slot + 1]
        hits.append(
            ((which >= start) & (which < start + tok) & (slot < used) & elsewhere).astype(F32)
        )
    running = dot(tri[...], sum(hits).astype(BF16))
    order = rank[...]
    asked = jnp.zeros(requested.shape, F32)
    there = jnp.zeros(hits[0].shape, F32)
    for slot in range(slots):
        mine = jnp.where(running == order, hits[slot], 0.0)
        there += mine
        offset = (ids[:, slot : slot + 1] - start).astype(F32)
        asked += jnp.sum(jnp.where(mine > 0, offset, 0.0), axis=0, keepdims=True)
        running += hits[slot]
    multiplicity[:, tok:] = there
    requested[...] = asked.astype(jnp.int32)


def prepare(total, place, left, own, right, gain, reach, neighbours, counts, shards):
    tok, width = own.shape
    points = neighbours.shape[0]
    remote = -(-shards * C // LANES) * LANES
    column = np.arange(remote)
    low = np.where(column < shards * C, column // C * tok, 1 << 30).astype(np.int32)[None]
    rank = (column % C).astype(np.float32)[None]
    tri = np.tril(np.ones((points, points), np.float32), -1).astype(BF16)
    operands = (left, own, right, gain, reach, neighbours, counts, low, rank, tri)
    outs = (
        jax.ShapeDtypeStruct((tok + 2 * HALF, width), BF16),
        jax.ShapeDtypeStruct((tok // HALF, HALF, 3 * HALF), F32),
        jax.ShapeDtypeStruct((points, tok + remote), F32),
        jax.ShapeDtypeStruct((1, remote), jnp.int32),
    )
    return pl.pallas_call(
        functools.partial(prepare_kernel, total),
        out_shape=outs,
        in_specs=[pl.BlockSpec(memory_space=pltpu.SMEM)]
        + [pl.BlockSpec(memory_space=pltpu.VMEM)] * len(operands),
        out_specs=[pl.BlockSpec(memory_space=pltpu.VMEM)] * len(outs),
        compiler_params=params(),
        cost_estimate=pl.CostEstimate(flops=20_000_000, bytes_accessed=4_000_000, transcendentals=0),
        name="prepare",
    )(place, *operands)


def pair_attend(queries, keys, values, bias, weights_of):
    rows = queries.shape[0]
    lane = lax.broadcasted_iota(jnp.int32, (rows, LANES), 1)
    first = lane < LANES // 2
    zero = jnp.zeros_like(queries)
    both = jnp.concatenate(
        [jnp.where(first, queries, zero), jnp.where(first, zero, queries)], axis=0
    )
    scores = dot_nt(both, keys)
    scores = scores + jnp.concatenate([bias, bias], axis=0)
    top = jnp.max(scores, axis=-1, keepdims=True)
    weights = weights_of(jnp.exp(scores - top)).astype(BF16)
    summed = dot(weights, jnp.concatenate([values, jnp.ones_like(values)], axis=1))
    share = summed[:, :LANES] / summed[:, LANES:]
    return jnp.where(first, share[:rows], share[rows:]).astype(BF16)


def start_loads(spots, pieces, layout, scratch, arrived, rows):
    copies = {}
    for n, (piece, (at, core, x)) in enumerate(zip(pieces, layout)):
        if at is None:
            source, target = piece.at[:, :, :, rows, :], scratch
        else:
            place = scratch.at[spots[at], spots[GROUPS] if core == 0 else 1 - spots[GROUPS]]
            source, target = (
                (piece.at[:, rows, :], place) if x is None else (piece.at[rows, :], place.at[x])
            )
        copy = pltpu.make_async_copy(source, target, arrived.at[n])
        copy.start()
        copies.setdefault(at or 0, []).append(copy)
    return copies


def wait_group(copies, at):
    for copy in copies.get(at, ()):
        copy.wait()


def group_weight(scratch, spot, depth, start, count):
    columns = []
    for group in range(count):
        part = scratch[spot, :, :, start + group * depth : start + (group + 1) * depth, :]
        columns.append(part.reshape(BANDS * depth, LANES))
    return jnp.concatenate(columns, axis=1)


def attend_kernel(layout, spots, normed, bias, *refs):
    pieces = refs[: len(layout)]
    attended, scratch, projected, arrived = refs[len(layout) :]
    width = normed.shape[1]
    depth = width // BANDS
    per = scratch.shape[3] // depth
    copies = start_loads(spots, pieces, layout, scratch, arrived, slice(None))
    for at in range(GROUPS):
        wait_group(copies, at)
        spot = spots[at]
        part = dot(normed[...], group_weight(scratch, spot, depth, 0, per)).astype(BF16)
        for group in range(per):
            projected[spot * per + group] = part[:, group * LANES : (group + 1) * LANES]

    pairs = width // LANES
    scale = BF16(1.0 / math.sqrt(width // HEADS))
    for pair in range(pairs):
        for block in range(bias.shape[0]):
            at = block * HALF
            attended[at : at + HALF, pair * LANES : (pair + 1) * LANES] = pair_attend(
                projected[pair, at + HALF : at + 2 * HALF, :] * scale,
                projected[pairs + pair, at : at + 3 * HALF, :],
                projected[2 * pairs + pair, at : at + 3 * HALF, :],
                bias[block],
                lambda weights: weights,
            )


SMEM = pl.BlockSpec(memory_space=pltpu.SMEM)
VMEM_SPEC = pl.BlockSpec(memory_space=pltpu.VMEM)
ANY = pl.BlockSpec(memory_space=pl.ANY)


def attend(spots, normed, bias, pieces, layout):
    rows, width = normed.shape
    tok = rows - 2 * HALF
    height = pieces[0].shape[-2]
    per = height * BANDS // width
    return pl.pallas_call(
        functools.partial(attend_kernel, layout),
        out_shape=jax.ShapeDtypeStruct((tok, width), BF16),
        in_specs=[SMEM, VMEM_SPEC, VMEM_SPEC] + [ANY] * len(pieces),
        out_specs=VMEM_SPEC,
        scratch_shapes=[
            pltpu.VMEM((GROUPS, 2, 2, height, LANES), BF16),
            pltpu.VMEM((GROUPS * per, rows, LANES), BF16),
            pltpu.SemaphoreType.DMA((len(pieces),)),
        ],
        compiler_params=params(),
        cost_estimate=pl.CostEstimate(
            flops=6_000_000_000, bytes_accessed=9_000_000, transcendentals=2_000_000
        ),
        name="attend",
    )(spots, normed, bias, *pieces)


def mix_kernel(layout, spots, states, attended, gain, ids, *refs):
    pieces = refs[: len(layout)]
    decoded, found, mixed, scratch, arrived = refs[len(layout) :]
    width = states.shape[1]
    depth = width // BANDS
    copies = start_loads(spots, pieces, layout, scratch, arrived, slice(0, depth))
    inputs = attended[...]
    inputs = jnp.concatenate(
        [inputs[:, band * depth : (band + 1) * depth] for band in CHUNKS], axis=1
    )
    for at in range(GROUPS):
        wait_group(copies, at)
        spot = spots[at]
        columns = pl.ds(pl.multiple_of(spot * LANES, LANES), LANES)
        total = dot(inputs, group_weight(scratch, spot, depth, 0, 1))
        mixed[:, columns] = (states[:, columns].astype(F32) + total).astype(BF16)
    rows = layer_norm(mixed[...], gain[...])
    decoded[...] = rows
    place = lax.broadcasted_iota(jnp.int32, (ids.shape[0], rows.shape[0]), 1)
    pick = (ids[...] == place).astype(BF16)
    found[...] = dot(pick, rows).astype(BF16)


def mix(spots, states, attended, gain, ids, pieces, layout):
    tok, width = states.shape
    return pl.pallas_call(
        functools.partial(mix_kernel, layout),
        out_shape=(
            jax.ShapeDtypeStruct((tok, width), BF16),
            jax.ShapeDtypeStruct((ids.shape[0], width), BF16),
        ),
        in_specs=[SMEM] + [VMEM_SPEC] * 4 + [ANY] * len(pieces),
        out_specs=(VMEM_SPEC, VMEM_SPEC),
        scratch_shapes=[
            pltpu.VMEM((tok, width), BF16),
            pltpu.VMEM((GROUPS, 2, 2, width // BANDS, LANES), BF16),
            pltpu.SemaphoreType.DMA((len(pieces),)),
        ],
        compiler_params=params(),
        cost_estimate=pl.CostEstimate(
            flops=600_000_000, bytes_accessed=4_000_000, transcendentals=0
        ),
        name="mix",
    )(spots, states, attended, gain, ids, *pieces)


def chunked(values, depth):
    return jnp.concatenate([values[:, b * depth : (b + 1) * depth] for b in CHUNKS], axis=1)


def keys_values_kernel(layout, spots, decoded, *refs):
    pieces = refs[: len(layout)]
    out, scratch, arrived = refs[len(layout) :]
    depth = decoded.shape[1] // BANDS
    per = scratch.shape[3] // depth
    copies = start_loads(
        spots, pieces, layout, scratch, arrived, slice(depth, depth + scratch.shape[3])
    )
    inputs = chunked(decoded[...], depth)
    for at in range(GROUPS):
        wait_group(copies, at)
        spot = spots[at]
        total = dot(inputs, group_weight(scratch, spot, depth, 0, per)).astype(BF16)
        for group in range(per):
            out[spot * per + group] = total[:, group * LANES : (group + 1) * LANES]


def keys_values(spots, decoded, pieces, layout):
    tok, width = decoded.shape
    height = 2 * width // GROUPS // LANES * (width // BANDS)
    return pl.pallas_call(
        functools.partial(keys_values_kernel, layout),
        out_shape=jax.ShapeDtypeStruct((2 * width // LANES, tok, LANES), BF16),
        in_specs=[SMEM, VMEM_SPEC] + [ANY] * len(pieces),
        out_specs=VMEM_SPEC,
        scratch_shapes=[
            pltpu.VMEM((GROUPS, 2, 2, height, LANES), BF16),
            pltpu.SemaphoreType.DMA((len(pieces),)),
        ],
        compiler_params=params(),
        cost_estimate=pl.CostEstimate(
            flops=1_100_000_000, bytes_accessed=6_000_000, transcendentals=0
        ),
        name="keys_values",
    )(spots, decoded, *pieces)


def decode_kernel(layout, each, spots, queries, local_rows, fetched, multiplicity, *refs):
    pieces = refs[: len(layout)]
    fields, scratch, table, arrived = refs[len(layout) :]
    points, width = queries.shape
    depth = width // BANDS
    count = fetched.shape[0]
    per = 2 * width // GROUPS // LANES
    skipped = depth
    kept = scratch.shape[3]
    copies = start_loads(spots, pieces, layout, scratch, arrived, slice(skipped, skipped + kept))
    inputs = chunked(fetched[...], depth)
    padding = jnp.zeros((table.shape[1] - count, LANES), BF16)
    for at in range(GROUPS):
        wait_group(copies, at)
        spot = spots[at]
        total = dot(inputs, group_weight(scratch, spot, depth, 0, per)).astype(BF16)
        for group in range(per):
            table[spot * per + group, :count, :] = total[:, group * LANES : (group + 1) * LANES]
            if table.shape[1] > count:
                table[spot * per + group, count:, :] = padding

    pairs = width // LANES
    scale = BF16(1.0 / math.sqrt(width // HEADS))
    times = multiplicity[...]
    bias = jnp.where(times > 0, 0.0, NEG)
    both = jnp.concatenate([times, times], axis=0)
    rows = []
    for pair in range(pairs):
        rows.append(
            pair_attend(
                queries[:, pair * LANES : (pair + 1) * LANES] * scale,
                jnp.concatenate([local_rows[pair], table[pair]], axis=0),
                jnp.concatenate([local_rows[pairs + pair], table[pairs + pair]], axis=0),
                bias,
                lambda weights: weights * both,
            )
        )
    gridded = jnp.concatenate(rows, axis=1)
    start = per * depth
    halves = depth // LANES
    height = (kept - start) // halves
    padded = jnp.zeros((GROUPS * height, points), F32)
    for chunk, band in enumerate(CHUNKS):
        for half in range(halves):
            at = start + half * height
            weight = scratch[:, chunk // 2, chunk % 2, at : at + height, :]
            first = band * depth + half * LANES
            padded += dot_nt(
                weight.reshape(GROUPS * height, LANES), gridded[:, first : first + LANES]
            )
    parts = [padded[group * height : group * height + each] for group in range(GROUPS)]
    fields[...] = jnp.concatenate(parts, axis=0).astype(BF16)


def decode(spots, queries, local_rows, fetched, multiplicity, pieces, layout, outputs):
    points, width = queries.shape
    tok = local_rows.shape[1]
    height = pieces[0].shape[-2] - width // BANDS
    remote = multiplicity.shape[1] - tok
    return pl.pallas_call(
        functools.partial(decode_kernel, layout, outputs // GROUPS),
        out_shape=jax.ShapeDtypeStruct((outputs, points), BF16),
        in_specs=[SMEM] + [VMEM_SPEC] * 4 + [ANY] * len(pieces),
        out_specs=VMEM_SPEC,
        scratch_shapes=[
            pltpu.VMEM((GROUPS, 2, 2, height, LANES), BF16),
            pltpu.VMEM((2 * width // LANES, remote, LANES), BF16),
            pltpu.SemaphoreType.DMA((len(pieces),)),
        ],
        compiler_params=params(),
        cost_estimate=pl.CostEstimate(
            flops=2_000_000_000, bytes_accessed=8_000_000, transcendentals=2_000_000
        ),
        name="decode",
    )(spots, queries, local_rows, fetched, multiplicity, *pieces)


def stacked(*weights):
    parts = []
    for weight in weights:
        for at in range(0, weight.shape[-1], LANES):
            parts.append(weight[..., at : at + LANES])
    return jnp.concatenate(parts, axis=-2)


def ring_pieces(block, band):
    swap_x = [(i, i ^ 2) for i in range(BANDS)]
    swap_core = [(i, i ^ 1) for i in range(BANDS)]
    onward = [(RING[i], RING[(i + 1) % GROUPS]) for i in range(GROUPS)]
    back = [(b, a) for a, b in onward]
    other = lax.ppermute(block, "band", swap_x)
    low = band < 2
    own = jnp.stack([jnp.where(low, block, other), jnp.where(low, other, block)])
    pieces, layout = [], []

    def add(piece, at, x=None):
        pieces.extend([piece, lax.ppermute(piece, "band", swap_core)])
        layout.extend([(at, 0, x), (at, 1, x)])

    add(own, 0)
    ahead = behind = own
    half = GROUPS // 2
    for step in range(1, half):
        ahead = lax.ppermute(ahead, "seq", onward)
        behind = lax.ppermute(behind, "seq", back)
        add(ahead, step)
        add(behind, GROUPS - step)
    add(lax.ppermute(ahead[0], "seq", onward), half, 0)
    add(lax.ppermute(behind[1], "seq", back), half, 1)
    return pieces, tuple(layout)


def gather_weights(w_qkv, w_out, w_kv, w_final):
    count = (lax.axis_size("seq"), lax.axis_size("band"))
    seq, band = lax.axis_index("seq"), lax.axis_index("band")
    each = w_final.shape[1] * count[0] // GROUPS
    height = -(-each // 16) * 16
    if count == (GROUPS, BANDS):
        final = jnp.pad(w_final.T, ((0, height - each), (0, 0)))
        qkv, layout = ring_pieces(stacked(w_qkv), band)
        rest, _ = ring_pieces(stacked(w_out, w_kv, final), band)
        table = np.zeros((GROUPS, GROUPS), np.int32)
        for i in range(GROUPS):
            for step in range(GROUPS):
                table[RING[i], step] = RING[(i - step) % GROUPS]
        spots = jnp.concatenate([jnp.asarray(table)[seq], (band % 2).astype(jnp.int32)[None]])
        return spots, qkv, rest, layout

    depth = w_qkv.shape[0] * count[1] // BANDS

    def blocks(weight):
        weight = lax.all_gather(weight, "seq", axis=1, tiled=True)
        weight = lax.all_gather(weight, "band", axis=0, tiled=True)
        columns = weight.shape[1] // GROUPS
        weight = weight.reshape(2, 2, depth, GROUPS, columns)
        return weight.transpose(3, 1, 0, 2, 4)

    final = jnp.pad(
        blocks(w_final).swapaxes(-1, -2), ((0, 0),) * 3 + ((0, height - each), (0, 0))
    )
    spots = jnp.concatenate([jnp.arange(GROUPS, dtype=jnp.int32), jnp.zeros((1,), jnp.int32)])
    qkv = [stacked(blocks(w_qkv))]
    rest = [stacked(blocks(w_out), blocks(w_kv), final)]
    return spots, qkv, rest, ((None, 0, None),)


def local(
    tokens, ln_gain, w_qkv, w_out, dec_gain, w_kv, w_final, reach, grid_query, neighbours, counts
):
    states = tokens[0]
    tok, width = states.shape
    shards = lax.axis_size("seq")
    place = lax.axis_index("seq").astype(jnp.int32).reshape(1)
    outputs = w_final.shape[1] * shards
    up = [(i, i + 1) for i in range(shards - 1)]
    down = [(i + 1, i) for i in range(shards - 1)]
    spots, qkv, rest, layout = gather_weights(w_qkv, w_out, w_kv, w_final)
    left = lax.ppermute(states[tok - HALF :], "seq", up)
    right = lax.ppermute(states[:HALF], "seq", down)
    normed, bias, multiplicity, requested = prepare(
        tok * shards, place, left, states, right, ln_gain.reshape(1, width),
        reach.reshape(tok, 1), neighbours, counts.reshape(-1, 1), shards,
    )
    requested = requested[:, : shards * C].reshape(shards, C)
    wanted = lax.all_to_all(requested, "seq", split_axis=0, concat_axis=0, tiled=True)
    attended = attend(spots, normed, bias, qkv, layout)
    decoded, found = mix(
        spots, states, attended, dec_gain.reshape(1, width), wanted.reshape(shards * C, 1),
        rest, layout,
    )
    fetched = lax.all_to_all(
        found.reshape(shards, C, width), "seq", split_axis=0, concat_axis=0, tiled=True
    )
    local_rows = keys_values(spots, decoded, rest, layout)
    fields = decode(
        spots, grid_query[0], local_rows, fetched.reshape(shards * C, width), multiplicity,
        rest, layout, outputs,
    )
    return fields[None]


def solution(mesh):
    return jax.shard_map(
        local,
        mesh=mesh,
        in_specs=(
            P("band", "seq", None),
            P(),
            P("band", "seq"),
            P("band", "seq"),
            P(),
            P("band", "seq"),
            P("band", "seq"),
            P("seq"),
            P("band", "seq", None),
            P("seq", None),
            P("seq"),
        ),
        out_specs=P("band", None, "seq"),
        check_vma=False,
    )
```

```python
import functools
import math

import jax
import jax.numpy as jnp
import numpy as np
from jax import lax
from jax.experimental import pallas as pl
from jax.experimental.pallas import tpu as pltpu
from jax.sharding import PartitionSpec as P

HEADS = 16
HALF = 128
C = 12
SLOTS = 16
EPSILON = 1e-05
NEG = -1e30
LANES = 128
GROUPS = 8
BANDS = 4
CHUNKS = (0, 2, 1, 3)
RING = (0, 2, 4, 6, 7, 5, 3, 1)
VMEM = 56 * 1024 * 1024
F32 = jnp.float32
BF16 = jnp.bfloat16


def dot(a, b):
    return jnp.dot(a, b, preferred_element_type=F32)


def dot_nt(a, b):
    return lax.dot_general(a, b, (((1,), (1,)), ((), ())), preferred_element_type=F32)


def layer_norm(values, gain):
    values = values.astype(F32)
    centred = values - jnp.mean(values, axis=-1, keepdims=True)
    spread = jnp.mean(centred * centred, axis=-1, keepdims=True)
    return (centred * lax.rsqrt(spread + EPSILON) * gain).astype(BF16)


def params(**more):
    return pltpu.CompilerParams(vmem_limit_bytes=VMEM, **more)


def full_spec(shape):
    return pl.BlockSpec(shape, lambda *_: (0,) * len(shape))


def prepare_kernel(
    total, place, left, own, right, gain, reach, neighbours, counts, low, rank, tri,
    normed, bias, multiplicity, requested,
):
    tok = own.shape[0]
    depth = own.shape[1] // BANDS
    for at, part in ((0, left), (HALF, own), (HALF + tok, right)):
        rows = layer_norm(part[...], gain[...])
        for chunk, band in enumerate(CHUNKS):
            normed[at : at + part.shape[0], chunk * depth : (chunk + 1) * depth] = rows[
                :, band * depth : (band + 1) * depth
            ]

    me = place[0]
    first = me * tok
    span = 3 * HALF
    row = lax.broadcasted_iota(jnp.int32, (HALF, span), 0)
    col = lax.broadcasted_iota(jnp.int32, (HALF, span), 1)
    away = jnp.abs(row + HALF - col)
    for block in range(tok // HALF):
        key = first + (block - 1) * HALF + col
        allowed = (away <= reach[block * HALF : (block + 1) * HALF, :]) & (key >= 0) & (key < total)
        bias[block] = jnp.where(allowed, 0.0, NEG)

    points, slots = neighbours.shape
    ids = neighbours[...]
    used = counts[...]
    mesh = lax.broadcasted_iota(jnp.int32, (points, tok), 1) + first
    here = jnp.zeros((points, tok), F32)
    for slot in range(slots):
        here += ((ids[:, slot : slot + 1] == mesh) & (slot < used)).astype(F32)
    multiplicity[:, :tok] = here

    start = low[...]
    elsewhere = start != first
    hits = []
    for slot in range(slots):
        which = ids[:, slot : slot + 1]
        hits.append(
            ((which >= start) & (which < start + tok) & (slot < used) & elsewhere).astype(F32)
        )
    running = dot(tri[...], sum(hits).astype(BF16))
    order = rank[...]
    asked = jnp.zeros(requested.shape, F32)
    there = jnp.zeros(hits[0].shape, F32)
    for slot in range(slots):
        mine = jnp.where(running == order, hits[slot], 0.0)
        there += mine
        offset = (ids[:, slot : slot + 1] - start).astype(F32)
        asked += jnp.sum(jnp.where(mine > 0, offset, 0.0), axis=0, keepdims=True)
        running += hits[slot]
    multiplicity[:, tok:] = there
    requested[...] = asked.astype(BF16)


def prepare(total, place, left, own, right, gain, reach, neighbours, counts, shards):
    tok, width = own.shape
    points = neighbours.shape[0]
    remote = shards * SLOTS
    column = np.arange(remote)
    low = (column // SLOTS * tok).astype(np.int32)[None]
    rank = (column % SLOTS).astype(np.float32)[None]
    tri = np.tril(np.ones((points, points), np.float32), -1).astype(BF16)
    operands = (left, own, right, gain, reach, neighbours, counts, low, rank, tri)
    outs = (
        jax.ShapeDtypeStruct((tok + 2 * HALF, width), BF16),
        jax.ShapeDtypeStruct((tok // HALF, HALF, 3 * HALF), F32),
        jax.ShapeDtypeStruct((points, tok + remote), F32),
        jax.ShapeDtypeStruct((1, remote), BF16),
    )
    return pl.pallas_call(
        functools.partial(prepare_kernel, total),
        out_shape=outs,
        in_specs=[pl.BlockSpec(memory_space=pltpu.SMEM)]
        + [pl.BlockSpec(memory_space=pltpu.VMEM)] * len(operands),
        out_specs=[pl.BlockSpec(memory_space=pltpu.VMEM)] * len(outs),
        compiler_params=params(),
        cost_estimate=pl.CostEstimate(flops=20_000_000, bytes_accessed=4_000_000, transcendentals=0),
        name="prepare",
    )(place, *operands)


def pair_attend(queries, keys, values, bias, weights_of):
    rows = queries.shape[0]
    lane = lax.broadcasted_iota(jnp.int32, (rows, LANES), 1)
    first = lane < LANES // 2
    zero = jnp.zeros_like(queries)
    both = jnp.concatenate(
        [jnp.where(first, queries, zero), jnp.where(first, zero, queries)], axis=0
    )
    scores = dot_nt(both, keys)
    scores = scores + jnp.concatenate([bias, bias], axis=0)
    top = jnp.max(scores, axis=-1, keepdims=True)
    weights = weights_of(jnp.exp(scores - top)).astype(BF16)
    summed = dot(weights, jnp.concatenate([values, jnp.ones_like(values)], axis=1))
    share = summed[:, :LANES] / summed[:, LANES:]
    return jnp.where(first, share[:rows], share[rows:]).astype(BF16)


def start_loads(spots, pieces, layout, scratch, arrived, rows):
    copies = {}
    for n, (piece, (at, core, x)) in enumerate(zip(pieces, layout)):
        if at is None:
            source, target = piece.at[:, :, :, rows, :], scratch
        else:
            place = scratch.at[spots[at], spots[GROUPS] if core == 0 else 1 - spots[GROUPS]]
            source, target = (
                (piece.at[:, rows, :], place) if x is None else (piece.at[rows, :], place.at[x])
            )
        copy = pltpu.make_async_copy(source, target, arrived.at[n])
        copy.start()
        copies.setdefault(at or 0, []).append(copy)
    return copies


def wait_group(copies, at):
    for copy in copies.get(at, ()):
        copy.wait()


def group_weight(scratch, spot, depth, start, count):
    columns = []
    for group in range(count):
        part = scratch[spot, :, :, start + group * depth : start + (group + 1) * depth, :]
        columns.append(part.reshape(BANDS * depth, LANES))
    return jnp.concatenate(columns, axis=1)


SMEM = pl.BlockSpec(memory_space=pltpu.SMEM)
VMEM_SPEC = pl.BlockSpec(memory_space=pltpu.VMEM)
ANY = pl.BlockSpec(memory_space=pl.ANY)


def project_kernel(layout, first, spots, normed, *refs):
    pieces = refs[: len(layout)]
    out, made, sent = refs[-3:]
    depth = normed.shape[1] // BANDS
    ats = sorted({at for at, _, _ in layout})
    core = spots[GROUPS]
    copies = []
    for n, at in enumerate(ats):
        total = None
        for piece, (to, other, x) in zip(pieces, layout):
            if to != at:
                continue
            start = (1 - core if other else core) * (2 * depth)
            count = 2 * depth
            weight = piece[...]
            if x is not None:
                start, count, weight = start + x * depth, depth, weight[None]
            per = weight.shape[1] // depth
            weight = jnp.concatenate(
                [
                    weight[:, g * depth : (g + 1) * depth].reshape(count, LANES)
                    for g in range(per)
                ],
                axis=1,
            )
            part = dot(normed[:, pl.ds(pl.multiple_of(start, depth), count)], weight)
            total = part if total is None else total + part
        total = total.astype(BF16)
        for group in range(per):
            made[n, group] = total[:, group * LANES : (group + 1) * LANES]
        copy = pltpu.make_async_copy(
            made.at[n], out.at[pl.ds(spots[at] * per, per)], sent.at[n]
        )
        copy.start()
        copies.append(copy)
    for copy in copies:
        copy.wait()


def project(spots, normed, pieces, before):
    rows, width = normed.shape
    layout = tuple(place for _, place in pieces)
    arrays = [array for array, _ in pieces]
    per = arrays[0].shape[-2] * BANDS // width
    count = len({at for at, _, _ in layout})
    shape = jax.ShapeDtypeStruct((GROUPS * per, rows, LANES), BF16)
    more = [] if before is None else [before]
    return pl.pallas_call(
        functools.partial(project_kernel, layout, before is None),
        out_shape=shape,
        in_specs=[SMEM] + [VMEM_SPEC] * (1 + len(arrays)) + [ANY] * len(more),
        out_specs=ANY,
        scratch_shapes=[
            pltpu.VMEM((count, per, rows, LANES), BF16),
            pltpu.SemaphoreType.DMA((count,)),
        ],
        input_output_aliases={2 + len(arrays): 0} if more else {},
        compiler_params=params(),
        cost_estimate=pl.CostEstimate(
            flops=2 * rows * width * per * LANES * count,
            bytes_accessed=(1 + 2 * count) * rows * width * 2,
            transcendentals=0,
        ),
        name="project",
    )(spots, normed, *arrays, *more)


def attend_kernel(queries, keys, values, bias, attended):
    scale = BF16(1.0 / math.sqrt(LANES // 2))
    for block in range(bias.shape[0]):
        at = block * HALF
        attended[at : at + HALF, :] = pair_attend(
            queries[0, at + HALF : at + 2 * HALF, :] * scale,
            keys[0, at : at + 3 * HALF, :],
            values[0, at : at + 3 * HALF, :],
            bias[block],
            lambda weights: weights,
        )


def attend(projected, bias, first, count):
    groups, rows, _ = projected.shape
    tok = rows - 2 * HALF
    pairs = groups // 3

    def part(which):
        return pl.BlockSpec((1, rows, LANES), lambda s: (which * pairs + first + s, 0, 0))

    return pl.pallas_call(
        attend_kernel,
        grid=(count,),
        out_shape=jax.ShapeDtypeStruct((tok, count * LANES), BF16),
        in_specs=[part(0), part(1), part(2), full_spec(bias.shape)],
        out_specs=pl.BlockSpec((tok, LANES), lambda s: (0, s)),
        compiler_params=params(),
        cost_estimate=pl.CostEstimate(
            flops=300_000_000 * count, bytes_accessed=500_000 * count, transcendentals=200_000 * count
        ),
        name="attend",
    )(projected, projected, projected, bias)


def picked_rows(place, ids, spots, rows, asked, arrived):
    tok = rows.shape[0]
    if spots is None:
        which = ids[...]
    else:
        for at in range(GROUPS):
            asked[pl.ds(spots[at] * SLOTS, SLOTS), :] = jnp.broadcast_to(
                arrived[at, 0:1, :].astype(F32), (SLOTS, LANES)
            )
        count = GROUPS * SLOTS
        lane = lax.broadcasted_iota(jnp.int32, (count, LANES), 1)
        slot = lax.broadcasted_iota(jnp.int32, (count, LANES), 0) % SLOTS
        mine = jnp.where(lane == place[0] * SLOTS + slot, asked[...], 0.0)
        which = jnp.sum(mine, axis=1, keepdims=True).astype(jnp.int32)
    here = lax.broadcasted_iota(jnp.int32, (which.shape[0], tok), 1)
    return dot((which == here).astype(BF16), rows).astype(BF16)


def mix_kernel(layout, riding, place, spots, states, gain, *refs):
    attended, refs = refs[:2], refs[2:]
    ids = None
    if not riding:
        ids, refs = refs[0], refs[1:]
    pieces = refs[: len(layout)]
    decoded, found, mixed, scratch, asked, notes, arrived, noted = refs[len(layout) :]
    width = states.shape[1]
    depth = width // BANDS
    copies = start_loads(spots, pieces, layout, scratch, arrived, slice(0, depth))
    reads = []
    if riding:
        for n, (piece, (at, core, x)) in enumerate(zip(pieces, layout)):
            if core == 0 and x in (None, 0):
                end = piece.shape[-2]
                source = piece.at[0] if x is None else piece
                reads.append(
                    pltpu.make_async_copy(
                        source.at[end - SLOTS : end, :], notes.at[at], noted.at[at]
                    )
                )
                reads[-1].start()
    inputs = chunked(jnp.concatenate([part[...] for part in attended], axis=1), depth)
    for at in range(GROUPS):
        wait_group(copies, at)
        spot = spots[at]
        columns = pl.ds(pl.multiple_of(spot * LANES, LANES), LANES)
        total = dot(inputs, group_weight(scratch, spot, depth, 0, 1))
        mixed[:, columns] = (states[:, columns].astype(F32) + total).astype(BF16)
    for read in reads:
        read.wait()
    rows = layer_norm(mixed[...], gain[...])
    decoded[...] = rows
    found[...] = picked_rows(place, ids, spots if riding else None, rows, asked, notes)


def mix(place, spots, states, attended, gain, ids, pieces, layout, shards):
    tok, width = states.shape
    more = [] if ids is None else [ids]
    return pl.pallas_call(
        functools.partial(mix_kernel, layout, ids is None),
        out_shape=(
            jax.ShapeDtypeStruct((tok, width), BF16),
            jax.ShapeDtypeStruct((shards * SLOTS, width), BF16),
        ),
        in_specs=[SMEM, SMEM] + [VMEM_SPEC] * (4 + len(more)) + [ANY] * len(pieces),
        out_specs=(VMEM_SPEC, VMEM_SPEC),
        scratch_shapes=[
            pltpu.VMEM((tok, width), BF16),
            pltpu.VMEM((GROUPS, 2, 2, width // BANDS, LANES), BF16),
            pltpu.VMEM((GROUPS * SLOTS, LANES), F32),
            pltpu.VMEM((GROUPS, SLOTS, LANES), BF16),
            pltpu.SemaphoreType.DMA((len(pieces),)),
            pltpu.SemaphoreType.DMA((GROUPS,)),
        ],
        compiler_params=params(),
        cost_estimate=pl.CostEstimate(
            flops=600_000_000, bytes_accessed=4_000_000, transcendentals=0
        ),
        name="mix",
    )(place, spots, states, gain, *attended, *more, *pieces)


def chunked(values, depth):
    return jnp.concatenate([values[:, b * depth : (b + 1) * depth] for b in CHUNKS], axis=1)


def keys_values_kernel(layout, spots, decoded, *refs):
    pieces = refs[: len(layout)]
    out, scratch, arrived = refs[len(layout) :]
    depth = decoded.shape[1] // BANDS
    per = scratch.shape[3] // depth
    copies = start_loads(
        spots, pieces, layout, scratch, arrived, slice(depth, depth + scratch.shape[3])
    )
    inputs = chunked(decoded[...], depth)
    for at in range(GROUPS):
        wait_group(copies, at)
        spot = spots[at]
        total = dot(inputs, group_weight(scratch, spot, depth, 0, per)).astype(BF16)
        for group in range(per):
            out[spot * per + group] = total[:, group * LANES : (group + 1) * LANES]


def keys_values(spots, decoded, pieces, layout):
    tok, width = decoded.shape
    height = 2 * width // GROUPS // LANES * (width // BANDS)
    return pl.pallas_call(
        functools.partial(keys_values_kernel, layout),
        out_shape=jax.ShapeDtypeStruct((2 * width // LANES, tok, LANES), BF16),
        in_specs=[SMEM, VMEM_SPEC] + [ANY] * len(pieces),
        out_specs=VMEM_SPEC,
        scratch_shapes=[
            pltpu.VMEM((GROUPS, 2, 2, height, LANES), BF16),
            pltpu.SemaphoreType.DMA((len(pieces),)),
        ],
        compiler_params=params(),
        cost_estimate=pl.CostEstimate(
            flops=1_100_000_000, bytes_accessed=6_000_000, transcendentals=0
        ),
        name="keys_values",
    )(spots, decoded, *pieces)


def decode_kernel(layout, each, spots, queries, local_rows, fetched, multiplicity, *refs):
    pieces = refs[: len(layout)]
    fields, scratch, table, arrived = refs[len(layout) :]
    points, width = queries.shape
    depth = width // BANDS
    count = fetched.shape[0]
    per = 2 * width // GROUPS // LANES
    skipped = depth
    kept = scratch.shape[3]
    copies = start_loads(spots, pieces, layout, scratch, arrived, slice(skipped, skipped + kept))
    inputs = chunked(fetched[...], depth)
    padding = jnp.zeros((table.shape[1] - count, LANES), BF16)
    for at in range(GROUPS):
        wait_group(copies, at)
        spot = spots[at]
        total = dot(inputs, group_weight(scratch, spot, depth, 0, per)).astype(BF16)
        for group in range(per):
            table[spot * per + group, :count, :] = total[:, group * LANES : (group + 1) * LANES]
            if table.shape[1] > count:
                table[spot * per + group, count:, :] = padding

    pairs = width // LANES
    scale = BF16(1.0 / math.sqrt(width // HEADS))
    times = multiplicity[...]
    bias = jnp.where(times > 0, 0.0, NEG)
    both = jnp.concatenate([times, times], axis=0)
    rows = []
    for pair in range(pairs):
        rows.append(
            pair_attend(
                queries[:, pair * LANES : (pair + 1) * LANES] * scale,
                jnp.concatenate([local_rows[pair], table[pair]], axis=0),
                jnp.concatenate([local_rows[pairs + pair], table[pairs + pair]], axis=0),
                bias,
                lambda weights: weights * both,
            )
        )
    gridded = jnp.concatenate(rows, axis=1)
    start = per * depth
    halves = depth // LANES
    height = (kept - start - SLOTS) // halves
    padded = jnp.zeros((GROUPS * height, points), F32)
    for chunk, band in enumerate(CHUNKS):
        for half in range(halves):
            at = start + half * height
            weight = scratch[:, chunk // 2, chunk % 2, at : at + height, :]
            first = band * depth + half * LANES
            padded += dot_nt(
                weight.reshape(GROUPS * height, LANES), gridded[:, first : first + LANES]
            )
    parts = [padded[group * height : group * height + each] for group in range(GROUPS)]
    fields[...] = jnp.concatenate(parts, axis=0).astype(BF16)


def decode(spots, queries, local_rows, fetched, multiplicity, pieces, layout, outputs):
    points, width = queries.shape
    tok = local_rows.shape[1]
    height = pieces[0].shape[-2] - width // BANDS
    remote = multiplicity.shape[1] - tok
    return pl.pallas_call(
        functools.partial(decode_kernel, layout, outputs // GROUPS),
        out_shape=jax.ShapeDtypeStruct((outputs, points), BF16),
        in_specs=[SMEM] + [VMEM_SPEC] * 4 + [ANY] * len(pieces),
        out_specs=VMEM_SPEC,
        scratch_shapes=[
            pltpu.VMEM((GROUPS, 2, 2, height, LANES), BF16),
            pltpu.VMEM((2 * width // LANES, remote, LANES), BF16),
            pltpu.SemaphoreType.DMA((len(pieces),)),
        ],
        compiler_params=params(),
        cost_estimate=pl.CostEstimate(
            flops=2_000_000_000, bytes_accessed=8_000_000, transcendentals=2_000_000
        ),
        name="decode",
    )(spots, queries, local_rows, fetched, multiplicity, *pieces)


def stacked(*weights):
    parts = []
    for weight in weights:
        for at in range(0, weight.shape[-1], LANES):
            parts.append(weight[..., at : at + LANES])
    return jnp.concatenate(parts, axis=-2)


def swap_x(block):
    other = lax.ppermute(block, "band", [(i, i ^ 2) for i in range(BANDS)])
    low = lax.axis_index("band") < 2
    return jnp.stack([jnp.where(low, block, other), jnp.where(low, other, block)])


def ring_pieces(own):
    swap_core = [(i, i ^ 1) for i in range(BANDS)]
    onward = [(RING[i], RING[(i + 1) % GROUPS]) for i in range(GROUPS)]
    back = [(b, a) for a, b in onward]
    pieces = []

    def add(piece, at, x=None):
        pieces.append((piece, (at, 0, x)))
        pieces.append((lax.ppermute(piece, "band", swap_core), (at, 1, x)))

    add(own, 0)
    ahead = behind = own
    half = GROUPS // 2
    for step in range(1, half):
        ahead = lax.ppermute(ahead, "seq", onward)
        behind = lax.ppermute(behind, "seq", back)
        add(ahead, step)
        add(behind, GROUPS - step)
    add(lax.ppermute(ahead[0], "seq", onward), half, 0)
    add(lax.ppermute(behind[1], "seq", back), half, 1)
    return pieces


def ring_spots():
    seq, band = lax.axis_index("seq"), lax.axis_index("band")
    table = np.zeros((GROUPS, GROUPS), np.int32)
    for i in range(GROUPS):
        for step in range(GROUPS):
            table[RING[i], step] = RING[(i - step) % GROUPS]
    return jnp.concatenate([jnp.asarray(table)[seq], (band % 2).astype(jnp.int32)[None]])


def whole_pieces(*weights):
    parts = []
    for weight, height in weights:
        weight = lax.all_gather(weight, "seq", axis=1, tiled=True)
        weight = lax.all_gather(weight, "band", axis=0, tiled=True)
        depth, columns = weight.shape[0] // BANDS, weight.shape[1] // GROUPS
        weight = weight.reshape(2, 2, depth, GROUPS, columns).transpose(3, 1, 0, 2, 4)
        if height:
            weight = jnp.pad(
                weight.swapaxes(-1, -2), ((0, 0),) * 3 + ((0, height - columns), (0, 0))
            )
        parts.append(weight)
    block = stacked(*parts)
    if len(weights) > 1:
        block = jnp.pad(block, ((0, 0),) * 3 + ((0, SLOTS), (0, 0)))
    return [(block[at, core], (at, core, None)) for at in range(GROUPS) for core in range(2)]


def local(
    tokens, ln_gain, w_qkv, w_out, dec_gain, w_kv, w_final, reach, grid_query, neighbours, counts
):
    states = tokens[0]
    tok, width = states.shape
    shards, bands = lax.axis_size("seq"), lax.axis_size("band")
    place = lax.axis_index("seq").astype(jnp.int32).reshape(1)
    outputs = w_final.shape[1] * shards
    height = -(-outputs // GROUPS // 16) * 16
    riding = (shards, bands) == (GROUPS, BANDS)
    up = [(i, i + 1) for i in range(shards - 1)]
    down = [(i + 1, i) for i in range(shards - 1)]
    if riding:
        own = swap_x(stacked(w_qkv))
    left = lax.ppermute(states[tok - HALF :], "seq", up)
    right = lax.ppermute(states[:HALF], "seq", down)
    normed, bias, multiplicity, requested = prepare(
        tok * shards, place, left, states, right, ln_gain.reshape(1, width),
        reach.reshape(tok, 1), neighbours, counts.reshape(-1, 1), shards,
    )
    if riding:
        spots = ring_spots()
        qkv = ring_pieces(own)
        final = jnp.pad(w_final.T, ((0, height - w_final.shape[1]), (0, 0)))
        notes = jnp.pad(requested, ((0, SLOTS - 1), (0, 0)))
        block = jnp.concatenate([stacked(w_out, w_kv, final), notes], axis=0)
        block, _ = lax.optimization_barrier((block, qkv[2][0]))
        later = swap_x(block)
        later, _, _ = lax.optimization_barrier((later, qkv[10][0], qkv[12][0]))
        rest = ring_pieces(later)
        ids = None
    else:
        spots = jnp.concatenate([jnp.arange(GROUPS, dtype=jnp.int32), jnp.zeros((1,), jnp.int32)])
        qkv = whole_pieces((w_qkv, 0))
        rest = whole_pieces((w_out, 0), (w_kv, 0), (w_final, height))
        ids = lax.all_to_all(
            requested.reshape(shards, SLOTS).astype(jnp.int32), "seq", 0, 0, tiled=True
        ).reshape(shards * SLOTS, 1)
    projected = None
    for ats in ((0,), (1, 7), (2, 6), (3, 5), (4,)):
        group = [piece for piece in qkv if piece[1][0] in ats]
        projected = project(spots, normed, group, projected)
    half = width // LANES // 2
    attended = [attend(projected, bias, 0, half), attend(projected, bias, half, half)]
    layout = tuple(at for _, at in rest)
    rest = [piece for piece, _ in rest]
    decoded, found = mix(
        place, spots, states, attended, dec_gain.reshape(1, width), ids, rest, layout, shards
    )
    fetched = lax.all_to_all(
        found.reshape(shards, SLOTS, width), "seq", split_axis=0, concat_axis=0, tiled=True
    )
    local_rows = keys_values(spots, decoded, rest, layout)
    fields = decode(
        spots, grid_query[0], local_rows, fetched.reshape(shards * SLOTS, width), multiplicity,
        rest, layout, outputs,
    )
    return fields[None]


def solution(mesh):
    return jax.shard_map(
        local,
        mesh=mesh,
        in_specs=(
            P("band", "seq", None),
            P(),
            P("band", "seq"),
            P("band", "seq"),
            P(),
            P("band", "seq"),
            P("band", "seq"),
            P("seq"),
            P("band", "seq", None),
            P("seq", None),
            P("seq"),
        ),
        out_specs=P("band", None, "seq"),
        check_vma=False,
    )
```

```python
import functools
import math

import jax
import jax.numpy as jnp
import numpy as np
from jax import lax
from jax.experimental import pallas as pl
from jax.experimental.pallas import tpu as pltpu
from jax.sharding import PartitionSpec as P

HEADS = 16
HALF = 128
C = 12
SLOTS = 16
EPSILON = 1e-05
NEG = -1e30
LANES = 128
GROUPS = 8
BANDS = 4
CHUNKS = (0, 2, 1, 3)
RING = (0, 2, 4, 6, 7, 5, 3, 1)
VMEM = 56 * 1024 * 1024
F32 = jnp.float32
BF16 = jnp.bfloat16


def dot(a, b):
    return jnp.dot(a, b, preferred_element_type=F32)


def dot_nt(a, b):
    return lax.dot_general(a, b, (((1,), (1,)), ((), ())), preferred_element_type=F32)


def layer_norm(values, gain):
    values = values.astype(F32)
    centred = values - jnp.mean(values, axis=-1, keepdims=True)
    spread = jnp.mean(centred * centred, axis=-1, keepdims=True)
    return (centred * lax.rsqrt(spread + EPSILON) * gain).astype(BF16)


def params(**more):
    return pltpu.CompilerParams(vmem_limit_bytes=VMEM, **more)


def full_spec(shape):
    return pl.BlockSpec(shape, lambda *_: (0,) * len(shape))


def prepare_kernel(total, place, left, own, right, gain, reach, normed, bias):
    tok = own.shape[0]
    depth = own.shape[1] // BANDS
    for at, part in ((0, left), (HALF, own), (HALF + tok, right)):
        rows = layer_norm(part[...], gain[...])
        for chunk, band in enumerate(CHUNKS):
            normed[at : at + part.shape[0], chunk * depth : (chunk + 1) * depth] = rows[
                :, band * depth : (band + 1) * depth
            ]

    first = place[0] * tok
    span = 3 * HALF
    row = lax.broadcasted_iota(jnp.int32, (HALF, span), 0)
    col = lax.broadcasted_iota(jnp.int32, (HALF, span), 1)
    away = jnp.abs(row + HALF - col)
    for block in range(tok // HALF):
        key = first + (block - 1) * HALF + col
        allowed = (away <= reach[block * HALF : (block + 1) * HALF, :]) & (key >= 0) & (key < total)
        bias[block] = jnp.where(allowed, 0.0, NEG)


def prepare(total, place, left, own, right, gain, reach):
    tok, width = own.shape
    operands = (left, own, right, gain, reach)
    outs = (
        jax.ShapeDtypeStruct((tok + 2 * HALF, width), BF16),
        jax.ShapeDtypeStruct((tok // HALF, HALF, 3 * HALF), F32),
    )
    return pl.pallas_call(
        functools.partial(prepare_kernel, total),
        out_shape=outs,
        in_specs=[pl.BlockSpec(memory_space=pltpu.SMEM)]
        + [pl.BlockSpec(memory_space=pltpu.VMEM)] * len(operands),
        out_specs=[pl.BlockSpec(memory_space=pltpu.VMEM)] * len(outs),
        compiler_params=params(),
        cost_estimate=pl.CostEstimate(flops=20_000_000, bytes_accessed=3_000_000, transcendentals=0),
        name="prepare",
    )(place, *operands)


def tables_kernel(tok, place, neighbours, counts, low, rank, tri, multiplicity, requested):
    first = place[0] * tok
    points, slots = neighbours.shape
    ids = neighbours[...]
    used = counts[...]
    mesh = lax.broadcasted_iota(jnp.int32, (points, tok), 1) + first
    here = jnp.zeros((points, tok), F32)
    for slot in range(slots):
        here += ((ids[:, slot : slot + 1] == mesh) & (slot < used)).astype(F32)
    multiplicity[:, :tok] = here

    start = low[...]
    elsewhere = start != first
    hits = []
    for slot in range(slots):
        which = ids[:, slot : slot + 1]
        hits.append(
            ((which >= start) & (which < start + tok) & (slot < used) & elsewhere).astype(F32)
        )
    running = dot(tri[...], sum(hits).astype(BF16))
    order = rank[...]
    asked = jnp.zeros(requested.shape, F32)
    there = jnp.zeros(hits[0].shape, F32)
    for slot in range(slots):
        mine = jnp.where(running == order, hits[slot], 0.0)
        there += mine
        offset = (ids[:, slot : slot + 1] - start).astype(F32)
        asked += jnp.sum(jnp.where(mine > 0, offset, 0.0), axis=0, keepdims=True)
        running += hits[slot]
    multiplicity[:, tok:] = there
    requested[...] = asked.astype(BF16)


def tables(tok, place, neighbours, counts, shards):
    points = neighbours.shape[0]
    remote = shards * SLOTS
    column = np.arange(remote)
    low = (column // SLOTS * tok).astype(np.int32)[None]
    rank = (column % SLOTS).astype(np.float32)[None]
    tri = np.tril(np.ones((points, points), np.float32), -1).astype(BF16)
    operands = (neighbours, counts, low, rank, tri)
    return pl.pallas_call(
        functools.partial(tables_kernel, tok),
        out_shape=(
            jax.ShapeDtypeStruct((points, tok + remote), F32),
            jax.ShapeDtypeStruct((1, remote), BF16),
        ),
        in_specs=[pl.BlockSpec(memory_space=pltpu.SMEM)]
        + [pl.BlockSpec(memory_space=pltpu.VMEM)] * len(operands),
        out_specs=[pl.BlockSpec(memory_space=pltpu.VMEM)] * 2,
        compiler_params=params(),
        cost_estimate=pl.CostEstimate(flops=20_000_000, bytes_accessed=1_000_000, transcendentals=0),
        name="tables",
    )(place, *operands)


def pair_attend(queries, keys, values, bias, weights_of):
    rows = queries.shape[0]
    lane = lax.broadcasted_iota(jnp.int32, (rows, LANES), 1)
    first = lane < LANES // 2
    zero = jnp.zeros_like(queries)
    both = jnp.concatenate(
        [jnp.where(first, queries, zero), jnp.where(first, zero, queries)], axis=0
    )
    scores = dot_nt(both, keys)
    scores = scores + jnp.concatenate([bias, bias], axis=0)
    top = jnp.max(scores, axis=-1, keepdims=True)
    weights = weights_of(jnp.exp(scores - top)).astype(BF16)
    summed = dot(weights, jnp.concatenate([values, jnp.ones_like(values)], axis=1))
    share = summed[:, :LANES] / summed[:, LANES:]
    return jnp.where(first, share[:rows], share[rows:]).astype(BF16)


def start_loads(spots, pieces, layout, scratch, arrived, rows):
    copies = {}
    for n, (piece, (at, core, x)) in enumerate(zip(pieces, layout)):
        if at is None:
            source, target = piece.at[:, :, :, rows, :], scratch
        else:
            place = scratch.at[spots[at], spots[GROUPS] if core == 0 else 1 - spots[GROUPS]]
            source, target = (
                (piece.at[:, rows, :], place) if x is None else (piece.at[rows, :], place.at[x])
            )
        copy = pltpu.make_async_copy(source, target, arrived.at[n])
        copy.start()
        copies.setdefault(at or 0, []).append(copy)
    return copies


def wait_group(copies, at):
    for copy in copies.get(at, ()):
        copy.wait()


def group_weight(scratch, spot, depth, start, count):
    columns = []
    for group in range(count):
        part = scratch[spot, :, :, start + group * depth : start + (group + 1) * depth, :]
        columns.append(part.reshape(BANDS * depth, LANES))
    return jnp.concatenate(columns, axis=1)


SMEM = pl.BlockSpec(memory_space=pltpu.SMEM)
VMEM_SPEC = pl.BlockSpec(memory_space=pltpu.VMEM)
ANY = pl.BlockSpec(memory_space=pl.ANY)


def project_kernel(layout, first, spots, normed, *refs):
    pieces = refs[: len(layout)]
    out, made, sent = refs[-3:]
    depth = normed.shape[1] // BANDS
    ats = sorted({at for at, _, _ in layout})
    core = spots[GROUPS]
    copies = []
    for n, at in enumerate(ats):
        total = None
        for piece, (to, other, x) in zip(pieces, layout):
            if to != at:
                continue
            start = (1 - core if other else core) * (2 * depth)
            count = 2 * depth
            weight = piece[...]
            if x is not None:
                start, count, weight = start + x * depth, depth, weight[None]
            per = made.shape[1]
            weight = jnp.concatenate(
                [
                    weight[:, g * depth : (g + 1) * depth].reshape(count, LANES)
                    for g in range(per)
                ],
                axis=1,
            )
            part = dot(normed[:, pl.ds(pl.multiple_of(start, depth), count)], weight)
            total = part if total is None else total + part
        total = total.astype(BF16)
        for group in range(per):
            made[n, group] = total[:, group * LANES : (group + 1) * LANES]
        copy = pltpu.make_async_copy(
            made.at[n], out.at[pl.ds(spots[at] * per, per)], sent.at[n]
        )
        copy.start()
        copies.append(copy)
    for copy in copies:
        copy.wait()


def project(spots, normed, pieces, before):
    rows, width = normed.shape
    layout = tuple(place for _, place in pieces)
    arrays = [array for array, _ in pieces]
    per = 3 * width // LANES // GROUPS
    height = per * (width // BANDS)
    blocks = [full_spec(array.shape[:-2] + (height, LANES)) for array in arrays]
    count = len({at for at, _, _ in layout})
    shape = jax.ShapeDtypeStruct((GROUPS * per, rows, LANES), BF16)
    more = [] if before is None else [before]
    return pl.pallas_call(
        functools.partial(project_kernel, layout, before is None),
        out_shape=shape,
        grid=(1,),
        in_specs=[SMEM, full_spec(normed.shape)] + blocks + [ANY] * len(more),
        out_specs=ANY,
        scratch_shapes=[
            pltpu.VMEM((count, per, rows, LANES), BF16),
            pltpu.SemaphoreType.DMA((count,)),
        ],
        input_output_aliases={2 + len(arrays): 0} if more else {},
        compiler_params=params(),
        cost_estimate=pl.CostEstimate(
            flops=2 * rows * width * per * LANES * count,
            bytes_accessed=(1 + 2 * count) * rows * width * 2,
            transcendentals=0,
        ),
        name="project",
    )(spots, normed, *arrays, *more)


def attend_kernel(queries, keys, values, bias, attended):
    scale = BF16(1.0 / math.sqrt(LANES // 2))
    for block in range(bias.shape[0]):
        at = block * HALF
        attended[at : at + HALF, :] = pair_attend(
            queries[0, at + HALF : at + 2 * HALF, :] * scale,
            keys[0, at : at + 3 * HALF, :],
            values[0, at : at + 3 * HALF, :],
            bias[block],
            lambda weights: weights,
        )


def attend(projected, bias, first, count):
    groups, rows, _ = projected.shape
    tok = rows - 2 * HALF
    pairs = groups // 3

    def part(which):
        return pl.BlockSpec((1, rows, LANES), lambda s: (which * pairs + first + s, 0, 0))

    return pl.pallas_call(
        attend_kernel,
        grid=(count,),
        out_shape=jax.ShapeDtypeStruct((tok, count * LANES), BF16),
        in_specs=[part(0), part(1), part(2), full_spec(bias.shape)],
        out_specs=pl.BlockSpec((tok, LANES), lambda s: (0, s)),
        compiler_params=params(),
        cost_estimate=pl.CostEstimate(
            flops=300_000_000 * count, bytes_accessed=500_000 * count, transcendentals=200_000 * count
        ),
        name="attend",
    )(projected, projected, projected, bias)


def picked_rows(place, ids, spots, rows, asked, arrived):
    tok = rows.shape[0]
    if spots is None:
        which = ids[...]
    else:
        for at in range(GROUPS):
            asked[pl.ds(spots[at] * SLOTS, SLOTS), :] = jnp.broadcast_to(
                arrived[at, 0:1, :].astype(F32), (SLOTS, LANES)
            )
        count = GROUPS * SLOTS
        lane = lax.broadcasted_iota(jnp.int32, (count, LANES), 1)
        slot = lax.broadcasted_iota(jnp.int32, (count, LANES), 0) % SLOTS
        mine = jnp.where(lane == place[0] * SLOTS + slot, asked[...], 0.0)
        which = jnp.sum(mine, axis=1, keepdims=True).astype(jnp.int32)
    here = lax.broadcasted_iota(jnp.int32, (which.shape[0], tok), 1)
    return dot((which == here).astype(BF16), rows).astype(BF16)


def mix_kernel(layout, riding, place, spots, states, gain, *refs):
    attended, refs = refs[:2], refs[2:]
    ids = None
    if not riding:
        ids, refs = refs[0], refs[1:]
    pieces = refs[: len(layout)]
    decoded, found, mixed, scratch, asked, notes, arrived, noted = refs[len(layout) :]
    width = states.shape[1]
    depth = width // BANDS
    start = 3 * width // GROUPS // LANES * depth
    copies = start_loads(spots, pieces, layout, scratch, arrived, slice(start, start + depth))
    reads = []
    if riding:
        for n, (piece, (at, core, x)) in enumerate(zip(pieces, layout)):
            if core == 0 and x in (None, 0):
                end = piece.shape[-2]
                source = piece.at[0] if x is None else piece
                reads.append(
                    pltpu.make_async_copy(
                        source.at[end - SLOTS : end, :], notes.at[at], noted.at[at]
                    )
                )
                reads[-1].start()
    inputs = chunked(jnp.concatenate([part[...] for part in attended], axis=1), depth)
    for at in range(GROUPS):
        wait_group(copies, at)
        spot = spots[at]
        columns = pl.ds(pl.multiple_of(spot * LANES, LANES), LANES)
        total = dot(inputs, group_weight(scratch, spot, depth, 0, 1))
        mixed[:, columns] = (states[:, columns].astype(F32) + total).astype(BF16)
    for read in reads:
        read.wait()
    rows = layer_norm(mixed[...], gain[...])
    decoded[...] = rows
    found[...] = picked_rows(place, ids, spots if riding else None, rows, asked, notes)


def mix(place, spots, states, attended, gain, ids, pieces, layout, shards):
    tok, width = states.shape
    more = [] if ids is None else [ids]
    return pl.pallas_call(
        functools.partial(mix_kernel, layout, ids is None),
        out_shape=(
            jax.ShapeDtypeStruct((tok, width), BF16),
            jax.ShapeDtypeStruct((shards * SLOTS, width), BF16),
        ),
        in_specs=[SMEM, SMEM] + [VMEM_SPEC] * (4 + len(more)) + [ANY] * len(pieces),
        out_specs=(VMEM_SPEC, VMEM_SPEC),
        scratch_shapes=[
            pltpu.VMEM((tok, width), BF16),
            pltpu.VMEM((GROUPS, 2, 2, width // BANDS, LANES), BF16),
            pltpu.VMEM((GROUPS * SLOTS, LANES), F32),
            pltpu.VMEM((GROUPS, SLOTS, LANES), BF16),
            pltpu.SemaphoreType.DMA((len(pieces),)),
            pltpu.SemaphoreType.DMA((GROUPS,)),
        ],
        compiler_params=params(),
        cost_estimate=pl.CostEstimate(
            flops=600_000_000, bytes_accessed=4_000_000, transcendentals=0
        ),
        name="mix",
    )(place, spots, states, gain, *attended, *more, *pieces)


def chunked(values, depth):
    return jnp.concatenate([values[:, b * depth : (b + 1) * depth] for b in CHUNKS], axis=1)


def start_whole(weight, scratch, arrived):
    copies = []
    for at in range(GROUPS):
        copies.append(pltpu.make_async_copy(weight.at[at], scratch.at[at], arrived.at[at]))
        copies[-1].start()
    return copies


def whole_group(scratch, at, depth):
    per = scratch.shape[2] // depth
    columns = [
        scratch[at, :, g * depth : (g + 1) * depth, :].reshape(BANDS * depth, LANES)
        for g in range(per)
    ]
    return jnp.concatenate(columns, axis=1)


def keys_values_kernel(decoded, weight, out, scratch, arrived):
    depth = decoded.shape[1] // BANDS
    per = scratch.shape[2] // depth
    copies = start_whole(weight, scratch, arrived)
    for at in range(GROUPS):
        copies[at].wait()
        total = dot(decoded[...], whole_group(scratch, at, depth)).astype(BF16)
        for group in range(per):
            out[at * per + group] = total[:, group * LANES : (group + 1) * LANES]


def keys_values(decoded, weight):
    tok, width = decoded.shape
    return pl.pallas_call(
        keys_values_kernel,
        out_shape=jax.ShapeDtypeStruct((2 * width // LANES, tok, LANES), BF16),
        in_specs=[VMEM_SPEC, ANY],
        out_specs=VMEM_SPEC,
        scratch_shapes=[pltpu.VMEM(weight.shape, BF16), pltpu.SemaphoreType.DMA((GROUPS,))],
        compiler_params=params(),
        cost_estimate=pl.CostEstimate(
            flops=1_100_000_000, bytes_accessed=6_000_000, transcendentals=0
        ),
        name="keys_values",
    )(decoded, weight)


def decode_kernel(layout, each, spots, queries, local_rows, fetched, multiplicity, weight, *refs):
    pieces = refs[: len(layout)]
    fields, scratch, table, last, arrived, landed = refs[len(layout) :]
    points, width = queries.shape
    depth = width // BANDS
    per = scratch.shape[2] // depth
    copies = start_whole(weight, scratch, arrived)
    end = pieces[0].shape[-2] - SLOTS
    finals = start_loads(
        spots, pieces, layout, last, landed, slice(end - last.shape[3], end)
    )
    for at in range(GROUPS):
        copies[at].wait()
        total = dot(fetched[...], whole_group(scratch, at, depth)).astype(BF16)
        for group in range(per):
            table[at * per + group] = total[:, group * LANES : (group + 1) * LANES]

    pairs = width // LANES
    scale = BF16(1.0 / math.sqrt(width // HEADS))
    times = multiplicity[...]
    bias = jnp.where(times > 0, 0.0, NEG)
    both = jnp.concatenate([times, times], axis=0)
    rows = []
    for pair in range(pairs):
        rows.append(
            pair_attend(
                queries[:, pair * LANES : (pair + 1) * LANES] * scale,
                jnp.concatenate([local_rows[pair], table[pair]], axis=0),
                jnp.concatenate([local_rows[pairs + pair], table[pairs + pair]], axis=0),
                bias,
                lambda weights: weights * both,
            )
        )
    gridded = jnp.concatenate(rows, axis=1)
    for at in range(GROUPS):
        wait_group(finals, at)
    halves = depth // LANES
    height = last.shape[3] // halves
    padded = jnp.zeros((GROUPS * height, points), F32)
    for chunk, band in enumerate(CHUNKS):
        for half in range(halves):
            part = last[:, chunk // 2, chunk % 2, half * height : (half + 1) * height, :]
            first = band * depth + half * LANES
            padded += dot_nt(
                part.reshape(GROUPS * height, LANES), gridded[:, first : first + LANES]
            )
    parts = [padded[group * height : group * height + each] for group in range(GROUPS)]
    fields[...] = jnp.concatenate(parts, axis=0).astype(BF16)


def decode(spots, queries, local_rows, fetched, multiplicity, weight, pieces, layout, outputs):
    points, width = queries.shape
    height = -(-outputs // GROUPS // 16) * 16 * (width // BANDS // LANES)
    return pl.pallas_call(
        functools.partial(decode_kernel, layout, outputs // GROUPS),
        out_shape=jax.ShapeDtypeStruct((outputs, points), BF16),
        in_specs=[SMEM] + [VMEM_SPEC] * 4 + [ANY] * (1 + len(pieces)),
        out_specs=VMEM_SPEC,
        scratch_shapes=[
            pltpu.VMEM(weight.shape, BF16),
            pltpu.VMEM((2 * width // LANES, fetched.shape[0], LANES), BF16),
            pltpu.VMEM((GROUPS, 2, 2, height, LANES), BF16),
            pltpu.SemaphoreType.DMA((GROUPS,)),
            pltpu.SemaphoreType.DMA((len(pieces),)),
        ],
        compiler_params=params(),
        cost_estimate=pl.CostEstimate(
            flops=2_000_000_000, bytes_accessed=8_000_000, transcendentals=2_000_000
        ),
        name="decode",
    )(spots, queries, local_rows, fetched, multiplicity, weight, *pieces)


def stacked(*weights):
    parts = []
    for weight in weights:
        for at in range(0, weight.shape[-1], LANES):
            parts.append(weight[..., at : at + LANES])
    return jnp.concatenate(parts, axis=-2)


def swap_x(block, notes):
    other = lax.ppermute(block, "band", [(i, i ^ 2) for i in range(BANDS)])
    low = lax.axis_index("band") < 2
    halves = [jnp.where(low, block, other), jnp.where(low, other, block)]
    return jnp.stack([jnp.concatenate([half, notes], axis=0) for half in halves])


def ring_pieces(own, work):
    swap_core = [(i, i ^ 1) for i in range(BANDS)]
    onward = [(RING[i], RING[(i + 1) % GROUPS]) for i in range(GROUPS)]
    back = [(b, a) for a, b in onward]
    half = GROUPS // 2
    pieces = []

    def both(piece, at, x=None):
        return [(piece, (at, 0, x)), (lax.ppermute(piece, "band", swap_core), (at, 1, x))]

    gate = done = None
    waiting = both(own, 0)
    ahead = behind = own
    for step in range(1, half + 1):
        if step > 2:
            ahead, behind, gate = lax.optimization_barrier((ahead, behind, gate))
        if step == half:
            ahead = lax.ppermute(ahead[0], "seq", onward)
            behind = lax.ppermute(behind[1], "seq", back)
            arrived = both(ahead, half, 0) + both(behind, half, 1)
        else:
            ahead = lax.ppermute(ahead, "seq", onward)
            behind = lax.ppermute(behind, "seq", back)
            arrived = both(ahead, step) + both(behind, GROUPS - step)
        gate, done = done, work(waiting, done)
        pieces += waiting
        waiting = arrived
    return pieces + waiting, work(waiting, done)


def ring_spots():
    seq, band = lax.axis_index("seq"), lax.axis_index("band")
    table = np.zeros((GROUPS, GROUPS), np.int32)
    for i in range(GROUPS):
        for step in range(GROUPS):
            table[RING[i], step] = RING[(i - step) % GROUPS]
    return jnp.concatenate([jnp.asarray(table)[seq], (band % 2).astype(jnp.int32)[None]])


def whole_pieces(*weights):
    parts = []
    for weight, height in weights:
        weight = lax.all_gather(weight, "seq", axis=1, tiled=True)
        weight = lax.all_gather(weight, "band", axis=0, tiled=True)
        depth, columns = weight.shape[0] // BANDS, weight.shape[1] // GROUPS
        weight = weight.reshape(2, 2, depth, GROUPS, columns).transpose(3, 1, 0, 2, 4)
        if height:
            weight = jnp.pad(
                weight.swapaxes(-1, -2), ((0, 0),) * 3 + ((0, height - columns), (0, 0))
            )
        parts.append(weight)
    return parts


def local(
    tokens, ln_gain, w_qkv, w_out, dec_gain, w_kv, w_final, reach, grid_query, neighbours, counts
):
    states = tokens[0]
    tok, width = states.shape
    shards, bands = lax.axis_size("seq"), lax.axis_size("band")
    place = lax.axis_index("seq").astype(jnp.int32).reshape(1)
    outputs = w_final.shape[1] * shards
    height = -(-outputs // GROUPS // 16) * 16
    riding = (shards, bands) == (GROUPS, BANDS)
    up = [(i, i + 1) for i in range(shards - 1)]
    down = [(i + 1, i) for i in range(shards - 1)]
    if riding:
        kv = lax.all_gather(stacked(w_kv), ("seq", "band"), axis=0, tiled=False)
        kv = kv.reshape((GROUPS, BANDS) + kv.shape[1:])
    left = lax.ppermute(states[tok - HALF :], "seq", up)
    right = lax.ppermute(states[:HALF], "seq", down)
    multiplicity, requested = tables(tok, place, neighbours, counts.reshape(-1, 1), shards)
    normed, bias = prepare(
        tok * shards, place, left, states, right, ln_gain.reshape(1, width), reach.reshape(tok, 1)
    )
    if riding:
        spots = ring_spots()
        final = jnp.pad(w_final.T, ((0, height - w_final.shape[1]), (0, 0)))
        notes = jnp.pad(requested, ((0, SLOTS - 1), (0, 0)))
        own = swap_x(stacked(w_qkv, w_out, final), notes)
        pieces, projected = ring_pieces(
            own, lambda group, before: project(spots, normed, group, before)
        )
        ids = None
    else:
        spots = jnp.concatenate([jnp.arange(GROUPS, dtype=jnp.int32), jnp.zeros((1,), jnp.int32)])
        parts = whole_pieces((w_qkv, 0), (w_out, 0), (w_final, height))
        block = jnp.pad(stacked(*parts), ((0, 0),) * 3 + ((0, SLOTS), (0, 0)))
        pieces = [(block[at, core], (at, core, None)) for at in range(GROUPS) for core in range(2)]
        kv = stacked(whole_pieces((w_kv, 0))[0])
        kv = kv.swapaxes(1, 2).reshape((GROUPS, BANDS) + kv.shape[3:])
        ids = lax.all_to_all(
            requested.reshape(shards, SLOTS).astype(jnp.int32), "seq", 0, 0, tiled=True
        ).reshape(shards * SLOTS, 1)
        projected = None
        for at in range(GROUPS):
            projected = project(spots, normed, pieces[2 * at : 2 * at + 2], projected)
    half = width // LANES // 2
    attended = [attend(projected, bias, 0, half), attend(projected, bias, half, half)]
    layout = tuple(at for _, at in pieces)
    pieces = [piece for piece, _ in pieces]
    decoded, found = mix(
        place, spots, states, attended, dec_gain.reshape(1, width), ids, pieces, layout, shards
    )
    fetched = lax.all_to_all(
        found.reshape(shards, SLOTS, width), "seq", split_axis=0, concat_axis=0, tiled=True
    )
    local_rows = keys_values(decoded, kv)
    fields = decode(
        spots, grid_query[0], local_rows, fetched.reshape(shards * SLOTS, width), multiplicity,
        kv, pieces, layout, outputs,
    )
    return fields[None]


def solution(mesh):
    return jax.shard_map(
        local,
        mesh=mesh,
        in_specs=(
            P("band", "seq", None),
            P(),
            P("band", "seq"),
            P("band", "seq"),
            P(),
            P("band", "seq"),
            P("band", "seq"),
            P("seq"),
            P("band", "seq", None),
            P("seq", None),
            P("seq"),
        ),
        out_specs=P("band", None, "seq"),
        check_vma=False,
    )
```

```python
import functools
import math

import jax
import jax.numpy as jnp
import numpy as np
from jax import lax
from jax.experimental import pallas as pl
from jax.experimental.pallas import tpu as pltpu
from jax.sharding import PartitionSpec as P

HEADS = 16
HALF = 128
C = 12
SLOTS = 16
EPSILON = 1e-05
NEG = -1e30
LANES = 128
GROUPS = 8
BANDS = 4
CHUNKS = (0, 2, 1, 3)
RING = (0, 2, 4, 6, 7, 5, 3, 1)
VMEM = 56 * 1024 * 1024
F32 = jnp.float32
BF16 = jnp.bfloat16


def dot(a, b):
    return jnp.dot(a, b, preferred_element_type=F32)


def dot_nt(a, b):
    return lax.dot_general(a, b, (((1,), (1,)), ((), ())), preferred_element_type=F32)


def layer_norm(values, gain):
    values = values.astype(F32)
    centred = values - jnp.mean(values, axis=-1, keepdims=True)
    spread = jnp.mean(centred * centred, axis=-1, keepdims=True)
    return (centred * lax.rsqrt(spread + EPSILON) * gain).astype(BF16)


def params(**more):
    return pltpu.CompilerParams(vmem_limit_bytes=VMEM, **more)


def full_spec(shape):
    return pl.BlockSpec(shape, lambda *_: (0,) * len(shape))


def prepare_kernel(total, place, left, own, right, gain, reach, normed, bias):
    tok = own.shape[0]
    depth = own.shape[1] // BANDS
    for at, part in ((0, left), (HALF, own), (HALF + tok, right)):
        rows = layer_norm(part[...], gain[...])
        for chunk, band in enumerate(CHUNKS):
            normed[at : at + part.shape[0], chunk * depth : (chunk + 1) * depth] = rows[
                :, band * depth : (band + 1) * depth
            ]

    first = place[0] * tok
    span = 3 * HALF
    row = lax.broadcasted_iota(jnp.int32, (HALF, span), 0)
    col = lax.broadcasted_iota(jnp.int32, (HALF, span), 1)
    away = jnp.abs(row + HALF - col)
    for block in range(tok // HALF):
        key = first + (block - 1) * HALF + col
        allowed = (away <= reach[block * HALF : (block + 1) * HALF, :]) & (key >= 0) & (key < total)
        bias[block] = jnp.where(allowed, 0.0, NEG)


def prepare(total, place, left, own, right, gain, reach):
    tok, width = own.shape
    operands = (left, own, right, gain, reach)
    outs = (
        jax.ShapeDtypeStruct((tok + 2 * HALF, width), BF16),
        jax.ShapeDtypeStruct((tok // HALF, HALF, 3 * HALF), F32),
    )
    return pl.pallas_call(
        functools.partial(prepare_kernel, total),
        out_shape=outs,
        in_specs=[pl.BlockSpec(memory_space=pltpu.SMEM)]
        + [pl.BlockSpec(memory_space=pltpu.VMEM)] * len(operands),
        out_specs=[pl.BlockSpec(memory_space=pltpu.VMEM)] * len(outs),
        compiler_params=params(),
        cost_estimate=pl.CostEstimate(flops=20_000_000, bytes_accessed=3_000_000, transcendentals=0),
        name="prepare",
    )(place, *operands)


def tables_kernel(tok, place, neighbours, counts, low, rank, tri, multiplicity, requested):
    first = place[0] * tok
    points, slots = neighbours.shape
    ids = neighbours[...]
    used = counts[...]
    mesh = lax.broadcasted_iota(jnp.int32, (points, tok), 1) + first
    here = jnp.zeros((points, tok), F32)
    for slot in range(slots):
        here += ((ids[:, slot : slot + 1] == mesh) & (slot < used)).astype(F32)
    multiplicity[:, :tok] = here

    start = low[...]
    elsewhere = start != first
    hits = []
    for slot in range(slots):
        which = ids[:, slot : slot + 1]
        hits.append(
            ((which >= start) & (which < start + tok) & (slot < used) & elsewhere).astype(F32)
        )
    running = dot(tri[...], sum(hits).astype(BF16))
    order = rank[...]
    asked = jnp.zeros(requested.shape, F32)
    there = jnp.zeros(hits[0].shape, F32)
    for slot in range(slots):
        mine = jnp.where(running == order, hits[slot], 0.0)
        there += mine
        offset = (ids[:, slot : slot + 1] - start).astype(F32)
        asked += jnp.sum(jnp.where(mine > 0, offset, 0.0), axis=0, keepdims=True)
        running += hits[slot]
    multiplicity[:, tok:] = there
    requested[...] = asked.astype(BF16)


def tables(tok, place, neighbours, counts, shards):
    points = neighbours.shape[0]
    remote = shards * SLOTS
    column = np.arange(remote)
    low = (column // SLOTS * tok).astype(np.int32)[None]
    rank = (column % SLOTS).astype(np.float32)[None]
    tri = np.tril(np.ones((points, points), np.float32), -1).astype(BF16)
    operands = (neighbours, counts, low, rank, tri)
    return pl.pallas_call(
        functools.partial(tables_kernel, tok),
        out_shape=(
            jax.ShapeDtypeStruct((points, tok + remote), F32),
            jax.ShapeDtypeStruct((1, remote), BF16),
        ),
        in_specs=[pl.BlockSpec(memory_space=pltpu.SMEM)]
        + [pl.BlockSpec(memory_space=pltpu.VMEM)] * len(operands),
        out_specs=[pl.BlockSpec(memory_space=pltpu.VMEM)] * 2,
        compiler_params=params(),
        cost_estimate=pl.CostEstimate(flops=20_000_000, bytes_accessed=1_000_000, transcendentals=0),
        name="tables",
    )(place, *operands)


def pair_attend(queries, keys, values, bias, weights_of):
    rows = queries.shape[0]
    lane = lax.broadcasted_iota(jnp.int32, (rows, LANES), 1)
    first = lane < LANES // 2
    zero = jnp.zeros_like(queries)
    both = jnp.concatenate(
        [jnp.where(first, queries, zero), jnp.where(first, zero, queries)], axis=0
    )
    scores = dot_nt(both, keys)
    scores = scores + jnp.concatenate([bias, bias], axis=0)
    top = jnp.max(scores, axis=-1, keepdims=True)
    weights = weights_of(jnp.exp(scores - top)).astype(BF16)
    summed = dot(weights, jnp.concatenate([values, jnp.ones_like(values)], axis=1))
    share = summed[:, :LANES] / summed[:, LANES:]
    return jnp.where(first, share[:rows], share[rows:]).astype(BF16)


def start_loads(spots, pieces, layout, scratch, arrived, rows):
    copies = {}
    for n, (piece, (at, core)) in enumerate(zip(pieces, layout)):
        place = scratch.at[spots[at]]
        if core is None:
            copy = pltpu.make_async_copy(piece.at[:, :, rows, :], place, arrived.at[n])
        else:
            mine = 1 - spots[GROUPS] if core else spots[GROUPS]
            copy = pltpu.make_async_copy(piece.at[:, rows, :], place.at[mine], arrived.at[n])
        copy.start()
        copies.setdefault(at, []).append(copy)
    return copies


def wait_group(copies, at):
    for copy in copies.get(at, ()):
        copy.wait()


def lanes_of(block, depth, start, count):
    rows = block.shape[0] * block.shape[1] * depth if block.ndim == 4 else block.shape[0] * depth
    columns = [
        block[..., start + g * depth : start + (g + 1) * depth, :].reshape(rows, LANES)
        for g in range(count)
    ]
    return columns[0] if count == 1 else jnp.concatenate(columns, axis=1)


SMEM = pl.BlockSpec(memory_space=pltpu.SMEM)
VMEM_SPEC = pl.BlockSpec(memory_space=pltpu.VMEM)
ANY = pl.BlockSpec(memory_space=pl.ANY)


def project_kernel(layout, spots, normed, *refs):
    pieces = refs[: len(layout)]
    out, made, sent = refs[-3:]
    per = made.shape[1]
    depth = normed.shape[1] // BANDS
    core = spots[GROUPS]
    copies = []
    for n, at in enumerate(sorted({at for at, _ in layout})):
        total = None
        for piece, (to, other) in zip(pieces, layout):
            if to != at:
                continue
            weight = lanes_of(piece[...], depth, 0, per)
            if other is None:
                total = dot(normed[...], weight)
            else:
                start = (1 - core if other else core) * (2 * depth)
                part = dot(normed[:, pl.ds(pl.multiple_of(start, 2 * depth), 2 * depth)], weight)
                total = part if total is None else total + part
        total = total.astype(BF16)
        for group in range(per):
            made[n, group] = total[:, group * LANES : (group + 1) * LANES]
        copy = pltpu.make_async_copy(
            made.at[n], out.at[pl.ds(spots[at] * per, per)], sent.at[n]
        )
        copy.start()
        copies.append(copy)
    for copy in copies:
        copy.wait()


def project(spots, normed, pieces, before):
    rows, width = normed.shape
    layout = tuple(place for _, place in pieces)
    arrays = [array for array, _ in pieces]
    per = 3 * width // LANES // GROUPS
    count = len({at for at, _ in layout})
    more = [] if before is None else [before]
    return pl.pallas_call(
        functools.partial(project_kernel, layout),
        out_shape=jax.ShapeDtypeStruct((GROUPS * per, rows, LANES), BF16),
        in_specs=[SMEM] + [VMEM_SPEC] * (1 + len(arrays)) + [ANY] * len(more),
        out_specs=ANY,
        scratch_shapes=[
            pltpu.VMEM((count, per, rows, LANES), BF16),
            pltpu.SemaphoreType.DMA((count,)),
        ],
        input_output_aliases={2 + len(arrays): 0} if more else {},
        compiler_params=params(),
        cost_estimate=pl.CostEstimate(
            flops=2 * rows * width * per * LANES * count,
            bytes_accessed=(1 + 2 * count) * rows * width * 2,
            transcendentals=0,
        ),
        name="project",
    )(spots, normed, *arrays, *more)


def attend_kernel(queries, keys, values, bias, attended):
    scale = BF16(1.0 / math.sqrt(LANES // 2))
    for block in range(bias.shape[0]):
        at = block * HALF
        attended[at : at + HALF, :] = pair_attend(
            queries[0, at + HALF : at + 2 * HALF, :] * scale,
            keys[0, at : at + 3 * HALF, :],
            values[0, at : at + 3 * HALF, :],
            bias[block],
            lambda weights: weights,
        )


def attend(projected, bias, first, count):
    groups, rows, _ = projected.shape
    tok = rows - 2 * HALF
    pairs = groups // 3

    def part(which):
        return pl.BlockSpec((1, rows, LANES), lambda s: (which * pairs + first + s, 0, 0))

    return pl.pallas_call(
        attend_kernel,
        grid=(count,),
        out_shape=jax.ShapeDtypeStruct((tok, count * LANES), BF16),
        in_specs=[part(0), part(1), part(2), full_spec(bias.shape)],
        out_specs=pl.BlockSpec((tok, LANES), lambda s: (0, s)),
        compiler_params=params(),
        cost_estimate=pl.CostEstimate(
            flops=300_000_000 * count, bytes_accessed=500_000 * count, transcendentals=200_000 * count
        ),
        name="attend",
    )(projected, projected, projected, bias)


def picked_rows(place, ids, spots, rows, asked, arrived):
    tok = rows.shape[0]
    if spots is None:
        which = ids[...]
    else:
        for at in range(GROUPS):
            asked[pl.ds(spots[at] * SLOTS, SLOTS), :] = jnp.broadcast_to(
                arrived[at, 0:1, :].astype(F32), (SLOTS, LANES)
            )
        count = GROUPS * SLOTS
        lane = lax.broadcasted_iota(jnp.int32, (count, LANES), 1)
        slot = lax.broadcasted_iota(jnp.int32, (count, LANES), 0) % SLOTS
        mine = jnp.where(lane == place[0] * SLOTS + slot, asked[...], 0.0)
        which = jnp.sum(mine, axis=1, keepdims=True).astype(jnp.int32)
    here = lax.broadcasted_iota(jnp.int32, (which.shape[0], tok), 1)
    return dot((which == here).astype(BF16), rows).astype(BF16)


def chunked(values, depth):
    return jnp.concatenate([values[:, b * depth : (b + 1) * depth] for b in CHUNKS], axis=1)


def mix_kernel(layout, riding, place, spots, states, gain, *refs):
    attended, refs = refs[:2], refs[2:]
    ids = None
    if not riding:
        ids, refs = refs[0], refs[1:]
    pieces = refs[: len(layout)]
    decoded, found, mixed, scratch, asked, notes, arrived, noted = refs[len(layout) :]
    width = states.shape[1]
    depth = width // BANDS
    copies = start_loads(spots, pieces, layout, scratch, arrived, slice(0, depth))
    reads = []
    if riding:
        for piece, (at, core) in zip(pieces, layout):
            if not core:
                end = piece.shape[-2]
                source = piece.at[0, 0] if core is None else piece.at[0]
                reads.append(
                    pltpu.make_async_copy(
                        source.at[end - SLOTS : end, :], notes.at[at], noted.at[at]
                    )
                )
                reads[-1].start()
    inputs = chunked(jnp.concatenate([part[...] for part in attended], axis=1), depth)
    for at in range(GROUPS):
        wait_group(copies, at)
        spot = spots[at]
        columns = pl.ds(pl.multiple_of(spot * LANES, LANES), LANES)
        total = dot(inputs, lanes_of(scratch[spot], depth, 0, 1))
        mixed[:, columns] = (states[:, columns].astype(F32) + total).astype(BF16)
    for read in reads:
        read.wait()
    rows = chunked(layer_norm(mixed[...], gain[...]), depth)
    decoded[...] = rows
    found[...] = picked_rows(place, ids, spots if riding else None, rows, asked, notes)


def mix(place, spots, states, attended, gain, ids, pieces, layout, shards):
    tok, width = states.shape
    more = [] if ids is None else [ids]
    return pl.pallas_call(
        functools.partial(mix_kernel, layout, ids is None),
        out_shape=(
            jax.ShapeDtypeStruct((tok, width), BF16),
            jax.ShapeDtypeStruct((shards * SLOTS, width), BF16),
        ),
        in_specs=[SMEM, SMEM] + [VMEM_SPEC] * (4 + len(more)) + [ANY] * len(pieces),
        out_specs=(VMEM_SPEC, VMEM_SPEC),
        scratch_shapes=[
            pltpu.VMEM((tok, width), BF16),
            pltpu.VMEM((GROUPS, 2, 2, width // BANDS, LANES), BF16),
            pltpu.VMEM((GROUPS * SLOTS, LANES), F32),
            pltpu.VMEM((GROUPS, SLOTS, LANES), BF16),
            pltpu.SemaphoreType.DMA((len(pieces),)),
            pltpu.SemaphoreType.DMA((GROUPS,)),
        ],
        compiler_params=params(),
        cost_estimate=pl.CostEstimate(
            flops=600_000_000, bytes_accessed=4_000_000, transcendentals=0
        ),
        name="mix",
    )(place, spots, states, gain, *attended, *more, *pieces)


def keys_values_kernel(layout, spots, decoded, *refs):
    pieces = refs[: len(layout)]
    out, scratch, arrived = refs[len(layout) :]
    depth = decoded.shape[1] // BANDS
    per = scratch.shape[3] // depth
    copies = start_loads(
        spots, pieces, layout, scratch, arrived, slice(depth, depth + scratch.shape[3])
    )
    for at in range(GROUPS):
        wait_group(copies, at)
        spot = spots[at]
        total = dot(decoded[...], lanes_of(scratch[spot], depth, 0, per)).astype(BF16)
        for group in range(per):
            out[spot * per + group] = total[:, group * LANES : (group + 1) * LANES]


def keys_values(spots, decoded, pieces, layout):
    tok, width = decoded.shape
    height = 2 * width // GROUPS // LANES * (width // BANDS)
    return pl.pallas_call(
        functools.partial(keys_values_kernel, layout),
        out_shape=jax.ShapeDtypeStruct((2 * width // LANES, tok, LANES), BF16),
        in_specs=[SMEM, VMEM_SPEC] + [ANY] * len(pieces),
        out_specs=VMEM_SPEC,
        scratch_shapes=[
            pltpu.VMEM((GROUPS, 2, 2, height, LANES), BF16),
            pltpu.SemaphoreType.DMA((len(pieces),)),
        ],
        compiler_params=params(),
        cost_estimate=pl.CostEstimate(
            flops=1_100_000_000, bytes_accessed=6_000_000, transcendentals=0
        ),
        name="keys_values",
    )(spots, decoded, *pieces)


def decode_kernel(layout, each, spots, queries, local_rows, fetched, multiplicity, *refs):
    pieces = refs[: len(layout)]
    fields, scratch, table, arrived = refs[len(layout) :]
    points, width = queries.shape
    depth = width // BANDS
    count = fetched.shape[0]
    per = 2 * width // GROUPS // LANES
    skipped = depth
    kept = scratch.shape[3]
    copies = start_loads(spots, pieces, layout, scratch, arrived, slice(skipped, skipped + kept))
    padding = jnp.zeros((table.shape[1] - count, LANES), BF16)
    for at in range(GROUPS):
        wait_group(copies, at)
        spot = spots[at]
        total = dot(fetched[...], lanes_of(scratch[spot], depth, 0, per)).astype(BF16)
        for group in range(per):
            table[spot * per + group, :count, :] = total[:, group * LANES : (group + 1) * LANES]
            if table.shape[1] > count:
                table[spot * per + group, count:, :] = padding

    pairs = width // LANES
    scale = BF16(1.0 / math.sqrt(width // HEADS))
    times = multiplicity[...]
    bias = jnp.where(times > 0, 0.0, NEG)
    both = jnp.concatenate([times, times], axis=0)
    rows = []
    for pair in range(pairs):
        rows.append(
            pair_attend(
                queries[:, pair * LANES : (pair + 1) * LANES] * scale,
                jnp.concatenate([local_rows[pair], table[pair]], axis=0),
                jnp.concatenate([local_rows[pairs + pair], table[pairs + pair]], axis=0),
                bias,
                lambda weights: weights * both,
            )
        )
    gridded = jnp.concatenate(rows, axis=1)
    start = per * depth
    halves = depth // LANES
    height = (kept - start - SLOTS) // halves
    padded = jnp.zeros((GROUPS * height, points), F32)
    for chunk, band in enumerate(CHUNKS):
        for half in range(halves):
            at = start + half * height
            weight = scratch[:, chunk // 2, chunk % 2, at : at + height, :]
            first = band * depth + half * LANES
            padded += dot_nt(
                weight.reshape(GROUPS * height, LANES), gridded[:, first : first + LANES]
            )
    parts = [padded[group * height : group * height + each] for group in range(GROUPS)]
    fields[...] = jnp.concatenate(parts, axis=0).astype(BF16)


def decode(spots, queries, local_rows, fetched, multiplicity, pieces, layout, outputs):
    points, width = queries.shape
    tok = local_rows.shape[1]
    height = pieces[0].shape[-2] - width // BANDS
    remote = multiplicity.shape[1] - tok
    return pl.pallas_call(
        functools.partial(decode_kernel, layout, outputs // GROUPS),
        out_shape=jax.ShapeDtypeStruct((outputs, points), BF16),
        in_specs=[SMEM] + [VMEM_SPEC] * 4 + [ANY] * len(pieces),
        out_specs=VMEM_SPEC,
        scratch_shapes=[
            pltpu.VMEM((GROUPS, 2, 2, height, LANES), BF16),
            pltpu.VMEM((2 * width // LANES, remote, LANES), BF16),
            pltpu.SemaphoreType.DMA((len(pieces),)),
        ],
        compiler_params=params(),
        cost_estimate=pl.CostEstimate(
            flops=2_000_000_000, bytes_accessed=8_000_000, transcendentals=2_000_000
        ),
        name="decode",
    )(spots, queries, local_rows, fetched, multiplicity, *pieces)


def stacked(*weights):
    parts = []
    for weight in weights:
        for at in range(0, weight.shape[-1], LANES):
            parts.append(weight[..., at : at + LANES])
    return jnp.concatenate(parts, axis=-2)


def chip_block(block, gate=None):
    if gate is not None:
        block, _ = lax.optimization_barrier((block, gate))
    band = lax.axis_index("band")
    other = lax.ppermute(block, "band", [(i, i ^ 2) for i in range(BANDS)])
    low = band < 2
    block = jnp.stack([jnp.where(low, block, other), jnp.where(low, other, block)])
    other = lax.ppermute(block, "band", [(i, i ^ 1) for i in range(BANDS)])
    low = band % 2 == 0
    return jnp.stack([jnp.where(low, block, other), jnp.where(low, other, block)])


def carry(block):
    pairs = []
    for i in range(GROUPS):
        here, there = RING[i] * BANDS, RING[(i + 1) % GROUPS] * BANDS
        for x in range(2):
            pairs.append((here + 2 * x, there + 2 * x))
            pairs.append((there + 2 * x + 1, here + 2 * x + 1))
    return lax.ppermute(block, ("seq", "band"), pairs)


def swap_core(block):
    return lax.ppermute(block, "band", [(i, i ^ 1) for i in range(BANDS)])


def ring_spots():
    seq, core = lax.axis_index("seq"), lax.axis_index("band") % 2
    table = np.zeros((2, GROUPS, GROUPS), np.int32)
    for i in range(GROUPS):
        for step in range(GROUPS):
            table[0, RING[i], step] = RING[(i - step) % GROUPS]
            table[1, RING[i], step] = RING[(i + step) % GROUPS]
    return jnp.concatenate([jnp.asarray(table)[core, seq], core.astype(jnp.int32)[None]])


def ring_step(block, step, gate=None):
    if gate is not None:
        block, _ = lax.optimization_barrier((block, gate))
    if step < GROUPS // 2:
        block = carry(block)
        return block, [(block, (step, None)), (swap_core(block), (GROUPS - step, None))]
    half = lax.dynamic_index_in_dim(block, lax.axis_index("band") % 2, 0, keepdims=False)
    half = carry(half)
    return half, [(half, (step, 0)), (swap_core(half), (step, 1))]


def whole_blocks(*weights):
    parts = []
    for weight, height in weights:
        weight = lax.all_gather(weight, "seq", axis=1, tiled=True)
        weight = lax.all_gather(weight, "band", axis=0, tiled=True)
        depth, columns = weight.shape[0] // BANDS, weight.shape[1] // GROUPS
        weight = weight.reshape(2, 2, depth, GROUPS, columns).transpose(3, 1, 0, 2, 4)
        if height:
            weight = jnp.pad(
                weight.swapaxes(-1, -2), ((0, 0),) * 3 + ((0, height - columns), (0, 0))
            )
        parts.append(weight)
    return stacked(*parts)


def local(
    tokens, ln_gain, w_qkv, w_out, dec_gain, w_kv, w_final, reach, grid_query, neighbours, counts
):
    states = tokens[0]
    tok, width = states.shape
    shards, bands = lax.axis_size("seq"), lax.axis_size("band")
    place = lax.axis_index("seq").astype(jnp.int32).reshape(1)
    outputs = w_final.shape[1] * shards
    height = -(-outputs // GROUPS // 16) * 16
    riding = (shards, bands) == (GROUPS, BANDS)
    up = [(i, i + 1) for i in range(shards - 1)]
    down = [(i + 1, i) for i in range(shards - 1)]
    if riding:
        first = chip_block(stacked(w_qkv))
    left = lax.ppermute(states[tok - HALF :], "seq", up)
    right = lax.ppermute(states[:HALF], "seq", down)
    multiplicity, requested = tables(tok, place, neighbours, counts.reshape(-1, 1), shards)
    normed, bias = prepare(
        tok * shards, place, left, states, right, ln_gain.reshape(1, width), reach.reshape(tok, 1)
    )
    pairs = width // LANES
    if riding:
        spots = ring_spots()
        final = jnp.pad(w_final.T, ((0, height - w_final.shape[1]), (0, 0)))
        notes = jnp.pad(requested, ((0, SLOTS - 1), (0, 0)))
        block, arrived = ring_step(first, 1)
        second = chip_block(
            jnp.concatenate([stacked(w_out, w_kv, final), notes], axis=0), block
        )
        made = project(spots, normed, [(first, (0, None))], None)
        block, later = ring_step(block, 2)
        made = project(spots, normed, arrived, made)
        block, arrived = ring_step(block, 3, made)
        made = project(spots, normed, later, made)
        _, later = ring_step(block, 4)
        pieces = [(second, (0, None))]
        second, _ = lax.optimization_barrier((second, block))
        block, more = ring_step(second, 1, made)
        pieces += more
        made = project(spots, normed, arrived, made)
        block, more = ring_step(block, 2, made)
        pieces += more
        made = project(spots, normed, later, made)
        attended = [attend(made, bias, 0, pairs // 2)]
        block, more = ring_step(block, 3, attended[0])
        pieces += more
        attended.append(attend(made, bias, pairs // 2, pairs - pairs // 2))
        _, more = ring_step(block, 4, attended[1])
        pieces += more
        ids = None
    else:
        spots = jnp.concatenate([jnp.arange(GROUPS, dtype=jnp.int32), jnp.zeros((1,), jnp.int32)])
        block = whole_blocks((w_qkv, 0))
        made = None
        for at in range(GROUPS):
            made = project(spots, normed, [(block[at], (at, None))], made)
        block = whole_blocks((w_out, 0), (w_kv, 0), (w_final, height))
        block = jnp.pad(block, ((0, 0),) * 3 + ((0, SLOTS), (0, 0)))
        pieces = [(block[at], (at, None)) for at in range(GROUPS)]
        attended = [attend(made, bias, 0, pairs // 2), attend(made, bias, pairs // 2, pairs // 2)]
        ids = lax.all_to_all(
            requested.reshape(shards, SLOTS).astype(jnp.int32), "seq", 0, 0, tiled=True
        ).reshape(shards * SLOTS, 1)
    layout = tuple(at for _, at in pieces)
    pieces = [piece for piece, _ in pieces]
    decoded, found = mix(
        place, spots, states, attended, dec_gain.reshape(1, width), ids, pieces, layout, shards
    )
    fetched = lax.all_to_all(
        found.reshape(shards, SLOTS, width), "seq", split_axis=0, concat_axis=0, tiled=True
    )
    local_rows = keys_values(spots, decoded, pieces, layout)
    fields = decode(
        spots, grid_query[0], local_rows, fetched.reshape(shards * SLOTS, width), multiplicity,
        pieces, layout, outputs,
    )
    return fields[None]


def solution(mesh):
    return jax.shard_map(
        local,
        mesh=mesh,
        in_specs=(
            P("band", "seq", None),
            P(),
            P("band", "seq"),
            P("band", "seq"),
            P(),
            P("band", "seq"),
            P("band", "seq"),
            P("seq"),
            P("band", "seq", None),
            P("seq", None),
            P("seq"),
        ),
        out_specs=P("band", None, "seq"),
        check_vma=False,
    )
```

```python
import functools
import math

import jax
import jax.numpy as jnp
import numpy as np
from jax import lax
from jax.experimental import pallas as pl
from jax.experimental.pallas import tpu as pltpu
from jax.sharding import PartitionSpec as P

HEADS = 16
HALF = 128
C = 12
SLOTS = 16
EPSILON = 1e-05
NEG = -1e30
LANES = 128
GROUPS = 8
BANDS = 4
CHUNKS = (0, 2, 1, 3)
RING = (0, 2, 4, 6, 7, 5, 3, 1)
VMEM = 56 * 1024 * 1024
F32 = jnp.float32
BF16 = jnp.bfloat16


def dot(a, b):
    return jnp.dot(a, b, preferred_element_type=F32)


def dot_nt(a, b):
    return lax.dot_general(a, b, (((1,), (1,)), ((), ())), preferred_element_type=F32)


def layer_norm(values, gain):
    values = values.astype(F32)
    centred = values - jnp.mean(values, axis=-1, keepdims=True)
    spread = jnp.mean(centred * centred, axis=-1, keepdims=True)
    return (centred * lax.rsqrt(spread + EPSILON) * gain).astype(BF16)


def params(**more):
    return pltpu.CompilerParams(vmem_limit_bytes=VMEM, **more)


def full_spec(shape):
    return pl.BlockSpec(shape, lambda *_: (0,) * len(shape))


def as_column(row):
    return jnp.broadcast_to(row, (8, row.shape[1])).T[:, :1]


def prepare_kernel(total, place, left, own, right, gain, reach, normed, bias):
    tok = own.shape[0]
    depth = own.shape[1] // BANDS
    for at, part in ((0, left), (HALF, own), (HALF + tok, right)):
        rows = layer_norm(part[...], gain[...])
        for chunk, band in enumerate(CHUNKS):
            normed[at : at + part.shape[0], chunk * depth : (chunk + 1) * depth] = rows[
                :, band * depth : (band + 1) * depth
            ]

    first = place[0] * tok
    span = 3 * HALF
    row = lax.broadcasted_iota(jnp.int32, (HALF, span), 0)
    col = lax.broadcasted_iota(jnp.int32, (HALF, span), 1)
    away = jnp.abs(row + HALF - col)
    limit = as_column(reach[...])
    for block in range(tok // HALF):
        key = first + (block - 1) * HALF + col
        allowed = (away <= limit[block * HALF : (block + 1) * HALF, :]) & (key >= 0) & (key < total)
        bias[block] = jnp.where(allowed, 0.0, NEG)


def prepare(total, place, left, own, right, gain, reach):
    tok, width = own.shape
    operands = (left, own, right, gain, reach)
    outs = (
        jax.ShapeDtypeStruct((tok + 2 * HALF, width), BF16),
        jax.ShapeDtypeStruct((tok // HALF, HALF, 3 * HALF), F32),
    )
    return pl.pallas_call(
        functools.partial(prepare_kernel, total),
        out_shape=outs,
        in_specs=[pl.BlockSpec(memory_space=pltpu.SMEM)]
        + [pl.BlockSpec(memory_space=pltpu.VMEM)] * len(operands),
        out_specs=[pl.BlockSpec(memory_space=pltpu.VMEM)] * len(outs),
        compiler_params=params(),
        cost_estimate=pl.CostEstimate(flops=20_000_000, bytes_accessed=3_000_000, transcendentals=0),
        name="prepare",
    )(place, *operands)


def tables_kernel(tok, place, neighbours, counts, low, rank, tri, multiplicity, requested):
    first = place[0] * tok
    slots, points = neighbours.shape
    ids = neighbours[...].T
    used = as_column(counts[...])
    mesh = lax.broadcasted_iota(jnp.int32, (points, tok), 1) + first
    here = jnp.zeros((points, tok), F32)
    for slot in range(slots):
        here += ((ids[:, slot : slot + 1] == mesh) & (slot < used)).astype(F32)
    multiplicity[:, :tok] = here

    start = low[...]
    elsewhere = start != first
    hits = []
    for slot in range(slots):
        which = ids[:, slot : slot + 1]
        hits.append(
            ((which >= start) & (which < start + tok) & (slot < used) & elsewhere).astype(F32)
        )
    running = dot(tri[...], sum(hits).astype(BF16))
    order = rank[...]
    asked = jnp.zeros(requested.shape, F32)
    there = jnp.zeros(hits[0].shape, F32)
    for slot in range(slots):
        mine = jnp.where(running == order, hits[slot], 0.0)
        there += mine
        offset = (ids[:, slot : slot + 1] - start).astype(F32)
        asked += jnp.sum(jnp.where(mine > 0, offset, 0.0), axis=0, keepdims=True)
        running += hits[slot]
    multiplicity[:, tok:] = there
    requested[...] = asked.astype(BF16)


def tables(tok, place, neighbours, counts, shards):
    points = neighbours.shape[1]
    remote = shards * SLOTS
    column = np.arange(remote)
    low = (column // SLOTS * tok).astype(np.int32)[None]
    rank = (column % SLOTS).astype(np.float32)[None]
    tri = np.tril(np.ones((points, points), np.float32), -1).astype(BF16)
    operands = (neighbours, counts, low, rank, tri)
    return pl.pallas_call(
        functools.partial(tables_kernel, tok),
        out_shape=(
            jax.ShapeDtypeStruct((points, tok + remote), F32),
            jax.ShapeDtypeStruct((1, remote), BF16),
        ),
        in_specs=[pl.BlockSpec(memory_space=pltpu.SMEM)]
        + [pl.BlockSpec(memory_space=pltpu.VMEM)] * len(operands),
        out_specs=[pl.BlockSpec(memory_space=pltpu.VMEM)] * 2,
        compiler_params=params(),
        cost_estimate=pl.CostEstimate(flops=20_000_000, bytes_accessed=1_000_000, transcendentals=0),
        name="tables",
    )(place, *operands)


def pair_attend(queries, keys, values, bias, weights_of):
    rows = queries.shape[0]
    lane = lax.broadcasted_iota(jnp.int32, (rows, LANES), 1)
    first = lane < LANES // 2
    zero = jnp.zeros_like(queries)
    both = jnp.concatenate(
        [jnp.where(first, queries, zero), jnp.where(first, zero, queries)], axis=0
    )
    scores = dot_nt(both, keys)
    scores = scores + jnp.concatenate([bias, bias], axis=0)
    top = jnp.max(scores, axis=-1, keepdims=True)
    weights = weights_of(jnp.exp(scores - top)).astype(BF16)
    summed = dot(weights, jnp.concatenate([values, jnp.ones_like(values)], axis=1))
    share = summed[:, :LANES] / summed[:, LANES:]
    return jnp.where(first, share[:rows], share[rows:]).astype(BF16)


def start_loads(spots, pieces, layout, scratch, arrived, rows):
    copies = {}
    for n, (piece, (at, core)) in enumerate(zip(pieces, layout)):
        place = scratch.at[spots[at]]
        if core is None:
            copy = pltpu.make_async_copy(piece.at[:, :, rows, :], place, arrived.at[n])
        else:
            mine = 1 - spots[GROUPS] if core else spots[GROUPS]
            copy = pltpu.make_async_copy(piece.at[:, rows, :], place.at[mine], arrived.at[n])
        copy.start()
        copies.setdefault(at, []).append(copy)
    return copies


def wait_group(copies, at):
    for copy in copies.get(at, ()):
        copy.wait()


def lanes_of(block, depth, start, count):
    rows = block.shape[0] * block.shape[1] * depth if block.ndim == 4 else block.shape[0] * depth
    columns = [
        block[..., start + g * depth : start + (g + 1) * depth, :].reshape(rows, LANES)
        for g in range(count)
    ]
    return columns[0] if count == 1 else jnp.concatenate(columns, axis=1)


SMEM = pl.BlockSpec(memory_space=pltpu.SMEM)
VMEM_SPEC = pl.BlockSpec(memory_space=pltpu.VMEM)
ANY = pl.BlockSpec(memory_space=pl.ANY)


def project_kernel(layout, spots, normed, *refs):
    pieces = refs[: len(layout)]
    out, scratch, made, arrived, sent = refs[len(layout) :]
    per = made.shape[1]
    depth = normed.shape[1] // BANDS
    copies = start_loads(spots, pieces, layout, scratch, arrived, slice(0, per * depth))
    writes = []
    for at in range(GROUPS):
        wait_group(copies, at)
        spot = spots[at]
        total = dot(normed[...], lanes_of(scratch[spot], depth, 0, per)).astype(BF16)
        for group in range(per):
            made[at, group] = total[:, group * LANES : (group + 1) * LANES]
        writes.append(
            pltpu.make_async_copy(made.at[at], out.at[pl.ds(spot * per, per)], sent.at[at])
        )
        writes[-1].start()
    for write in writes:
        write.wait()


def project(spots, normed, pieces, layout):
    rows, width = normed.shape
    per = 3 * width // LANES // GROUPS
    return pl.pallas_call(
        functools.partial(project_kernel, layout),
        out_shape=jax.ShapeDtypeStruct((GROUPS * per, rows, LANES), BF16),
        in_specs=[SMEM, VMEM_SPEC] + [ANY] * len(pieces),
        out_specs=ANY,
        scratch_shapes=[
            pltpu.VMEM((GROUPS, 2, 2, per * width // BANDS, LANES), BF16),
            pltpu.VMEM((GROUPS, per, rows, LANES), BF16),
            pltpu.SemaphoreType.DMA((len(pieces),)),
            pltpu.SemaphoreType.DMA((GROUPS,)),
        ],
        compiler_params=params(),
        cost_estimate=pl.CostEstimate(
            flops=6 * rows * width * width, bytes_accessed=10_000_000, transcendentals=0
        ),
        name="project",
    )(spots, normed, *pieces)


def attend_kernel(queries, keys, values, bias, attended):
    scale = BF16(1.0 / math.sqrt(LANES // 2))
    for block in range(bias.shape[0]):
        at = block * HALF
        attended[at : at + HALF, :] = pair_attend(
            queries[0, at + HALF : at + 2 * HALF, :] * scale,
            keys[0, at : at + 3 * HALF, :],
            values[0, at : at + 3 * HALF, :],
            bias[block],
            lambda weights: weights,
        )


def attend(projected, bias, first, count):
    groups, rows, _ = projected.shape
    tok = rows - 2 * HALF
    pairs = groups // 3

    def part(which):
        return pl.BlockSpec((1, rows, LANES), lambda s: (which * pairs + first + s, 0, 0))

    return pl.pallas_call(
        attend_kernel,
        grid=(count,),
        out_shape=jax.ShapeDtypeStruct((tok, count * LANES), BF16),
        in_specs=[part(0), part(1), part(2), full_spec(bias.shape)],
        out_specs=pl.BlockSpec((tok, LANES), lambda s: (0, s)),
        compiler_params=params(),
        cost_estimate=pl.CostEstimate(
            flops=300_000_000 * count, bytes_accessed=500_000 * count, transcendentals=200_000 * count
        ),
        name="attend",
    )(projected, projected, projected, bias)


def picked_rows(place, ids, spots, rows, asked, arrived):
    tok = rows.shape[0]
    if spots is None:
        which = ids[...]
    else:
        for at in range(GROUPS):
            asked[pl.ds(spots[at] * SLOTS, SLOTS), :] = jnp.broadcast_to(
                arrived[at, 0:1, :].astype(F32), (SLOTS, LANES)
            )
        count = GROUPS * SLOTS
        lane = lax.broadcasted_iota(jnp.int32, (count, LANES), 1)
        slot = lax.broadcasted_iota(jnp.int32, (count, LANES), 0) % SLOTS
        mine = jnp.where(lane == place[0] * SLOTS + slot, asked[...], 0.0)
        which = jnp.sum(mine, axis=1, keepdims=True).astype(jnp.int32)
    here = lax.broadcasted_iota(jnp.int32, (which.shape[0], tok), 1)
    return dot((which == here).astype(BF16), rows).astype(BF16)


def chunked(values, depth):
    return jnp.concatenate([values[:, b * depth : (b + 1) * depth] for b in CHUNKS], axis=1)


def mix_kernel(layout, riding, place, spots, states, gain, *refs):
    attended, refs = refs[:2], refs[2:]
    ids = None
    if not riding:
        ids, refs = refs[0], refs[1:]
    pieces = refs[: len(layout)]
    decoded, found, mixed, scratch, asked, notes, arrived, noted = refs[len(layout) :]
    width = states.shape[1]
    depth = width // BANDS
    start = 3 * width // GROUPS // LANES * depth
    copies = start_loads(spots, pieces, layout, scratch, arrived, slice(start, start + depth))
    reads = []
    if riding:
        for piece, (at, core) in zip(pieces, layout):
            if not core:
                end = piece.shape[-2]
                source = piece.at[0, 0] if core is None else piece.at[0]
                reads.append(
                    pltpu.make_async_copy(
                        source.at[end - SLOTS : end, :], notes.at[at], noted.at[at]
                    )
                )
                reads[-1].start()
    inputs = chunked(jnp.concatenate([part[...] for part in attended], axis=1), depth)
    for at in range(GROUPS):
        wait_group(copies, at)
        spot = spots[at]
        columns = pl.ds(pl.multiple_of(spot * LANES, LANES), LANES)
        total = dot(inputs, lanes_of(scratch[spot], depth, 0, 1))
        mixed[:, columns] = (states[:, columns].astype(F32) + total).astype(BF16)
    for read in reads:
        read.wait()
    rows = chunked(layer_norm(mixed[...], gain[...]), depth)
    decoded[...] = rows
    found[...] = picked_rows(place, ids, spots if riding else None, rows, asked, notes)


def mix(place, spots, states, attended, gain, ids, pieces, layout, shards):
    tok, width = states.shape
    more = [] if ids is None else [ids]
    return pl.pallas_call(
        functools.partial(mix_kernel, layout, ids is None),
        out_shape=(
            jax.ShapeDtypeStruct((tok, width), BF16),
            jax.ShapeDtypeStruct((shards * SLOTS, width), BF16),
        ),
        in_specs=[SMEM, SMEM] + [VMEM_SPEC] * (4 + len(more)) + [ANY] * len(pieces),
        out_specs=(VMEM_SPEC, VMEM_SPEC),
        scratch_shapes=[
            pltpu.VMEM((tok, width), BF16),
            pltpu.VMEM((GROUPS, 2, 2, width // BANDS, LANES), BF16),
            pltpu.VMEM((GROUPS * SLOTS, LANES), F32),
            pltpu.VMEM((GROUPS, SLOTS, LANES), BF16),
            pltpu.SemaphoreType.DMA((len(pieces),)),
            pltpu.SemaphoreType.DMA((GROUPS,)),
        ],
        compiler_params=params(),
        cost_estimate=pl.CostEstimate(
            flops=600_000_000, bytes_accessed=4_000_000, transcendentals=0
        ),
        name="mix",
    )(place, spots, states, gain, *attended, *more, *pieces)


def keys_values_kernel(layout, spots, decoded, *refs):
    pieces = refs[: len(layout)]
    out, scratch, arrived = refs[len(layout) :]
    depth = decoded.shape[1] // BANDS
    per = scratch.shape[3] // depth
    copies = start_loads(
        spots, pieces, layout, scratch, arrived, slice(0, scratch.shape[3])
    )
    for at in range(GROUPS):
        wait_group(copies, at)
        spot = spots[at]
        total = dot(decoded[...], lanes_of(scratch[spot], depth, 0, per)).astype(BF16)
        for group in range(per):
            out[spot * per + group] = total[:, group * LANES : (group + 1) * LANES]


def keys_values(spots, decoded, pieces, layout):
    tok, width = decoded.shape
    height = 2 * width // GROUPS // LANES * (width // BANDS)
    return pl.pallas_call(
        functools.partial(keys_values_kernel, layout),
        out_shape=jax.ShapeDtypeStruct((2 * width // LANES, tok, LANES), BF16),
        in_specs=[SMEM, VMEM_SPEC] + [ANY] * len(pieces),
        out_specs=VMEM_SPEC,
        scratch_shapes=[
            pltpu.VMEM((GROUPS, 2, 2, height, LANES), BF16),
            pltpu.SemaphoreType.DMA((len(pieces),)),
        ],
        compiler_params=params(),
        cost_estimate=pl.CostEstimate(
            flops=1_100_000_000, bytes_accessed=6_000_000, transcendentals=0
        ),
        name="keys_values",
    )(spots, decoded, *pieces)


def decode_kernel(layout, each, spots, queries, local_rows, fetched, multiplicity, *refs):
    pieces = refs[: len(layout)]
    fields, scratch, table, arrived = refs[len(layout) :]
    points, width = queries.shape
    depth = width // BANDS
    count = fetched.shape[0]
    per = 2 * width // GROUPS // LANES
    kept = scratch.shape[3]
    copies = start_loads(spots, pieces, layout, scratch, arrived, slice(0, kept))
    padding = jnp.zeros((table.shape[1] - count, LANES), BF16)
    for at in range(GROUPS):
        wait_group(copies, at)
        spot = spots[at]
        total = dot(fetched[...], lanes_of(scratch[spot], depth, 0, per)).astype(BF16)
        for group in range(per):
            table[spot * per + group, :count, :] = total[:, group * LANES : (group + 1) * LANES]
            if table.shape[1] > count:
                table[spot * per + group, count:, :] = padding

    pairs = width // LANES
    scale = BF16(1.0 / math.sqrt(width // HEADS))
    times = multiplicity[...]
    bias = jnp.where(times > 0, 0.0, NEG)
    both = jnp.concatenate([times, times], axis=0)
    rows = []
    for pair in range(pairs):
        rows.append(
            pair_attend(
                queries[:, pair * LANES : (pair + 1) * LANES] * scale,
                jnp.concatenate([local_rows[pair], table[pair]], axis=0),
                jnp.concatenate([local_rows[pairs + pair], table[pairs + pair]], axis=0),
                bias,
                lambda weights: weights * both,
            )
        )
    gridded = jnp.concatenate(rows, axis=1)
    start = per * depth
    halves = depth // LANES
    height = (kept - start) // halves
    padded = jnp.zeros((GROUPS * height, points), F32)
    for chunk, band in enumerate(CHUNKS):
        for half in range(halves):
            at = start + half * height
            weight = scratch[:, chunk // 2, chunk % 2, at : at + height, :]
            first = band * depth + half * LANES
            padded += dot_nt(
                weight.reshape(GROUPS * height, LANES), gridded[:, first : first + LANES]
            )
    parts = [padded[group * height : group * height + each] for group in range(GROUPS)]
    fields[...] = jnp.concatenate(parts, axis=0).astype(BF16)


def decode(spots, queries, local_rows, fetched, multiplicity, pieces, layout, outputs):
    points, width = queries.shape
    tok = local_rows.shape[1]
    height = pieces[0].shape[-2]
    remote = multiplicity.shape[1] - tok
    return pl.pallas_call(
        functools.partial(decode_kernel, layout, outputs // GROUPS),
        out_shape=jax.ShapeDtypeStruct((outputs, points), BF16),
        in_specs=[SMEM] + [VMEM_SPEC] * 4 + [ANY] * len(pieces),
        out_specs=VMEM_SPEC,
        scratch_shapes=[
            pltpu.VMEM((GROUPS, 2, 2, height, LANES), BF16),
            pltpu.VMEM((2 * width // LANES, remote, LANES), BF16),
            pltpu.SemaphoreType.DMA((len(pieces),)),
        ],
        compiler_params=params(),
        cost_estimate=pl.CostEstimate(
            flops=2_000_000_000, bytes_accessed=8_000_000, transcendentals=2_000_000
        ),
        name="decode",
    )(spots, queries, local_rows, fetched, multiplicity, *pieces)


def stacked(*weights):
    parts = []
    for weight in weights:
        for at in range(0, weight.shape[-1], LANES):
            parts.append(weight[..., at : at + LANES])
    return jnp.concatenate(parts, axis=-2)


def chip_block(block, gate=None):
    if gate is not None:
        block, _ = lax.optimization_barrier((block, gate))
    band = lax.axis_index("band")
    other = lax.ppermute(block, "band", [(i, i ^ 2) for i in range(BANDS)])
    low = band < 2
    block = jnp.stack([jnp.where(low, block, other), jnp.where(low, other, block)])
    other = swap_core(block)
    low = band % 2 == 0
    return jnp.stack([jnp.where(low, block, other), jnp.where(low, other, block)])


def carry(block):
    pairs = []
    for i in range(GROUPS):
        here, there = RING[i] * BANDS, RING[(i + 1) % GROUPS] * BANDS
        for x in range(2):
            pairs.append((here + 2 * x, there + 2 * x))
            pairs.append((there + 2 * x + 1, here + 2 * x + 1))
    return lax.ppermute(block, ("seq", "band"), pairs)


def swap_core(block):
    return lax.ppermute(block, "band", [(i, i ^ 1) for i in range(BANDS)])


def ring_spots():
    seq, core = lax.axis_index("seq"), lax.axis_index("band") % 2
    table = np.zeros((2, GROUPS, GROUPS), np.int32)
    for i in range(GROUPS):
        for step in range(GROUPS):
            table[0, RING[i], step] = RING[(i - step) % GROUPS]
            table[1, RING[i], step] = RING[(i + step) % GROUPS]
    return jnp.concatenate([jnp.asarray(table)[core, seq], core.astype(jnp.int32)[None]])


def ring_step(block, step, gate=None):
    if gate is not None:
        block, _ = lax.optimization_barrier((block, gate))
    if step < GROUPS // 2:
        block = carry(block)
        return block, [(block, (step, None)), (swap_core(block), (GROUPS - step, None))]
    half = lax.dynamic_index_in_dim(block, lax.axis_index("band") % 2, 0, keepdims=False)
    half = carry(half)
    return half, [(half, (step, 0)), (swap_core(half), (step, 1))]


def whole_blocks(*weights):
    parts = []
    for weight, height in weights:
        weight = lax.all_gather(weight, "seq", axis=1, tiled=True)
        weight = lax.all_gather(weight, "band", axis=0, tiled=True)
        depth, columns = weight.shape[0] // BANDS, weight.shape[1] // GROUPS
        weight = weight.reshape(2, 2, depth, GROUPS, columns).transpose(3, 1, 0, 2, 4)
        if height:
            weight = jnp.pad(
                weight.swapaxes(-1, -2), ((0, 0),) * 3 + ((0, height - columns), (0, 0))
            )
        parts.append(weight)
    return stacked(*parts)


def local(
    tokens, ln_gain, w_qkv, w_out, dec_gain, w_kv, w_final, reach, grid_query, neighbours, counts
):
    states = tokens[0]
    tok, width = states.shape
    shards, bands = lax.axis_size("seq"), lax.axis_size("band")
    place = lax.axis_index("seq").astype(jnp.int32).reshape(1)
    outputs = w_final.shape[1] * shards
    height = -(-outputs // GROUPS // 16) * 16
    riding = (shards, bands) == (GROUPS, BANDS)
    up = [(i, i + 1) for i in range(shards - 1)]
    down = [(i + 1, i) for i in range(shards - 1)]
    left = lax.ppermute(states[tok - HALF :], "seq", up)
    right = lax.ppermute(states[:HALF], "seq", down)
    multiplicity, requested = tables(tok, place, neighbours.T, counts.reshape(1, -1), shards)
    normed, bias = prepare(
        tok * shards, place, left, states, right, ln_gain.reshape(1, width), reach.reshape(1, tok)
    )
    pairs = width // LANES
    if riding:
        spots = ring_spots()
        notes = jnp.broadcast_to(requested, (2, 1, SLOTS, LANES))
        block = jnp.pad(stacked(w_qkv, w_out), ((0, SLOTS), (0, 0)))
        first = chip_block(block).at[:, :1, block.shape[0] - SLOTS :].set(notes)
        first, left, right = lax.optimization_barrier((first, left, right))
        pieces = [(first, (0, None))]
        block, more = ring_step(first, 1)
        pieces += more
        final = jnp.pad(w_final.T, ((0, height - w_final.shape[1]), (0, 0)))
        second = chip_block(stacked(w_kv, final), block)
        block, more = ring_step(block, 2)
        pieces += more
        block, more = ring_step(block, 3)
        pieces += more
        later = [(second, (0, None))]
        second, _ = lax.optimization_barrier((second, block))
        _, more = ring_step(block, 4)
        pieces += more
        layout = tuple(at for _, at in pieces)
        pieces = [piece for piece, _ in pieces]
        block, more = ring_step(second, 1)
        later += more
        made = project(spots, normed, pieces, layout)
        block, more = ring_step(block, 2)
        later += more
        block, more = ring_step(block, 3, made)
        later += more
        attended = [attend(made, bias, 0, pairs // 2)]
        _, more = ring_step(block, 4, attended[0])
        later += more
        attended.append(attend(made, bias, pairs // 2, pairs - pairs // 2))
        ids = None
    else:
        spots = jnp.concatenate([jnp.arange(GROUPS, dtype=jnp.int32), jnp.zeros((1,), jnp.int32)])
        block = whole_blocks((w_qkv, 0), (w_out, 0))
        block = jnp.pad(block, ((0, 0),) * 3 + ((0, SLOTS), (0, 0)))
        pieces = [block[at] for at in range(GROUPS)]
        layout = tuple((at, None) for at in range(GROUPS))
        block = whole_blocks((w_kv, 0), (w_final, height))
        later = [(block[at], (at, None)) for at in range(GROUPS)]
        made = project(spots, normed, pieces, layout)
        attended = [attend(made, bias, 0, pairs // 2), attend(made, bias, pairs // 2, pairs // 2)]
        ids = lax.all_to_all(
            requested.reshape(shards, SLOTS).astype(jnp.int32), "seq", 0, 0, tiled=True
        ).reshape(shards * SLOTS, 1)
    decoded, found = mix(
        place, spots, states, attended, dec_gain.reshape(1, width), ids, pieces, layout, shards
    )
    fetched = lax.all_to_all(
        found.reshape(shards, SLOTS, width), "seq", split_axis=0, concat_axis=0, tiled=True
    )
    layout = tuple(at for _, at in later)
    pieces = [piece for piece, _ in later]
    local_rows = keys_values(spots, decoded, pieces, layout)
    fields = decode(
        spots, grid_query[0], local_rows, fetched.reshape(shards * SLOTS, width), multiplicity,
        pieces, layout, outputs,
    )
    return fields[None]


def solution(mesh):
    return jax.shard_map(
        local,
        mesh=mesh,
        in_specs=(
            P("band", "seq", None),
            P(),
            P("band", "seq"),
            P("band", "seq"),
            P(),
            P("band", "seq"),
            P("band", "seq"),
            P("seq"),
            P("band", "seq", None),
            P("seq", None),
            P("seq"),
        ),
        out_specs=P("band", None, "seq"),
        check_vma=False,
    )
```

```python
import functools
import math

import jax
import jax.numpy as jnp
import numpy as np
from jax import lax
from jax.experimental import pallas as pl
from jax.experimental.pallas import tpu as pltpu
from jax.sharding import PartitionSpec as P

HEADS = 16
HALF = 128
C = 12
SLOTS = 16
EPSILON = 1e-05
NEG = -1e30
LANES = 128
GROUPS = 8
BANDS = 4
CHUNKS = (0, 2, 1, 3)
RING = (0, 2, 4, 6, 7, 5, 3, 1)
VMEM = 56 * 1024 * 1024
F32 = jnp.float32
BF16 = jnp.bfloat16


def dot(a, b):
    return jnp.dot(a, b, preferred_element_type=F32)


def dot_nt(a, b):
    return lax.dot_general(a, b, (((1,), (1,)), ((), ())), preferred_element_type=F32)


def layer_norm(values, gain):
    values = values.astype(F32)
    centred = values - jnp.mean(values, axis=-1, keepdims=True)
    spread = jnp.mean(centred * centred, axis=-1, keepdims=True)
    return (centred * lax.rsqrt(spread + EPSILON) * gain).astype(BF16)


def params(**more):
    return pltpu.CompilerParams(vmem_limit_bytes=VMEM, **more)


def full_spec(shape):
    return pl.BlockSpec(shape, lambda *_: (0,) * len(shape))


def own_first(rows, core, depth):
    parts = [rows[:, b * depth : (b + 1) * depth] for b in range(BANDS)]
    order = ((0, 1), (2, 3), (1, 0), (3, 2))
    return jnp.concatenate([jnp.where(core == 0, parts[a], parts[b]) for a, b in order], axis=1)


def as_column(row):
    return jnp.broadcast_to(row, (8, row.shape[1])).T[:, :1]


def prepare_kernel(total, place, left, own, right, gain, reach, normed, bias):
    tok = own.shape[0]
    depth = own.shape[1] // BANDS
    for at, part in ((0, left), (HALF, own), (HALF + tok, right)):
        rows = layer_norm(part[...], gain[...])
        normed[at : at + part.shape[0], :] = own_first(rows, place[1], depth)

    first = place[0] * tok
    span = 3 * HALF
    row = lax.broadcasted_iota(jnp.int32, (HALF, span), 0)
    col = lax.broadcasted_iota(jnp.int32, (HALF, span), 1)
    away = jnp.abs(row + HALF - col)
    limit = as_column(reach[...])
    for block in range(tok // HALF):
        key = first + (block - 1) * HALF + col
        allowed = (away <= limit[block * HALF : (block + 1) * HALF, :]) & (key >= 0) & (key < total)
        bias[block] = jnp.where(allowed, 0.0, NEG)


def prepare(total, place, left, own, right, gain, reach):
    tok, width = own.shape
    operands = (left, own, right, gain, reach)
    outs = (
        jax.ShapeDtypeStruct((tok + 2 * HALF, width), BF16),
        jax.ShapeDtypeStruct((tok // HALF, HALF, 3 * HALF), F32),
    )
    return pl.pallas_call(
        functools.partial(prepare_kernel, total),
        out_shape=outs,
        in_specs=[pl.BlockSpec(memory_space=pltpu.SMEM)]
        + [pl.BlockSpec(memory_space=pltpu.VMEM)] * len(operands),
        out_specs=[pl.BlockSpec(memory_space=pltpu.VMEM)] * len(outs),
        compiler_params=params(),
        cost_estimate=pl.CostEstimate(flops=20_000_000, bytes_accessed=3_000_000, transcendentals=0),
        name="prepare",
    )(place, *operands)


def tables_kernel(tok, count, place, neighbours, counts, low, rank, tri, *refs):
    weights, (multiplicity, requested) = refs[:count], refs[count : count + 2]
    first = place[0] * tok
    slots, points = neighbours.shape
    ids = neighbours[...].T
    used = as_column(counts[...])
    mesh = lax.broadcasted_iota(jnp.int32, (points, tok), 1) + first
    here = jnp.zeros((points, tok), F32)
    for slot in range(slots):
        here += ((ids[:, slot : slot + 1] == mesh) & (slot < used)).astype(F32)
    multiplicity[:, :tok] = here

    start = low[...]
    elsewhere = start != first
    hits = []
    for slot in range(slots):
        which = ids[:, slot : slot + 1]
        hits.append(
            ((which >= start) & (which < start + tok) & (slot < used) & elsewhere).astype(F32)
        )
    running = dot(tri[...], sum(hits).astype(BF16))
    order = rank[...]
    asked = jnp.zeros(requested.shape, F32)
    there = jnp.zeros(hits[0].shape, F32)
    for slot in range(slots):
        mine = jnp.where(running == order, hits[slot], 0.0)
        there += mine
        offset = (ids[:, slot : slot + 1] - start).astype(F32)
        asked += jnp.sum(jnp.where(mine > 0, offset, 0.0), axis=0, keepdims=True)
        running += hits[slot]
    multiplicity[:, tok:] = there
    requested[...] = asked.astype(BF16)
    if weights:
        payload = refs[-1]
        at = 0
        for weight in weights:
            depth, columns = weight.shape
            for first in range(0, columns, LANES):
                payload[at : at + depth, :] = weight[:, first : first + LANES]
                at += depth
        payload[at:, :] = jnp.broadcast_to(asked, (SLOTS, LANES)).astype(BF16)


def tables(tok, place, neighbours, counts, shards, weights):
    points = neighbours.shape[1]
    remote = shards * SLOTS
    column = np.arange(remote)
    low = (column // SLOTS * tok).astype(np.int32)[None]
    rank = (column % SLOTS).astype(np.float32)[None]
    tri = np.tril(np.ones((points, points), np.float32), -1).astype(BF16)
    operands = (neighbours, counts, low, rank, tri) + weights
    outs = (
        jax.ShapeDtypeStruct((points, tok + remote), F32),
        jax.ShapeDtypeStruct((1, remote), BF16),
    )
    if weights:
        rows = sum(weight.shape[0] * weight.shape[1] // LANES for weight in weights) + SLOTS
        outs += (jax.ShapeDtypeStruct((rows, LANES), BF16),)
    return pl.pallas_call(
        functools.partial(tables_kernel, tok, len(weights)),
        out_shape=outs,
        in_specs=[pl.BlockSpec(memory_space=pltpu.SMEM)]
        + [pl.BlockSpec(memory_space=pltpu.VMEM)] * len(operands),
        out_specs=[pl.BlockSpec(memory_space=pltpu.VMEM)] * len(outs),
        compiler_params=params(),
        cost_estimate=pl.CostEstimate(flops=20_000_000, bytes_accessed=1_000_000, transcendentals=0),
        name="tables",
    )(place, *operands)


def pair_attend(queries, keys, values, bias, weights_of):
    rows = queries.shape[0]
    lane = lax.broadcasted_iota(jnp.int32, (rows, LANES), 1)
    first = lane < LANES // 2
    zero = jnp.zeros_like(queries)
    both = jnp.concatenate(
        [jnp.where(first, queries, zero), jnp.where(first, zero, queries)], axis=0
    )
    scores = dot_nt(both, keys)
    scores = scores + jnp.concatenate([bias, bias], axis=0)
    top = jnp.max(scores, axis=-1, keepdims=True)
    weights = weights_of(jnp.exp(scores - top)).astype(BF16)
    summed = dot(weights, jnp.concatenate([values, jnp.ones_like(values)], axis=1))
    share = summed[:, :LANES] / summed[:, LANES:]
    return jnp.where(first, share[:rows], share[rows:]).astype(BF16)


def start_loads(spots, pieces, layout, scratch, arrived, rows, core=None):
    copies = {}
    for n, (piece, (at, half)) in enumerate(zip(pieces, layout)):
        place = scratch.at[spots[at]]
        if half is None:
            copy = pltpu.make_async_copy(piece.at[:, :, rows, :], place, arrived.at[n])
        else:
            to = half if core is None else (1 - core if half else core)
            copy = pltpu.make_async_copy(piece.at[:, rows, :], place.at[to], arrived.at[n])
        copy.start()
        copies.setdefault(at, []).append(copy)
    return copies


def wait_group(copies, at):
    for copy in copies.get(at, ()):
        copy.wait()


def lanes_of(block, depth, start, count):
    rows = block.shape[0] * block.shape[1] * depth if block.ndim == 4 else block.shape[0] * depth
    columns = [
        block[..., start + g * depth : start + (g + 1) * depth, :].reshape(rows, LANES)
        for g in range(count)
    ]
    return columns[0] if count == 1 else jnp.concatenate(columns, axis=1)


SMEM = pl.BlockSpec(memory_space=pltpu.SMEM)
VMEM_SPEC = pl.BlockSpec(memory_space=pltpu.VMEM)
ANY = pl.BlockSpec(memory_space=pl.ANY)


def projection(normed, halves, depth, per):
    weight = jnp.concatenate([lanes_of(halves[n], depth, 0, per) for n in range(2)], axis=0)
    return dot(normed, weight).astype(BF16)


def by_group(pieces, layout):
    groups = {}
    for piece, (at, half) in zip(pieces, layout):
        groups.setdefault(at, {})[half] = piece[...]
    return groups


def project_kernel(layout, spots, normed, *refs):
    pieces = refs[: len(layout)]
    out, made, sent = refs[-3:]
    per = made.shape[1]
    depth = normed.shape[1] // BANDS
    writes = []
    for n, (at, halves) in enumerate(by_group(pieces, layout).items()):
        total = projection(normed[...], halves, depth, per)
        for group in range(per):
            made[n, group] = total[:, group * LANES : (group + 1) * LANES]
        writes.append(
            pltpu.make_async_copy(made.at[n], out.at[pl.ds(spots[at] * per, per)], sent.at[n])
        )
        writes[-1].start()
    for write in writes:
        write.wait()


def half_specs(arrays, height):
    return [full_spec((array.shape[0], height, LANES)) for array in arrays]


def project(spots, normed, pieces, before):
    rows, width = normed.shape
    layout = tuple(place for _, place in pieces)
    arrays = [array for array, _ in pieces]
    per = 3 * width // LANES // GROUPS
    count = len({at for at, _ in layout})
    more = [] if before is None else [before]
    return pl.pallas_call(
        functools.partial(project_kernel, layout),
        grid=(1,),
        out_shape=jax.ShapeDtypeStruct((GROUPS * per, rows, LANES), BF16),
        in_specs=[SMEM, full_spec(normed.shape)]
        + half_specs(arrays, per * width // BANDS)
        + [ANY] * len(more),
        out_specs=ANY,
        scratch_shapes=[
            pltpu.VMEM((count, per, rows, LANES), BF16),
            pltpu.SemaphoreType.DMA((count,)),
        ],
        input_output_aliases={2 + len(arrays): 0} if more else {},
        compiler_params=params(),
        cost_estimate=pl.CostEstimate(
            flops=2 * rows * width * per * LANES * count,
            bytes_accessed=(1 + 2 * count) * rows * width * 2,
            transcendentals=0,
        ),
        name="project",
    )(spots, normed, *arrays, *more)


def attend_kernel(layout, ready, spots, normed, bias, *refs):
    pieces = refs[: len(layout)]
    made, attended, projected, loaded = refs[len(layout) :]
    width = normed.shape[1]
    depth = width // BANDS
    per = projected.shape[0] // GROUPS
    reads = []
    for n, at in enumerate(ready):
        place = pl.ds(spots[at] * per, per)
        reads.append(pltpu.make_async_copy(made.at[place], projected.at[place], loaded.at[n]))
        reads[-1].start()
    for at, halves in by_group(pieces, layout).items():
        total = projection(normed[...], halves, depth, per)
        for group in range(per):
            projected[spots[at] * per + group] = total[:, group * LANES : (group + 1) * LANES]
    for read in reads:
        read.wait()
    pairs = width // LANES
    scale = BF16(1.0 / math.sqrt(width // HEADS))
    for pair in range(pairs):
        for block in range(bias.shape[0]):
            at = block * HALF
            attended[at : at + HALF, pair * LANES : (pair + 1) * LANES] = pair_attend(
                projected[pair, at + HALF : at + 2 * HALF, :] * scale,
                projected[pairs + pair, at : at + 3 * HALF, :],
                projected[2 * pairs + pair, at : at + 3 * HALF, :],
                bias[block],
                lambda weights: weights,
            )


def attend(spots, normed, bias, pieces, made, ready):
    rows, width = normed.shape
    tok = rows - 2 * HALF
    layout = tuple(place for _, place in pieces)
    arrays = [array for array, _ in pieces]
    per = made.shape[0] // GROUPS
    return pl.pallas_call(
        functools.partial(attend_kernel, layout, ready),
        grid=(1,),
        out_shape=jax.ShapeDtypeStruct((tok, width), BF16),
        in_specs=[SMEM, full_spec(normed.shape), full_spec(bias.shape)]
        + half_specs(arrays, per * width // BANDS)
        + [ANY],
        out_specs=full_spec((tok, width)),
        scratch_shapes=[
            pltpu.VMEM(made.shape, BF16),
            pltpu.SemaphoreType.DMA((len(ready),)),
        ],
        compiler_params=params(),
        cost_estimate=pl.CostEstimate(
            flops=3_500_000_000, bytes_accessed=8_000_000, transcendentals=2_000_000
        ),
        name="attend",
    )(spots, normed, bias, *arrays, made)


def picked_rows(place, ids, spots, rows, asked, arrived):
    tok = rows.shape[0]
    if spots is None:
        which = ids[...]
    else:
        for at in range(GROUPS):
            asked[pl.ds(spots[at] * SLOTS, SLOTS), :] = jnp.broadcast_to(
                arrived[at, 0:1, :].astype(F32), (SLOTS, LANES)
            )
        count = GROUPS * SLOTS
        lane = lax.broadcasted_iota(jnp.int32, (count, LANES), 1)
        slot = lax.broadcasted_iota(jnp.int32, (count, LANES), 0) % SLOTS
        mine = jnp.where(lane == place[0] * SLOTS + slot, asked[...], 0.0)
        which = jnp.sum(mine, axis=1, keepdims=True).astype(jnp.int32)
    here = lax.broadcasted_iota(jnp.int32, (which.shape[0], tok), 1)
    return dot((which == here).astype(BF16), rows).astype(BF16)


def chunked(values, depth):
    return jnp.concatenate([values[:, b * depth : (b + 1) * depth] for b in CHUNKS], axis=1)


def mix_kernel(layout, riding, place, spots, states, gain, *refs):
    attended, refs = refs[0], refs[1:]
    ids = None
    if not riding:
        ids, refs = refs[0], refs[1:]
    pieces = refs[: len(layout)]
    decoded, found, mixed, scratch, asked, notes, arrived, noted = refs[len(layout) :]
    width = states.shape[1]
    depth = width // BANDS
    start = 3 * width // GROUPS // LANES * depth
    copies = start_loads(spots, pieces, layout, scratch, arrived, slice(start, start + depth))
    reads = []
    if riding:
        for piece, (at, core) in zip(pieces, layout):
            if core == 0:
                end = piece.shape[-2]
                reads.append(
                    pltpu.make_async_copy(
                        piece.at[0, end - SLOTS : end, :], notes.at[at], noted.at[at]
                    )
                )
                reads[-1].start()
    inputs = own_first(attended[...], place[1], depth)
    for at in range(GROUPS):
        wait_group(copies, at)
        spot = spots[at]
        columns = pl.ds(pl.multiple_of(spot * LANES, LANES), LANES)
        total = dot(inputs, lanes_of(scratch[spot], depth, 0, 1))
        mixed[:, columns] = (states[:, columns].astype(F32) + total).astype(BF16)
    for read in reads:
        read.wait()
    rows = chunked(layer_norm(mixed[...], gain[...]), depth)
    decoded[...] = rows
    found[...] = picked_rows(place, ids, spots if riding else None, rows, asked, notes)


def mix(place, spots, states, attended, gain, ids, pieces, layout, shards):
    tok, width = states.shape
    more = [] if ids is None else [ids]
    return pl.pallas_call(
        functools.partial(mix_kernel, layout, ids is None),
        out_shape=(
            jax.ShapeDtypeStruct((tok, width), BF16),
            jax.ShapeDtypeStruct((shards * SLOTS, width), BF16),
        ),
        in_specs=[SMEM, SMEM] + [VMEM_SPEC] * (3 + len(more)) + [ANY] * len(pieces),
        out_specs=(VMEM_SPEC, VMEM_SPEC),
        scratch_shapes=[
            pltpu.VMEM((tok, width), BF16),
            pltpu.VMEM((GROUPS, 2, 2, width // BANDS, LANES), BF16),
            pltpu.VMEM((GROUPS * SLOTS, LANES), F32),
            pltpu.VMEM((GROUPS, SLOTS, LANES), BF16),
            pltpu.SemaphoreType.DMA((len(pieces),)),
            pltpu.SemaphoreType.DMA((GROUPS,)),
        ],
        compiler_params=params(),
        cost_estimate=pl.CostEstimate(
            flops=600_000_000, bytes_accessed=4_000_000, transcendentals=0
        ),
        name="mix",
    )(place, spots, states, gain, attended, *more, *pieces)


def keys_values_kernel(layout, spots, decoded, *refs):
    pieces = refs[: len(layout)]
    out, scratch, arrived = refs[len(layout) :]
    depth = decoded.shape[1] // BANDS
    per = scratch.shape[3] // depth
    copies = start_loads(
        spots, pieces, layout, scratch, arrived, slice(0, scratch.shape[3]), spots[GROUPS]
    )
    for at in range(GROUPS):
        wait_group(copies, at)
        spot = spots[at]
        total = dot(decoded[...], lanes_of(scratch[spot], depth, 0, per)).astype(BF16)
        for group in range(per):
            out[spot * per + group] = total[:, group * LANES : (group + 1) * LANES]


def keys_values(spots, decoded, pieces, layout):
    tok, width = decoded.shape
    height = 2 * width // GROUPS // LANES * (width // BANDS)
    return pl.pallas_call(
        functools.partial(keys_values_kernel, layout),
        out_shape=jax.ShapeDtypeStruct((2 * width // LANES, tok, LANES), BF16),
        in_specs=[SMEM, VMEM_SPEC] + [ANY] * len(pieces),
        out_specs=VMEM_SPEC,
        scratch_shapes=[
            pltpu.VMEM((GROUPS, 2, 2, height, LANES), BF16),
            pltpu.SemaphoreType.DMA((len(pieces),)),
        ],
        compiler_params=params(),
        cost_estimate=pl.CostEstimate(
            flops=1_100_000_000, bytes_accessed=6_000_000, transcendentals=0
        ),
        name="keys_values",
    )(spots, decoded, *pieces)


def decode_kernel(layout, each, spots, queries, local_rows, fetched, multiplicity, *refs):
    pieces = refs[: len(layout)]
    fields, scratch, table, arrived = refs[len(layout) :]
    points, width = queries.shape
    depth = width // BANDS
    count = fetched.shape[0]
    per = 2 * width // GROUPS // LANES
    kept = scratch.shape[3]
    copies = start_loads(
        spots, pieces, layout, scratch, arrived, slice(0, kept), spots[GROUPS]
    )
    padding = jnp.zeros((table.shape[1] - count, LANES), BF16)
    for at in range(GROUPS):
        wait_group(copies, at)
        spot = spots[at]
        total = dot(fetched[...], lanes_of(scratch[spot], depth, 0, per)).astype(BF16)
        for group in range(per):
            table[spot * per + group, :count, :] = total[:, group * LANES : (group + 1) * LANES]
            if table.shape[1] > count:
                table[spot * per + group, count:, :] = padding

    pairs = width // LANES
    scale = BF16(1.0 / math.sqrt(width // HEADS))
    times = multiplicity[...]
    bias = jnp.where(times > 0, 0.0, NEG)
    both = jnp.concatenate([times, times], axis=0)
    rows = []
    for pair in range(pairs):
        rows.append(
            pair_attend(
                queries[:, pair * LANES : (pair + 1) * LANES] * scale,
                jnp.concatenate([local_rows[pair], table[pair]], axis=0),
                jnp.concatenate([local_rows[pairs + pair], table[pairs + pair]], axis=0),
                bias,
                lambda weights: weights * both,
            )
        )
    gridded = jnp.concatenate(rows, axis=1)
    start = per * depth
    halves = depth // LANES
    height = (kept - start) // halves
    padded = jnp.zeros((GROUPS * height, points), F32)
    for chunk, band in enumerate(CHUNKS):
        for half in range(halves):
            at = start + half * height
            weight = scratch[:, chunk // 2, chunk % 2, at : at + height, :]
            first = band * depth + half * LANES
            padded += dot_nt(
                weight.reshape(GROUPS * height, LANES), gridded[:, first : first + LANES]
            )
    parts = [padded[group * height : group * height + each] for group in range(GROUPS)]
    fields[...] = jnp.concatenate(parts, axis=0).astype(BF16)


def decode(spots, queries, local_rows, fetched, multiplicity, pieces, layout, outputs):
    points, width = queries.shape
    tok = local_rows.shape[1]
    height = pieces[0].shape[-2]
    remote = multiplicity.shape[1] - tok
    return pl.pallas_call(
        functools.partial(decode_kernel, layout, outputs // GROUPS),
        out_shape=jax.ShapeDtypeStruct((outputs, points), BF16),
        in_specs=[SMEM] + [VMEM_SPEC] * 4 + [ANY] * len(pieces),
        out_specs=VMEM_SPEC,
        scratch_shapes=[
            pltpu.VMEM((GROUPS, 2, 2, height, LANES), BF16),
            pltpu.VMEM((2 * width // LANES, remote, LANES), BF16),
            pltpu.SemaphoreType.DMA((len(pieces),)),
        ],
        compiler_params=params(),
        cost_estimate=pl.CostEstimate(
            flops=2_000_000_000, bytes_accessed=8_000_000, transcendentals=2_000_000
        ),
        name="decode",
    )(spots, queries, local_rows, fetched, multiplicity, *pieces)


def stacked(*weights):
    parts = []
    for weight in weights:
        for at in range(0, weight.shape[-1], LANES):
            parts.append(weight[..., at : at + LANES])
    return jnp.concatenate(parts, axis=-2)


def pair_x(block, gate=None):
    if gate is not None:
        block, _ = lax.optimization_barrier((block, gate))
    other = lax.ppermute(block, "band", [(i, i ^ 2) for i in range(BANDS)])
    low = lax.axis_index("band") < 2
    return jnp.stack([jnp.where(low, block, other), jnp.where(low, other, block)])


def pair_core(block):
    other = swap_core(block)
    low = lax.axis_index("band") % 2 == 0
    return jnp.stack([jnp.where(low, block, other), jnp.where(low, other, block)])


def carry(block):
    pairs = []
    for i in range(GROUPS):
        here, there = RING[i] * BANDS, RING[(i + 1) % GROUPS] * BANDS
        for x in range(2):
            pairs.append((here + 2 * x, there + 2 * x))
            pairs.append((there + 2 * x + 1, here + 2 * x + 1))
    return lax.ppermute(block, ("seq", "band"), pairs)


def swap_core(block):
    return lax.ppermute(block, "band", [(i, i ^ 1) for i in range(BANDS)])


def ring_spots():
    seq, core = lax.axis_index("seq"), lax.axis_index("band") % 2
    table = np.zeros((2, GROUPS, GROUPS), np.int32)
    for i in range(GROUPS):
        for step in range(GROUPS):
            table[0, RING[i], step] = RING[(i - step) % GROUPS]
            table[1, RING[i], step] = RING[(i + step) % GROUPS]
    return jnp.concatenate([jnp.asarray(table)[core, seq], core.astype(jnp.int32)[None]])


def chain_step(chains, step, gate=None):
    if gate is not None:
        *chains, _ = lax.optimization_barrier((*chains, gate))
    chains = [carry(block) for block in chains]
    pieces = []
    for half, block in enumerate(chains):
        pieces.append((block, (step, half)))
        pieces.append((swap_core(block), (GROUPS - step, 1 - half)))
    return chains, pieces


def ring_step(block, step, gate=None):
    if gate is not None:
        block, _ = lax.optimization_barrier((block, gate))
    if step < GROUPS // 2:
        block = carry(block)
        return block, [(block, (step, None)), (swap_core(block), (GROUPS - step, None))]
    half = lax.dynamic_index_in_dim(block, lax.axis_index("band") % 2, 0, keepdims=False)
    half = carry(half)
    return half, [(half, (step, 0)), (swap_core(half), (step, 1))]


def whole_blocks(*weights):
    parts = []
    for weight, height in weights:
        weight = lax.all_gather(weight, "seq", axis=1, tiled=True)
        weight = lax.all_gather(weight, "band", axis=0, tiled=True)
        depth, columns = weight.shape[0] // BANDS, weight.shape[1] // GROUPS
        weight = weight.reshape(2, 2, depth, GROUPS, columns).transpose(3, 1, 0, 2, 4)
        if height:
            weight = jnp.pad(
                weight.swapaxes(-1, -2), ((0, 0),) * 3 + ((0, height - columns), (0, 0))
            )
        parts.append(weight)
    return stacked(*parts)


def local(
    tokens, ln_gain, w_qkv, w_out, dec_gain, w_kv, w_final, reach, grid_query, neighbours, counts
):
    states = tokens[0]
    tok, width = states.shape
    shards, bands = lax.axis_size("seq"), lax.axis_size("band")
    place = jnp.stack([lax.axis_index("seq"), lax.axis_index("band") % 2]).astype(jnp.int32)
    outputs = w_final.shape[1] * shards
    height = -(-outputs // GROUPS // 16) * 16
    riding = (shards, bands) == (GROUPS, BANDS)
    up = [(i, i + 1) for i in range(shards - 1)]
    down = [(i + 1, i) for i in range(shards - 1)]
    left = lax.ppermute(states[tok - HALF :], "seq", up)
    right = lax.ppermute(states[:HALF], "seq", down)
    if not riding:
        place = place * jnp.array([1, 0], jnp.int32)
    multiplicity, requested, *payload = tables(
        tok, place, neighbours.T, counts.reshape(1, -1), shards, (w_qkv, w_out) if riding else ()
    )
    normed, bias = prepare(
        tok * shards, place, left, states, right, ln_gain.reshape(1, width), reach.reshape(1, tok)
    )
    if riding:
        spots = ring_spots()
        mine = pair_x(payload[0])
        other = swap_core(mine)
        pieces = [(mine, (0, 0)), (other, (0, 1))]
        chains, more = chain_step([mine, other], 1)
        pieces += more
        final = jnp.pad(w_final.T, ((0, height - w_final.shape[1]), (0, 0)))
        second = pair_core(pair_x(stacked(w_kv, final), chains[0]))
        made = project(spots, normed, pieces[:2], None)
        chains, more = chain_step(chains, 2)
        pieces += more
        second, _ = lax.optimization_barrier((second, chains[0]))
        later = [(second, (0, None))]
        chains, more = chain_step(chains, 3, made)
        pieces += more
        made = project(spots, normed, pieces[2:6], made)
        block, more = ring_step(second, 1)
        later += more
        _, more = chain_step(chains[:1], 4, made)
        pieces += more
        made = project(spots, normed, pieces[6:10], made)
        block, more = ring_step(block, 2, made)
        later += more
        block, more = ring_step(block, 3)
        later += more
        attended = attend(spots, normed, bias, pieces[10:], made, (0, 1, 7, 2, 6))
        _, more = ring_step(block, 4)
        later += more
        ids = None
    else:
        spots = jnp.concatenate([jnp.arange(GROUPS, dtype=jnp.int32), jnp.zeros((1,), jnp.int32)])
        block = whole_blocks((w_qkv, 0), (w_out, 0))
        block = jnp.pad(block, ((0, 0),) * 3 + ((0, SLOTS), (0, 0)))
        pieces = [(block[at, half], (at, half)) for at in range(GROUPS) for half in range(2)]
        block = whole_blocks((w_kv, 0), (w_final, height))
        later = [(block[at], (at, None)) for at in range(GROUPS)]
        made = project(spots, normed, pieces[:10], None)
        attended = attend(spots, normed, bias, pieces[10:], made, (0, 1, 2, 3, 4))
        ids = lax.all_to_all(
            requested.reshape(shards, SLOTS).astype(jnp.int32), "seq", 0, 0, tiled=True
        ).reshape(shards * SLOTS, 1)
    layout = tuple(at for _, at in pieces)
    pieces = [piece for piece, _ in pieces]
    decoded, found = mix(
        place, spots, states, attended, dec_gain.reshape(1, width), ids, pieces, layout, shards
    )
    fetched = lax.all_to_all(
        found.reshape(shards, SLOTS, width), "seq", split_axis=0, concat_axis=0, tiled=True
    )
    layout = tuple(at for _, at in later)
    pieces = [piece for piece, _ in later]
    local_rows = keys_values(spots, decoded, pieces, layout)
    fields = decode(
        spots, grid_query[0], local_rows, fetched.reshape(shards * SLOTS, width), multiplicity,
        pieces, layout, outputs,
    )
    return fields[None]


def solution(mesh):
    return jax.shard_map(
        local,
        mesh=mesh,
        in_specs=(
            P("band", "seq", None),
            P(),
            P("band", "seq"),
            P("band", "seq"),
            P(),
            P("band", "seq"),
            P("band", "seq"),
            P("seq"),
            P("band", "seq", None),
            P("seq", None),
            P("seq"),
        ),
        out_specs=P("band", None, "seq"),
        check_vma=False,
    )
```

```python
import functools
import math

import jax
import jax.numpy as jnp
import numpy as np
from jax import lax
from jax.experimental import pallas as pl
from jax.experimental.pallas import tpu as pltpu
from jax.sharding import PartitionSpec as P

HEADS = 16
HALF = 128
C = 12
SLOTS = 16
EPSILON = 1e-05
NEG = -1e30
LANES = 128
GROUPS = 8
BANDS = 4
CHUNKS = (0, 2, 1, 3)
RING = (0, 2, 4, 6, 7, 5, 3, 1)
VMEM = 56 * 1024 * 1024
SMALL = pl.CostEstimate(flops=1000, bytes_accessed=1000, transcendentals=0)
F32 = jnp.float32
BF16 = jnp.bfloat16


def dot(a, b):
    return jnp.dot(a, b, preferred_element_type=F32)


def dot_nt(a, b):
    return lax.dot_general(a, b, (((1,), (1,)), ((), ())), preferred_element_type=F32)


def layer_norm(values, gain):
    values = values.astype(F32)
    centred = values - jnp.mean(values, axis=-1, keepdims=True)
    spread = jnp.mean(centred * centred, axis=-1, keepdims=True)
    return (centred * lax.rsqrt(spread + EPSILON) * gain).astype(BF16)


def params(**more):
    return pltpu.CompilerParams(vmem_limit_bytes=VMEM, **more)


def full_spec(shape):
    return pl.BlockSpec(shape, lambda *_: (0,) * len(shape))


def own_first(rows, core, depth):
    parts = [rows[:, b * depth : (b + 1) * depth] for b in range(BANDS)]
    order = ((0, 1), (2, 3), (1, 0), (3, 2))
    return jnp.concatenate([jnp.where(core == 0, parts[a], parts[b]) for a, b in order], axis=1)


def as_column(row):
    return jnp.broadcast_to(row, (8, row.shape[1])).T[:, :1]


def prepare_kernel(
    total, place, left, own, right, gain, reach, neighbours, counts, normed, bias, multiplicity
):
    tok = own.shape[0]
    depth = own.shape[1] // BANDS
    for at, part in ((0, left), (HALF, own), (HALF + tok, right)):
        rows = layer_norm(part[...], gain[...])
        normed[at : at + part.shape[0], :] = own_first(rows, place[1], depth)

    first = place[0] * tok
    span = 3 * HALF
    row = lax.broadcasted_iota(jnp.int32, (HALF, span), 0)
    col = lax.broadcasted_iota(jnp.int32, (HALF, span), 1)
    away = jnp.abs(row + HALF - col)
    limit = as_column(reach[...])
    for block in range(tok // HALF):
        key = first + (block - 1) * HALF + col
        allowed = (away <= limit[block * HALF : (block + 1) * HALF, :]) & (key >= 0) & (key < total)
        bias[block] = jnp.where(allowed, 0.0, NEG)

    ids = neighbours[...].T
    used = as_column(counts[...])
    mesh = lax.broadcasted_iota(jnp.int32, multiplicity.shape, 1) + first
    here = jnp.zeros(multiplicity.shape, F32)
    for slot in range(ids.shape[1]):
        here += ((ids[:, slot : slot + 1] == mesh) & (slot < used)).astype(F32)
    multiplicity[...] = here


def prepare(total, place, left, own, right, gain, reach, neighbours, counts):
    tok, width = own.shape
    operands = (left, own, right, gain, reach, neighbours, counts)
    outs = (
        jax.ShapeDtypeStruct((tok + 2 * HALF, width), BF16),
        jax.ShapeDtypeStruct((tok // HALF, HALF, 3 * HALF), F32),
        jax.ShapeDtypeStruct((neighbours.shape[1], tok), F32),
    )
    return pl.pallas_call(
        functools.partial(prepare_kernel, total),
        out_shape=outs,
        in_specs=[pl.BlockSpec(memory_space=pltpu.SMEM)]
        + [pl.BlockSpec(memory_space=pltpu.VMEM)] * len(operands),
        out_specs=[pl.BlockSpec(memory_space=pltpu.VMEM)] * len(outs),
        compiler_params=params(),
        cost_estimate=SMALL,
        name="prepare",
    )(place, *operands)


def tables_kernel(tok, count, neighbours, counts, low, rank, tri, *refs):
    weights, (multiplicity, requested) = refs[:count], refs[count : count + 2]
    first = lax.axis_index("seq") * tok
    slots = neighbours.shape[0]
    ids = neighbours[...].T
    used = as_column(counts[...])
    start = low[...]
    elsewhere = start != first
    hits = []
    for slot in range(slots):
        which = ids[:, slot : slot + 1]
        hits.append(
            ((which >= start) & (which < start + tok) & (slot < used) & elsewhere).astype(F32)
        )
    running = dot(tri[...], sum(hits).astype(BF16))
    order = rank[...]
    asked = jnp.zeros(hits[0].shape, F32)
    there = jnp.zeros(hits[0].shape, F32)
    for slot in range(slots):
        mine = jnp.where(running == order, hits[slot], 0.0)
        there += mine
        offset = (ids[:, slot : slot + 1] - start).astype(F32)
        asked += jnp.where(mine > 0, offset, 0.0)
        running += hits[slot]
    multiplicity[...] = there
    asked = jnp.sum(asked, axis=0, keepdims=True)
    requested[...] = asked.astype(BF16)
    if weights:
        payload = refs[-1]
        at = 0
        for weight in weights:
            depth, columns = weight.shape
            for first in range(0, columns, LANES):
                payload[at : at + depth, :] = weight[:, first : first + LANES]
                at += depth
        payload[at:, :] = jnp.broadcast_to(asked, (SLOTS, LANES)).astype(BF16)


def tables(tok, neighbours, counts, shards, weights):
    points = neighbours.shape[1]
    remote = shards * SLOTS
    column = np.arange(remote)
    low = (column // SLOTS * tok).astype(np.int32)[None]
    rank = (column % SLOTS).astype(np.float32)[None]
    tri = np.tril(np.ones((points, points), np.float32), -1).astype(BF16)
    operands = (neighbours, counts, low, rank, tri) + weights
    outs = (
        jax.ShapeDtypeStruct((points, remote), F32),
        jax.ShapeDtypeStruct((1, remote), BF16),
    )
    if weights:
        rows = sum(weight.shape[0] * weight.shape[1] // LANES for weight in weights) + SLOTS
        outs += (jax.ShapeDtypeStruct((rows, LANES), BF16),)
    return pl.pallas_call(
        functools.partial(tables_kernel, tok, len(weights)),
        out_shape=outs,
        in_specs=[pl.BlockSpec(memory_space=pltpu.VMEM)] * len(operands),
        out_specs=[pl.BlockSpec(memory_space=pltpu.VMEM)] * len(outs),
        compiler_params=params(),
        cost_estimate=SMALL,
        name="tables",
    )(*operands)


def pair_attend(queries, keys, values, bias, weights_of):
    rows = queries.shape[0]
    lane = lax.broadcasted_iota(jnp.int32, (rows, LANES), 1)
    first = lane < LANES // 2
    zero = jnp.zeros_like(queries)
    both = jnp.concatenate(
        [jnp.where(first, queries, zero), jnp.where(first, zero, queries)], axis=0
    )
    scores = dot_nt(both, keys)
    scores = scores + jnp.concatenate([bias, bias], axis=0)
    top = jnp.max(scores, axis=-1, keepdims=True)
    weights = weights_of(jnp.exp(scores - top)).astype(BF16)
    summed = dot(weights, jnp.concatenate([values, jnp.ones_like(values)], axis=1))
    share = summed[:, :LANES] / summed[:, LANES:]
    return jnp.where(first, share[:rows], share[rows:]).astype(BF16)


def start_loads(spots, pieces, layout, scratch, arrived, rows, core=None):
    copies = {}
    for n, (piece, (at, half)) in enumerate(zip(pieces, layout)):
        place = scratch.at[spots[at]]
        if half is None:
            copy = pltpu.make_async_copy(piece.at[:, :, rows, :], place, arrived.at[n])
        else:
            to = half if core is None else (1 - core if half else core)
            copy = pltpu.make_async_copy(piece.at[:, rows, :], place.at[to], arrived.at[n])
        copy.start()
        copies.setdefault(at, []).append(copy)
    return copies


def wait_group(copies, at):
    for copy in copies.get(at, ()):
        copy.wait()


def lanes_of(block, depth, start, count):
    rows = block.shape[0] * block.shape[1] * depth if block.ndim == 4 else block.shape[0] * depth
    columns = [
        block[..., start + g * depth : start + (g + 1) * depth, :].reshape(rows, LANES)
        for g in range(count)
    ]
    return columns[0] if count == 1 else jnp.concatenate(columns, axis=1)


SMEM = pl.BlockSpec(memory_space=pltpu.SMEM)
VMEM_SPEC = pl.BlockSpec(memory_space=pltpu.VMEM)
ANY = pl.BlockSpec(memory_space=pl.ANY)


def projection(normed, weight, depth, per):
    return dot(normed, lanes_of(weight[...], depth, 0, per)).astype(BF16)


def project_kernel(layout, spots, normed, *refs):
    pieces = refs[: len(layout)]
    out, scratch, made, arrived, sent = refs[-5:]
    per = made.shape[1]
    depth = normed.shape[1] // BANDS
    copies = start_loads(spots, pieces, layout, scratch, arrived, slice(0, per * depth))
    writes = []
    for n, at in enumerate(copies):
        wait_group(copies, at)
        total = projection(normed[...], scratch.at[spots[at]], depth, per)
        for group in range(per):
            made[n, group] = total[:, group * LANES : (group + 1) * LANES]
        writes.append(
            pltpu.make_async_copy(made.at[n], out.at[pl.ds(spots[at] * per, per)], sent.at[n])
        )
        writes[-1].start()
    for write in writes:
        write.wait()


def project(spots, normed, pieces, before):
    rows, width = normed.shape
    layout = tuple(place for _, place in pieces)
    arrays = [array for array, _ in pieces]
    per = 3 * width // LANES // GROUPS
    count = len({at for at, _ in layout})
    more = [] if before is None else [before]
    return pl.pallas_call(
        functools.partial(project_kernel, layout),
        out_shape=jax.ShapeDtypeStruct((GROUPS * per, rows, LANES), BF16),
        in_specs=[SMEM, VMEM_SPEC] + [ANY] * (len(arrays) + len(more)),
        out_specs=ANY,
        scratch_shapes=[
            pltpu.VMEM((GROUPS, 2, 2, per * width // BANDS, LANES), BF16),
            pltpu.VMEM((count, per, rows, LANES), BF16),
            pltpu.SemaphoreType.DMA((len(arrays),)),
            pltpu.SemaphoreType.DMA((count,)),
        ],
        input_output_aliases={2 + len(arrays): 0} if more else {},
        compiler_params=params(),
        cost_estimate=SMALL,
        name="project",
    )(spots, normed, *arrays, *more)


def attend_kernel(layout, ready, spots, normed, bias, *refs):
    pieces = refs[: len(layout)]
    made, attended, scratch, projected, arrived, loaded = refs[len(layout) :]
    width = normed.shape[1]
    depth = width // BANDS
    per = projected.shape[0] // GROUPS
    copies = start_loads(spots, pieces, layout, scratch, arrived, slice(0, per * depth))
    reads = []
    for n, at in enumerate(ready):
        place = pl.ds(spots[at] * per, per)
        reads.append(pltpu.make_async_copy(made.at[place], projected.at[place], loaded.at[n]))
        reads[-1].start()
    for at in copies:
        wait_group(copies, at)
        total = projection(normed[...], scratch.at[spots[at]], depth, per)
        for group in range(per):
            projected[spots[at] * per + group] = total[:, group * LANES : (group + 1) * LANES]
    for read in reads:
        read.wait()
    pairs = width // LANES
    scale = BF16(1.0 / math.sqrt(width // HEADS))
    for pair in range(pairs):
        for block in range(bias.shape[0]):
            at = block * HALF
            attended[at : at + HALF, pair * LANES : (pair + 1) * LANES] = pair_attend(
                projected[pair, at + HALF : at + 2 * HALF, :] * scale,
                projected[pairs + pair, at : at + 3 * HALF, :],
                projected[2 * pairs + pair, at : at + 3 * HALF, :],
                bias[block],
                lambda weights: weights,
            )


def attend(spots, normed, bias, pieces, made, ready):
    rows, width = normed.shape
    tok = rows - 2 * HALF
    layout = tuple(place for _, place in pieces)
    arrays = [array for array, _ in pieces]
    per = made.shape[0] // GROUPS
    return pl.pallas_call(
        functools.partial(attend_kernel, layout, ready),
        out_shape=jax.ShapeDtypeStruct((tok, width), BF16),
        in_specs=[SMEM, VMEM_SPEC, VMEM_SPEC] + [ANY] * (len(arrays) + 1),
        out_specs=VMEM_SPEC,
        scratch_shapes=[
            pltpu.VMEM((GROUPS, 2, 2, per * width // BANDS, LANES), BF16),
            pltpu.VMEM(made.shape, BF16),
            pltpu.SemaphoreType.DMA((len(arrays),)),
            pltpu.SemaphoreType.DMA((len(ready),)),
        ],
        compiler_params=params(),
        cost_estimate=SMALL,
        name="attend",
    )(spots, normed, bias, *arrays, made)


def picked_rows(place, ids, spots, rows, asked, arrived):
    tok = rows.shape[0]
    if spots is None:
        which = ids[...]
    else:
        for at in range(GROUPS):
            asked[pl.ds(spots[at] * SLOTS, SLOTS), :] = jnp.broadcast_to(
                arrived[at, 0:1, :].astype(F32), (SLOTS, LANES)
            )
        count = GROUPS * SLOTS
        lane = lax.broadcasted_iota(jnp.int32, (count, LANES), 1)
        slot = lax.broadcasted_iota(jnp.int32, (count, LANES), 0) % SLOTS
        mine = jnp.where(lane == place[0] * SLOTS + slot, asked[...], 0.0)
        which = jnp.sum(mine, axis=1, keepdims=True).astype(jnp.int32)
    here = lax.broadcasted_iota(jnp.int32, (which.shape[0], tok), 1)
    return dot((which == here).astype(BF16), rows).astype(BF16)


def chunked(values, depth):
    return jnp.concatenate([values[:, b * depth : (b + 1) * depth] for b in CHUNKS], axis=1)


def mix_kernel(layout, riding, place, spots, states, gain, *refs):
    attended, refs = refs[0], refs[1:]
    ids = None
    if not riding:
        ids, refs = refs[0], refs[1:]
    pieces = refs[: len(layout)]
    decoded, found, mixed, scratch, asked, notes, arrived, noted = refs[len(layout) :]
    width = states.shape[1]
    depth = width // BANDS
    start = 3 * width // GROUPS // LANES * depth
    copies = start_loads(spots, pieces, layout, scratch, arrived, slice(start, start + depth))
    reads = []
    if riding:
        for piece, (at, core) in zip(pieces, layout):
            if core == 0:
                end = piece.shape[-2]
                reads.append(
                    pltpu.make_async_copy(
                        piece.at[0, end - SLOTS : end, :], notes.at[at], noted.at[at]
                    )
                )
                reads[-1].start()
    inputs = own_first(attended[...], place[1], depth)
    for at in range(GROUPS):
        wait_group(copies, at)
        spot = spots[at]
        columns = pl.ds(pl.multiple_of(spot * LANES, LANES), LANES)
        total = dot(inputs, lanes_of(scratch[spot], depth, 0, 1))
        mixed[:, columns] = (states[:, columns].astype(F32) + total).astype(BF16)
    for read in reads:
        read.wait()
    rows = chunked(layer_norm(mixed[...], gain[...]), depth)
    decoded[...] = rows
    found[...] = picked_rows(place, ids, spots if riding else None, rows, asked, notes)


def mix(place, spots, states, attended, gain, ids, pieces, layout, shards):
    tok, width = states.shape
    more = [] if ids is None else [ids]
    return pl.pallas_call(
        functools.partial(mix_kernel, layout, ids is None),
        out_shape=(
            jax.ShapeDtypeStruct((tok, width), BF16),
            jax.ShapeDtypeStruct((shards * SLOTS, width), BF16),
        ),
        in_specs=[SMEM, SMEM] + [VMEM_SPEC] * (3 + len(more)) + [ANY] * len(pieces),
        out_specs=(VMEM_SPEC, VMEM_SPEC),
        scratch_shapes=[
            pltpu.VMEM((tok, width), BF16),
            pltpu.VMEM((GROUPS, 2, 2, width // BANDS, LANES), BF16),
            pltpu.VMEM((GROUPS * SLOTS, LANES), F32),
            pltpu.VMEM((GROUPS, SLOTS, LANES), BF16),
            pltpu.SemaphoreType.DMA((len(pieces),)),
            pltpu.SemaphoreType.DMA((GROUPS,)),
        ],
        compiler_params=params(),
        cost_estimate=SMALL,
        name="mix",
    )(place, spots, states, gain, attended, *more, *pieces)


def keys_values_kernel(layout, spots, decoded, *refs):
    pieces = refs[: len(layout)]
    out, scratch, arrived = refs[len(layout) :]
    depth = decoded.shape[1] // BANDS
    per = scratch.shape[3] // depth
    copies = start_loads(
        spots, pieces, layout, scratch, arrived, slice(0, scratch.shape[3]), spots[GROUPS]
    )
    for at in range(GROUPS):
        wait_group(copies, at)
        spot = spots[at]
        total = dot(decoded[...], lanes_of(scratch[spot], depth, 0, per)).astype(BF16)
        for group in range(per):
            out[spot * per + group] = total[:, group * LANES : (group + 1) * LANES]


def keys_values(spots, decoded, pieces, layout):
    tok, width = decoded.shape
    height = 2 * width // GROUPS // LANES * (width // BANDS)
    return pl.pallas_call(
        functools.partial(keys_values_kernel, layout),
        out_shape=jax.ShapeDtypeStruct((2 * width // LANES, tok, LANES), BF16),
        in_specs=[SMEM, VMEM_SPEC] + [ANY] * len(pieces),
        out_specs=VMEM_SPEC,
        scratch_shapes=[
            pltpu.VMEM((GROUPS, 2, 2, height, LANES), BF16),
            pltpu.SemaphoreType.DMA((len(pieces),)),
        ],
        compiler_params=params(),
        cost_estimate=SMALL,
        name="keys_values",
    )(spots, decoded, *pieces)


def decode_kernel(layout, each, spots, queries, local_rows, fetched, here, there, *refs):
    pieces = refs[: len(layout)]
    fields, scratch, table, arrived = refs[len(layout) :]
    points, width = queries.shape
    depth = width // BANDS
    count = fetched.shape[0]
    per = 2 * width // GROUPS // LANES
    kept = scratch.shape[3]
    copies = start_loads(
        spots, pieces, layout, scratch, arrived, slice(0, kept), spots[GROUPS]
    )
    padding = jnp.zeros((table.shape[1] - count, LANES), BF16)
    for at in range(GROUPS):
        wait_group(copies, at)
        spot = spots[at]
        total = dot(fetched[...], lanes_of(scratch[spot], depth, 0, per)).astype(BF16)
        for group in range(per):
            table[spot * per + group, :count, :] = total[:, group * LANES : (group + 1) * LANES]
            if table.shape[1] > count:
                table[spot * per + group, count:, :] = padding

    pairs = width // LANES
    scale = BF16(1.0 / math.sqrt(width // HEADS))
    times = jnp.concatenate([here[...], there[...]], axis=1)
    bias = jnp.where(times > 0, 0.0, NEG)
    both = jnp.concatenate([times, times], axis=0)
    rows = []
    for pair in range(pairs):
        rows.append(
            pair_attend(
                queries[:, pair * LANES : (pair + 1) * LANES] * scale,
                jnp.concatenate([local_rows[pair], table[pair]], axis=0),
                jnp.concatenate([local_rows[pairs + pair], table[pairs + pair]], axis=0),
                bias,
                lambda weights: weights * both,
            )
        )
    gridded = jnp.concatenate(rows, axis=1)
    start = per * depth
    halves = depth // LANES
    height = (kept - start) // halves
    padded = jnp.zeros((GROUPS * height, points), F32)
    for chunk, band in enumerate(CHUNKS):
        for half in range(halves):
            at = start + half * height
            weight = scratch[:, chunk // 2, chunk % 2, at : at + height, :]
            first = band * depth + half * LANES
            padded += dot_nt(
                weight.reshape(GROUPS * height, LANES), gridded[:, first : first + LANES]
            )
    parts = [padded[group * height : group * height + each] for group in range(GROUPS)]
    fields[...] = jnp.concatenate(parts, axis=0).astype(BF16)


def decode(spots, queries, local_rows, fetched, here, there, pieces, layout, outputs):
    points, width = queries.shape
    height = pieces[0].shape[-2]
    remote = there.shape[1]
    return pl.pallas_call(
        functools.partial(decode_kernel, layout, outputs // GROUPS),
        out_shape=jax.ShapeDtypeStruct((outputs, points), BF16),
        in_specs=[SMEM] + [VMEM_SPEC] * 5 + [ANY] * len(pieces),
        out_specs=VMEM_SPEC,
        scratch_shapes=[
            pltpu.VMEM((GROUPS, 2, 2, height, LANES), BF16),
            pltpu.VMEM((2 * width // LANES, remote, LANES), BF16),
            pltpu.SemaphoreType.DMA((len(pieces),)),
        ],
        compiler_params=params(),
        cost_estimate=SMALL,
        name="decode",
    )(spots, queries, local_rows, fetched, here, there, *pieces)


def stacked(*weights):
    parts = []
    for weight in weights:
        for at in range(0, weight.shape[-1], LANES):
            parts.append(weight[..., at : at + LANES])
    return jnp.concatenate(parts, axis=-2)


def pair_x(block, gate=None):
    if gate is not None:
        block, _ = lax.optimization_barrier((block, gate))
    other = lax.ppermute(block, "band", [(i, i ^ 2) for i in range(BANDS)])
    low = lax.axis_index("band") < 2
    return jnp.stack([jnp.where(low, block, other), jnp.where(low, other, block)])


def pair_core(block):
    other = swap_core(block)
    low = lax.axis_index("band") % 2 == 0
    return jnp.stack([jnp.where(low, block, other), jnp.where(low, other, block)])


def carry(block):
    pairs = []
    for i in range(GROUPS):
        here, there = RING[i] * BANDS, RING[(i + 1) % GROUPS] * BANDS
        for x in range(2):
            pairs.append((here + 2 * x, there + 2 * x))
            pairs.append((there + 2 * x + 1, here + 2 * x + 1))
    return lax.ppermute(block, ("seq", "band"), pairs)


def swap_core(block):
    return lax.ppermute(block, "band", [(i, i ^ 1) for i in range(BANDS)])


def ring_spots():
    seq, core = lax.axis_index("seq"), lax.axis_index("band") % 2
    table = np.zeros((2, GROUPS, GROUPS), np.int32)
    for i in range(GROUPS):
        for step in range(GROUPS):
            table[0, RING[i], step] = RING[(i - step) % GROUPS]
            table[1, RING[i], step] = RING[(i + step) % GROUPS]
    return jnp.concatenate([jnp.asarray(table)[core, seq], core.astype(jnp.int32)[None]])


def chain_step(chains, step, gate=None):
    if gate is not None:
        *chains, _ = lax.optimization_barrier((*chains, gate))
    chains = [carry(block) for block in chains]
    pieces = []
    for half, block in enumerate(chains):
        pieces.append((block, (step, half)))
        pieces.append((swap_core(block), (GROUPS - step, 1 - half)))
    return chains, pieces


def ring_step(block, step, gate=None):
    if gate is not None:
        block, _ = lax.optimization_barrier((block, gate))
    if step < GROUPS // 2:
        block = carry(block)
        return block, [(block, (step, None)), (swap_core(block), (GROUPS - step, None))]
    half = lax.dynamic_index_in_dim(block, lax.axis_index("band") % 2, 0, keepdims=False)
    half = carry(half)
    return half, [(half, (step, 0)), (swap_core(half), (step, 1))]


def whole_blocks(*weights):
    parts = []
    for weight, height in weights:
        weight = lax.all_gather(weight, "seq", axis=1, tiled=True)
        weight = lax.all_gather(weight, "band", axis=0, tiled=True)
        depth, columns = weight.shape[0] // BANDS, weight.shape[1] // GROUPS
        weight = weight.reshape(2, 2, depth, GROUPS, columns).transpose(3, 1, 0, 2, 4)
        if height:
            weight = jnp.pad(
                weight.swapaxes(-1, -2), ((0, 0),) * 3 + ((0, height - columns), (0, 0))
            )
        parts.append(weight)
    return stacked(*parts)


def local(
    tokens, ln_gain, w_qkv, w_out, dec_gain, w_kv, w_final, reach, grid_query, neighbours, counts
):
    states = tokens[0]
    tok, width = states.shape
    shards, bands = lax.axis_size("seq"), lax.axis_size("band")
    place = jnp.stack([lax.axis_index("seq"), lax.axis_index("band") % 2]).astype(jnp.int32)
    outputs = w_final.shape[1] * shards
    height = -(-outputs // GROUPS // 16) * 16
    riding = (shards, bands) == (GROUPS, BANDS)
    up = [(i, i + 1) for i in range(shards - 1)]
    down = [(i + 1, i) for i in range(shards - 1)]
    left = lax.ppermute(states[tok - HALF :], "seq", up)
    right = lax.ppermute(states[:HALF], "seq", down)
    if not riding:
        place = place * jnp.array([1, 0], jnp.int32)
    slots = (neighbours.T, counts.reshape(1, -1))
    there, requested, *payload = tables(tok, *slots, shards, (w_qkv, w_out) if riding else ())
    normed, bias, here = prepare(
        tok * shards, place, left, states, right, ln_gain.reshape(1, width),
        reach.reshape(1, tok), *slots,
    )
    if riding:
        spots = ring_spots()
        mine = pair_x(payload[0])
        mine, _, _ = lax.optimization_barrier((mine, left, right))
        other = swap_core(mine)
        pieces = [(mine, (0, 0)), (other, (0, 1))]
        chains, more = chain_step([mine, other], 1)
        pieces += more
        final = jnp.pad(w_final.T, ((0, height - w_final.shape[1]), (0, 0)))
        second = pair_core(pair_x(stacked(w_kv, final), chains[0]))
        later = [(second, (0, None))]
        chains, more = chain_step(chains, 2)
        pieces += more
        chains, more = chain_step(chains, 3)
        pieces += more
        second, *_ = lax.optimization_barrier((second, *chains))
        last, more = chain_step(chains[:1], 4)
        pieces += more
        made = project(spots, normed, pieces[:6], None)
        block, more = ring_step(second, 1, made)
        later += more
        made = project(spots, normed, pieces[6:10], made)
        block, more = ring_step(block, 2, (made, last[0], pieces[11][0], pieces[13][0]))
        later += more
        attended = attend(spots, normed, bias, pieces[10:], made, (0, 1, 7, 2, 6))
        block, more = ring_step(block, 3, attended)
        later += more
        ids = None
    else:
        spots = jnp.concatenate([jnp.arange(GROUPS, dtype=jnp.int32), jnp.zeros((1,), jnp.int32)])
        block = whole_blocks((w_qkv, 0), (w_out, 0))
        block = jnp.pad(block, ((0, 0),) * 3 + ((0, SLOTS), (0, 0)))
        pieces = [(block[at, half], (at, half)) for at in range(GROUPS) for half in range(2)]
        block = whole_blocks((w_kv, 0), (w_final, height))
        later = [(block[at], (at, None)) for at in range(GROUPS)]
        made = project(spots, normed, pieces[:10], None)
        attended = attend(spots, normed, bias, pieces[10:], made, (0, 1, 2, 3, 4))
        ids = lax.all_to_all(
            requested.reshape(shards, SLOTS).astype(jnp.int32), "seq", 0, 0, tiled=True
        ).reshape(shards * SLOTS, 1)
    layout = tuple(at for _, at in pieces)
    pieces = [piece for piece, _ in pieces]
    decoded, found = mix(
        place, spots, states, attended, dec_gain.reshape(1, width), ids, pieces, layout, shards
    )
    if riding:
        _, more = ring_step(block, 4, found)
        later += more
    fetched = lax.all_to_all(
        found.reshape(shards, SLOTS, width), "seq", split_axis=0, concat_axis=0, tiled=True
    )
    layout = tuple(at for _, at in later)
    pieces = [piece for piece, _ in later]
    local_rows = keys_values(spots, decoded, pieces, layout)
    fields = decode(
        spots, grid_query[0], local_rows, fetched.reshape(shards * SLOTS, width), here, there,
        pieces, layout, outputs,
    )
    return fields[None]


def solution(mesh):
    return jax.shard_map(
        local,
        mesh=mesh,
        in_specs=(
            P("band", "seq", None),
            P(),
            P("band", "seq"),
            P("band", "seq"),
            P(),
            P("band", "seq"),
            P("band", "seq"),
            P("seq"),
            P("band", "seq", None),
            P("seq", None),
            P("seq"),
        ),
        out_specs=P("band", None, "seq"),
        check_vma=False,
    )
```

```python
import functools
import math

import jax
import jax.numpy as jnp
import numpy as np
from jax import lax
from jax.experimental import pallas as pl
from jax.experimental.pallas import tpu as pltpu
from jax.sharding import PartitionSpec as P

HEADS = 16
HALF = 128
C = 12
SLOTS = 16
EPSILON = 1e-05
NEG = -1e30
LANES = 128
GROUPS = 8
BANDS = 4
CHUNKS = (0, 2, 1, 3)
RING = (0, 2, 4, 6, 7, 5, 3, 1)
VMEM = 20 * 1024 * 1024
SMALL = pl.CostEstimate(flops=1000, bytes_accessed=1000, transcendentals=0)
F32 = jnp.float32
BF16 = jnp.bfloat16


def dot(a, b):
    return jnp.dot(a, b, preferred_element_type=F32)


def dot_nt(a, b):
    return lax.dot_general(a, b, (((1,), (1,)), ((), ())), preferred_element_type=F32)


def layer_norm(values, gain):
    values = values.astype(F32)
    centred = values - jnp.mean(values, axis=-1, keepdims=True)
    spread = jnp.mean(centred * centred, axis=-1, keepdims=True)
    return (centred * lax.rsqrt(spread + EPSILON) * gain).astype(BF16)


def params(**more):
    return pltpu.CompilerParams(vmem_limit_bytes=VMEM, **more)


def full_spec(shape):
    return pl.BlockSpec(shape, lambda *_: (0,) * len(shape))


def own_first(rows, core, depth):
    parts = [rows[:, b * depth : (b + 1) * depth] for b in range(BANDS)]
    order = ((0, 1), (2, 3), (1, 0), (3, 2))
    return jnp.concatenate([jnp.where(core == 0, parts[a], parts[b]) for a, b in order], axis=1)


def as_column(row):
    return jnp.broadcast_to(row, (8, row.shape[1])).T[:, :1]


def prepare_kernel(
    total, place, left, own, right, gain, reach, neighbours, counts, normed, bias, multiplicity
):
    tok = own.shape[0]
    depth = own.shape[1] // BANDS
    for at, part in ((0, left), (HALF, own), (HALF + tok, right)):
        rows = layer_norm(part[...], gain[...])
        normed[at : at + part.shape[0], :] = own_first(rows, place[1], depth)

    first = place[0] * tok
    span = 3 * HALF
    row = lax.broadcasted_iota(jnp.int32, (HALF, span), 0)
    col = lax.broadcasted_iota(jnp.int32, (HALF, span), 1)
    away = jnp.abs(row + HALF - col)
    limit = as_column(reach[...])
    for block in range(tok // HALF):
        key = first + (block - 1) * HALF + col
        allowed = (away <= limit[block * HALF : (block + 1) * HALF, :]) & (key >= 0) & (key < total)
        bias[block] = jnp.where(allowed, 0.0, NEG)

    ids = neighbours[...].T
    used = as_column(counts[...])
    mesh = lax.broadcasted_iota(jnp.int32, multiplicity.shape, 1) + first
    here = jnp.zeros(multiplicity.shape, F32)
    for slot in range(ids.shape[1]):
        here += ((ids[:, slot : slot + 1] == mesh) & (slot < used)).astype(F32)
    multiplicity[...] = here


def prepare(total, place, left, own, right, gain, reach, neighbours, counts):
    tok, width = own.shape
    operands = (left, own, right, gain, reach, neighbours, counts)
    outs = (
        jax.ShapeDtypeStruct((tok + 2 * HALF, width), BF16),
        jax.ShapeDtypeStruct((tok // HALF, HALF, 3 * HALF), F32),
        jax.ShapeDtypeStruct((neighbours.shape[1], tok), F32),
    )
    return pl.pallas_call(
        functools.partial(prepare_kernel, total),
        out_shape=outs,
        in_specs=[pl.BlockSpec(memory_space=pltpu.SMEM)]
        + [pl.BlockSpec(memory_space=pltpu.VMEM)] * len(operands),
        out_specs=[pl.BlockSpec(memory_space=pltpu.VMEM)] * len(outs),
        compiler_params=params(),
        cost_estimate=SMALL,
        name="prepare",
    )(place, *operands)


def tables_kernel(tok, count, neighbours, counts, low, rank, tri, *refs):
    weights, (multiplicity, requested) = refs[:count], refs[count : count + 2]
    first = lax.axis_index("seq") * tok
    slots = neighbours.shape[0]
    ids = neighbours[...].T
    used = as_column(counts[...])
    start = low[...]
    elsewhere = start != first
    hits = []
    for slot in range(slots):
        which = ids[:, slot : slot + 1]
        hits.append(
            ((which >= start) & (which < start + tok) & (slot < used) & elsewhere).astype(F32)
        )
    running = dot(tri[...], sum(hits).astype(BF16))
    order = rank[...]
    asked = jnp.zeros(hits[0].shape, F32)
    there = jnp.zeros(hits[0].shape, F32)
    for slot in range(slots):
        mine = jnp.where(running == order, hits[slot], 0.0)
        there += mine
        offset = (ids[:, slot : slot + 1] - start).astype(F32)
        asked += jnp.where(mine > 0, offset, 0.0)
        running += hits[slot]
    multiplicity[...] = there
    asked = jnp.sum(asked, axis=0, keepdims=True)
    requested[...] = asked.astype(BF16)
    if weights:
        payload = refs[-1]
        at = 0
        for weight in weights:
            depth, columns = weight.shape
            for first in range(0, columns, LANES):
                payload[at : at + depth, :] = weight[:, first : first + LANES]
                at += depth
        payload[at:, :] = jnp.broadcast_to(asked, (SLOTS, LANES)).astype(BF16)


def tables(tok, neighbours, counts, shards, weights):
    points = neighbours.shape[1]
    remote = shards * SLOTS
    column = np.arange(remote)
    low = (column // SLOTS * tok).astype(np.int32)[None]
    rank = (column % SLOTS).astype(np.float32)[None]
    tri = np.tril(np.ones((points, points), np.float32), -1).astype(BF16)
    operands = (neighbours, counts, low, rank, tri) + weights
    outs = (
        jax.ShapeDtypeStruct((points, remote), F32),
        jax.ShapeDtypeStruct((1, remote), BF16),
    )
    if weights:
        rows = sum(weight.shape[0] * weight.shape[1] // LANES for weight in weights) + SLOTS
        outs += (jax.ShapeDtypeStruct((rows, LANES), BF16),)
    return pl.pallas_call(
        functools.partial(tables_kernel, tok, len(weights)),
        out_shape=outs,
        in_specs=[pl.BlockSpec(memory_space=pltpu.VMEM)] * len(operands),
        out_specs=[pl.BlockSpec(memory_space=pltpu.VMEM)] * len(outs),
        compiler_params=params(),
        cost_estimate=SMALL,
        name="tables",
    )(*operands)


def pair_attend(queries, keys, values, bias, weights_of):
    rows = queries.shape[0]
    lane = lax.broadcasted_iota(jnp.int32, (rows, LANES), 1)
    first = lane < LANES // 2
    zero = jnp.zeros_like(queries)
    both = jnp.concatenate(
        [jnp.where(first, queries, zero), jnp.where(first, zero, queries)], axis=0
    )
    scores = dot_nt(both, keys)
    scores = scores + jnp.concatenate([bias, bias], axis=0)
    top = jnp.max(scores, axis=-1, keepdims=True)
    weights = weights_of(jnp.exp(scores - top)).astype(BF16)
    summed = dot(weights, jnp.concatenate([values, jnp.ones_like(values)], axis=1))
    share = summed[:, :LANES] / summed[:, LANES:]
    return jnp.where(first, share[:rows], share[rows:]).astype(BF16)


def start_loads(spots, pieces, layout, scratch, arrived, rows, core=None):
    copies = {}
    for n, (piece, (at, half)) in enumerate(zip(pieces, layout)):
        copies.setdefault(at, [])
        place = scratch.at[list(copies).index(at) if spots is None else spots[at]]
        if half is None:
            copy = pltpu.make_async_copy(piece.at[:, :, rows, :], place, arrived.at[n])
        else:
            to = half if core is None else (1 - core if half else core)
            copy = pltpu.make_async_copy(piece.at[:, rows, :], place.at[to], arrived.at[n])
        copy.start()
        copies[at].append(copy)
    return copies


def wait_group(copies, at):
    for copy in copies.get(at, ()):
        copy.wait()


def lanes_of(block, depth, start, count):
    rows = block.shape[0] * block.shape[1] * depth if block.ndim == 4 else block.shape[0] * depth
    columns = [
        block[..., start + g * depth : start + (g + 1) * depth, :].reshape(rows, LANES)
        for g in range(count)
    ]
    return columns[0] if count == 1 else jnp.concatenate(columns, axis=1)


SMEM = pl.BlockSpec(memory_space=pltpu.SMEM)
VMEM_SPEC = pl.BlockSpec(memory_space=pltpu.VMEM)
ANY = pl.BlockSpec(memory_space=pl.ANY)


def projection(normed, weight, depth, per):
    return dot(normed, lanes_of(weight[...], depth, 0, per)).astype(BF16)


def project_kernel(layout, spots, normed, *refs):
    pieces = refs[: len(layout)]
    out, scratch, made, arrived, sent = refs[-5:]
    per = made.shape[1]
    depth = normed.shape[1] // BANDS
    copies = start_loads(None, pieces, layout, scratch, arrived, slice(0, per * depth))
    writes = []
    for n, at in enumerate(copies):
        wait_group(copies, at)
        total = projection(normed[...], scratch.at[n], depth, per)
        for group in range(per):
            made[n, group] = total[:, group * LANES : (group + 1) * LANES]
        writes.append(
            pltpu.make_async_copy(made.at[n], out.at[pl.ds(spots[at] * per, per)], sent.at[n])
        )
        writes[-1].start()
    for write in writes:
        write.wait()


def project(spots, normed, pieces, before):
    rows, width = normed.shape
    layout = tuple(place for _, place in pieces)
    arrays = [array for array, _ in pieces]
    per = 3 * width // LANES // GROUPS
    count = len({at for at, _ in layout})
    more = [] if before is None else [before]
    return pl.pallas_call(
        functools.partial(project_kernel, layout),
        out_shape=jax.ShapeDtypeStruct((GROUPS * per, rows, LANES), BF16),
        in_specs=[SMEM, VMEM_SPEC] + [ANY] * (len(arrays) + len(more)),
        out_specs=ANY,
        scratch_shapes=[
            pltpu.VMEM((count, 2, 2, per * width // BANDS, LANES), BF16),
            pltpu.VMEM((count, per, rows, LANES), BF16),
            pltpu.SemaphoreType.DMA((len(arrays),)),
            pltpu.SemaphoreType.DMA((count,)),
        ],
        input_output_aliases={2 + len(arrays): 0} if more else {},
        compiler_params=params(),
        cost_estimate=SMALL,
        name="project",
    )(spots, normed, *arrays, *more)


def attend_kernel(layout, ready, spots, normed, bias, *refs):
    pieces = refs[: len(layout)]
    made, attended, scratch, projected, arrived, loaded = refs[len(layout) :]
    width = normed.shape[1]
    depth = width // BANDS
    per = projected.shape[0] // GROUPS
    copies = start_loads(None, pieces, layout, scratch, arrived, slice(0, per * depth))
    reads = []
    for n, at in enumerate(ready):
        place = pl.ds(spots[at] * per, per)
        reads.append(pltpu.make_async_copy(made.at[place], projected.at[place], loaded.at[n]))
        reads[-1].start()
    for n, at in enumerate(copies):
        wait_group(copies, at)
        total = projection(normed[...], scratch.at[n], depth, per)
        for group in range(per):
            projected[spots[at] * per + group] = total[:, group * LANES : (group + 1) * LANES]
    for read in reads:
        read.wait()
    pairs = width // LANES
    scale = BF16(1.0 / math.sqrt(width // HEADS))
    for pair in range(pairs):
        for block in range(bias.shape[0]):
            at = block * HALF
            attended[at : at + HALF, pair * LANES : (pair + 1) * LANES] = pair_attend(
                projected[pair, at + HALF : at + 2 * HALF, :] * scale,
                projected[pairs + pair, at : at + 3 * HALF, :],
                projected[2 * pairs + pair, at : at + 3 * HALF, :],
                bias[block],
                lambda weights: weights,
            )


def attend(spots, normed, bias, pieces, made, ready):
    rows, width = normed.shape
    tok = rows - 2 * HALF
    layout = tuple(place for _, place in pieces)
    arrays = [array for array, _ in pieces]
    per = made.shape[0] // GROUPS
    return pl.pallas_call(
        functools.partial(attend_kernel, layout, ready),
        out_shape=jax.ShapeDtypeStruct((tok, width), BF16),
        in_specs=[SMEM, VMEM_SPEC, VMEM_SPEC] + [ANY] * (len(arrays) + 1),
        out_specs=VMEM_SPEC,
        scratch_shapes=[
            pltpu.VMEM((len({at for at, _ in layout}), 2, 2, per * width // BANDS, LANES), BF16),
            pltpu.VMEM(made.shape, BF16),
            pltpu.SemaphoreType.DMA((len(arrays),)),
            pltpu.SemaphoreType.DMA((len(ready),)),
        ],
        compiler_params=params(),
        cost_estimate=SMALL,
        name="attend",
    )(spots, normed, bias, *arrays, made)


def picked_rows(place, ids, spots, rows, asked, arrived):
    tok = rows.shape[0]
    if spots is None:
        which = ids[...]
    else:
        for at in range(GROUPS):
            asked[pl.ds(spots[at] * SLOTS, SLOTS), :] = jnp.broadcast_to(
                arrived[at, 0:1, :].astype(F32), (SLOTS, LANES)
            )
        count = GROUPS * SLOTS
        lane = lax.broadcasted_iota(jnp.int32, (count, LANES), 1)
        slot = lax.broadcasted_iota(jnp.int32, (count, LANES), 0) % SLOTS
        mine = jnp.where(lane == place[0] * SLOTS + slot, asked[...], 0.0)
        which = jnp.sum(mine, axis=1, keepdims=True).astype(jnp.int32)
    here = lax.broadcasted_iota(jnp.int32, (which.shape[0], tok), 1)
    return dot((which == here).astype(BF16), rows).astype(BF16)


def chunked(values, depth):
    return jnp.concatenate([values[:, b * depth : (b + 1) * depth] for b in CHUNKS], axis=1)


def mix_kernel(layout, riding, place, spots, states, gain, *refs):
    attended, refs = refs[0], refs[1:]
    ids = None
    if not riding:
        ids, refs = refs[0], refs[1:]
    pieces = refs[: len(layout)]
    decoded, found, mixed, scratch, asked, notes, arrived, noted = refs[len(layout) :]
    width = states.shape[1]
    depth = width // BANDS
    start = 3 * width // GROUPS // LANES * depth
    copies = start_loads(spots, pieces, layout, scratch, arrived, slice(start, start + depth))
    reads = []
    if riding:
        for piece, (at, core) in zip(pieces, layout):
            if core == 0:
                end = piece.shape[-2]
                reads.append(
                    pltpu.make_async_copy(
                        piece.at[0, end - SLOTS : end, :], notes.at[at], noted.at[at]
                    )
                )
                reads[-1].start()
    inputs = own_first(attended[...], place[1], depth)
    for at in range(GROUPS):
        wait_group(copies, at)
        spot = spots[at]
        columns = pl.ds(pl.multiple_of(spot * LANES, LANES), LANES)
        total = dot(inputs, lanes_of(scratch[spot], depth, 0, 1))
        mixed[:, columns] = (states[:, columns].astype(F32) + total).astype(BF16)
    for read in reads:
        read.wait()
    rows = chunked(layer_norm(mixed[...], gain[...]), depth)
    decoded[...] = rows
    found[...] = picked_rows(place, ids, spots if riding else None, rows, asked, notes)


def mix(place, spots, states, attended, gain, ids, pieces, layout, shards):
    tok, width = states.shape
    more = [] if ids is None else [ids]
    return pl.pallas_call(
        functools.partial(mix_kernel, layout, ids is None),
        out_shape=(
            jax.ShapeDtypeStruct((tok, width), BF16),
            jax.ShapeDtypeStruct((shards * SLOTS, width), BF16),
        ),
        in_specs=[SMEM, SMEM] + [VMEM_SPEC] * (3 + len(more)) + [ANY] * len(pieces),
        out_specs=(VMEM_SPEC, VMEM_SPEC),
        scratch_shapes=[
            pltpu.VMEM((tok, width), BF16),
            pltpu.VMEM((GROUPS, 2, 2, width // BANDS, LANES), BF16),
            pltpu.VMEM((GROUPS * SLOTS, LANES), F32),
            pltpu.VMEM((GROUPS, SLOTS, LANES), BF16),
            pltpu.SemaphoreType.DMA((len(pieces),)),
            pltpu.SemaphoreType.DMA((GROUPS,)),
        ],
        compiler_params=params(),
        cost_estimate=SMALL,
        name="mix",
    )(place, spots, states, gain, attended, *more, *pieces)


def keys_values_kernel(layout, spots, decoded, *refs):
    pieces = refs[: len(layout)]
    out, scratch, arrived = refs[len(layout) :]
    depth = decoded.shape[1] // BANDS
    per = scratch.shape[3] // depth
    copies = start_loads(
        spots, pieces, layout, scratch, arrived, slice(0, scratch.shape[3]), spots[GROUPS]
    )
    for at in range(GROUPS):
        wait_group(copies, at)
        spot = spots[at]
        total = dot(decoded[...], lanes_of(scratch[spot], depth, 0, per)).astype(BF16)
        for group in range(per):
            out[spot * per + group] = total[:, group * LANES : (group + 1) * LANES]


def keys_values(spots, decoded, pieces, layout):
    tok, width = decoded.shape
    height = 2 * width // GROUPS // LANES * (width // BANDS)
    return pl.pallas_call(
        functools.partial(keys_values_kernel, layout),
        out_shape=jax.ShapeDtypeStruct((2 * width // LANES, tok, LANES), BF16),
        in_specs=[SMEM, VMEM_SPEC] + [ANY] * len(pieces),
        out_specs=VMEM_SPEC,
        scratch_shapes=[
            pltpu.VMEM((GROUPS, 2, 2, height, LANES), BF16),
            pltpu.SemaphoreType.DMA((len(pieces),)),
        ],
        compiler_params=params(),
        cost_estimate=SMALL,
        name="keys_values",
    )(spots, decoded, *pieces)


def decode_kernel(layout, each, spots, queries, local_rows, fetched, here, there, *refs):
    pieces = refs[: len(layout)]
    fields, scratch, table, arrived = refs[len(layout) :]
    points, width = queries.shape
    depth = width // BANDS
    count = fetched.shape[0]
    per = 2 * width // GROUPS // LANES
    kept = scratch.shape[3]
    copies = start_loads(
        spots, pieces, layout, scratch, arrived, slice(0, kept), spots[GROUPS]
    )
    padding = jnp.zeros((table.shape[1] - count, LANES), BF16)
    for at in range(GROUPS):
        wait_group(copies, at)
        spot = spots[at]
        total = dot(fetched[...], lanes_of(scratch[spot], depth, 0, per)).astype(BF16)
        for group in range(per):
            table[spot * per + group, :count, :] = total[:, group * LANES : (group + 1) * LANES]
            if table.shape[1] > count:
                table[spot * per + group, count:, :] = padding

    pairs = width // LANES
    scale = BF16(1.0 / math.sqrt(width // HEADS))
    times = jnp.concatenate([here[...], there[...]], axis=1)
    bias = jnp.where(times > 0, 0.0, NEG)
    both = jnp.concatenate([times, times], axis=0)
    rows = []
    for pair in range(pairs):
        rows.append(
            pair_attend(
                queries[:, pair * LANES : (pair + 1) * LANES] * scale,
                jnp.concatenate([local_rows[pair], table[pair]], axis=0),
                jnp.concatenate([local_rows[pairs + pair], table[pairs + pair]], axis=0),
                bias,
                lambda weights: weights * both,
            )
        )
    gridded = jnp.concatenate(rows, axis=1)
    start = per * depth
    halves = depth // LANES
    height = (kept - start) // halves
    padded = jnp.zeros((GROUPS * height, points), F32)
    for chunk, band in enumerate(CHUNKS):
        for half in range(halves):
            at = start + half * height
            weight = scratch[:, chunk // 2, chunk % 2, at : at + height, :]
            first = band * depth + half * LANES
            padded += dot_nt(
                weight.reshape(GROUPS * height, LANES), gridded[:, first : first + LANES]
            )
    parts = [padded[group * height : group * height + each] for group in range(GROUPS)]
    fields[...] = jnp.concatenate(parts, axis=0).astype(BF16)


def decode(spots, queries, local_rows, fetched, here, there, pieces, layout, outputs):
    points, width = queries.shape
    height = pieces[0].shape[-2]
    remote = there.shape[1]
    return pl.pallas_call(
        functools.partial(decode_kernel, layout, outputs // GROUPS),
        out_shape=jax.ShapeDtypeStruct((outputs, points), BF16),
        in_specs=[SMEM] + [VMEM_SPEC] * 5 + [ANY] * len(pieces),
        out_specs=VMEM_SPEC,
        scratch_shapes=[
            pltpu.VMEM((GROUPS, 2, 2, height, LANES), BF16),
            pltpu.VMEM((2 * width // LANES, remote, LANES), BF16),
            pltpu.SemaphoreType.DMA((len(pieces),)),
        ],
        compiler_params=params(),
        cost_estimate=SMALL,
        name="decode",
    )(spots, queries, local_rows, fetched, here, there, *pieces)


def stacked(*weights):
    parts = []
    for weight in weights:
        for at in range(0, weight.shape[-1], LANES):
            parts.append(weight[..., at : at + LANES])
    return jnp.concatenate(parts, axis=-2)


def pair_x(block, gate=None):
    if gate is not None:
        block, _ = lax.optimization_barrier((block, gate))
    other = lax.ppermute(block, "band", [(i, i ^ 2) for i in range(BANDS)])
    low = lax.axis_index("band") < 2
    return jnp.stack([jnp.where(low, block, other), jnp.where(low, other, block)])


def pair_core(block):
    other = swap_core(block)
    low = lax.axis_index("band") % 2 == 0
    return jnp.stack([jnp.where(low, block, other), jnp.where(low, other, block)])


def carry(block):
    pairs = []
    for i in range(GROUPS):
        here, there = RING[i] * BANDS, RING[(i + 1) % GROUPS] * BANDS
        for x in range(2):
            pairs.append((here + 2 * x, there + 2 * x))
            pairs.append((there + 2 * x + 1, here + 2 * x + 1))
    return lax.ppermute(block, ("seq", "band"), pairs)


def swap_core(block):
    return lax.ppermute(block, "band", [(i, i ^ 1) for i in range(BANDS)])


def ring_spots():
    seq, core = lax.axis_index("seq"), lax.axis_index("band") % 2
    table = np.zeros((2, GROUPS, GROUPS), np.int32)
    for i in range(GROUPS):
        for step in range(GROUPS):
            table[0, RING[i], step] = RING[(i - step) % GROUPS]
            table[1, RING[i], step] = RING[(i + step) % GROUPS]
    return jnp.concatenate([jnp.asarray(table)[core, seq], core.astype(jnp.int32)[None]])


def chain_step(block, step, half, gate=None):
    if gate is not None:
        block, _ = lax.optimization_barrier((block, gate))
    block = carry(block)
    return block, [(block, (step, half)), (swap_core(block), (GROUPS - step, 1 - half))]


def ring_step(block, step, gate=None):
    if gate is not None:
        block, _ = lax.optimization_barrier((block, gate))
    if step < GROUPS // 2:
        block = carry(block)
        return block, [(block, (step, None)), (swap_core(block), (GROUPS - step, None))]
    half = lax.dynamic_index_in_dim(block, lax.axis_index("band") % 2, 0, keepdims=False)
    half = carry(half)
    return half, [(half, (step, 0)), (swap_core(half), (step, 1))]


def whole_blocks(*weights):
    parts = []
    for weight, height in weights:
        weight = lax.all_gather(weight, "seq", axis=1, tiled=True)
        weight = lax.all_gather(weight, "band", axis=0, tiled=True)
        depth, columns = weight.shape[0] // BANDS, weight.shape[1] // GROUPS
        weight = weight.reshape(2, 2, depth, GROUPS, columns).transpose(3, 1, 0, 2, 4)
        if height:
            weight = jnp.pad(
                weight.swapaxes(-1, -2), ((0, 0),) * 3 + ((0, height - columns), (0, 0))
            )
        parts.append(weight)
    return stacked(*parts)


def local(
    tokens, ln_gain, w_qkv, w_out, dec_gain, w_kv, w_final, reach, grid_query, neighbours, counts
):
    states = tokens[0]
    tok, width = states.shape
    shards, bands = lax.axis_size("seq"), lax.axis_size("band")
    place = jnp.stack([lax.axis_index("seq"), lax.axis_index("band") % 2]).astype(jnp.int32)
    outputs = w_final.shape[1] * shards
    height = -(-outputs // GROUPS // 16) * 16
    riding = (shards, bands) == (GROUPS, BANDS)
    up = [(i, i + 1) for i in range(shards - 1)]
    down = [(i + 1, i) for i in range(shards - 1)]
    left = lax.ppermute(states[tok - HALF :], "seq", up)
    right = lax.ppermute(states[:HALF], "seq", down)
    if not riding:
        place = place * jnp.array([1, 0], jnp.int32)
    slots = (neighbours.T, counts.reshape(1, -1))
    there, requested, *payload = tables(tok, *slots, shards, (w_qkv, w_out) if riding else ())
    normed, bias, here = prepare(
        tok * shards, place, left, states, right, ln_gain.reshape(1, width),
        reach.reshape(1, tok), *slots,
    )
    if riding:
        spots = ring_spots()
        mine = pair_x(payload[0])
        other = swap_core(mine)
        own = [(mine, (0, 0)), (other, (0, 1))]
        final = jnp.pad(w_final.T, ((0, height - w_final.shape[1]), (0, 0)))
        one, first = chain_step(mine, 1, 0)
        second = pair_core(pair_x(stacked(w_kv, final), one))
        two, more = chain_step(other, 1, 1, (left, right))
        first += more
        one, pieces = chain_step(one, 2, 0)
        two, more = chain_step(two, 2, 1, normed)
        pieces += more
        made = project(spots, normed, own, None)
        one, last = chain_step(one, 3, 0, made)
        two, more = chain_step(two, 3, 1)
        last += more
        made = project(spots, normed, first, made)
        second, _, _ = lax.optimization_barrier((second, one, two))
        later = [(second, (0, None))]
        end, more = chain_step(one, 4, 0, made)
        made = project(spots, normed, pieces, made)
        waits = (made, end, last[1][0], last[3][0])
        last += more
        pieces = own + first + pieces + last
        block, more = ring_step(second, 1)
        later += more
        block, more = ring_step(block, 2, waits)
        later += more
        attended = attend(spots, normed, bias, pieces[10:], made, (0, 1, 7, 2, 6))
        block, more = ring_step(block, 3, attended)
        later += more
        ids = None
    else:
        spots = jnp.concatenate([jnp.arange(GROUPS, dtype=jnp.int32), jnp.zeros((1,), jnp.int32)])
        block = whole_blocks((w_qkv, 0), (w_out, 0))
        block = jnp.pad(block, ((0, 0),) * 3 + ((0, SLOTS), (0, 0)))
        pieces = [(block[at, half], (at, half)) for at in range(GROUPS) for half in range(2)]
        block = whole_blocks((w_kv, 0), (w_final, height))
        later = [(block[at], (at, None)) for at in range(GROUPS)]
        made = project(spots, normed, pieces[:10], None)
        attended = attend(spots, normed, bias, pieces[10:], made, (0, 1, 2, 3, 4))
        ids = lax.all_to_all(
            requested.reshape(shards, SLOTS).astype(jnp.int32), "seq", 0, 0, tiled=True
        ).reshape(shards * SLOTS, 1)
    layout = tuple(at for _, at in pieces)
    pieces = [piece for piece, _ in pieces]
    decoded, found = mix(
        place, spots, states, attended, dec_gain.reshape(1, width), ids, pieces, layout, shards
    )
    if riding:
        _, more = ring_step(block, 4, found)
        later += more
    fetched = lax.all_to_all(
        found.reshape(shards, SLOTS, width), "seq", split_axis=0, concat_axis=0, tiled=True
    )
    layout = tuple(at for _, at in later)
    pieces = [piece for piece, _ in later]
    local_rows = keys_values(spots, decoded, pieces, layout)
    fields = decode(
        spots, grid_query[0], local_rows, fetched.reshape(shards * SLOTS, width), here, there,
        pieces, layout, outputs,
    )
    return fields[None]


def solution(mesh):
    return jax.shard_map(
        local,
        mesh=mesh,
        in_specs=(
            P("band", "seq", None),
            P(),
            P("band", "seq"),
            P("band", "seq"),
            P(),
            P("band", "seq"),
            P("band", "seq"),
            P("seq"),
            P("band", "seq", None),
            P("seq", None),
            P("seq"),
        ),
        out_specs=P("band", None, "seq"),
        check_vma=False,
    )
```

```python
import functools
import math

import jax
import jax.numpy as jnp
import numpy as np
from jax import lax
from jax.experimental import pallas as pl
from jax.experimental.pallas import tpu as pltpu
from jax.sharding import PartitionSpec as P

HEADS = 16
HALF = 128
C = 12
SLOTS = 16
EPSILON = 1e-05
NEG = -1e30
LANES = 128
GROUPS = 8
BANDS = 4
CHUNKS = (0, 2, 1, 3)
RING = (0, 2, 4, 6, 7, 5, 3, 1)
VMEM = 56 * 1024 * 1024
SMALL = pl.CostEstimate(flops=1000, bytes_accessed=1000, transcendentals=0)
F32 = jnp.float32
BF16 = jnp.bfloat16


def dot(a, b):
    return jnp.dot(a, b, preferred_element_type=F32)


def dot_nt(a, b):
    return lax.dot_general(a, b, (((1,), (1,)), ((), ())), preferred_element_type=F32)


def layer_norm(values, gain):
    values = values.astype(F32)
    centred = values - jnp.mean(values, axis=-1, keepdims=True)
    spread = jnp.mean(centred * centred, axis=-1, keepdims=True)
    return (centred * lax.rsqrt(spread + EPSILON) * gain).astype(BF16)


def params(**more):
    return pltpu.CompilerParams(vmem_limit_bytes=VMEM, **more)


def full_spec(shape):
    return pl.BlockSpec(shape, lambda *_: (0,) * len(shape))


def own_first(rows, core, depth):
    parts = [rows[:, b * depth : (b + 1) * depth] for b in range(BANDS)]
    order = ((0, 1), (2, 3), (1, 0), (3, 2))
    return jnp.concatenate([jnp.where(core == 0, parts[a], parts[b]) for a, b in order], axis=1)


def as_column(row):
    return jnp.broadcast_to(row, (8, row.shape[1])).T[:, :1]


def prepare_kernel(
    total, place, left, own, right, gain, reach, neighbours, counts, normed, bias, multiplicity
):
    tok = own.shape[0]
    depth = own.shape[1] // BANDS
    for at, part in ((0, left), (HALF, own), (HALF + tok, right)):
        rows = layer_norm(part[...], gain[...])
        normed[at : at + part.shape[0], :] = own_first(rows, place[1], depth)

    first = place[0] * tok
    span = 3 * HALF
    row = lax.broadcasted_iota(jnp.int32, (HALF, span), 0)
    col = lax.broadcasted_iota(jnp.int32, (HALF, span), 1)
    away = jnp.abs(row + HALF - col)
    limit = as_column(reach[...])
    for block in range(tok // HALF):
        key = first + (block - 1) * HALF + col
        allowed = (away <= limit[block * HALF : (block + 1) * HALF, :]) & (key >= 0) & (key < total)
        bias[block] = jnp.where(allowed, 0.0, NEG)

    ids = neighbours[...].T
    used = as_column(counts[...])
    mesh = lax.broadcasted_iota(jnp.int32, multiplicity.shape, 1) + first
    here = jnp.zeros(multiplicity.shape, F32)
    for slot in range(ids.shape[1]):
        here += ((ids[:, slot : slot + 1] == mesh) & (slot < used)).astype(F32)
    multiplicity[...] = here


def prepare(total, place, left, own, right, gain, reach, neighbours, counts):
    tok, width = own.shape
    operands = (left, own, right, gain, reach, neighbours, counts)
    outs = (
        jax.ShapeDtypeStruct((tok + 2 * HALF, width), BF16),
        jax.ShapeDtypeStruct((tok // HALF, HALF, 3 * HALF), F32),
        jax.ShapeDtypeStruct((neighbours.shape[1], tok), F32),
    )
    return pl.pallas_call(
        functools.partial(prepare_kernel, total),
        out_shape=outs,
        in_specs=[pl.BlockSpec(memory_space=pltpu.SMEM)]
        + [pl.BlockSpec(memory_space=pltpu.VMEM)] * len(operands),
        out_specs=[pl.BlockSpec(memory_space=pltpu.VMEM)] * len(outs),
        compiler_params=params(),
        cost_estimate=SMALL,
        name="prepare",
    )(place, *operands)


def tables_kernel(tok, count, neighbours, counts, low, rank, tri, *refs):
    weights, (multiplicity, requested) = refs[:count], refs[count : count + 2]
    first = lax.axis_index("seq") * tok
    slots = neighbours.shape[0]
    ids = neighbours[...].T
    used = as_column(counts[...])
    start = low[...]
    elsewhere = start != first
    hits = []
    for slot in range(slots):
        which = ids[:, slot : slot + 1]
        hits.append(
            ((which >= start) & (which < start + tok) & (slot < used) & elsewhere).astype(F32)
        )
    running = dot(tri[...], sum(hits).astype(BF16))
    order = rank[...]
    asked = jnp.zeros(hits[0].shape, F32)
    there = jnp.zeros(hits[0].shape, F32)
    for slot in range(slots):
        mine = jnp.where(running == order, hits[slot], 0.0)
        there += mine
        offset = (ids[:, slot : slot + 1] - start).astype(F32)
        asked += jnp.where(mine > 0, offset, 0.0)
        running += hits[slot]
    multiplicity[...] = there
    asked = jnp.sum(asked, axis=0, keepdims=True)
    requested[...] = asked.astype(BF16)
    if weights:
        payload = refs[-1]
        at = 0
        for weight in weights:
            depth, columns = weight.shape
            for first in range(0, columns, LANES):
                payload[at : at + depth, :] = weight[:, first : first + LANES]
                at += depth
        payload[at:, :] = jnp.broadcast_to(asked, (SLOTS, LANES)).astype(BF16)


def tables(tok, neighbours, counts, shards, weights):
    points = neighbours.shape[1]
    remote = shards * SLOTS
    column = np.arange(remote)
    low = (column // SLOTS * tok).astype(np.int32)[None]
    rank = (column % SLOTS).astype(np.float32)[None]
    tri = np.tril(np.ones((points, points), np.float32), -1).astype(BF16)
    operands = (neighbours, counts, low, rank, tri) + weights
    outs = (
        jax.ShapeDtypeStruct((points, remote), F32),
        jax.ShapeDtypeStruct((1, remote), BF16),
    )
    if weights:
        rows = sum(weight.shape[0] * weight.shape[1] // LANES for weight in weights) + SLOTS
        outs += (jax.ShapeDtypeStruct((rows, LANES), BF16),)
    return pl.pallas_call(
        functools.partial(tables_kernel, tok, len(weights)),
        out_shape=outs,
        in_specs=[pl.BlockSpec(memory_space=pltpu.VMEM)] * len(operands),
        out_specs=[pl.BlockSpec(memory_space=pltpu.VMEM)] * len(outs),
        compiler_params=params(),
        cost_estimate=SMALL,
        name="tables",
    )(*operands)


def pair_attend(queries, keys, values, bias, weights_of):
    rows = queries.shape[0]
    lane = lax.broadcasted_iota(jnp.int32, (rows, LANES), 1)
    first = lane < LANES // 2
    zero = jnp.zeros_like(queries)
    both = jnp.concatenate(
        [jnp.where(first, queries, zero), jnp.where(first, zero, queries)], axis=0
    )
    scores = dot_nt(both, keys)
    scores = scores + jnp.concatenate([bias, bias], axis=0)
    top = jnp.max(scores, axis=-1, keepdims=True)
    weights = weights_of(jnp.exp(scores - top)).astype(BF16)
    summed = dot(weights, jnp.concatenate([values, jnp.ones_like(values)], axis=1))
    share = summed[:, :LANES] / summed[:, LANES:]
    return jnp.where(first, share[:rows], share[rows:]).astype(BF16)


def start_loads(spots, pieces, layout, scratch, arrived, rows, core=None):
    copies = {}
    for n, (piece, (at, half)) in enumerate(zip(pieces, layout)):
        place = scratch.at[spots[at]]
        if half is None:
            copy = pltpu.make_async_copy(piece.at[:, :, rows, :], place, arrived.at[n])
        else:
            to = half if core is None else (1 - core if half else core)
            copy = pltpu.make_async_copy(piece.at[:, rows, :], place.at[to], arrived.at[n])
        copy.start()
        copies.setdefault(at, []).append(copy)
    return copies


def wait_group(copies, at):
    for copy in copies.get(at, ()):
        copy.wait()


def lanes_of(block, depth, start, count):
    rows = block.shape[0] * block.shape[1] * depth if block.ndim == 4 else block.shape[0] * depth
    columns = [
        block[..., start + g * depth : start + (g + 1) * depth, :].reshape(rows, LANES)
        for g in range(count)
    ]
    return columns[0] if count == 1 else jnp.concatenate(columns, axis=1)


SMEM = pl.BlockSpec(memory_space=pltpu.SMEM)
VMEM_SPEC = pl.BlockSpec(memory_space=pltpu.VMEM)
ANY = pl.BlockSpec(memory_space=pl.ANY)


def projection(normed, weight, depth, per):
    return dot(normed, lanes_of(weight[...], depth, 0, per)).astype(BF16)


def project_kernel(layout, spots, normed, *refs):
    pieces = refs[: len(layout)]
    out, scratch, made, arrived, sent = refs[-5:]
    per = made.shape[1]
    depth = normed.shape[1] // BANDS
    copies = start_loads(spots, pieces, layout, scratch, arrived, slice(0, per * depth))
    writes = []
    for n, at in enumerate(copies):
        wait_group(copies, at)
        total = projection(normed[...], scratch.at[spots[at]], depth, per)
        for group in range(per):
            made[n, group] = total[:, group * LANES : (group + 1) * LANES]
        writes.append(
            pltpu.make_async_copy(made.at[n], out.at[pl.ds(spots[at] * per, per)], sent.at[n])
        )
        writes[-1].start()
    for write in writes:
        write.wait()


def project(spots, normed, pieces, before):
    rows, width = normed.shape
    layout = tuple(place for _, place in pieces)
    arrays = [array for array, _ in pieces]
    per = 3 * width // LANES // GROUPS
    count = len({at for at, _ in layout})
    more = [] if before is None else [before]
    return pl.pallas_call(
        functools.partial(project_kernel, layout),
        out_shape=jax.ShapeDtypeStruct((GROUPS * per, rows, LANES), BF16),
        in_specs=[SMEM, VMEM_SPEC] + [ANY] * (len(arrays) + len(more)),
        out_specs=ANY,
        scratch_shapes=[
            pltpu.VMEM((GROUPS, 2, 2, per * width // BANDS, LANES), BF16),
            pltpu.VMEM((count, per, rows, LANES), BF16),
            pltpu.SemaphoreType.DMA((len(arrays),)),
            pltpu.SemaphoreType.DMA((count,)),
        ],
        input_output_aliases={2 + len(arrays): 0} if more else {},
        compiler_params=params(),
        cost_estimate=SMALL,
        name="project",
    )(spots, normed, *arrays, *more)


def attend_kernel(layout, ready, spots, normed, bias, *refs):
    pieces = refs[: len(layout)]
    made, attended, scratch, projected, arrived, loaded = refs[len(layout) :]
    width = normed.shape[1]
    depth = width // BANDS
    per = projected.shape[0] // GROUPS
    copies = start_loads(spots, pieces, layout, scratch, arrived, slice(0, per * depth))
    reads = []
    for n, at in enumerate(ready):
        place = pl.ds(spots[at] * per, per)
        reads.append(pltpu.make_async_copy(made.at[place], projected.at[place], loaded.at[n]))
        reads[-1].start()
    for at in copies:
        wait_group(copies, at)
        total = projection(normed[...], scratch.at[spots[at]], depth, per)
        for group in range(per):
            projected[spots[at] * per + group] = total[:, group * LANES : (group + 1) * LANES]
    for read in reads:
        read.wait()
    pairs = width // LANES
    scale = BF16(1.0 / math.sqrt(width // HEADS))
    for pair in range(pairs):
        for block in range(bias.shape[0]):
            at = block * HALF
            attended[at : at + HALF, pair * LANES : (pair + 1) * LANES] = pair_attend(
                projected[pair, at + HALF : at + 2 * HALF, :] * scale,
                projected[pairs + pair, at : at + 3 * HALF, :],
                projected[2 * pairs + pair, at : at + 3 * HALF, :],
                bias[block],
                lambda weights: weights,
            )


def attend(spots, normed, bias, pieces, made, ready):
    rows, width = normed.shape
    tok = rows - 2 * HALF
    layout = tuple(place for _, place in pieces)
    arrays = [array for array, _ in pieces]
    per = made.shape[0] // GROUPS
    return pl.pallas_call(
        functools.partial(attend_kernel, layout, ready),
        out_shape=jax.ShapeDtypeStruct((tok, width), BF16),
        in_specs=[SMEM, VMEM_SPEC, VMEM_SPEC] + [ANY] * (len(arrays) + 1),
        out_specs=VMEM_SPEC,
        scratch_shapes=[
            pltpu.VMEM((GROUPS, 2, 2, per * width // BANDS, LANES), BF16),
            pltpu.VMEM(made.shape, BF16),
            pltpu.SemaphoreType.DMA((len(arrays),)),
            pltpu.SemaphoreType.DMA((len(ready),)),
        ],
        compiler_params=params(),
        cost_estimate=SMALL,
        name="attend",
    )(spots, normed, bias, *arrays, made)


def picked_rows(place, ids, spots, rows, asked, arrived):
    tok = rows.shape[0]
    if spots is None:
        which = ids[...]
    else:
        for at in range(GROUPS):
            asked[pl.ds(spots[at] * SLOTS, SLOTS), :] = jnp.broadcast_to(
                arrived[at, 0:1, :].astype(F32), (SLOTS, LANES)
            )
        count = GROUPS * SLOTS
        lane = lax.broadcasted_iota(jnp.int32, (count, LANES), 1)
        slot = lax.broadcasted_iota(jnp.int32, (count, LANES), 0) % SLOTS
        mine = jnp.where(lane == place[0] * SLOTS + slot, asked[...], 0.0)
        which = jnp.sum(mine, axis=1, keepdims=True).astype(jnp.int32)
    here = lax.broadcasted_iota(jnp.int32, (which.shape[0], tok), 1)
    return dot((which == here).astype(BF16), rows).astype(BF16)


def chunked(values, depth):
    return jnp.concatenate([values[:, b * depth : (b + 1) * depth] for b in CHUNKS], axis=1)


def mix_kernel(layout, riding, place, spots, states, gain, *refs):
    attended, refs = refs[0], refs[1:]
    ids = None
    if not riding:
        ids, refs = refs[0], refs[1:]
    pieces = refs[: len(layout)]
    decoded, found, mixed, scratch, asked, notes, arrived, noted = refs[len(layout) :]
    width = states.shape[1]
    depth = width // BANDS
    start = 3 * width // GROUPS // LANES * depth
    copies = start_loads(spots, pieces, layout, scratch, arrived, slice(start, start + depth))
    reads = []
    if riding:
        for piece, (at, core) in zip(pieces, layout):
            if core == 0:
                end = piece.shape[-2]
                reads.append(
                    pltpu.make_async_copy(
                        piece.at[0, end - SLOTS : end, :], notes.at[at], noted.at[at]
                    )
                )
                reads[-1].start()
    inputs = own_first(attended[...], place[1], depth)
    for at in range(GROUPS):
        wait_group(copies, at)
        spot = spots[at]
        columns = pl.ds(pl.multiple_of(spot * LANES, LANES), LANES)
        total = dot(inputs, lanes_of(scratch[spot], depth, 0, 1))
        mixed[:, columns] = (states[:, columns].astype(F32) + total).astype(BF16)
    for read in reads:
        read.wait()
    rows = chunked(layer_norm(mixed[...], gain[...]), depth)
    decoded[...] = rows
    found[...] = picked_rows(place, ids, spots if riding else None, rows, asked, notes)


def mix(place, spots, states, attended, gain, ids, pieces, layout, shards):
    tok, width = states.shape
    more = [] if ids is None else [ids]
    return pl.pallas_call(
        functools.partial(mix_kernel, layout, ids is None),
        out_shape=(
            jax.ShapeDtypeStruct((tok, width), BF16),
            jax.ShapeDtypeStruct((shards * SLOTS, width), BF16),
        ),
        in_specs=[SMEM, SMEM] + [VMEM_SPEC] * (3 + len(more)) + [ANY] * len(pieces),
        out_specs=(VMEM_SPEC, VMEM_SPEC),
        scratch_shapes=[
            pltpu.VMEM((tok, width), BF16),
            pltpu.VMEM((GROUPS, 2, 2, width // BANDS, LANES), BF16),
            pltpu.VMEM((GROUPS * SLOTS, LANES), F32),
            pltpu.VMEM((GROUPS, SLOTS, LANES), BF16),
            pltpu.SemaphoreType.DMA((len(pieces),)),
            pltpu.SemaphoreType.DMA((GROUPS,)),
        ],
        compiler_params=params(),
        cost_estimate=SMALL,
        name="mix",
    )(place, spots, states, gain, attended, *more, *pieces)


def keys_values_kernel(layout, spots, decoded, *refs):
    pieces = refs[: len(layout)]
    out, scratch, arrived = refs[len(layout) :]
    depth = decoded.shape[1] // BANDS
    per = scratch.shape[3] // depth
    copies = start_loads(
        spots, pieces, layout, scratch, arrived, slice(0, scratch.shape[3]), spots[GROUPS]
    )
    for at in range(GROUPS):
        wait_group(copies, at)
        spot = spots[at]
        total = dot(decoded[...], lanes_of(scratch[spot], depth, 0, per)).astype(BF16)
        for group in range(per):
            out[spot * per + group] = total[:, group * LANES : (group + 1) * LANES]


def keys_values(spots, decoded, pieces, layout):
    tok, width = decoded.shape
    height = 2 * width // GROUPS // LANES * (width // BANDS)
    return pl.pallas_call(
        functools.partial(keys_values_kernel, layout),
        out_shape=jax.ShapeDtypeStruct((2 * width // LANES, tok, LANES), BF16),
        in_specs=[SMEM, VMEM_SPEC] + [ANY] * len(pieces),
        out_specs=VMEM_SPEC,
        scratch_shapes=[
            pltpu.VMEM((GROUPS, 2, 2, height, LANES), BF16),
            pltpu.SemaphoreType.DMA((len(pieces),)),
        ],
        compiler_params=params(),
        cost_estimate=SMALL,
        name="keys_values",
    )(spots, decoded, *pieces)


def decode_kernel(layout, each, spots, queries, local_rows, fetched, here, there, *refs):
    pieces = refs[: len(layout)]
    fields, scratch, table, arrived = refs[len(layout) :]
    points, width = queries.shape
    depth = width // BANDS
    count = fetched.shape[0]
    per = 2 * width // GROUPS // LANES
    kept = scratch.shape[3]
    copies = start_loads(
        spots, pieces, layout, scratch, arrived, slice(0, kept), spots[GROUPS]
    )
    padding = jnp.zeros((table.shape[1] - count, LANES), BF16)
    for at in range(GROUPS):
        wait_group(copies, at)
        spot = spots[at]
        total = dot(fetched[...], lanes_of(scratch[spot], depth, 0, per)).astype(BF16)
        for group in range(per):
            table[spot * per + group, :count, :] = total[:, group * LANES : (group + 1) * LANES]
            if table.shape[1] > count:
                table[spot * per + group, count:, :] = padding

    pairs = width // LANES
    scale = BF16(1.0 / math.sqrt(width // HEADS))
    times = jnp.concatenate([here[...], there[...]], axis=1)
    bias = jnp.where(times > 0, 0.0, NEG)
    both = jnp.concatenate([times, times], axis=0)
    rows = []
    for pair in range(pairs):
        rows.append(
            pair_attend(
                queries[:, pair * LANES : (pair + 1) * LANES] * scale,
                jnp.concatenate([local_rows[pair], table[pair]], axis=0),
                jnp.concatenate([local_rows[pairs + pair], table[pairs + pair]], axis=0),
                bias,
                lambda weights: weights * both,
            )
        )
    gridded = jnp.concatenate(rows, axis=1)
    start = per * depth
    halves = depth // LANES
    height = (kept - start) // halves
    padded = jnp.zeros((GROUPS * height, points), F32)
    for chunk, band in enumerate(CHUNKS):
        for half in range(halves):
            at = start + half * height
            weight = scratch[:, chunk // 2, chunk % 2, at : at + height, :]
            first = band * depth + half * LANES
            padded += dot_nt(
                weight.reshape(GROUPS * height, LANES), gridded[:, first : first + LANES]
            )
    parts = [padded[group * height : group * height + each] for group in range(GROUPS)]
    fields[...] = jnp.concatenate(parts, axis=0).astype(BF16)


def decode(spots, queries, local_rows, fetched, here, there, pieces, layout, outputs):
    points, width = queries.shape
    height = pieces[0].shape[-2]
    remote = there.shape[1]
    return pl.pallas_call(
        functools.partial(decode_kernel, layout, outputs // GROUPS),
        out_shape=jax.ShapeDtypeStruct((outputs, points), BF16),
        in_specs=[SMEM] + [VMEM_SPEC] * 5 + [ANY] * len(pieces),
        out_specs=VMEM_SPEC,
        scratch_shapes=[
            pltpu.VMEM((GROUPS, 2, 2, height, LANES), BF16),
            pltpu.VMEM((2 * width // LANES, remote, LANES), BF16),
            pltpu.SemaphoreType.DMA((len(pieces),)),
        ],
        compiler_params=params(),
        cost_estimate=SMALL,
        name="decode",
    )(spots, queries, local_rows, fetched, here, there, *pieces)


def stacked(*weights):
    parts = []
    for weight in weights:
        for at in range(0, weight.shape[-1], LANES):
            parts.append(weight[..., at : at + LANES])
    return jnp.concatenate(parts, axis=-2)


def pair_x(block, gate=None):
    if gate is not None:
        block, _ = lax.optimization_barrier((block, gate))
    other = lax.ppermute(block, "band", [(i, i ^ 2) for i in range(BANDS)])
    low = lax.axis_index("band") < 2
    return jnp.stack([jnp.where(low, block, other), jnp.where(low, other, block)])


def pair_core(block):
    other = swap_core(block)
    low = lax.axis_index("band") % 2 == 0
    return jnp.stack([jnp.where(low, block, other), jnp.where(low, other, block)])


def carry(block):
    pairs = []
    for i in range(GROUPS):
        here, there = RING[i] * BANDS, RING[(i + 1) % GROUPS] * BANDS
        for x in range(2):
            pairs.append((here + 2 * x, there + 2 * x))
            pairs.append((there + 2 * x + 1, here + 2 * x + 1))
    return lax.ppermute(block, ("seq", "band"), pairs)


def swap_core(block):
    return lax.ppermute(block, "band", [(i, i ^ 1) for i in range(BANDS)])


def ring_spots():
    seq, core = lax.axis_index("seq"), lax.axis_index("band") % 2
    table = np.zeros((2, GROUPS, GROUPS), np.int32)
    for i in range(GROUPS):
        for step in range(GROUPS):
            table[0, RING[i], step] = RING[(i - step) % GROUPS]
            table[1, RING[i], step] = RING[(i + step) % GROUPS]
    return jnp.concatenate([jnp.asarray(table)[core, seq], core.astype(jnp.int32)[None]])


def chain_step(chains, step, gate=None):
    if gate is not None:
        *chains, _ = lax.optimization_barrier((*chains, gate))
    chains = [carry(block) for block in chains]
    pieces = []
    for half, block in enumerate(chains):
        pieces.append((block, (step, half)))
        pieces.append((swap_core(block), (GROUPS - step, 1 - half)))
    return chains, pieces


def ring_step(block, step, gate=None):
    if gate is not None:
        block, _ = lax.optimization_barrier((block, gate))
    if step < GROUPS // 2:
        block = carry(block)
        return block, [(block, (step, None)), (swap_core(block), (GROUPS - step, None))]
    half = lax.dynamic_index_in_dim(block, lax.axis_index("band") % 2, 0, keepdims=False)
    half = carry(half)
    return half, [(half, (step, 0)), (swap_core(half), (step, 1))]


def whole_blocks(*weights):
    parts = []
    for weight, height in weights:
        weight = lax.all_gather(weight, "seq", axis=1, tiled=True)
        weight = lax.all_gather(weight, "band", axis=0, tiled=True)
        depth, columns = weight.shape[0] // BANDS, weight.shape[1] // GROUPS
        weight = weight.reshape(2, 2, depth, GROUPS, columns).transpose(3, 1, 0, 2, 4)
        if height:
            weight = jnp.pad(
                weight.swapaxes(-1, -2), ((0, 0),) * 3 + ((0, height - columns), (0, 0))
            )
        parts.append(weight)
    return stacked(*parts)


def local(
    tokens, ln_gain, w_qkv, w_out, dec_gain, w_kv, w_final, reach, grid_query, neighbours, counts
):
    states = tokens[0]
    tok, width = states.shape
    shards, bands = lax.axis_size("seq"), lax.axis_size("band")
    place = jnp.stack([lax.axis_index("seq"), lax.axis_index("band") % 2]).astype(jnp.int32)
    outputs = w_final.shape[1] * shards
    height = -(-outputs // GROUPS // 16) * 16
    riding = (shards, bands) == (GROUPS, BANDS)
    up = [(i, i + 1) for i in range(shards - 1)]
    down = [(i + 1, i) for i in range(shards - 1)]
    left = lax.ppermute(states[tok - HALF :], "seq", up)
    right = lax.ppermute(states[:HALF], "seq", down)
    if not riding:
        place = place * jnp.array([1, 0], jnp.int32)
    slots = (neighbours.T, counts.reshape(1, -1))
    there, requested, *payload = tables(tok, *slots, shards, (w_qkv, w_out) if riding else ())
    normed, bias, here = prepare(
        tok * shards, place, left, states, right, ln_gain.reshape(1, width),
        reach.reshape(1, tok), *slots,
    )
    if riding:
        spots = ring_spots()
        mine = pair_x(payload[0])
        mine, _, _ = lax.optimization_barrier((mine, left, right))
        other = swap_core(mine)
        pieces = [(mine, (0, 0)), (other, (0, 1))]
        chains, more = chain_step([mine, other], 1)
        pieces += more
        final = jnp.pad(w_final.T, ((0, height - w_final.shape[1]), (0, 0)))
        second = pair_core(pair_x(stacked(w_kv, final), chains[0]))
        later = [(second, (0, None))]
        chains, more = chain_step(chains, 2)
        pieces += more
        chains[1], _ = lax.optimization_barrier((chains[1], normed))
        chains, more = chain_step(chains, 3)
        pieces += more
        second, *_ = lax.optimization_barrier((second, *chains, pieces[3][0], pieces[5][0]))
        last, more = chain_step(chains[:1], 4)
        pieces += more
        block, more = ring_step(second, 1)
        later += more
        normed, _ = lax.optimization_barrier((normed, chains[0]))
        made = project(spots, normed, pieces[:6], None)
        made = project(spots, normed, pieces[6:10], made)
        block, more = ring_step(block, 2, (made, last[0], pieces[11][0], pieces[13][0]))
        later += more
        attended = attend(spots, normed, bias, pieces[10:], made, (0, 1, 7, 2, 6))
        block, more = ring_step(block, 3, attended)
        later += more
        ids = None
    else:
        spots = jnp.concatenate([jnp.arange(GROUPS, dtype=jnp.int32), jnp.zeros((1,), jnp.int32)])
        block = whole_blocks((w_qkv, 0), (w_out, 0))
        block = jnp.pad(block, ((0, 0),) * 3 + ((0, SLOTS), (0, 0)))
        pieces = [(block[at, half], (at, half)) for at in range(GROUPS) for half in range(2)]
        block = whole_blocks((w_kv, 0), (w_final, height))
        later = [(block[at], (at, None)) for at in range(GROUPS)]
        made = project(spots, normed, pieces[:10], None)
        attended = attend(spots, normed, bias, pieces[10:], made, (0, 1, 2, 3, 4))
        ids = lax.all_to_all(
            requested.reshape(shards, SLOTS).astype(jnp.int32), "seq", 0, 0, tiled=True
        ).reshape(shards * SLOTS, 1)
    layout = tuple(at for _, at in pieces)
    pieces = [piece for piece, _ in pieces]
    decoded, found = mix(
        place, spots, states, attended, dec_gain.reshape(1, width), ids, pieces, layout, shards
    )
    if riding:
        _, more = ring_step(block, 4, found)
        later += more
    fetched = lax.all_to_all(
        found.reshape(shards, SLOTS, width), "seq", split_axis=0, concat_axis=0, tiled=True
    )
    layout = tuple(at for _, at in later)
    pieces = [piece for piece, _ in later]
    local_rows = keys_values(spots, decoded, pieces, layout)
    fields = decode(
        spots, grid_query[0], local_rows, fetched.reshape(shards * SLOTS, width), here, there,
        pieces, layout, outputs,
    )
    return fields[None]


def solution(mesh):
    return jax.shard_map(
        local,
        mesh=mesh,
        in_specs=(
            P("band", "seq", None),
            P(),
            P("band", "seq"),
            P("band", "seq"),
            P(),
            P("band", "seq"),
            P("band", "seq"),
            P("seq"),
            P("band", "seq", None),
            P("seq", None),
            P("seq"),
        ),
        out_specs=P("band", None, "seq"),
        check_vma=False,
    )
```

```python
import functools
import math

import jax
import jax.numpy as jnp
import numpy as np
from jax import lax
from jax.experimental import pallas as pl
from jax.experimental.pallas import tpu as pltpu
from jax.sharding import PartitionSpec as P

HEADS = 16
HALF = 128
C = 12
SLOTS = 16
EPSILON = 1e-05
NEG = -1e30
LANES = 128
GROUPS = 8
BANDS = 4
CHUNKS = (0, 2, 1, 3)
RING = (0, 2, 4, 6, 7, 5, 3, 1)
VMEM = 60 * 1024 * 1024
SMALL = pl.CostEstimate(flops=1000, bytes_accessed=1000, transcendentals=0)
F32 = jnp.float32
BF16 = jnp.bfloat16


def dot(a, b):
    return jnp.dot(a, b, preferred_element_type=F32)


def dot_nt(a, b):
    return lax.dot_general(a, b, (((1,), (1,)), ((), ())), preferred_element_type=F32)


def layer_norm(values, gain):
    values = values.astype(F32)
    centred = values - jnp.mean(values, axis=-1, keepdims=True)
    spread = jnp.mean(centred * centred, axis=-1, keepdims=True)
    return (centred * lax.rsqrt(spread + EPSILON) * gain).astype(BF16)


def here_at(riding):
    return lax.axis_index("seq"), (lax.axis_index("band") % 2 if riding else 0)


def ring_spots(riding):
    if not riding:
        return list(range(GROUPS)) + [0]
    seq, core = here_at(True)
    at_ring = jnp.where(seq % 2 == 0, seq // 2, GROUPS - 1 - seq // 2)
    turn = jnp.where(core == 0, GROUPS - 1, 1)
    spots = []
    for at in range(GROUPS):
        step = (at_ring + turn * at) % GROUPS
        spots.append(jnp.where(step < GROUPS // 2, 2 * step, 2 * GROUPS - 1 - 2 * step))
    return spots + [core]


def params(**more):
    return pltpu.CompilerParams(vmem_limit_bytes=VMEM, **more)


def full_spec(shape):
    return pl.BlockSpec(shape, lambda *_: (0,) * len(shape))


def own_first(rows, core, depth):
    parts = [rows[:, b * depth : (b + 1) * depth] for b in range(BANDS)]
    order = ((0, 1), (2, 3), (1, 0), (3, 2))
    return jnp.concatenate([jnp.where(core == 0, parts[a], parts[b]) for a, b in order], axis=1)


def as_column(row):
    return jnp.broadcast_to(row, (8, row.shape[1])).T[:, :1]


def prepare_kernel(
    total, riding, left, own, right, gain, reach, neighbours, counts, normed, bias, multiplicity
):
    place = here_at(riding)
    tok = own.shape[0]
    depth = own.shape[1] // BANDS
    for at, part in ((0, left), (HALF, own), (HALF + tok, right)):
        rows = layer_norm(part[...], gain[...])
        normed[at : at + part.shape[0], :] = own_first(rows, place[1], depth)

    first = place[0] * tok
    span = 3 * HALF
    row = lax.broadcasted_iota(jnp.int32, (HALF, span), 0)
    col = lax.broadcasted_iota(jnp.int32, (HALF, span), 1)
    away = jnp.abs(row + HALF - col)
    limit = as_column(reach[...])
    for block in range(tok // HALF):
        key = first + (block - 1) * HALF + col
        allowed = (away <= limit[block * HALF : (block + 1) * HALF, :]) & (key >= 0) & (key < total)
        bias[block] = jnp.where(allowed, 0.0, NEG)

    ids = neighbours[...].T
    used = as_column(counts[...])
    mesh = lax.broadcasted_iota(jnp.int32, multiplicity.shape, 1) + first
    here = jnp.zeros(multiplicity.shape, F32)
    for slot in range(ids.shape[1]):
        here += ((ids[:, slot : slot + 1] == mesh) & (slot < used)).astype(F32)
    multiplicity[...] = here


def prepare(total, riding, left, own, right, gain, reach, neighbours, counts):
    tok, width = own.shape
    operands = (left, own, right, gain, reach, neighbours, counts)
    outs = (
        jax.ShapeDtypeStruct((tok + 2 * HALF, width), BF16),
        jax.ShapeDtypeStruct((tok // HALF, HALF, 3 * HALF), F32),
        jax.ShapeDtypeStruct((neighbours.shape[1], tok), F32),
    )
    return pl.pallas_call(
        functools.partial(prepare_kernel, total, riding),
        out_shape=outs,
        in_specs=[pl.BlockSpec(memory_space=pltpu.VMEM)] * len(operands),
        out_specs=[pl.BlockSpec(memory_space=pltpu.VMEM)] * len(outs),
        compiler_params=params(),
        cost_estimate=SMALL,
        name="prepare",
    )(*operands)


def tables_kernel(tok, count, neighbours, counts, low, rank, tri, *refs):
    weights, (multiplicity, requested) = refs[:count], refs[count : count + 2]
    first = lax.axis_index("seq") * tok
    slots = neighbours.shape[0]
    ids = neighbours[...].T
    used = as_column(counts[...])
    start = low[...]
    elsewhere = start != first
    hits = []
    for slot in range(slots):
        which = ids[:, slot : slot + 1]
        hits.append(
            ((which >= start) & (which < start + tok) & (slot < used) & elsewhere).astype(F32)
        )
    running = dot(tri[...], sum(hits).astype(BF16))
    order = rank[...]
    asked = jnp.zeros(hits[0].shape, F32)
    there = jnp.zeros(hits[0].shape, F32)
    for slot in range(slots):
        mine = jnp.where(running == order, hits[slot], 0.0)
        there += mine
        offset = (ids[:, slot : slot + 1] - start).astype(F32)
        asked += jnp.where(mine > 0, offset, 0.0)
        running += hits[slot]
    multiplicity[...] = there
    asked = jnp.sum(asked, axis=0, keepdims=True)
    requested[...] = asked.astype(BF16)
    if weights:
        payload = refs[-1]
        at = 0
        for weight in weights:
            depth, columns = weight.shape
            for first in range(0, columns, LANES):
                payload[at : at + depth, :] = weight[:, first : first + LANES]
                at += depth
        payload[at:, :] = jnp.broadcast_to(asked, (SLOTS, LANES)).astype(BF16)


def tables(tok, neighbours, counts, shards, weights):
    points = neighbours.shape[1]
    remote = shards * SLOTS
    column = np.arange(remote)
    low = (column // SLOTS * tok).astype(np.int32)[None]
    rank = (column % SLOTS).astype(np.float32)[None]
    tri = np.tril(np.ones((points, points), np.float32), -1).astype(BF16)
    operands = (neighbours, counts, low, rank, tri) + weights
    outs = (
        jax.ShapeDtypeStruct((points, remote), F32),
        jax.ShapeDtypeStruct((1, remote), BF16),
    )
    if weights:
        rows = sum(weight.shape[0] * weight.shape[1] // LANES for weight in weights) + SLOTS
        outs += (jax.ShapeDtypeStruct((rows, LANES), BF16),)
    return pl.pallas_call(
        functools.partial(tables_kernel, tok, len(weights)),
        out_shape=outs,
        in_specs=[pl.BlockSpec(memory_space=pltpu.VMEM)] * len(operands),
        out_specs=[pl.BlockSpec(memory_space=pltpu.VMEM)] * len(outs),
        compiler_params=params(),
        cost_estimate=SMALL,
        name="tables",
    )(*operands)


def pair_attend(queries, keys, values, bias, weights_of):
    rows = queries.shape[0]
    lane = lax.broadcasted_iota(jnp.int32, (rows, LANES), 1)
    first = lane < LANES // 2
    zero = jnp.zeros_like(queries)
    both = jnp.concatenate(
        [jnp.where(first, queries, zero), jnp.where(first, zero, queries)], axis=0
    )
    scores = dot_nt(both, keys)
    scores = scores + jnp.concatenate([bias, bias], axis=0)
    top = jnp.max(scores, axis=-1, keepdims=True)
    weights = weights_of(jnp.exp(scores - top)).astype(BF16)
    summed = dot(weights, jnp.concatenate([values, jnp.ones_like(values)], axis=1))
    share = summed[:, :LANES] / summed[:, LANES:]
    return jnp.where(first, share[:rows], share[rows:]).astype(BF16)


def start_loads(spots, pieces, layout, scratch, arrived, rows, core=None):
    copies = {}
    for n, (piece, (at, half)) in enumerate(zip(pieces, layout)):
        place = scratch.at[spots[at]]
        if half is None:
            copy = pltpu.make_async_copy(piece.at[:, :, rows, :], place, arrived.at[n])
        else:
            to = half if core is None else (1 - core if half else core)
            copy = pltpu.make_async_copy(piece.at[:, rows, :], place.at[to], arrived.at[n])
        copy.start()
        copies.setdefault(at, []).append(copy)
    return copies


def wait_group(copies, at):
    for copy in copies.get(at, ()):
        copy.wait()


def lanes_of(block, depth, start, count):
    rows = block.shape[0] * block.shape[1] * depth if block.ndim == 4 else block.shape[0] * depth
    columns = [
        block[..., start + g * depth : start + (g + 1) * depth, :].reshape(rows, LANES)
        for g in range(count)
    ]
    return columns[0] if count == 1 else jnp.concatenate(columns, axis=1)


SMEM = pl.BlockSpec(memory_space=pltpu.SMEM)
VMEM_SPEC = pl.BlockSpec(memory_space=pltpu.VMEM)
ANY = pl.BlockSpec(memory_space=pl.ANY)


def projection(normed, weight, depth, per):
    return dot(normed, lanes_of(weight[...], depth, 0, per)).astype(BF16)


def project_kernel(layout, riding, normed, *refs):
    spots = ring_spots(riding)
    pieces = refs[: len(layout)]
    out, scratch, made, arrived, sent = refs[-5:]
    per = made.shape[1]
    depth = normed.shape[1] // BANDS
    copies = start_loads(spots, pieces, layout, scratch, arrived, slice(0, per * depth))
    writes = []
    for n, at in enumerate(copies):
        wait_group(copies, at)
        total = projection(normed[...], scratch.at[spots[at]], depth, per)
        for group in range(per):
            made[n, group] = total[:, group * LANES : (group + 1) * LANES]
        writes.append(
            pltpu.make_async_copy(made.at[n], out.at[pl.ds(spots[at] * per, per)], sent.at[n])
        )
        writes[-1].start()
    for write in writes:
        write.wait()


def project(riding, normed, pieces, before):
    rows, width = normed.shape
    layout = tuple(place for _, place in pieces)
    arrays = [array for array, _ in pieces]
    per = 3 * width // LANES // GROUPS
    count = len({at for at, _ in layout})
    more = [] if before is None else [before]
    return pl.pallas_call(
        functools.partial(project_kernel, layout, riding),
        out_shape=jax.ShapeDtypeStruct((GROUPS * per, rows, LANES), BF16),
        in_specs=[VMEM_SPEC] + [ANY] * (len(arrays) + len(more)),
        out_specs=ANY,
        scratch_shapes=[
            pltpu.VMEM((GROUPS, 2, 2, per * width // BANDS, LANES), BF16),
            pltpu.VMEM((count, per, rows, LANES), BF16),
            pltpu.SemaphoreType.DMA((len(arrays),)),
            pltpu.SemaphoreType.DMA((count,)),
        ],
        input_output_aliases={1 + len(arrays): 0} if more else {},
        compiler_params=params(),
        cost_estimate=SMALL,
        name="project",
    )(normed, *arrays, *more)


def attend_kernel(layout, ready, riding, normed, bias, *refs):
    spots = ring_spots(riding)
    pieces = refs[: len(layout)]
    made, attended, scratch, projected, arrived, loaded = refs[len(layout) :]
    width = normed.shape[1]
    depth = width // BANDS
    per = projected.shape[0] // GROUPS
    copies = start_loads(spots, pieces, layout, scratch, arrived, slice(0, per * depth))
    reads = []
    for n, at in enumerate(ready):
        place = pl.ds(spots[at] * per, per)
        reads.append(pltpu.make_async_copy(made.at[place], projected.at[place], loaded.at[n]))
        reads[-1].start()
    for at in copies:
        wait_group(copies, at)
        total = projection(normed[...], scratch.at[spots[at]], depth, per)
        for group in range(per):
            projected[spots[at] * per + group] = total[:, group * LANES : (group + 1) * LANES]
    for read in reads:
        read.wait()
    pairs = width // LANES
    scale = BF16(1.0 / math.sqrt(width // HEADS))
    for pair in range(pairs):
        for block in range(bias.shape[0]):
            at = block * HALF
            attended[at : at + HALF, pair * LANES : (pair + 1) * LANES] = pair_attend(
                projected[pair, at + HALF : at + 2 * HALF, :] * scale,
                projected[pairs + pair, at : at + 3 * HALF, :],
                projected[2 * pairs + pair, at : at + 3 * HALF, :],
                bias[block],
                lambda weights: weights,
            )


def attend(riding, normed, bias, pieces, made, ready):
    rows, width = normed.shape
    tok = rows - 2 * HALF
    layout = tuple(place for _, place in pieces)
    arrays = [array for array, _ in pieces]
    per = made.shape[0] // GROUPS
    return pl.pallas_call(
        functools.partial(attend_kernel, layout, ready, riding),
        out_shape=jax.ShapeDtypeStruct((tok, width), BF16),
        in_specs=[VMEM_SPEC, VMEM_SPEC] + [ANY] * (len(arrays) + 1),
        out_specs=VMEM_SPEC,
        scratch_shapes=[
            pltpu.VMEM((GROUPS, 2, 2, per * width // BANDS, LANES), BF16),
            pltpu.VMEM(made.shape, BF16),
            pltpu.SemaphoreType.DMA((len(arrays),)),
            pltpu.SemaphoreType.DMA((len(ready),)),
        ],
        compiler_params=params(),
        cost_estimate=SMALL,
        name="attend",
    )(normed, bias, *arrays, made)


def picked_rows(place, ids, spots, rows, asked, arrived):
    tok = rows.shape[0]
    if spots is None:
        which = ids[...]
    else:
        for at in range(GROUPS):
            asked[pl.ds(spots[at] * SLOTS, SLOTS), :] = jnp.broadcast_to(
                arrived[at, 0:1, :].astype(F32), (SLOTS, LANES)
            )
        count = GROUPS * SLOTS
        lane = lax.broadcasted_iota(jnp.int32, (count, LANES), 1)
        slot = lax.broadcasted_iota(jnp.int32, (count, LANES), 0) % SLOTS
        mine = jnp.where(lane == place[0] * SLOTS + slot, asked[...], 0.0)
        which = jnp.sum(mine, axis=1, keepdims=True).astype(jnp.int32)
    here = lax.broadcasted_iota(jnp.int32, (which.shape[0], tok), 1)
    return dot((which == here).astype(BF16), rows).astype(BF16)


def chunked(values, depth):
    return jnp.concatenate([values[:, b * depth : (b + 1) * depth] for b in CHUNKS], axis=1)


def mix_kernel(layout, riding, states, gain, *refs):
    place, spots = here_at(riding), ring_spots(riding)
    attended, refs = refs[0], refs[1:]
    ids = None
    if not riding:
        ids, refs = refs[0], refs[1:]
    pieces = refs[: len(layout)]
    decoded, found, mixed, scratch, asked, notes, arrived, noted = refs[len(layout) :]
    width = states.shape[1]
    depth = width // BANDS
    start = 3 * width // GROUPS // LANES * depth
    copies = start_loads(spots, pieces, layout, scratch, arrived, slice(start, start + depth))
    reads = []
    if riding:
        for piece, (at, core) in zip(pieces, layout):
            if core == 0:
                end = piece.shape[-2]
                reads.append(
                    pltpu.make_async_copy(
                        piece.at[0, end - SLOTS : end, :], notes.at[at], noted.at[at]
                    )
                )
                reads[-1].start()
    inputs = own_first(attended[...], place[1], depth)
    for at in range(GROUPS):
        wait_group(copies, at)
    for at in range(0, GROUPS, 2):
        columns = slice(at * LANES, (at + 2) * LANES)
        weight = [lanes_of(scratch[at + n], depth, 0, 1) for n in range(2)]
        total = dot(inputs, jnp.concatenate(weight, axis=1))
        mixed[:, columns] = (states[:, columns].astype(F32) + total).astype(BF16)
    for read in reads:
        read.wait()
    rows = chunked(layer_norm(mixed[...], gain[...]), depth)
    decoded[...] = rows
    found[...] = picked_rows(place, ids, spots if riding else None, rows, asked, notes)


def mix(states, attended, gain, ids, pieces, layout, shards):
    tok, width = states.shape
    more = [] if ids is None else [ids]
    return pl.pallas_call(
        functools.partial(mix_kernel, layout, ids is None),
        out_shape=(
            jax.ShapeDtypeStruct((tok, width), BF16),
            jax.ShapeDtypeStruct((shards * SLOTS, width), BF16),
        ),
        in_specs=[VMEM_SPEC] * (3 + len(more)) + [ANY] * len(pieces),
        out_specs=(VMEM_SPEC, VMEM_SPEC),
        scratch_shapes=[
            pltpu.VMEM((tok, width), BF16),
            pltpu.VMEM((GROUPS, 2, 2, width // BANDS, LANES), BF16),
            pltpu.VMEM((GROUPS * SLOTS, LANES), F32),
            pltpu.VMEM((GROUPS, SLOTS, LANES), BF16),
            pltpu.SemaphoreType.DMA((len(pieces),)),
            pltpu.SemaphoreType.DMA((GROUPS,)),
        ],
        compiler_params=params(),
        cost_estimate=SMALL,
        name="mix",
    )(states, gain, attended, *more, *pieces)


def keys_values_kernel(layout, riding, decoded, *refs):
    spots = ring_spots(riding)
    pieces = refs[: len(layout)]
    out, scratch, arrived = refs[len(layout) :]
    depth = decoded.shape[1] // BANDS
    per = scratch.shape[3] // depth
    copies = start_loads(
        spots, pieces, layout, scratch, arrived, slice(0, scratch.shape[3]), spots[GROUPS]
    )
    for at in range(GROUPS):
        wait_group(copies, at)
        spot = spots[at]
        total = dot(decoded[...], lanes_of(scratch[spot], depth, 0, per)).astype(BF16)
        for group in range(per):
            out[spot * per + group] = total[:, group * LANES : (group + 1) * LANES]


def keys_values(riding, decoded, pieces, layout):
    tok, width = decoded.shape
    height = 2 * width // GROUPS // LANES * (width // BANDS)
    return pl.pallas_call(
        functools.partial(keys_values_kernel, layout, riding),
        out_shape=jax.ShapeDtypeStruct((2 * width // LANES, tok, LANES), BF16),
        in_specs=[VMEM_SPEC] + [ANY] * len(pieces),
        out_specs=VMEM_SPEC,
        scratch_shapes=[
            pltpu.VMEM((GROUPS, 2, 2, height, LANES), BF16),
            pltpu.SemaphoreType.DMA((len(pieces),)),
        ],
        compiler_params=params(),
        cost_estimate=SMALL,
        name="keys_values",
    )(decoded, *pieces)


def decode_kernel(layout, each, riding, queries, local_rows, fetched, here, there, *refs):
    spots = ring_spots(riding)
    pieces = refs[: len(layout)]
    fields, scratch, table, arrived = refs[len(layout) :]
    points, width = queries.shape
    depth = width // BANDS
    count = fetched.shape[0]
    per = 2 * width // GROUPS // LANES
    kept = scratch.shape[3]
    copies = start_loads(
        spots, pieces, layout, scratch, arrived, slice(0, kept), spots[GROUPS]
    )
    padding = jnp.zeros((table.shape[1] - count, LANES), BF16)
    for at in range(GROUPS):
        wait_group(copies, at)
        spot = spots[at]
        total = dot(fetched[...], lanes_of(scratch[spot], depth, 0, per)).astype(BF16)
        for group in range(per):
            table[spot * per + group, :count, :] = total[:, group * LANES : (group + 1) * LANES]
            if table.shape[1] > count:
                table[spot * per + group, count:, :] = padding

    pairs = width // LANES
    scale = BF16(1.0 / math.sqrt(width // HEADS))
    times = jnp.concatenate([here[...], there[...]], axis=1)
    bias = jnp.where(times > 0, 0.0, NEG)
    both = jnp.concatenate([times, times], axis=0)
    rows = []
    for pair in range(pairs):
        rows.append(
            pair_attend(
                queries[:, pair * LANES : (pair + 1) * LANES] * scale,
                jnp.concatenate([local_rows[pair], table[pair]], axis=0),
                jnp.concatenate([local_rows[pairs + pair], table[pairs + pair]], axis=0),
                bias,
                lambda weights: weights * both,
            )
        )
    gridded = jnp.concatenate(rows, axis=1)
    start = per * depth
    halves = depth // LANES
    height = (kept - start) // halves
    padded = jnp.zeros((GROUPS * height, points), F32)
    for chunk, band in enumerate(CHUNKS):
        for half in range(halves):
            at = start + half * height
            weight = scratch[:, chunk // 2, chunk % 2, at : at + height, :]
            first = band * depth + half * LANES
            padded += dot_nt(
                weight.reshape(GROUPS * height, LANES), gridded[:, first : first + LANES]
            )
    parts = [padded[group * height : group * height + each] for group in range(GROUPS)]
    fields[...] = jnp.concatenate(parts, axis=0).astype(BF16)


def decode(riding, queries, local_rows, fetched, here, there, pieces, layout, outputs):
    points, width = queries.shape
    height = pieces[0].shape[-2]
    remote = there.shape[1]
    return pl.pallas_call(
        functools.partial(decode_kernel, layout, outputs // GROUPS, riding),
        out_shape=jax.ShapeDtypeStruct((outputs, points), BF16),
        in_specs=[VMEM_SPEC] * 5 + [ANY] * len(pieces),
        out_specs=VMEM_SPEC,
        scratch_shapes=[
            pltpu.VMEM((GROUPS, 2, 2, height, LANES), BF16),
            pltpu.VMEM((2 * width // LANES, remote, LANES), BF16),
            pltpu.SemaphoreType.DMA((len(pieces),)),
        ],
        compiler_params=params(),
        cost_estimate=SMALL,
        name="decode",
    )(queries, local_rows, fetched, here, there, *pieces)


def stacked(*weights):
    parts = []
    for weight in weights:
        for at in range(0, weight.shape[-1], LANES):
            parts.append(weight[..., at : at + LANES])
    return jnp.concatenate(parts, axis=-2)


def pair_x(block, gate=None):
    if gate is not None:
        block, _ = lax.optimization_barrier((block, gate))
    other = lax.ppermute(block, "band", [(i, i ^ 2) for i in range(BANDS)])
    low = lax.axis_index("band") < 2
    return jnp.stack([jnp.where(low, block, other), jnp.where(low, other, block)])


def pair_core(block):
    other = swap_core(block)
    low = lax.axis_index("band") % 2 == 0
    return jnp.stack([jnp.where(low, block, other), jnp.where(low, other, block)])


def carry(block):
    pairs = []
    for i in range(GROUPS):
        here, there = RING[i] * BANDS, RING[(i + 1) % GROUPS] * BANDS
        for x in range(2):
            pairs.append((here + 2 * x, there + 2 * x))
            pairs.append((there + 2 * x + 1, here + 2 * x + 1))
    return lax.ppermute(block, ("seq", "band"), pairs)


def swap_core(block):
    return lax.ppermute(block, "band", [(i, i ^ 1) for i in range(BANDS)])


def chain_step(chains, step, gate=None):
    if gate is not None:
        *chains, _ = lax.optimization_barrier((*chains, gate))
    chains = [carry(block) for block in chains]
    pieces = []
    for half, block in enumerate(chains):
        pieces.append((block, (step, half)))
        pieces.append((swap_core(block), (GROUPS - step, 1 - half)))
    return chains, pieces


def ring_step(block, step, gate=None):
    if gate is not None:
        block, _ = lax.optimization_barrier((block, gate))
    if step < GROUPS // 2:
        block = carry(block)
        return block, [(block, (step, None)), (swap_core(block), (GROUPS - step, None))]
    half = lax.dynamic_index_in_dim(block, lax.axis_index("band") % 2, 0, keepdims=False)
    half = carry(half)
    return half, [(half, (step, 0)), (swap_core(half), (step, 1))]


def whole_blocks(*weights):
    parts = []
    for weight, height in weights:
        weight = lax.all_gather(weight, "seq", axis=1, tiled=True)
        weight = lax.all_gather(weight, "band", axis=0, tiled=True)
        depth, columns = weight.shape[0] // BANDS, weight.shape[1] // GROUPS
        weight = weight.reshape(2, 2, depth, GROUPS, columns).transpose(3, 1, 0, 2, 4)
        if height:
            weight = jnp.pad(
                weight.swapaxes(-1, -2), ((0, 0),) * 3 + ((0, height - columns), (0, 0))
            )
        parts.append(weight)
    return stacked(*parts)


def local(
    tokens, ln_gain, w_qkv, w_out, dec_gain, w_kv, w_final, reach, grid_query, neighbours, counts
):
    states = tokens[0]
    tok, width = states.shape
    shards, bands = lax.axis_size("seq"), lax.axis_size("band")
    outputs = w_final.shape[1] * shards
    height = -(-outputs // GROUPS // 16) * 16
    riding = (shards, bands) == (GROUPS, BANDS)
    up = [(i, i + 1) for i in range(shards - 1)]
    down = [(i + 1, i) for i in range(shards - 1)]
    left = lax.ppermute(states[tok - HALF :], "seq", up)
    right = lax.ppermute(states[:HALF], "seq", down)
    slots = (neighbours.T, counts.reshape(1, -1))
    there, requested, *payload = tables(tok, *slots, shards, (w_qkv, w_out) if riding else ())
    normed, bias, here = prepare(
        tok * shards, riding, left, states, right, ln_gain.reshape(1, width),
        reach.reshape(1, tok), *slots,
    )
    if riding:
        mine = pair_x(payload[0])
        mine, _, _ = lax.optimization_barrier((mine, left, right))
        other = swap_core(mine)
        pieces = [(mine, (0, 0)), (other, (0, 1))]
        chains, more = chain_step([mine, other], 1)
        pieces += more
        final = jnp.pad(w_final.T, ((0, height - w_final.shape[1]), (0, 0)))
        second = pair_core(pair_x(stacked(w_kv, final), chains[0]))
        later = [(second, (0, None))]
        chains, more = chain_step(chains, 2)
        pieces += more
        chains[1], _ = lax.optimization_barrier((chains[1], normed))
        chains, more = chain_step(chains, 3)
        pieces += more
        last, more = chain_step(chains[:1], 4)
        pieces += more
        normed, _ = lax.optimization_barrier((normed, chains[0]))
        made = project(riding, normed, pieces[:6], None)
        second, *_ = lax.optimization_barrier((second, chains[1], last[0], made))
        later = [(second, (0, None))]
        block, more = ring_step(second, 1)
        later += more
        made = project(riding, normed, pieces[6:10], made)
        block, more = ring_step(block, 2, made)
        later += more
        attended = attend(riding, normed, bias, pieces[10:], made, (0, 1, 7, 2, 6))
        block, more = ring_step(block, 3, attended)
        later += more
        ids = None
    else:
        block = whole_blocks((w_qkv, 0), (w_out, 0))
        block = jnp.pad(block, ((0, 0),) * 3 + ((0, SLOTS), (0, 0)))
        pieces = [(block[at, half], (at, half)) for at in range(GROUPS) for half in range(2)]
        block = whole_blocks((w_kv, 0), (w_final, height))
        later = [(block[at], (at, None)) for at in range(GROUPS)]
        made = project(riding, normed, pieces[:10], None)
        attended = attend(riding, normed, bias, pieces[10:], made, (0, 1, 2, 3, 4))
        ids = lax.all_to_all(
            requested.reshape(shards, SLOTS).astype(jnp.int32), "seq", 0, 0, tiled=True
        ).reshape(shards * SLOTS, 1)
    layout = tuple(at for _, at in pieces)
    pieces = [piece for piece, _ in pieces]
    decoded, found = mix(
        states, attended, dec_gain.reshape(1, width), ids, pieces, layout, shards
    )
    if riding:
        _, more = ring_step(block, 4, found)
        later += more
    fetched = lax.all_to_all(
        found.reshape(shards, SLOTS, width), "seq", split_axis=0, concat_axis=0, tiled=True
    )
    layout = tuple(at for _, at in later)
    pieces = [piece for piece, _ in later]
    local_rows = keys_values(riding, decoded, pieces, layout)
    fields = decode(
        riding, grid_query[0], local_rows, fetched.reshape(shards * SLOTS, width), here, there,
        pieces, layout, outputs,
    )
    return fields[None]


def solution(mesh):
    return jax.shard_map(
        local,
        mesh=mesh,
        in_specs=(
            P("band", "seq", None),
            P(),
            P("band", "seq"),
            P("band", "seq"),
            P(),
            P("band", "seq"),
            P("band", "seq"),
            P("seq"),
            P("band", "seq", None),
            P("seq", None),
            P("seq"),
        ),
        out_specs=P("band", None, "seq"),
        check_vma=False,
    )
```

```python
import functools
import math

import jax
import jax.numpy as jnp
import numpy as np
from jax import lax
from jax.experimental import pallas as pl
from jax.experimental.pallas import tpu as pltpu
from jax.sharding import PartitionSpec as P

HEADS = 16
HALF = 128
C = 12
SLOTS = 16
EPSILON = 1e-05
NEG = -1e30
LANES = 128
GROUPS = 8
BANDS = 4
CHUNKS = (0, 2, 1, 3)
RING = (0, 2, 4, 6, 7, 5, 3, 1)
VMEM = 60 * 1024 * 1024
SMALL = pl.CostEstimate(flops=1000, bytes_accessed=1000, transcendentals=0)
F32 = jnp.float32
BF16 = jnp.bfloat16


def dot(a, b):
    return jnp.dot(a, b, preferred_element_type=F32)


def dot_nt(a, b):
    return lax.dot_general(a, b, (((1,), (1,)), ((), ())), preferred_element_type=F32)


def layer_norm(values, gain):
    values = values.astype(F32)
    centred = values - jnp.mean(values, axis=-1, keepdims=True)
    spread = jnp.mean(centred * centred, axis=-1, keepdims=True)
    return (centred * lax.rsqrt(spread + EPSILON) * gain).astype(BF16)


def here_at(riding):
    return lax.axis_index("seq"), (lax.axis_index("band") % 2 if riding else 0)


def ring_spots(riding):
    if not riding:
        return list(range(GROUPS)) + [0]
    seq, core = here_at(True)
    at_ring = jnp.where(seq % 2 == 0, seq // 2, GROUPS - 1 - seq // 2)
    turn = jnp.where(core == 0, GROUPS - 1, 1)
    spots = []
    for at in range(GROUPS):
        step = (at_ring + turn * at) % GROUPS
        spots.append(jnp.where(step < GROUPS // 2, 2 * step, 2 * GROUPS - 1 - 2 * step))
    return spots + [core]


def params(**more):
    return pltpu.CompilerParams(vmem_limit_bytes=VMEM, **more)


def full_spec(shape):
    return pl.BlockSpec(shape, lambda *_: (0,) * len(shape))


def own_first(rows, core, depth):
    parts = [rows[:, b * depth : (b + 1) * depth] for b in range(BANDS)]
    order = ((0, 1), (2, 3), (1, 0), (3, 2))
    return jnp.concatenate([jnp.where(core == 0, parts[a], parts[b]) for a, b in order], axis=1)


def as_column(row):
    return jnp.broadcast_to(row, (8, row.shape[1])).T[:, :1]


def prepare_kernel(
    total, riding, left, own, right, gain, reach, neighbours, counts, normed, bias, multiplicity
):
    place = here_at(riding)
    tok = own.shape[0]
    depth = own.shape[1] // BANDS
    for at, part in ((0, left), (HALF, own), (HALF + tok, right)):
        rows = layer_norm(part[...], gain[...])
        normed[at : at + part.shape[0], :] = own_first(rows, place[1], depth)

    first = place[0] * tok
    span = 3 * HALF
    row = lax.broadcasted_iota(jnp.int32, (HALF, span), 0)
    col = lax.broadcasted_iota(jnp.int32, (HALF, span), 1)
    away = jnp.abs(row + HALF - col)
    limit = as_column(reach[...])
    for block in range(tok // HALF):
        key = first + (block - 1) * HALF + col
        allowed = (away <= limit[block * HALF : (block + 1) * HALF, :]) & (key >= 0) & (key < total)
        bias[block] = jnp.where(allowed, 0.0, NEG)

    ids = neighbours[...].T
    used = as_column(counts[...])
    mesh = lax.broadcasted_iota(jnp.int32, multiplicity.shape, 1) + first
    here = jnp.zeros(multiplicity.shape, F32)
    for slot in range(ids.shape[1]):
        here += ((ids[:, slot : slot + 1] == mesh) & (slot < used)).astype(F32)
    multiplicity[...] = here


def prepare(total, riding, left, own, right, gain, reach, neighbours, counts):
    tok, width = own.shape
    operands = (left, own, right, gain, reach, neighbours, counts)
    outs = (
        jax.ShapeDtypeStruct((tok + 2 * HALF, width), BF16),
        jax.ShapeDtypeStruct((tok // HALF, HALF, 3 * HALF), F32),
        jax.ShapeDtypeStruct((neighbours.shape[1], tok), F32),
    )
    return pl.pallas_call(
        functools.partial(prepare_kernel, total, riding),
        out_shape=outs,
        in_specs=[pl.BlockSpec(memory_space=pltpu.VMEM)] * len(operands),
        out_specs=[pl.BlockSpec(memory_space=pltpu.VMEM)] * len(outs),
        compiler_params=params(),
        cost_estimate=SMALL,
        name="prepare",
    )(*operands)


def tables_kernel(tok, count, neighbours, counts, low, rank, tri, *refs):
    weights, (multiplicity, requested) = refs[:count], refs[count : count + 2]
    first = lax.axis_index("seq") * tok
    slots = neighbours.shape[0]
    ids = neighbours[...].T
    used = as_column(counts[...])
    start = low[...]
    elsewhere = start != first
    hits = []
    for slot in range(slots):
        which = ids[:, slot : slot + 1]
        hits.append(
            ((which >= start) & (which < start + tok) & (slot < used) & elsewhere).astype(F32)
        )
    running = dot(tri[...], sum(hits).astype(BF16))
    order = rank[...]
    asked = jnp.zeros(hits[0].shape, F32)
    there = jnp.zeros(hits[0].shape, F32)
    for slot in range(slots):
        mine = jnp.where(running == order, hits[slot], 0.0)
        there += mine
        offset = (ids[:, slot : slot + 1] - start).astype(F32)
        asked += jnp.where(mine > 0, offset, 0.0)
        running += hits[slot]
    multiplicity[...] = there
    asked = jnp.sum(asked, axis=0, keepdims=True)
    requested[...] = asked.astype(BF16)
    if weights:
        payload = refs[-1]
        at = 0
        for weight in weights:
            depth, columns = weight.shape
            for first in range(0, columns, LANES):
                payload[at : at + depth, :] = weight[:, first : first + LANES]
                at += depth
        payload[at:, :] = jnp.broadcast_to(asked, (SLOTS, LANES)).astype(BF16)


def tables(tok, neighbours, counts, shards, weights):
    points = neighbours.shape[1]
    remote = shards * SLOTS
    column = np.arange(remote)
    low = (column // SLOTS * tok).astype(np.int32)[None]
    rank = (column % SLOTS).astype(np.float32)[None]
    tri = np.tril(np.ones((points, points), np.float32), -1).astype(BF16)
    operands = (neighbours, counts, low, rank, tri) + weights
    outs = (
        jax.ShapeDtypeStruct((points, remote), F32),
        jax.ShapeDtypeStruct((1, remote), BF16),
    )
    if weights:
        rows = sum(weight.shape[0] * weight.shape[1] // LANES for weight in weights) + SLOTS
        outs += (jax.ShapeDtypeStruct((rows, LANES), BF16),)
    return pl.pallas_call(
        functools.partial(tables_kernel, tok, len(weights)),
        out_shape=outs,
        in_specs=[pl.BlockSpec(memory_space=pltpu.VMEM)] * len(operands),
        out_specs=[pl.BlockSpec(memory_space=pltpu.VMEM)] * len(outs),
        compiler_params=params(),
        cost_estimate=SMALL,
        name="tables",
    )(*operands)


def pair_attend(queries, keys, values, bias, weights_of):
    rows = queries.shape[0]
    lane = lax.broadcasted_iota(jnp.int32, (rows, LANES), 1)
    first = lane < LANES // 2
    zero = jnp.zeros_like(queries)
    both = jnp.concatenate(
        [jnp.where(first, queries, zero), jnp.where(first, zero, queries)], axis=0
    )
    scores = dot_nt(both, keys)
    scores = scores + jnp.concatenate([bias, bias], axis=0)
    top = jnp.max(scores, axis=-1, keepdims=True)
    weights = weights_of(jnp.exp(scores - top)).astype(BF16)
    summed = dot(weights, jnp.concatenate([values, jnp.ones_like(values)], axis=1))
    share = summed[:, :LANES] / summed[:, LANES:]
    return jnp.where(first, share[:rows], share[rows:]).astype(BF16)


def start_loads(spots, pieces, layout, scratch, arrived, rows, core=None):
    copies = {}
    for n, (piece, (at, half)) in enumerate(zip(pieces, layout)):
        place = scratch.at[spots[at]]
        if half is None:
            copy = pltpu.make_async_copy(piece.at[:, :, rows, :], place, arrived.at[n])
        else:
            to = half if core is None else (1 - core if half else core)
            copy = pltpu.make_async_copy(piece.at[:, rows, :], place.at[to], arrived.at[n])
        copy.start()
        copies.setdefault(at, []).append(copy)
    return copies


def wait_group(copies, at):
    for copy in copies.get(at, ()):
        copy.wait()


def lanes_of(block, depth, start, count):
    rows = block.shape[0] * block.shape[1] * depth if block.ndim == 4 else block.shape[0] * depth
    columns = [
        block[..., start + g * depth : start + (g + 1) * depth, :].reshape(rows, LANES)
        for g in range(count)
    ]
    return columns[0] if count == 1 else jnp.concatenate(columns, axis=1)


SMEM = pl.BlockSpec(memory_space=pltpu.SMEM)
VMEM_SPEC = pl.BlockSpec(memory_space=pltpu.VMEM)
ANY = pl.BlockSpec(memory_space=pl.ANY)


def projection(normed, weight, depth, per):
    return dot(normed, lanes_of(weight[...], depth, 0, per)).astype(BF16)


def project_kernel(layout, riding, normed, *refs):
    spots = ring_spots(riding)
    pieces = refs[: len(layout)]
    out, scratch, made, arrived, sent = refs[-5:]
    per = made.shape[1]
    depth = normed.shape[1] // BANDS
    copies = start_loads(spots, pieces, layout, scratch, arrived, slice(0, per * depth))
    writes = []
    for n, at in enumerate(copies):
        wait_group(copies, at)
        total = projection(normed[...], scratch.at[spots[at]], depth, per)
        for group in range(per):
            made[n, group] = total[:, group * LANES : (group + 1) * LANES]
        writes.append(
            pltpu.make_async_copy(made.at[n], out.at[pl.ds(spots[at] * per, per)], sent.at[n])
        )
        writes[-1].start()
    for write in writes:
        write.wait()


def project(riding, normed, pieces, before):
    rows, width = normed.shape
    layout = tuple(place for _, place in pieces)
    arrays = [array for array, _ in pieces]
    per = 3 * width // LANES // GROUPS
    count = len({at for at, _ in layout})
    more = [] if before is None else [before]
    return pl.pallas_call(
        functools.partial(project_kernel, layout, riding),
        out_shape=jax.ShapeDtypeStruct((GROUPS * per, rows, LANES), BF16),
        in_specs=[VMEM_SPEC] + [ANY] * (len(arrays) + len(more)),
        out_specs=ANY,
        scratch_shapes=[
            pltpu.VMEM((GROUPS, 2, 2, per * width // BANDS, LANES), BF16),
            pltpu.VMEM((count, per, rows, LANES), BF16),
            pltpu.SemaphoreType.DMA((len(arrays),)),
            pltpu.SemaphoreType.DMA((count,)),
        ],
        input_output_aliases={1 + len(arrays): 0} if more else {},
        compiler_params=params(),
        cost_estimate=SMALL,
        name="project",
    )(normed, *arrays, *more)


def attend_kernel(layout, ready, riding, normed, bias, *refs):
    spots = ring_spots(riding)
    pieces = refs[: len(layout)]
    made, attended, scratch, projected, arrived, loaded = refs[len(layout) :]
    width = normed.shape[1]
    depth = width // BANDS
    per = projected.shape[0] // GROUPS
    copies = start_loads(spots, pieces, layout, scratch, arrived, slice(0, per * depth))
    reads = []
    for n, at in enumerate(ready):
        place = pl.ds(spots[at] * per, per)
        reads.append(pltpu.make_async_copy(made.at[place], projected.at[place], loaded.at[n]))
        reads[-1].start()
    for at in copies:
        wait_group(copies, at)
        total = projection(normed[...], scratch.at[spots[at]], depth, per)
        for group in range(per):
            projected[spots[at] * per + group] = total[:, group * LANES : (group + 1) * LANES]
    for read in reads:
        read.wait()
    pairs = width // LANES
    scale = BF16(1.0 / math.sqrt(width // HEADS))
    for pair in range(pairs):
        for block in range(bias.shape[0]):
            at = block * HALF
            attended[at : at + HALF, pair * LANES : (pair + 1) * LANES] = pair_attend(
                projected[pair, at + HALF : at + 2 * HALF, :] * scale,
                projected[pairs + pair, at : at + 3 * HALF, :],
                projected[2 * pairs + pair, at : at + 3 * HALF, :],
                bias[block],
                lambda weights: weights,
            )


def attend(riding, normed, bias, pieces, made, ready):
    rows, width = normed.shape
    tok = rows - 2 * HALF
    layout = tuple(place for _, place in pieces)
    arrays = [array for array, _ in pieces]
    per = made.shape[0] // GROUPS
    return pl.pallas_call(
        functools.partial(attend_kernel, layout, ready, riding),
        out_shape=jax.ShapeDtypeStruct((tok, width), BF16),
        in_specs=[VMEM_SPEC, VMEM_SPEC] + [ANY] * (len(arrays) + 1),
        out_specs=VMEM_SPEC,
        scratch_shapes=[
            pltpu.VMEM((GROUPS, 2, 2, per * width // BANDS, LANES), BF16),
            pltpu.VMEM(made.shape, BF16),
            pltpu.SemaphoreType.DMA((len(arrays),)),
            pltpu.SemaphoreType.DMA((len(ready),)),
        ],
        compiler_params=params(),
        cost_estimate=SMALL,
        name="attend",
    )(normed, bias, *arrays, made)


def picked_rows(place, ids, spots, rows, asked, arrived):
    tok = rows.shape[0]
    if spots is None:
        which = ids[...]
    else:
        for at in range(GROUPS):
            asked[pl.ds(spots[at] * SLOTS, SLOTS), :] = jnp.broadcast_to(
                arrived[at, 0:1, :].astype(F32), (SLOTS, LANES)
            )
        count = GROUPS * SLOTS
        lane = lax.broadcasted_iota(jnp.int32, (count, LANES), 1)
        slot = lax.broadcasted_iota(jnp.int32, (count, LANES), 0) % SLOTS
        mine = jnp.where(lane == place[0] * SLOTS + slot, asked[...], 0.0)
        which = jnp.sum(mine, axis=1, keepdims=True).astype(jnp.int32)
    here = lax.broadcasted_iota(jnp.int32, (which.shape[0], tok), 1)
    return dot((which == here).astype(BF16), rows).astype(BF16)


def chunked(values, depth):
    return jnp.concatenate([values[:, b * depth : (b + 1) * depth] for b in CHUNKS], axis=1)


def mix_kernel(layout, riding, states, gain, *refs):
    place, spots = here_at(riding), ring_spots(riding)
    attended, refs = refs[0], refs[1:]
    ids = None
    if not riding:
        ids, refs = refs[0], refs[1:]
    pieces = refs[: len(layout)]
    decoded, found, mixed, scratch, asked, notes, arrived, noted = refs[len(layout) :]
    width = states.shape[1]
    depth = width // BANDS
    start = 3 * width // GROUPS // LANES * depth
    copies = start_loads(spots, pieces, layout, scratch, arrived, slice(start, start + depth))
    reads = []
    if riding:
        for piece, (at, core) in zip(pieces, layout):
            if core == 0:
                end = piece.shape[-2]
                reads.append(
                    pltpu.make_async_copy(
                        piece.at[0, end - SLOTS : end, :], notes.at[at], noted.at[at]
                    )
                )
                reads[-1].start()
    inputs = own_first(attended[...], place[1], depth)
    for at in range(GROUPS):
        wait_group(copies, at)
    for at in range(0, GROUPS, 2):
        columns = slice(at * LANES, (at + 2) * LANES)
        weight = [lanes_of(scratch[at + n], depth, 0, 1) for n in range(2)]
        total = dot(inputs, jnp.concatenate(weight, axis=1))
        mixed[:, columns] = (states[:, columns].astype(F32) + total).astype(BF16)
    for read in reads:
        read.wait()
    rows = chunked(layer_norm(mixed[...], gain[...]), depth)
    decoded[...] = rows
    found[...] = picked_rows(place, ids, spots if riding else None, rows, asked, notes)


def mix(states, attended, gain, ids, pieces, layout, shards):
    tok, width = states.shape
    more = [] if ids is None else [ids]
    return pl.pallas_call(
        functools.partial(mix_kernel, layout, ids is None),
        out_shape=(
            jax.ShapeDtypeStruct((tok, width), BF16),
            jax.ShapeDtypeStruct((shards * SLOTS, width), BF16),
        ),
        in_specs=[VMEM_SPEC] * (3 + len(more)) + [ANY] * len(pieces),
        out_specs=(VMEM_SPEC, VMEM_SPEC),
        scratch_shapes=[
            pltpu.VMEM((tok, width), BF16),
            pltpu.VMEM((GROUPS, 2, 2, width // BANDS, LANES), BF16),
            pltpu.VMEM((GROUPS * SLOTS, LANES), F32),
            pltpu.VMEM((GROUPS, SLOTS, LANES), BF16),
            pltpu.SemaphoreType.DMA((len(pieces),)),
            pltpu.SemaphoreType.DMA((GROUPS,)),
        ],
        compiler_params=params(),
        cost_estimate=SMALL,
        name="mix",
    )(states, gain, attended, *more, *pieces)


def keys_values_kernel(layout, riding, decoded, *refs):
    spots = ring_spots(riding)
    pieces = refs[: len(layout)]
    out, scratch, arrived = refs[len(layout) :]
    depth = decoded.shape[1] // BANDS
    per = scratch.shape[3] // depth
    copies = start_loads(
        spots, pieces, layout, scratch, arrived, slice(0, scratch.shape[3]), spots[GROUPS]
    )
    for at in range(GROUPS):
        wait_group(copies, at)
        spot = spots[at]
        total = dot(decoded[...], lanes_of(scratch[spot], depth, 0, per)).astype(BF16)
        for group in range(per):
            out[spot * per + group] = total[:, group * LANES : (group + 1) * LANES]


def keys_values(riding, decoded, pieces, layout):
    tok, width = decoded.shape
    height = 2 * width // GROUPS // LANES * (width // BANDS)
    return pl.pallas_call(
        functools.partial(keys_values_kernel, layout, riding),
        out_shape=jax.ShapeDtypeStruct((2 * width // LANES, tok, LANES), BF16),
        in_specs=[VMEM_SPEC] + [ANY] * len(pieces),
        out_specs=VMEM_SPEC,
        scratch_shapes=[
            pltpu.VMEM((GROUPS, 2, 2, height, LANES), BF16),
            pltpu.SemaphoreType.DMA((len(pieces),)),
        ],
        compiler_params=params(),
        cost_estimate=SMALL,
        name="keys_values",
    )(decoded, *pieces)


def decode_kernel(layout, each, riding, queries, local_rows, fetched, here, there, *refs):
    spots = ring_spots(riding)
    pieces = refs[: len(layout)]
    fields, scratch, table, arrived = refs[len(layout) :]
    points, width = queries.shape
    depth = width // BANDS
    count = fetched.shape[0]
    per = 2 * width // GROUPS // LANES
    kept = scratch.shape[3]
    copies = start_loads(
        spots, pieces, layout, scratch, arrived, slice(0, kept), spots[GROUPS]
    )
    padding = jnp.zeros((table.shape[1] - count, LANES), BF16)
    for at in range(GROUPS):
        wait_group(copies, at)
        spot = spots[at]
        total = dot(fetched[...], lanes_of(scratch[spot], depth, 0, per)).astype(BF16)
        for group in range(per):
            table[spot * per + group, :count, :] = total[:, group * LANES : (group + 1) * LANES]
            if table.shape[1] > count:
                table[spot * per + group, count:, :] = padding

    pairs = width // LANES
    scale = BF16(1.0 / math.sqrt(width // HEADS))
    times = jnp.concatenate([here[...], there[...]], axis=1)
    bias = jnp.where(times > 0, 0.0, NEG)
    both = jnp.concatenate([times, times], axis=0)
    rows = []
    for pair in range(pairs):
        rows.append(
            pair_attend(
                queries[:, pair * LANES : (pair + 1) * LANES] * scale,
                jnp.concatenate([local_rows[pair], table[pair]], axis=0),
                jnp.concatenate([local_rows[pairs + pair], table[pairs + pair]], axis=0),
                bias,
                lambda weights: weights * both,
            )
        )
    gridded = jnp.concatenate(rows, axis=1)
    start = per * depth
    halves = depth // LANES
    height = (kept - start) // halves
    padded = jnp.zeros((GROUPS * height, points), F32)
    for chunk, band in enumerate(CHUNKS):
        for half in range(halves):
            at = start + half * height
            weight = scratch[:, chunk // 2, chunk % 2, at : at + height, :]
            first = band * depth + half * LANES
            padded += dot_nt(
                weight.reshape(GROUPS * height, LANES), gridded[:, first : first + LANES]
            )
    parts = [padded[group * height : group * height + each] for group in range(GROUPS)]
    fields[...] = jnp.concatenate(parts, axis=0).astype(BF16)


def decode(riding, queries, local_rows, fetched, here, there, pieces, layout, outputs):
    points, width = queries.shape
    height = pieces[0].shape[-2]
    remote = there.shape[1]
    return pl.pallas_call(
        functools.partial(decode_kernel, layout, outputs // GROUPS, riding),
        out_shape=jax.ShapeDtypeStruct((outputs, points), BF16),
        in_specs=[VMEM_SPEC] * 5 + [ANY] * len(pieces),
        out_specs=VMEM_SPEC,
        scratch_shapes=[
            pltpu.VMEM((GROUPS, 2, 2, height, LANES), BF16),
            pltpu.VMEM((2 * width // LANES, remote, LANES), BF16),
            pltpu.SemaphoreType.DMA((len(pieces),)),
        ],
        compiler_params=params(),
        cost_estimate=SMALL,
        name="decode",
    )(queries, local_rows, fetched, here, there, *pieces)


def stacked(*weights):
    parts = []
    for weight in weights:
        for at in range(0, weight.shape[-1], LANES):
            parts.append(weight[..., at : at + LANES])
    return jnp.concatenate(parts, axis=-2)


def pair_x(block, gate=None):
    if gate is not None:
        block, _ = lax.optimization_barrier((block, gate))
    other = lax.ppermute(block, "band", [(i, i ^ 2) for i in range(BANDS)])
    low = lax.axis_index("band") < 2
    return jnp.stack([jnp.where(low, block, other), jnp.where(low, other, block)])


def pair_core(block):
    other = swap_core(block)
    low = lax.axis_index("band") % 2 == 0
    return jnp.stack([jnp.where(low, block, other), jnp.where(low, other, block)])


def carry(block):
    pairs = []
    for i in range(GROUPS):
        here, there = RING[i] * BANDS, RING[(i + 1) % GROUPS] * BANDS
        for x in range(2):
            pairs.append((here + 2 * x, there + 2 * x))
            pairs.append((there + 2 * x + 1, here + 2 * x + 1))
    return lax.ppermute(block, ("seq", "band"), pairs)


def swap_core(block):
    return lax.ppermute(block, "band", [(i, i ^ 1) for i in range(BANDS)])


def chain_step(chains, step, gate=None):
    if gate is not None:
        *chains, _ = lax.optimization_barrier((*chains, gate))
    chains = [carry(block) for block in chains]
    pieces = []
    for half, block in enumerate(chains):
        pieces.append((block, (step, half)))
        pieces.append((swap_core(block), (GROUPS - step, 1 - half)))
    return chains, pieces


def ring_step(block, step, gate=None):
    if gate is not None:
        block, _ = lax.optimization_barrier((block, gate))
    if step < GROUPS // 2:
        block = carry(block)
        return block, [(block, (step, None)), (swap_core(block), (GROUPS - step, None))]
    half = lax.dynamic_index_in_dim(block, lax.axis_index("band") % 2, 0, keepdims=False)
    half = carry(half)
    return half, [(half, (step, 0)), (swap_core(half), (step, 1))]


def whole_blocks(*weights):
    parts = []
    for weight, height in weights:
        weight = lax.all_gather(weight, "seq", axis=1, tiled=True)
        weight = lax.all_gather(weight, "band", axis=0, tiled=True)
        depth, columns = weight.shape[0] // BANDS, weight.shape[1] // GROUPS
        weight = weight.reshape(2, 2, depth, GROUPS, columns).transpose(3, 1, 0, 2, 4)
        if height:
            weight = jnp.pad(
                weight.swapaxes(-1, -2), ((0, 0),) * 3 + ((0, height - columns), (0, 0))
            )
        parts.append(weight)
    return stacked(*parts)


def local(
    tokens, ln_gain, w_qkv, w_out, dec_gain, w_kv, w_final, reach, grid_query, neighbours, counts
):
    states = tokens[0]
    tok, width = states.shape
    shards, bands = lax.axis_size("seq"), lax.axis_size("band")
    outputs = w_final.shape[1] * shards
    height = -(-outputs // GROUPS // 16) * 16
    riding = (shards, bands) == (GROUPS, BANDS)
    up = [(i, i + 1) for i in range(shards - 1)]
    down = [(i + 1, i) for i in range(shards - 1)]
    left = lax.ppermute(states[tok - HALF :], "seq", up)
    right = lax.ppermute(states[:HALF], "seq", down)
    slots = (neighbours.T, counts.reshape(1, -1))
    there, requested, *payload = tables(tok, *slots, shards, (w_qkv, w_out) if riding else ())
    normed, bias, here = prepare(
        tok * shards, riding, left, states, right, ln_gain.reshape(1, width),
        reach.reshape(1, tok), *slots,
    )
    if riding:
        mine = pair_x(payload[0])
        mine, _, _ = lax.optimization_barrier((mine, left, right))
        other = swap_core(mine)
        pieces = [(mine, (0, 0)), (other, (0, 1))]
        chains, more = chain_step([mine, other], 1)
        pieces += more
        final = jnp.pad(w_final.T, ((0, height - w_final.shape[1]), (0, 0)))
        second = pair_core(pair_x(stacked(w_kv, final), chains[0]))
        later = [(second, (0, None))]
        chains, more = chain_step(chains, 2)
        pieces += more
        normed, _ = lax.optimization_barrier((normed, chains[0]))
        made = project(riding, normed, pieces[:6], None)
        chains, more = chain_step(chains, 3)
        pieces += more
        last, more = chain_step(chains[:1], 4, (chains[1], made))
        pieces += more
        made = project(riding, normed, pieces[6:10], made)
        second, *_ = lax.optimization_barrier((second, last[0], made))
        later = [(second, (0, None))]
        block, more = ring_step(second, 1)
        later += more
        block, more = ring_step(block, 2, [pieces[n][0] for n in (11, 13, 15)])
        later += more
        attended = attend(riding, normed, bias, pieces[10:], made, (0, 1, 7, 2, 6))
        block, more = ring_step(block, 3, attended)
        later += more
        ids = None
    else:
        block = whole_blocks((w_qkv, 0), (w_out, 0))
        block = jnp.pad(block, ((0, 0),) * 3 + ((0, SLOTS), (0, 0)))
        pieces = [(block[at, half], (at, half)) for at in range(GROUPS) for half in range(2)]
        block = whole_blocks((w_kv, 0), (w_final, height))
        later = [(block[at], (at, None)) for at in range(GROUPS)]
        made = project(riding, normed, pieces[:10], None)
        attended = attend(riding, normed, bias, pieces[10:], made, (0, 1, 2, 3, 4))
        ids = lax.all_to_all(
            requested.reshape(shards, SLOTS).astype(jnp.int32), "seq", 0, 0, tiled=True
        ).reshape(shards * SLOTS, 1)
    layout = tuple(at for _, at in pieces)
    pieces = [piece for piece, _ in pieces]
    decoded, found = mix(
        states, attended, dec_gain.reshape(1, width), ids, pieces, layout, shards
    )
    if riding:
        _, more = ring_step(block, 4, found)
        later += more
    fetched = lax.all_to_all(
        found.reshape(shards, SLOTS, width), "seq", split_axis=0, concat_axis=0, tiled=True
    )
    layout = tuple(at for _, at in later)
    pieces = [piece for piece, _ in later]
    local_rows = keys_values(riding, decoded, pieces, layout)
    fields = decode(
        riding, grid_query[0], local_rows, fetched.reshape(shards * SLOTS, width), here, there,
        pieces, layout, outputs,
    )
    return fields[None]


def solution(mesh):
    return jax.shard_map(
        local,
        mesh=mesh,
        in_specs=(
            P("band", "seq", None),
            P(),
            P("band", "seq"),
            P("band", "seq"),
            P(),
            P("band", "seq"),
            P("band", "seq"),
            P("seq"),
            P("band", "seq", None),
            P("seq", None),
            P("seq"),
        ),
        out_specs=P("band", None, "seq"),
        check_vma=False,
    )
```

```python
import functools
import math

import jax
import jax.numpy as jnp
import numpy as np
from jax import lax
from jax.experimental import pallas as pl
from jax.experimental.pallas import tpu as pltpu
from jax.sharding import PartitionSpec as P

HEADS = 16
HALF = 128
C = 12
SLOTS = 16
EPSILON = 1e-05
NEG = -1e30
LANES = 128
GROUPS = 8
BANDS = 4
CHUNKS = (0, 2, 1, 3)
RING = (0, 2, 4, 6, 7, 5, 3, 1)
VMEM = 60 * 1024 * 1024
SMALL = pl.CostEstimate(flops=1000, bytes_accessed=1000, transcendentals=0)
F32 = jnp.float32
BF16 = jnp.bfloat16


def dot(a, b):
    return jnp.dot(a, b, preferred_element_type=F32)


def dot_nt(a, b):
    return lax.dot_general(a, b, (((1,), (1,)), ((), ())), preferred_element_type=F32)


def layer_norm(values, gain):
    values = values.astype(F32)
    centred = values - jnp.mean(values, axis=-1, keepdims=True)
    spread = jnp.mean(centred * centred, axis=-1, keepdims=True)
    return (centred * lax.rsqrt(spread + EPSILON) * gain).astype(BF16)


def here_at(riding):
    return lax.axis_index("seq"), (lax.axis_index("band") % 2 if riding else 0)


def ring_spots(riding):
    if not riding:
        return list(range(GROUPS)) + [0]
    seq, core = here_at(True)
    at_ring = jnp.where(seq % 2 == 0, seq // 2, GROUPS - 1 - seq // 2)
    turn = jnp.where(core == 0, GROUPS - 1, 1)
    spots = []
    for at in range(GROUPS):
        step = (at_ring + turn * at) % GROUPS
        spots.append(jnp.where(step < GROUPS // 2, 2 * step, 2 * GROUPS - 1 - 2 * step))
    return spots + [core]


def params(**more):
    return pltpu.CompilerParams(vmem_limit_bytes=VMEM, **more)


def full_spec(shape):
    return pl.BlockSpec(shape, lambda *_: (0,) * len(shape))


def own_first(rows, core, depth):
    parts = [rows[:, b * depth : (b + 1) * depth] for b in range(BANDS)]
    order = ((0, 1), (2, 3), (1, 0), (3, 2))
    return jnp.concatenate([jnp.where(core == 0, parts[a], parts[b]) for a, b in order], axis=1)


def as_column(row):
    return jnp.broadcast_to(row, (8, row.shape[1])).T[:, :1]


def prepare_kernel(
    total, riding, left, own, right, gain, reach, neighbours, counts, normed, bias, multiplicity
):
    place = here_at(riding)
    tok = own.shape[0]
    depth = own.shape[1] // BANDS
    for at, part in ((0, left), (HALF, own), (HALF + tok, right)):
        rows = layer_norm(part[...], gain[...])
        normed[at : at + part.shape[0], :] = own_first(rows, place[1], depth)

    first = place[0] * tok
    span = 3 * HALF
    row = lax.broadcasted_iota(jnp.int32, (HALF, span), 0)
    col = lax.broadcasted_iota(jnp.int32, (HALF, span), 1)
    away = jnp.abs(row + HALF - col)
    limit = as_column(reach[...])
    for block in range(tok // HALF):
        key = first + (block - 1) * HALF + col
        allowed = (away <= limit[block * HALF : (block + 1) * HALF, :]) & (key >= 0) & (key < total)
        bias[block] = jnp.where(allowed, 0.0, NEG)

    ids = neighbours[...].T
    used = as_column(counts[...])
    mesh = lax.broadcasted_iota(jnp.int32, multiplicity.shape, 1) + first
    here = jnp.zeros(multiplicity.shape, F32)
    for slot in range(ids.shape[1]):
        here += ((ids[:, slot : slot + 1] == mesh) & (slot < used)).astype(F32)
    multiplicity[...] = here


def prepare(total, riding, left, own, right, gain, reach, neighbours, counts):
    tok, width = own.shape
    operands = (left, own, right, gain, reach, neighbours, counts)
    outs = (
        jax.ShapeDtypeStruct((tok + 2 * HALF, width), BF16),
        jax.ShapeDtypeStruct((tok // HALF, HALF, 3 * HALF), F32),
        jax.ShapeDtypeStruct((neighbours.shape[1], tok), F32),
    )
    return pl.pallas_call(
        functools.partial(prepare_kernel, total, riding),
        out_shape=outs,
        in_specs=[pl.BlockSpec(memory_space=pltpu.VMEM)] * len(operands),
        out_specs=[pl.BlockSpec(memory_space=pltpu.VMEM)] * len(outs),
        compiler_params=params(),
        cost_estimate=SMALL,
        name="prepare",
    )(*operands)


def tables_kernel(tok, count, neighbours, counts, low, rank, tri, *refs):
    weights, (multiplicity, requested) = refs[:count], refs[count : count + 2]
    first = lax.axis_index("seq") * tok
    slots = neighbours.shape[0]
    ids = neighbours[...].T
    used = as_column(counts[...])
    start = low[...]
    elsewhere = start != first
    hits = []
    for slot in range(slots):
        which = ids[:, slot : slot + 1]
        hits.append(
            ((which >= start) & (which < start + tok) & (slot < used) & elsewhere).astype(F32)
        )
    running = dot(tri[...], sum(hits).astype(BF16))
    order = rank[...]
    asked = jnp.zeros(hits[0].shape, F32)
    there = jnp.zeros(hits[0].shape, F32)
    for slot in range(slots):
        mine = jnp.where(running == order, hits[slot], 0.0)
        there += mine
        offset = (ids[:, slot : slot + 1] - start).astype(F32)
        asked += jnp.where(mine > 0, offset, 0.0)
        running += hits[slot]
    multiplicity[...] = there
    asked = jnp.sum(asked, axis=0, keepdims=True)
    requested[...] = asked.astype(BF16)
    if weights:
        payload = refs[-1]
        at = 0
        for weight in weights:
            depth, columns = weight.shape
            for first in range(0, columns, LANES):
                payload[at : at + depth, :] = weight[:, first : first + LANES]
                at += depth
        payload[at:, :] = jnp.broadcast_to(asked, (SLOTS, LANES)).astype(BF16)


def tables(tok, neighbours, counts, shards, weights):
    points = neighbours.shape[1]
    remote = shards * SLOTS
    column = np.arange(remote)
    low = (column // SLOTS * tok).astype(np.int32)[None]
    rank = (column % SLOTS).astype(np.float32)[None]
    tri = np.tril(np.ones((points, points), np.float32), -1).astype(BF16)
    operands = (neighbours, counts, low, rank, tri) + weights
    outs = (
        jax.ShapeDtypeStruct((points, remote), F32),
        jax.ShapeDtypeStruct((1, remote), BF16),
    )
    if weights:
        rows = sum(weight.shape[0] * weight.shape[1] // LANES for weight in weights) + SLOTS
        outs += (jax.ShapeDtypeStruct((rows, LANES), BF16),)
    return pl.pallas_call(
        functools.partial(tables_kernel, tok, len(weights)),
        out_shape=outs,
        in_specs=[pl.BlockSpec(memory_space=pltpu.VMEM)] * len(operands),
        out_specs=[pl.BlockSpec(memory_space=pltpu.VMEM)] * len(outs),
        compiler_params=params(),
        cost_estimate=SMALL,
        name="tables",
    )(*operands)


def pair_attend(queries, keys, values, bias, weights_of):
    rows = queries.shape[0]
    lane = lax.broadcasted_iota(jnp.int32, (rows, LANES), 1)
    first = lane < LANES // 2
    zero = jnp.zeros_like(queries)
    both = jnp.concatenate(
        [jnp.where(first, queries, zero), jnp.where(first, zero, queries)], axis=0
    )
    scores = dot_nt(both, keys)
    scores = scores + jnp.concatenate([bias, bias], axis=0)
    top = jnp.max(scores, axis=-1, keepdims=True)
    weights = weights_of(jnp.exp(scores - top)).astype(BF16)
    summed = dot(weights, jnp.concatenate([values, jnp.ones_like(values)], axis=1))
    share = summed[:, :LANES] / summed[:, LANES:]
    return jnp.where(first, share[:rows], share[rows:]).astype(BF16)


def start_loads(spots, pieces, layout, scratch, arrived, rows, core=None):
    copies = {}
    for n, (piece, (at, half)) in enumerate(zip(pieces, layout)):
        place = scratch.at[spots[at]]
        if half is None:
            copy = pltpu.make_async_copy(piece.at[:, :, rows, :], place, arrived.at[n])
        else:
            to = half if core is None else (1 - core if half else core)
            copy = pltpu.make_async_copy(piece.at[:, rows, :], place.at[to], arrived.at[n])
        copy.start()
        copies.setdefault(at, []).append(copy)
    return copies


def wait_group(copies, at):
    for copy in copies.get(at, ()):
        copy.wait()


def lanes_of(block, depth, start, count):
    rows = block.shape[0] * block.shape[1] * depth if block.ndim == 4 else block.shape[0] * depth
    columns = [
        block[..., start + g * depth : start + (g + 1) * depth, :].reshape(rows, LANES)
        for g in range(count)
    ]
    return columns[0] if count == 1 else jnp.concatenate(columns, axis=1)


SMEM = pl.BlockSpec(memory_space=pltpu.SMEM)
VMEM_SPEC = pl.BlockSpec(memory_space=pltpu.VMEM)
ANY = pl.BlockSpec(memory_space=pl.ANY)


def projection(normed, weight, depth, per):
    return dot(normed, lanes_of(weight[...], depth, 0, per)).astype(BF16)


def project_kernel(layout, riding, normed, *refs):
    spots = ring_spots(riding)
    pieces = refs[: len(layout)]
    out, scratch, made, arrived, sent = refs[-5:]
    per = made.shape[1]
    depth = normed.shape[1] // BANDS
    copies = start_loads(spots, pieces, layout, scratch, arrived, slice(0, per * depth))
    writes = []
    for n, at in enumerate(copies):
        wait_group(copies, at)
        total = projection(normed[...], scratch.at[spots[at]], depth, per)
        for group in range(per):
            made[n, group] = total[:, group * LANES : (group + 1) * LANES]
        writes.append(
            pltpu.make_async_copy(made.at[n], out.at[pl.ds(spots[at] * per, per)], sent.at[n])
        )
        writes[-1].start()
    for write in writes:
        write.wait()


def project(riding, normed, pieces, before):
    rows, width = normed.shape
    layout = tuple(place for _, place in pieces)
    arrays = [array for array, _ in pieces]
    per = 3 * width // LANES // GROUPS
    count = len({at for at, _ in layout})
    more = [] if before is None else [before]
    return pl.pallas_call(
        functools.partial(project_kernel, layout, riding),
        out_shape=jax.ShapeDtypeStruct((GROUPS * per, rows, LANES), BF16),
        in_specs=[VMEM_SPEC] + [ANY] * (len(arrays) + len(more)),
        out_specs=ANY,
        scratch_shapes=[
            pltpu.VMEM((GROUPS, 2, 2, per * width // BANDS, LANES), BF16),
            pltpu.VMEM((count, per, rows, LANES), BF16),
            pltpu.SemaphoreType.DMA((len(arrays),)),
            pltpu.SemaphoreType.DMA((count,)),
        ],
        input_output_aliases={1 + len(arrays): 0} if more else {},
        compiler_params=params(),
        cost_estimate=SMALL,
        name="project",
    )(normed, *arrays, *more)


def attend_kernel(layout, ready, riding, normed, bias, *refs):
    spots = ring_spots(riding)
    pieces = refs[: len(layout)]
    made, attended, scratch, projected, arrived, loaded = refs[len(layout) :]
    width = normed.shape[1]
    depth = width // BANDS
    per = projected.shape[0] // GROUPS
    copies = start_loads(spots, pieces, layout, scratch, arrived, slice(0, per * depth))
    reads = []
    for n, at in enumerate(ready):
        place = pl.ds(spots[at] * per, per)
        reads.append(pltpu.make_async_copy(made.at[place], projected.at[place], loaded.at[n]))
        reads[-1].start()
    for at in copies:
        wait_group(copies, at)
        total = projection(normed[...], scratch.at[spots[at]], depth, per)
        for group in range(per):
            projected[spots[at] * per + group] = total[:, group * LANES : (group + 1) * LANES]
    for read in reads:
        read.wait()
    pairs = width // LANES
    scale = BF16(1.0 / math.sqrt(width // HEADS))
    for pair in range(pairs):
        for block in range(bias.shape[0]):
            at = block * HALF
            attended[at : at + HALF, pair * LANES : (pair + 1) * LANES] = pair_attend(
                projected[pair, at + HALF : at + 2 * HALF, :] * scale,
                projected[pairs + pair, at : at + 3 * HALF, :],
                projected[2 * pairs + pair, at : at + 3 * HALF, :],
                bias[block],
                lambda weights: weights,
            )


def attend(riding, normed, bias, pieces, made, ready):
    rows, width = normed.shape
    tok = rows - 2 * HALF
    layout = tuple(place for _, place in pieces)
    arrays = [array for array, _ in pieces]
    per = made.shape[0] // GROUPS
    return pl.pallas_call(
        functools.partial(attend_kernel, layout, ready, riding),
        out_shape=jax.ShapeDtypeStruct((tok, width), BF16),
        in_specs=[VMEM_SPEC, VMEM_SPEC] + [ANY] * (len(arrays) + 1),
        out_specs=VMEM_SPEC,
        scratch_shapes=[
            pltpu.VMEM((GROUPS, 2, 2, per * width // BANDS, LANES), BF16),
            pltpu.VMEM(made.shape, BF16),
            pltpu.SemaphoreType.DMA((len(arrays),)),
            pltpu.SemaphoreType.DMA((len(ready),)),
        ],
        compiler_params=params(),
        cost_estimate=SMALL,
        name="attend",
    )(normed, bias, *arrays, made)


def picked_rows(place, ids, spots, rows, asked, arrived):
    tok = rows.shape[0]
    if spots is None:
        which = ids[...]
    else:
        for at in range(GROUPS):
            asked[pl.ds(spots[at] * SLOTS, SLOTS), :] = jnp.broadcast_to(
                arrived[at, 0:1, :].astype(F32), (SLOTS, LANES)
            )
        count = GROUPS * SLOTS
        lane = lax.broadcasted_iota(jnp.int32, (count, LANES), 1)
        slot = lax.broadcasted_iota(jnp.int32, (count, LANES), 0) % SLOTS
        mine = jnp.where(lane == place[0] * SLOTS + slot, asked[...], 0.0)
        which = jnp.sum(mine, axis=1, keepdims=True).astype(jnp.int32)
    here = lax.broadcasted_iota(jnp.int32, (which.shape[0], tok), 1)
    return dot((which == here).astype(BF16), rows).astype(BF16)


def chunked(values, depth):
    return jnp.concatenate([values[:, b * depth : (b + 1) * depth] for b in CHUNKS], axis=1)


def mix_kernel(layout, riding, states, gain, *refs):
    place, spots = here_at(riding), ring_spots(riding)
    attended, refs = refs[0], refs[1:]
    ids = None
    if not riding:
        ids, refs = refs[0], refs[1:]
    pieces = refs[: len(layout)]
    decoded, found, mixed, scratch, asked, notes, arrived, noted = refs[len(layout) :]
    width = states.shape[1]
    depth = width // BANDS
    start = 3 * width // GROUPS // LANES * depth
    copies = start_loads(spots, pieces, layout, scratch, arrived, slice(start, start + depth))
    reads = []
    if riding:
        for piece, (at, core) in zip(pieces, layout):
            if core == 0:
                end = piece.shape[-2]
                reads.append(
                    pltpu.make_async_copy(
                        piece.at[0, end - SLOTS : end, :], notes.at[at], noted.at[at]
                    )
                )
                reads[-1].start()
    inputs = own_first(attended[...], place[1], depth)
    for at in range(GROUPS):
        wait_group(copies, at)
    for at in range(0, GROUPS, 2):
        columns = slice(at * LANES, (at + 2) * LANES)
        weight = [lanes_of(scratch[at + n], depth, 0, 1) for n in range(2)]
        total = dot(inputs, jnp.concatenate(weight, axis=1))
        mixed[:, columns] = (states[:, columns].astype(F32) + total).astype(BF16)
    for read in reads:
        read.wait()
    rows = chunked(layer_norm(mixed[...], gain[...]), depth)
    decoded[...] = rows
    found[...] = picked_rows(place, ids, spots if riding else None, rows, asked, notes)


def mix(states, attended, gain, ids, pieces, layout, shards):
    tok, width = states.shape
    more = [] if ids is None else [ids]
    return pl.pallas_call(
        functools.partial(mix_kernel, layout, ids is None),
        out_shape=(
            jax.ShapeDtypeStruct((tok, width), BF16),
            jax.ShapeDtypeStruct((shards * SLOTS, width), BF16),
        ),
        in_specs=[VMEM_SPEC] * (3 + len(more)) + [ANY] * len(pieces),
        out_specs=(VMEM_SPEC, VMEM_SPEC),
        scratch_shapes=[
            pltpu.VMEM((tok, width), BF16),
            pltpu.VMEM((GROUPS, 2, 2, width // BANDS, LANES), BF16),
            pltpu.VMEM((GROUPS * SLOTS, LANES), F32),
            pltpu.VMEM((GROUPS, SLOTS, LANES), BF16),
            pltpu.SemaphoreType.DMA((len(pieces),)),
            pltpu.SemaphoreType.DMA((GROUPS,)),
        ],
        compiler_params=params(),
        cost_estimate=SMALL,
        name="mix",
    )(states, gain, attended, *more, *pieces)


def keys_values_kernel(layout, riding, decoded, *refs):
    spots = ring_spots(riding)
    pieces = refs[: len(layout)]
    out, scratch, arrived = refs[len(layout) :]
    depth = decoded.shape[1] // BANDS
    per = scratch.shape[3] // depth
    copies = start_loads(
        spots, pieces, layout, scratch, arrived, slice(0, scratch.shape[3]), spots[GROUPS]
    )
    for at in range(GROUPS):
        wait_group(copies, at)
        spot = spots[at]
        total = dot(decoded[...], lanes_of(scratch[spot], depth, 0, per)).astype(BF16)
        for group in range(per):
            out[spot * per + group] = total[:, group * LANES : (group + 1) * LANES]


def keys_values(riding, decoded, pieces, layout):
    tok, width = decoded.shape
    height = 2 * width // GROUPS // LANES * (width // BANDS)
    return pl.pallas_call(
        functools.partial(keys_values_kernel, layout, riding),
        out_shape=jax.ShapeDtypeStruct((2 * width // LANES, tok, LANES), BF16),
        in_specs=[VMEM_SPEC] + [ANY] * len(pieces),
        out_specs=VMEM_SPEC,
        scratch_shapes=[
            pltpu.VMEM((GROUPS, 2, 2, height, LANES), BF16),
            pltpu.SemaphoreType.DMA((len(pieces),)),
        ],
        compiler_params=params(),
        cost_estimate=SMALL,
        name="keys_values",
    )(decoded, *pieces)


def decode_kernel(layout, each, riding, queries, local_rows, fetched, here, there, *refs):
    spots = ring_spots(riding)
    pieces = refs[: len(layout)]
    fields, scratch, table, arrived = refs[len(layout) :]
    points, width = queries.shape
    depth = width // BANDS
    count = fetched.shape[0]
    per = 2 * width // GROUPS // LANES
    kept = scratch.shape[3]
    copies = start_loads(
        spots, pieces, layout, scratch, arrived, slice(0, kept), spots[GROUPS]
    )
    padding = jnp.zeros((table.shape[1] - count, LANES), BF16)
    for at in range(GROUPS):
        wait_group(copies, at)
        spot = spots[at]
        total = dot(fetched[...], lanes_of(scratch[spot], depth, 0, per)).astype(BF16)
        for group in range(per):
            table[spot * per + group, :count, :] = total[:, group * LANES : (group + 1) * LANES]
            if table.shape[1] > count:
                table[spot * per + group, count:, :] = padding

    pairs = width // LANES
    scale = BF16(1.0 / math.sqrt(width // HEADS))
    times = jnp.concatenate([here[...], there[...]], axis=1)
    bias = jnp.where(times > 0, 0.0, NEG)
    both = jnp.concatenate([times, times], axis=0)
    rows = []
    for pair in range(pairs):
        rows.append(
            pair_attend(
                queries[:, pair * LANES : (pair + 1) * LANES] * scale,
                jnp.concatenate([local_rows[pair], table[pair]], axis=0),
                jnp.concatenate([local_rows[pairs + pair], table[pairs + pair]], axis=0),
                bias,
                lambda weights: weights * both,
            )
        )
    gridded = jnp.concatenate(rows, axis=1)
    start = per * depth
    halves = depth // LANES
    height = (kept - start) // halves
    padded = jnp.zeros((GROUPS * height, points), F32)
    for chunk, band in enumerate(CHUNKS):
        for half in range(halves):
            at = start + half * height
            weight = scratch[:, chunk // 2, chunk % 2, at : at + height, :]
            first = band * depth + half * LANES
            padded += dot_nt(
                weight.reshape(GROUPS * height, LANES), gridded[:, first : first + LANES]
            )
    parts = [padded[group * height : group * height + each] for group in range(GROUPS)]
    fields[...] = jnp.concatenate(parts, axis=0).astype(BF16)


def decode(riding, queries, local_rows, fetched, here, there, pieces, layout, outputs):
    points, width = queries.shape
    height = pieces[0].shape[-2]
    remote = there.shape[1]
    return pl.pallas_call(
        functools.partial(decode_kernel, layout, outputs // GROUPS, riding),
        out_shape=jax.ShapeDtypeStruct((outputs, points), BF16),
        in_specs=[VMEM_SPEC] * 5 + [ANY] * len(pieces),
        out_specs=VMEM_SPEC,
        scratch_shapes=[
            pltpu.VMEM((GROUPS, 2, 2, height, LANES), BF16),
            pltpu.VMEM((2 * width // LANES, remote, LANES), BF16),
            pltpu.SemaphoreType.DMA((len(pieces),)),
        ],
        compiler_params=params(),
        cost_estimate=SMALL,
        name="decode",
    )(queries, local_rows, fetched, here, there, *pieces)


def stacked(*weights):
    parts = []
    for weight in weights:
        for at in range(0, weight.shape[-1], LANES):
            parts.append(weight[..., at : at + LANES])
    return jnp.concatenate(parts, axis=-2)


def pair_x(block, gate=None):
    if gate is not None:
        block, _ = lax.optimization_barrier((block, gate))
    other = lax.ppermute(block, "band", [(i, i ^ 2) for i in range(BANDS)])
    low = lax.axis_index("band") < 2
    return jnp.stack([jnp.where(low, block, other), jnp.where(low, other, block)])


def pair_core(block):
    other = swap_core(block)
    low = lax.axis_index("band") % 2 == 0
    return jnp.stack([jnp.where(low, block, other), jnp.where(low, other, block)])


def carry(block):
    pairs = []
    for i in range(GROUPS):
        here, there = RING[i] * BANDS, RING[(i + 1) % GROUPS] * BANDS
        for x in range(2):
            pairs.append((here + 2 * x, there + 2 * x))
            pairs.append((there + 2 * x + 1, here + 2 * x + 1))
    return lax.ppermute(block, ("seq", "band"), pairs)


def swap_core(block):
    return lax.ppermute(block, "band", [(i, i ^ 1) for i in range(BANDS)])


def chain_step(chains, step, gate=None):
    if gate is not None:
        *chains, _ = lax.optimization_barrier((*chains, gate))
    chains = [carry(block) for block in chains]
    pieces = []
    for half, block in enumerate(chains):
        pieces.append((block, (step, half)))
        pieces.append((swap_core(block), (GROUPS - step, 1 - half)))
    return chains, pieces


def ring_step(block, step, gate=None):
    if gate is not None:
        block, _ = lax.optimization_barrier((block, gate))
    if step < GROUPS // 2:
        block = carry(block)
        return block, [(block, (step, None)), (swap_core(block), (GROUPS - step, None))]
    half = lax.dynamic_index_in_dim(block, lax.axis_index("band") % 2, 0, keepdims=False)
    half = carry(half)
    return half, [(half, (step, 0)), (swap_core(half), (step, 1))]


def whole_blocks(*weights):
    parts = []
    for weight, height in weights:
        weight = lax.all_gather(weight, "seq", axis=1, tiled=True)
        weight = lax.all_gather(weight, "band", axis=0, tiled=True)
        depth, columns = weight.shape[0] // BANDS, weight.shape[1] // GROUPS
        weight = weight.reshape(2, 2, depth, GROUPS, columns).transpose(3, 1, 0, 2, 4)
        if height:
            weight = jnp.pad(
                weight.swapaxes(-1, -2), ((0, 0),) * 3 + ((0, height - columns), (0, 0))
            )
        parts.append(weight)
    return stacked(*parts)


def local(
    tokens, ln_gain, w_qkv, w_out, dec_gain, w_kv, w_final, reach, grid_query, neighbours, counts
):
    states = tokens[0]
    tok, width = states.shape
    shards, bands = lax.axis_size("seq"), lax.axis_size("band")
    outputs = w_final.shape[1] * shards
    height = -(-outputs // GROUPS // 16) * 16
    riding = (shards, bands) == (GROUPS, BANDS)
    up = [(i, i + 1) for i in range(shards - 1)]
    down = [(i + 1, i) for i in range(shards - 1)]
    left = lax.ppermute(states[tok - HALF :], "seq", up)
    right = lax.ppermute(states[:HALF], "seq", down)
    slots = (neighbours.T, counts.reshape(1, -1))
    there, requested, *payload = tables(tok, *slots, shards, (w_qkv, w_out) if riding else ())
    normed, bias, here = prepare(
        tok * shards, riding, left, states, right, ln_gain.reshape(1, width),
        reach.reshape(1, tok), *slots,
    )
    if riding:
        mine = pair_x(payload[0])
        mine, _, _ = lax.optimization_barrier((mine, left, right))
        other = swap_core(mine)
        pieces = [(mine, (0, 0)), (other, (0, 1))]
        chains, more = chain_step([mine, other], 1)
        pieces += more
        final = jnp.pad(w_final.T, ((0, height - w_final.shape[1]), (0, 0)))
        second = pair_core(pair_x(stacked(w_kv, final), chains[0]))
        later = [(second, (0, None))]
        chains[1], _ = lax.optimization_barrier((chains[1], normed))
        chains, more = chain_step(chains, 2)
        pieces += more
        normed, _ = lax.optimization_barrier((normed, chains[0]))
        made = project(riding, normed, pieces[:2], None)
        normed, _ = lax.optimization_barrier((normed, chains[1]))
        chains[1], _ = lax.optimization_barrier((chains[1], made))
        chains, more = chain_step(chains, 3)
        pieces += more
        made = project(riding, normed, pieces[2:6], made)
        last, more = chain_step(chains[:1], 4, (chains[1], made))
        pieces += more
        made = project(riding, normed, pieces[6:10], made)
        second, *_ = lax.optimization_barrier((second, chains[1], made))
        later = [(second, (0, None))]
        block, more = ring_step(second, 1)
        later += more
        made = project(riding, normed, pieces[10:14], made)
        block, more = ring_step(block, 2, (made, pieces[15][0]))
        later += more
        attended = attend(riding, normed, bias, pieces[14:], made, (0, 1, 7, 2, 6, 3, 5))
        block, more = ring_step(block, 3, attended)
        later += more
        ids = None
    else:
        block = whole_blocks((w_qkv, 0), (w_out, 0))
        block = jnp.pad(block, ((0, 0),) * 3 + ((0, SLOTS), (0, 0)))
        pieces = [(block[at, half], (at, half)) for at in range(GROUPS) for half in range(2)]
        block = whole_blocks((w_kv, 0), (w_final, height))
        later = [(block[at], (at, None)) for at in range(GROUPS)]
        made = project(riding, normed, pieces[:14], None)
        attended = attend(riding, normed, bias, pieces[14:], made, tuple(range(7)))
        ids = lax.all_to_all(
            requested.reshape(shards, SLOTS).astype(jnp.int32), "seq", 0, 0, tiled=True
        ).reshape(shards * SLOTS, 1)
    layout = tuple(at for _, at in pieces)
    pieces = [piece for piece, _ in pieces]
    decoded, found = mix(
        states, attended, dec_gain.reshape(1, width), ids, pieces, layout, shards
    )
    if riding:
        _, more = ring_step(block, 4, found)
        later += more
    fetched = lax.all_to_all(
        found.reshape(shards, SLOTS, width), "seq", split_axis=0, concat_axis=0, tiled=True
    )
    layout = tuple(at for _, at in later)
    pieces = [piece for piece, _ in later]
    local_rows = keys_values(riding, decoded, pieces, layout)
    fields = decode(
        riding, grid_query[0], local_rows, fetched.reshape(shards * SLOTS, width), here, there,
        pieces, layout, outputs,
    )
    return fields[None]


def solution(mesh):
    return jax.shard_map(
        local,
        mesh=mesh,
        in_specs=(
            P("band", "seq", None),
            P(),
            P("band", "seq"),
            P("band", "seq"),
            P(),
            P("band", "seq"),
            P("band", "seq"),
            P("seq"),
            P("band", "seq", None),
            P("seq", None),
            P("seq"),
        ),
        out_specs=P("band", None, "seq"),
        check_vma=False,
    )
```

```python
import functools
import math

import jax
import jax.numpy as jnp
import numpy as np
from jax import lax
from jax.experimental import pallas as pl
from jax.experimental.pallas import tpu as pltpu
from jax.sharding import PartitionSpec as P

HEADS = 16
HALF = 128
C = 12
SLOTS = 16
EPSILON = 1e-05
NEG = -1e30
LANES = 128
GROUPS = 8
BANDS = 4
CHUNKS = (0, 2, 1, 3)
RING = (0, 2, 4, 6, 7, 5, 3, 1)
VMEM = 60 * 1024 * 1024
SMALL = pl.CostEstimate(flops=1000, bytes_accessed=1000, transcendentals=0)
F32 = jnp.float32
BF16 = jnp.bfloat16


def dot(a, b):
    return jnp.dot(a, b, preferred_element_type=F32)


def dot_nt(a, b):
    return lax.dot_general(a, b, (((1,), (1,)), ((), ())), preferred_element_type=F32)


def layer_norm(values, gain):
    values = values.astype(F32)
    centred = values - jnp.mean(values, axis=-1, keepdims=True)
    spread = jnp.mean(centred * centred, axis=-1, keepdims=True)
    return (centred * lax.rsqrt(spread + EPSILON) * gain).astype(BF16)


def here_at(riding):
    return lax.axis_index("seq"), (lax.axis_index("band") % 2 if riding else 0)


def ring_spots(riding):
    if not riding:
        return list(range(GROUPS)) + [0]
    seq, core = here_at(True)
    at_ring = jnp.where(seq % 2 == 0, seq // 2, GROUPS - 1 - seq // 2)
    turn = jnp.where(core == 0, GROUPS - 1, 1)
    spots = []
    for at in range(GROUPS):
        step = (at_ring + turn * at) % GROUPS
        spots.append(jnp.where(step < GROUPS // 2, 2 * step, 2 * GROUPS - 1 - 2 * step))
    return spots + [core]


def params(**more):
    return pltpu.CompilerParams(vmem_limit_bytes=VMEM, **more)


def full_spec(shape):
    return pl.BlockSpec(shape, lambda *_: (0,) * len(shape))


def own_first(rows, core, depth):
    parts = [rows[:, b * depth : (b + 1) * depth] for b in range(BANDS)]
    order = ((0, 1), (2, 3), (1, 0), (3, 2))
    return jnp.concatenate([jnp.where(core == 0, parts[a], parts[b]) for a, b in order], axis=1)


def as_column(row):
    return jnp.broadcast_to(row, (8, row.shape[1])).T[:, :1]


def prepare_kernel(
    total, riding, left, own, right, gain, reach, neighbours, counts, normed, bias, multiplicity
):
    place = here_at(riding)
    tok = own.shape[0]
    depth = own.shape[1] // BANDS
    for at, part in ((0, left), (HALF, own), (HALF + tok, right)):
        rows = layer_norm(part[...], gain[...])
        normed[at : at + part.shape[0], :] = own_first(rows, place[1], depth)

    first = place[0] * tok
    span = 3 * HALF
    row = lax.broadcasted_iota(jnp.int32, (HALF, span), 0)
    col = lax.broadcasted_iota(jnp.int32, (HALF, span), 1)
    away = jnp.abs(row + HALF - col)
    limit = as_column(reach[...])
    for block in range(tok // HALF):
        key = first + (block - 1) * HALF + col
        allowed = (away <= limit[block * HALF : (block + 1) * HALF, :]) & (key >= 0) & (key < total)
        bias[block] = jnp.where(allowed, 0.0, NEG)

    ids = neighbours[...].T
    used = as_column(counts[...])
    mesh = lax.broadcasted_iota(jnp.int32, multiplicity.shape, 1) + first
    here = jnp.zeros(multiplicity.shape, F32)
    for slot in range(ids.shape[1]):
        here += ((ids[:, slot : slot + 1] == mesh) & (slot < used)).astype(F32)
    multiplicity[...] = here


def prepare(total, riding, left, own, right, gain, reach, neighbours, counts):
    tok, width = own.shape
    operands = (left, own, right, gain, reach, neighbours, counts)
    outs = (
        jax.ShapeDtypeStruct((tok + 2 * HALF, width), BF16),
        jax.ShapeDtypeStruct((tok // HALF, HALF, 3 * HALF), F32),
        jax.ShapeDtypeStruct((neighbours.shape[1], tok), F32),
    )
    return pl.pallas_call(
        functools.partial(prepare_kernel, total, riding),
        out_shape=outs,
        in_specs=[pl.BlockSpec(memory_space=pltpu.VMEM)] * len(operands),
        out_specs=[pl.BlockSpec(memory_space=pltpu.VMEM)] * len(outs),
        compiler_params=params(),
        cost_estimate=SMALL,
        name="prepare",
    )(*operands)


def tables_kernel(tok, count, neighbours, counts, low, rank, tri, *refs):
    weights, (multiplicity, requested) = refs[:count], refs[count : count + 2]
    first = lax.axis_index("seq") * tok
    slots = neighbours.shape[0]
    ids = neighbours[...].T
    used = as_column(counts[...])
    start = low[...]
    elsewhere = start != first
    hits = []
    for slot in range(slots):
        which = ids[:, slot : slot + 1]
        hits.append(
            ((which >= start) & (which < start + tok) & (slot < used) & elsewhere).astype(F32)
        )
    running = dot(tri[...], sum(hits).astype(BF16))
    order = rank[...]
    asked = jnp.zeros(hits[0].shape, F32)
    there = jnp.zeros(hits[0].shape, F32)
    for slot in range(slots):
        mine = jnp.where(running == order, hits[slot], 0.0)
        there += mine
        offset = (ids[:, slot : slot + 1] - start).astype(F32)
        asked += jnp.where(mine > 0, offset, 0.0)
        running += hits[slot]
    multiplicity[...] = there
    asked = jnp.sum(asked, axis=0, keepdims=True)
    requested[...] = asked.astype(BF16)
    if weights:
        payload = refs[-1]
        at = 0
        for weight in weights:
            depth, columns = weight.shape
            for first in range(0, columns, LANES):
                payload[at : at + depth, :] = weight[:, first : first + LANES]
                at += depth
        payload[at:, :] = jnp.broadcast_to(asked, (SLOTS, LANES)).astype(BF16)


def tables(tok, neighbours, counts, shards, weights):
    points = neighbours.shape[1]
    remote = shards * SLOTS
    column = np.arange(remote)
    low = (column // SLOTS * tok).astype(np.int32)[None]
    rank = (column % SLOTS).astype(np.float32)[None]
    tri = np.tril(np.ones((points, points), np.float32), -1).astype(BF16)
    operands = (neighbours, counts, low, rank, tri) + weights
    outs = (
        jax.ShapeDtypeStruct((points, remote), F32),
        jax.ShapeDtypeStruct((1, remote), BF16),
    )
    if weights:
        rows = sum(weight.shape[0] * weight.shape[1] // LANES for weight in weights) + SLOTS
        outs += (jax.ShapeDtypeStruct((rows, LANES), BF16),)
    return pl.pallas_call(
        functools.partial(tables_kernel, tok, len(weights)),
        out_shape=outs,
        in_specs=[pl.BlockSpec(memory_space=pltpu.VMEM)] * len(operands),
        out_specs=[pl.BlockSpec(memory_space=pltpu.VMEM)] * len(outs),
        compiler_params=params(),
        cost_estimate=SMALL,
        name="tables",
    )(*operands)


def pair_attend(queries, keys, values, bias, weights_of):
    rows = queries.shape[0]
    lane = lax.broadcasted_iota(jnp.int32, (rows, LANES), 1)
    first = lane < LANES // 2
    zero = jnp.zeros_like(queries)
    both = jnp.concatenate(
        [jnp.where(first, queries, zero), jnp.where(first, zero, queries)], axis=0
    )
    scores = dot_nt(both, keys)
    scores = scores + jnp.concatenate([bias, bias], axis=0)
    top = jnp.max(scores, axis=-1, keepdims=True)
    weights = weights_of(jnp.exp(scores - top)).astype(BF16)
    summed = dot(weights, jnp.concatenate([values, jnp.ones_like(values)], axis=1))
    share = summed[:, :LANES] / summed[:, LANES:]
    return jnp.where(first, share[:rows], share[rows:]).astype(BF16)


def start_loads(spots, pieces, layout, scratch, arrived, rows, core=None):
    copies = {}
    for n, (piece, (at, half)) in enumerate(zip(pieces, layout)):
        place = scratch.at[spots[at]]
        if half is None:
            copy = pltpu.make_async_copy(piece.at[:, :, rows, :], place, arrived.at[n])
        else:
            to = half if core is None else (1 - core if half else core)
            copy = pltpu.make_async_copy(piece.at[:, rows, :], place.at[to], arrived.at[n])
        copy.start()
        copies.setdefault(at, []).append(copy)
    return copies


def wait_group(copies, at):
    for copy in copies.get(at, ()):
        copy.wait()


def lanes_of(block, depth, start, count):
    rows = block.shape[0] * block.shape[1] * depth if block.ndim == 4 else block.shape[0] * depth
    columns = [
        block[..., start + g * depth : start + (g + 1) * depth, :].reshape(rows, LANES)
        for g in range(count)
    ]
    return columns[0] if count == 1 else jnp.concatenate(columns, axis=1)


SMEM = pl.BlockSpec(memory_space=pltpu.SMEM)
VMEM_SPEC = pl.BlockSpec(memory_space=pltpu.VMEM)
ANY = pl.BlockSpec(memory_space=pl.ANY)


def projection(normed, weight, depth, per):
    return dot(normed, lanes_of(weight[...], depth, 0, per)).astype(BF16)


def project_kernel(layout, riding, normed, *refs):
    spots = ring_spots(riding)
    pieces = refs[: len(layout)]
    out, scratch, made, arrived, sent = refs[-5:]
    per = made.shape[1]
    depth = normed.shape[1] // BANDS
    copies = start_loads(spots, pieces, layout, scratch, arrived, slice(0, per * depth))
    writes = []
    for n, at in enumerate(copies):
        wait_group(copies, at)
        total = projection(normed[...], scratch.at[spots[at]], depth, per)
        for group in range(per):
            made[n, group] = total[:, group * LANES : (group + 1) * LANES]
        writes.append(
            pltpu.make_async_copy(made.at[n], out.at[pl.ds(spots[at] * per, per)], sent.at[n])
        )
        writes[-1].start()
    for write in writes:
        write.wait()


def project(riding, normed, pieces, before):
    rows, width = normed.shape
    layout = tuple(place for _, place in pieces)
    arrays = [array for array, _ in pieces]
    per = 3 * width // LANES // GROUPS
    count = len({at for at, _ in layout})
    more = [] if before is None else [before]
    return pl.pallas_call(
        functools.partial(project_kernel, layout, riding),
        out_shape=jax.ShapeDtypeStruct((GROUPS * per, rows, LANES), BF16),
        in_specs=[VMEM_SPEC] + [ANY] * (len(arrays) + len(more)),
        out_specs=ANY,
        scratch_shapes=[
            pltpu.VMEM((GROUPS, 2, 2, per * width // BANDS, LANES), BF16),
            pltpu.VMEM((count, per, rows, LANES), BF16),
            pltpu.SemaphoreType.DMA((len(arrays),)),
            pltpu.SemaphoreType.DMA((count,)),
        ],
        input_output_aliases={1 + len(arrays): 0} if more else {},
        compiler_params=params(),
        cost_estimate=SMALL,
        name="project",
    )(normed, *arrays, *more)


def attend_kernel(layout, ready, riding, normed, bias, *refs):
    spots = ring_spots(riding)
    pieces = refs[: len(layout)]
    made, attended, scratch, projected, arrived, loaded = refs[len(layout) :]
    width = normed.shape[1]
    depth = width // BANDS
    per = projected.shape[0] // GROUPS
    copies = start_loads(spots, pieces, layout, scratch, arrived, slice(0, per * depth))
    reads = []
    for n, at in enumerate(ready):
        place = pl.ds(spots[at] * per, per)
        reads.append(pltpu.make_async_copy(made.at[place], projected.at[place], loaded.at[n]))
        reads[-1].start()
    for at in copies:
        wait_group(copies, at)
        total = projection(normed[...], scratch.at[spots[at]], depth, per)
        for group in range(per):
            projected[spots[at] * per + group] = total[:, group * LANES : (group + 1) * LANES]
    for read in reads:
        read.wait()
    pairs = width // LANES
    scale = BF16(1.0 / math.sqrt(width // HEADS))
    for pair in range(pairs):
        for block in range(bias.shape[0]):
            at = block * HALF
            attended[at : at + HALF, pair * LANES : (pair + 1) * LANES] = pair_attend(
                projected[pair, at + HALF : at + 2 * HALF, :] * scale,
                projected[pairs + pair, at : at + 3 * HALF, :],
                projected[2 * pairs + pair, at : at + 3 * HALF, :],
                bias[block],
                lambda weights: weights,
            )


def attend(riding, normed, bias, pieces, made, ready):
    rows, width = normed.shape
    tok = rows - 2 * HALF
    layout = tuple(place for _, place in pieces)
    arrays = [array for array, _ in pieces]
    per = made.shape[0] // GROUPS
    return pl.pallas_call(
        functools.partial(attend_kernel, layout, ready, riding),
        out_shape=jax.ShapeDtypeStruct((tok, width), BF16),
        in_specs=[VMEM_SPEC, VMEM_SPEC] + [ANY] * (len(arrays) + 1),
        out_specs=VMEM_SPEC,
        scratch_shapes=[
            pltpu.VMEM((GROUPS, 2, 2, per * width // BANDS, LANES), BF16),
            pltpu.VMEM(made.shape, BF16),
            pltpu.SemaphoreType.DMA((len(arrays),)),
            pltpu.SemaphoreType.DMA((len(ready),)),
        ],
        compiler_params=params(),
        cost_estimate=SMALL,
        name="attend",
    )(normed, bias, *arrays, made)


def picked_rows(place, ids, spots, rows, asked, arrived):
    tok = rows.shape[0]
    if spots is None:
        which = ids[...]
    else:
        for at in range(GROUPS):
            asked[pl.ds(spots[at] * SLOTS, SLOTS), :] = jnp.broadcast_to(
                arrived[at, 0:1, :].astype(F32), (SLOTS, LANES)
            )
        count = GROUPS * SLOTS
        lane = lax.broadcasted_iota(jnp.int32, (count, LANES), 1)
        slot = lax.broadcasted_iota(jnp.int32, (count, LANES), 0) % SLOTS
        mine = jnp.where(lane == place[0] * SLOTS + slot, asked[...], 0.0)
        which = jnp.sum(mine, axis=1, keepdims=True).astype(jnp.int32)
    here = lax.broadcasted_iota(jnp.int32, (which.shape[0], tok), 1)
    return dot((which == here).astype(BF16), rows).astype(BF16)


def chunked(values, depth):
    return jnp.concatenate([values[:, b * depth : (b + 1) * depth] for b in CHUNKS], axis=1)


def mix_kernel(layout, riding, states, gain, *refs):
    place, spots = here_at(riding), ring_spots(riding)
    attended, refs = refs[0], refs[1:]
    ids = None
    if not riding:
        ids, refs = refs[0], refs[1:]
    pieces = refs[: len(layout)]
    decoded, found, mixed, scratch, asked, notes, arrived, noted = refs[len(layout) :]
    width = states.shape[1]
    depth = width // BANDS
    start = 3 * width // GROUPS // LANES * depth
    copies = start_loads(spots, pieces, layout, scratch, arrived, slice(start, start + depth))
    reads = []
    if riding:
        for piece, (at, core) in zip(pieces, layout):
            if core == 0:
                end = piece.shape[-2]
                reads.append(
                    pltpu.make_async_copy(
                        piece.at[0, end - SLOTS : end, :], notes.at[at], noted.at[at]
                    )
                )
                reads[-1].start()
    inputs = own_first(attended[...], place[1], depth)
    for at in range(GROUPS):
        wait_group(copies, at)
    for at in range(0, GROUPS, 2):
        columns = slice(at * LANES, (at + 2) * LANES)
        weight = [lanes_of(scratch[at + n], depth, 0, 1) for n in range(2)]
        total = dot(inputs, jnp.concatenate(weight, axis=1))
        mixed[:, columns] = (states[:, columns].astype(F32) + total).astype(BF16)
    for read in reads:
        read.wait()
    rows = chunked(layer_norm(mixed[...], gain[...]), depth)
    decoded[...] = rows
    found[...] = picked_rows(place, ids, spots if riding else None, rows, asked, notes)


def mix(states, attended, gain, ids, pieces, layout, shards):
    tok, width = states.shape
    more = [] if ids is None else [ids]
    return pl.pallas_call(
        functools.partial(mix_kernel, layout, ids is None),
        out_shape=(
            jax.ShapeDtypeStruct((tok, width), BF16),
            jax.ShapeDtypeStruct((shards * SLOTS, width), BF16),
        ),
        in_specs=[VMEM_SPEC] * (3 + len(more)) + [ANY] * len(pieces),
        out_specs=(VMEM_SPEC, VMEM_SPEC),
        scratch_shapes=[
            pltpu.VMEM((tok, width), BF16),
            pltpu.VMEM((GROUPS, 2, 2, width // BANDS, LANES), BF16),
            pltpu.VMEM((GROUPS * SLOTS, LANES), F32),
            pltpu.VMEM((GROUPS, SLOTS, LANES), BF16),
            pltpu.SemaphoreType.DMA((len(pieces),)),
            pltpu.SemaphoreType.DMA((GROUPS,)),
        ],
        compiler_params=params(),
        cost_estimate=SMALL,
        name="mix",
    )(states, gain, attended, *more, *pieces)


def keys_values_kernel(layout, riding, decoded, *refs):
    spots = ring_spots(riding)
    pieces = refs[: len(layout)]
    out, scratch, arrived = refs[len(layout) :]
    depth = decoded.shape[1] // BANDS
    per = scratch.shape[3] // depth
    copies = start_loads(
        spots, pieces, layout, scratch, arrived, slice(0, scratch.shape[3]), spots[GROUPS]
    )
    for at in range(GROUPS):
        wait_group(copies, at)
        spot = spots[at]
        total = dot(decoded[...], lanes_of(scratch[spot], depth, 0, per)).astype(BF16)
        for group in range(per):
            out[spot * per + group] = total[:, group * LANES : (group + 1) * LANES]


def keys_values(riding, decoded, pieces, layout):
    tok, width = decoded.shape
    height = 2 * width // GROUPS // LANES * (width // BANDS)
    return pl.pallas_call(
        functools.partial(keys_values_kernel, layout, riding),
        out_shape=jax.ShapeDtypeStruct((2 * width // LANES, tok, LANES), BF16),
        in_specs=[VMEM_SPEC] + [ANY] * len(pieces),
        out_specs=VMEM_SPEC,
        scratch_shapes=[
            pltpu.VMEM((GROUPS, 2, 2, height, LANES), BF16),
            pltpu.SemaphoreType.DMA((len(pieces),)),
        ],
        compiler_params=params(),
        cost_estimate=SMALL,
        name="keys_values",
    )(decoded, *pieces)


def decode_kernel(layout, each, riding, queries, local_rows, fetched, here, there, *refs):
    spots = ring_spots(riding)
    pieces = refs[: len(layout)]
    fields, scratch, table, arrived = refs[len(layout) :]
    points, width = queries.shape
    depth = width // BANDS
    count = fetched.shape[0]
    per = 2 * width // GROUPS // LANES
    kept = scratch.shape[3]
    copies = start_loads(
        spots, pieces, layout, scratch, arrived, slice(0, kept), spots[GROUPS]
    )
    padding = jnp.zeros((table.shape[1] - count, LANES), BF16)
    for at in range(GROUPS):
        wait_group(copies, at)
        spot = spots[at]
        total = dot(fetched[...], lanes_of(scratch[spot], depth, 0, per)).astype(BF16)
        for group in range(per):
            table[spot * per + group, :count, :] = total[:, group * LANES : (group + 1) * LANES]
            if table.shape[1] > count:
                table[spot * per + group, count:, :] = padding

    pairs = width // LANES
    scale = BF16(1.0 / math.sqrt(width // HEADS))
    times = jnp.concatenate([here[...], there[...]], axis=1)
    bias = jnp.where(times > 0, 0.0, NEG)
    both = jnp.concatenate([times, times], axis=0)
    rows = []
    for pair in range(pairs):
        rows.append(
            pair_attend(
                queries[:, pair * LANES : (pair + 1) * LANES] * scale,
                jnp.concatenate([local_rows[pair], table[pair]], axis=0),
                jnp.concatenate([local_rows[pairs + pair], table[pairs + pair]], axis=0),
                bias,
                lambda weights: weights * both,
            )
        )
    gridded = jnp.concatenate(rows, axis=1)
    start = per * depth
    halves = depth // LANES
    height = (kept - start) // halves
    padded = jnp.zeros((GROUPS * height, points), F32)
    for chunk, band in enumerate(CHUNKS):
        for half in range(halves):
            at = start + half * height
            weight = scratch[:, chunk // 2, chunk % 2, at : at + height, :]
            first = band * depth + half * LANES
            padded += dot_nt(
                weight.reshape(GROUPS * height, LANES), gridded[:, first : first + LANES]
            )
    parts = [padded[group * height : group * height + each] for group in range(GROUPS)]
    fields[...] = jnp.concatenate(parts, axis=0).astype(BF16)


def decode(riding, queries, local_rows, fetched, here, there, pieces, layout, outputs):
    points, width = queries.shape
    height = pieces[0].shape[-2]
    remote = there.shape[1]
    return pl.pallas_call(
        functools.partial(decode_kernel, layout, outputs // GROUPS, riding),
        out_shape=jax.ShapeDtypeStruct((outputs, points), BF16),
        in_specs=[VMEM_SPEC] * 5 + [ANY] * len(pieces),
        out_specs=VMEM_SPEC,
        scratch_shapes=[
            pltpu.VMEM((GROUPS, 2, 2, height, LANES), BF16),
            pltpu.VMEM((2 * width // LANES, remote, LANES), BF16),
            pltpu.SemaphoreType.DMA((len(pieces),)),
        ],
        compiler_params=params(),
        cost_estimate=SMALL,
        name="decode",
    )(queries, local_rows, fetched, here, there, *pieces)


def stacked(*weights):
    parts = []
    for weight in weights:
        for at in range(0, weight.shape[-1], LANES):
            parts.append(weight[..., at : at + LANES])
    return jnp.concatenate(parts, axis=-2)


def pair_x(block, gate=None):
    if gate is not None:
        block, _ = lax.optimization_barrier((block, gate))
    other = lax.ppermute(block, "band", [(i, i ^ 2) for i in range(BANDS)])
    low = lax.axis_index("band") < 2
    return jnp.stack([jnp.where(low, block, other), jnp.where(low, other, block)])


def pair_core(block):
    other = swap_core(block)
    low = lax.axis_index("band") % 2 == 0
    return jnp.stack([jnp.where(low, block, other), jnp.where(low, other, block)])


def carry(block):
    pairs = []
    for i in range(GROUPS):
        here, there = RING[i] * BANDS, RING[(i + 1) % GROUPS] * BANDS
        for x in range(2):
            pairs.append((here + 2 * x, there + 2 * x))
            pairs.append((there + 2 * x + 1, here + 2 * x + 1))
    return lax.ppermute(block, ("seq", "band"), pairs)


def swap_core(block):
    return lax.ppermute(block, "band", [(i, i ^ 1) for i in range(BANDS)])


def chain_step(chains, step, gate=None):
    if gate is not None:
        *chains, _ = lax.optimization_barrier((*chains, gate))
    chains = [carry(block) for block in chains]
    pieces = []
    for half, block in enumerate(chains):
        pieces.append((block, (step, half)))
        pieces.append((swap_core(block), (GROUPS - step, 1 - half)))
    return chains, pieces


def ring_step(block, step, gate=None):
    if gate is not None:
        block, _ = lax.optimization_barrier((block, gate))
    if step < GROUPS // 2:
        block = carry(block)
        return block, [(block, (step, None)), (swap_core(block), (GROUPS - step, None))]
    half = lax.dynamic_index_in_dim(block, lax.axis_index("band") % 2, 0, keepdims=False)
    half = carry(half)
    return half, [(half, (step, 0)), (swap_core(half), (step, 1))]


def whole_blocks(*weights):
    parts = []
    for weight, height in weights:
        weight = lax.all_gather(weight, "seq", axis=1, tiled=True)
        weight = lax.all_gather(weight, "band", axis=0, tiled=True)
        depth, columns = weight.shape[0] // BANDS, weight.shape[1] // GROUPS
        weight = weight.reshape(2, 2, depth, GROUPS, columns).transpose(3, 1, 0, 2, 4)
        if height:
            weight = jnp.pad(
                weight.swapaxes(-1, -2), ((0, 0),) * 3 + ((0, height - columns), (0, 0))
            )
        parts.append(weight)
    return stacked(*parts)


def local(
    tokens, ln_gain, w_qkv, w_out, dec_gain, w_kv, w_final, reach, grid_query, neighbours, counts
):
    states = tokens[0]
    tok, width = states.shape
    shards, bands = lax.axis_size("seq"), lax.axis_size("band")
    outputs = w_final.shape[1] * shards
    height = -(-outputs // GROUPS // 16) * 16
    riding = (shards, bands) == (GROUPS, BANDS)
    up = [(i, i + 1) for i in range(shards - 1)]
    down = [(i + 1, i) for i in range(shards - 1)]
    left = lax.ppermute(states[tok - HALF :], "seq", up)
    right = lax.ppermute(states[:HALF], "seq", down)
    slots = (neighbours.T, counts.reshape(1, -1))
    there, requested, *payload = tables(tok, *slots, shards, (w_qkv, w_out) if riding else ())
    normed, bias, here = prepare(
        tok * shards, riding, left, states, right, ln_gain.reshape(1, width),
        reach.reshape(1, tok), *slots,
    )
    if riding:
        mine = pair_x(payload[0])
        mine, _, _ = lax.optimization_barrier((mine, left, right))
        other = swap_core(mine)
        pieces = [(mine, (0, 0)), (other, (0, 1))]
        chains, more = chain_step([mine, other], 1)
        pieces += more
        final = jnp.pad(w_final.T, ((0, height - w_final.shape[1]), (0, 0)))
        second = pair_core(pair_x(stacked(w_kv, final), chains[0]))
        later = [(second, (0, None))]
        chains[1], _ = lax.optimization_barrier((chains[1], normed))
        chains, more = chain_step(chains, 2)
        pieces += more
        normed, _ = lax.optimization_barrier((normed, chains[1]))
        made = project(riding, normed, pieces[:6], None)
        chains, more = chain_step(chains, 3)
        pieces += more
        last, more = chain_step(chains[:1], 4, (chains[1], made))
        pieces += more
        second, *_ = lax.optimization_barrier((second, chains[1], made, pieces[7][0], pieces[9][0]))
        later = [(second, (0, None))]
        block, more = ring_step(second, 1)
        later += more
        block, more = ring_step(block, 2, [pieces[n][0] for n in (11, 13, 15)])
        later += more
        attended = attend(riding, normed, bias, pieces[6:], made, (0, 1, 7))
        block, more = ring_step(block, 3, attended)
        later += more
        ids = None
    else:
        block = whole_blocks((w_qkv, 0), (w_out, 0))
        block = jnp.pad(block, ((0, 0),) * 3 + ((0, SLOTS), (0, 0)))
        pieces = [(block[at, half], (at, half)) for at in range(GROUPS) for half in range(2)]
        block = whole_blocks((w_kv, 0), (w_final, height))
        later = [(block[at], (at, None)) for at in range(GROUPS)]
        made = project(riding, normed, pieces[:6], None)
        attended = attend(riding, normed, bias, pieces[6:], made, tuple(range(3)))
        ids = lax.all_to_all(
            requested.reshape(shards, SLOTS).astype(jnp.int32), "seq", 0, 0, tiled=True
        ).reshape(shards * SLOTS, 1)
    layout = tuple(at for _, at in pieces)
    pieces = [piece for piece, _ in pieces]
    decoded, found = mix(
        states, attended, dec_gain.reshape(1, width), ids, pieces, layout, shards
    )
    if riding:
        _, more = ring_step(block, 4, found)
        later += more
    fetched = lax.all_to_all(
        found.reshape(shards, SLOTS, width), "seq", split_axis=0, concat_axis=0, tiled=True
    )
    layout = tuple(at for _, at in later)
    pieces = [piece for piece, _ in later]
    local_rows = keys_values(riding, decoded, pieces, layout)
    fields = decode(
        riding, grid_query[0], local_rows, fetched.reshape(shards * SLOTS, width), here, there,
        pieces, layout, outputs,
    )
    return fields[None]


def solution(mesh):
    return jax.shard_map(
        local,
        mesh=mesh,
        in_specs=(
            P("band", "seq", None),
            P(),
            P("band", "seq"),
            P("band", "seq"),
            P(),
            P("band", "seq"),
            P("band", "seq"),
            P("seq"),
            P("band", "seq", None),
            P("seq", None),
            P("seq"),
        ),
        out_specs=P("band", None, "seq"),
        check_vma=False,
    )
```

```python
import functools
import math

import jax
import jax.numpy as jnp
import numpy as np
from jax import lax
from jax.experimental import pallas as pl
from jax.experimental.pallas import tpu as pltpu
from jax.sharding import PartitionSpec as P

HEADS = 16
HALF = 128
C = 12
SLOTS = 16
EPSILON = 1e-05
NEG = -1e30
LANES = 128
GROUPS = 8
BANDS = 4
CHUNKS = (0, 2, 1, 3)
RING = (0, 2, 4, 6, 7, 5, 3, 1)
VMEM = 60 * 1024 * 1024
SMALL = pl.CostEstimate(flops=1000, bytes_accessed=1000, transcendentals=0)
F32 = jnp.float32
BF16 = jnp.bfloat16


def dot(a, b):
    return jnp.dot(a, b, preferred_element_type=F32)


def dot_nt(a, b):
    return lax.dot_general(a, b, (((1,), (1,)), ((), ())), preferred_element_type=F32)


def layer_norm(values, gain):
    values = values.astype(F32)
    centred = values - jnp.mean(values, axis=-1, keepdims=True)
    spread = jnp.mean(centred * centred, axis=-1, keepdims=True)
    return (centred * lax.rsqrt(spread + EPSILON) * gain).astype(BF16)


def here_at(riding):
    return lax.axis_index("seq"), (lax.axis_index("band") % 2 if riding else 0)


def ring_spots(riding):
    if not riding:
        return list(range(GROUPS)) + [0]
    seq, core = here_at(True)
    at_ring = jnp.where(seq % 2 == 0, seq // 2, GROUPS - 1 - seq // 2)
    turn = jnp.where(core == 0, GROUPS - 1, 1)
    spots = []
    for at in range(GROUPS):
        step = (at_ring + turn * at) % GROUPS
        spots.append(jnp.where(step < GROUPS // 2, 2 * step, 2 * GROUPS - 1 - 2 * step))
    return spots + [core]


def params(**more):
    return pltpu.CompilerParams(vmem_limit_bytes=VMEM, **more)


def full_spec(shape):
    return pl.BlockSpec(shape, lambda *_: (0,) * len(shape))


def own_first(rows, core, depth):
    parts = [rows[:, b * depth : (b + 1) * depth] for b in range(BANDS)]
    order = ((0, 1), (2, 3), (1, 0), (3, 2))
    return jnp.concatenate([jnp.where(core == 0, parts[a], parts[b]) for a, b in order], axis=1)


def as_column(row):
    return jnp.broadcast_to(row, (8, row.shape[1])).T[:, :1]


def prepare_kernel(
    total, riding, left, own, right, gain, reach, neighbours, counts, normed, bias, multiplicity
):
    place = here_at(riding)
    tok = own.shape[0]
    depth = own.shape[1] // BANDS
    for at, part in ((0, left), (HALF, own), (HALF + tok, right)):
        rows = layer_norm(part[...], gain[...])
        normed[at : at + part.shape[0], :] = own_first(rows, place[1], depth)

    first = place[0] * tok
    span = 3 * HALF
    row = lax.broadcasted_iota(jnp.int32, (HALF, span), 0)
    col = lax.broadcasted_iota(jnp.int32, (HALF, span), 1)
    away = jnp.abs(row + HALF - col)
    limit = as_column(reach[...])
    for block in range(tok // HALF):
        key = first + (block - 1) * HALF + col
        allowed = (away <= limit[block * HALF : (block + 1) * HALF, :]) & (key >= 0) & (key < total)
        bias[block] = jnp.where(allowed, 0.0, NEG)

    ids = neighbours[...].T
    used = as_column(counts[...])
    mesh = lax.broadcasted_iota(jnp.int32, multiplicity.shape, 1) + first
    here = jnp.zeros(multiplicity.shape, F32)
    for slot in range(ids.shape[1]):
        here += ((ids[:, slot : slot + 1] == mesh) & (slot < used)).astype(F32)
    multiplicity[...] = here


def prepare(total, riding, left, own, right, gain, reach, neighbours, counts):
    tok, width = own.shape
    operands = (left, own, right, gain, reach, neighbours, counts)
    outs = (
        jax.ShapeDtypeStruct((tok + 2 * HALF, width), BF16),
        jax.ShapeDtypeStruct((tok // HALF, HALF, 3 * HALF), F32),
        jax.ShapeDtypeStruct((neighbours.shape[1], tok), F32),
    )
    return pl.pallas_call(
        functools.partial(prepare_kernel, total, riding),
        out_shape=outs,
        in_specs=[pl.BlockSpec(memory_space=pltpu.VMEM)] * len(operands),
        out_specs=[pl.BlockSpec(memory_space=pltpu.VMEM)] * len(outs),
        compiler_params=params(),
        cost_estimate=SMALL,
        name="prepare",
    )(*operands)


def tables_kernel(tok, count, neighbours, counts, low, rank, tri, *refs):
    weights, (multiplicity, requested) = refs[:count], refs[count : count + 2]
    first = lax.axis_index("seq") * tok
    slots = neighbours.shape[0]
    ids = neighbours[...].T
    used = as_column(counts[...])
    start = low[...]
    elsewhere = start != first
    hits = []
    for slot in range(slots):
        which = ids[:, slot : slot + 1]
        hits.append(
            ((which >= start) & (which < start + tok) & (slot < used) & elsewhere).astype(F32)
        )
    running = dot(tri[...], sum(hits).astype(BF16))
    order = rank[...]
    asked = jnp.zeros(hits[0].shape, F32)
    there = jnp.zeros(hits[0].shape, F32)
    for slot in range(slots):
        mine = jnp.where(running == order, hits[slot], 0.0)
        there += mine
        offset = (ids[:, slot : slot + 1] - start).astype(F32)
        asked += jnp.where(mine > 0, offset, 0.0)
        running += hits[slot]
    multiplicity[...] = there
    asked = jnp.sum(asked, axis=0, keepdims=True)
    requested[...] = asked.astype(BF16)
    if weights:
        payload = refs[-1]
        at = 0
        for weight in weights:
            depth, columns = weight.shape
            for first in range(0, columns, LANES):
                payload[at : at + depth, :] = weight[:, first : first + LANES]
                at += depth
        payload[at:, :] = jnp.broadcast_to(asked, (SLOTS, LANES)).astype(BF16)


def tables(tok, neighbours, counts, shards, weights):
    points = neighbours.shape[1]
    remote = shards * SLOTS
    column = np.arange(remote)
    low = (column // SLOTS * tok).astype(np.int32)[None]
    rank = (column % SLOTS).astype(np.float32)[None]
    tri = np.tril(np.ones((points, points), np.float32), -1).astype(BF16)
    operands = (neighbours, counts, low, rank, tri) + weights
    outs = (
        jax.ShapeDtypeStruct((points, remote), F32),
        jax.ShapeDtypeStruct((1, remote), BF16),
    )
    if weights:
        rows = sum(weight.shape[0] * weight.shape[1] // LANES for weight in weights) + SLOTS
        outs += (jax.ShapeDtypeStruct((rows, LANES), BF16),)
    return pl.pallas_call(
        functools.partial(tables_kernel, tok, len(weights)),
        out_shape=outs,
        in_specs=[pl.BlockSpec(memory_space=pltpu.VMEM)] * len(operands),
        out_specs=[pl.BlockSpec(memory_space=pltpu.VMEM)] * len(outs),
        compiler_params=params(),
        cost_estimate=SMALL,
        name="tables",
    )(*operands)


def pair_attend(queries, keys, values, bias, weights_of):
    rows = queries.shape[0]
    lane = lax.broadcasted_iota(jnp.int32, (rows, LANES), 1)
    first = lane < LANES // 2
    zero = jnp.zeros_like(queries)
    both = jnp.concatenate(
        [jnp.where(first, queries, zero), jnp.where(first, zero, queries)], axis=0
    )
    scores = dot_nt(both, keys)
    scores = scores + jnp.concatenate([bias, bias], axis=0)
    top = jnp.max(scores, axis=-1, keepdims=True)
    weights = weights_of(jnp.exp(scores - top)).astype(BF16)
    summed = dot(weights, jnp.concatenate([values, jnp.ones_like(values)], axis=1))
    share = summed[:, :LANES] / summed[:, LANES:]
    return jnp.where(first, share[:rows], share[rows:]).astype(BF16)


def start_loads(spots, pieces, layout, scratch, arrived, rows, core=None):
    copies = {}
    for n, (piece, (at, half)) in enumerate(zip(pieces, layout)):
        place = scratch.at[spots[at]]
        if half is None:
            copy = pltpu.make_async_copy(piece.at[:, :, rows, :], place, arrived.at[n])
        else:
            to = half if core is None else (1 - core if half else core)
            copy = pltpu.make_async_copy(piece.at[:, rows, :], place.at[to], arrived.at[n])
        copy.start()
        copies.setdefault(at, []).append(copy)
    return copies


def wait_group(copies, at):
    for copy in copies.get(at, ()):
        copy.wait()


def lanes_of(block, depth, start, count):
    rows = block.shape[0] * block.shape[1] * depth if block.ndim == 4 else block.shape[0] * depth
    columns = [
        block[..., start + g * depth : start + (g + 1) * depth, :].reshape(rows, LANES)
        for g in range(count)
    ]
    return columns[0] if count == 1 else jnp.concatenate(columns, axis=1)


SMEM = pl.BlockSpec(memory_space=pltpu.SMEM)
VMEM_SPEC = pl.BlockSpec(memory_space=pltpu.VMEM)
ANY = pl.BlockSpec(memory_space=pl.ANY)


def projection(normed, weight, depth, per):
    return dot(normed, lanes_of(weight[...], depth, 0, per)).astype(BF16)


def project_kernel(layout, riding, normed, *refs):
    spots = ring_spots(riding)
    pieces = refs[: len(layout)]
    out, scratch, made, arrived, sent = refs[-5:]
    per = made.shape[1]
    depth = normed.shape[1] // BANDS
    copies = start_loads(spots, pieces, layout, scratch, arrived, slice(0, per * depth))
    writes = []
    for n, at in enumerate(copies):
        wait_group(copies, at)
        total = projection(normed[...], scratch.at[spots[at]], depth, per)
        for group in range(per):
            made[n, group] = total[:, group * LANES : (group + 1) * LANES]
        writes.append(
            pltpu.make_async_copy(made.at[n], out.at[pl.ds(spots[at] * per, per)], sent.at[n])
        )
        writes[-1].start()
    for write in writes:
        write.wait()


def project(riding, normed, pieces, before):
    rows, width = normed.shape
    layout = tuple(place for _, place in pieces)
    arrays = [array for array, _ in pieces]
    per = 3 * width // LANES // GROUPS
    count = len({at for at, _ in layout})
    more = [] if before is None else [before]
    return pl.pallas_call(
        functools.partial(project_kernel, layout, riding),
        out_shape=jax.ShapeDtypeStruct((GROUPS * per, rows, LANES), BF16),
        in_specs=[VMEM_SPEC] + [ANY] * (len(arrays) + len(more)),
        out_specs=ANY,
        scratch_shapes=[
            pltpu.VMEM((GROUPS, 2, 2, per * width // BANDS, LANES), BF16),
            pltpu.VMEM((count, per, rows, LANES), BF16),
            pltpu.SemaphoreType.DMA((len(arrays),)),
            pltpu.SemaphoreType.DMA((count,)),
        ],
        input_output_aliases={1 + len(arrays): 0} if more else {},
        compiler_params=params(),
        cost_estimate=SMALL,
        name="project",
    )(normed, *arrays, *more)


def attend_kernel(layout, ready, riding, normed, bias, *refs):
    spots = ring_spots(riding)
    pieces = refs[: len(layout)]
    made, attended, scratch, projected, arrived, loaded = refs[len(layout) :]
    width = normed.shape[1]
    depth = width // BANDS
    per = projected.shape[0] // GROUPS
    copies = start_loads(spots, pieces, layout, scratch, arrived, slice(0, per * depth))
    reads = []
    for n, at in enumerate(ready):
        place = pl.ds(spots[at] * per, per)
        reads.append(pltpu.make_async_copy(made.at[place], projected.at[place], loaded.at[n]))
        reads[-1].start()
    for at in copies:
        wait_group(copies, at)
        total = projection(normed[...], scratch.at[spots[at]], depth, per)
        for group in range(per):
            projected[spots[at] * per + group] = total[:, group * LANES : (group + 1) * LANES]
    for read in reads:
        read.wait()
    pairs = width // LANES
    scale = BF16(1.0 / math.sqrt(width // HEADS))
    for pair in range(pairs):
        for block in range(bias.shape[0]):
            at = block * HALF
            attended[at : at + HALF, pair * LANES : (pair + 1) * LANES] = pair_attend(
                projected[pair, at + HALF : at + 2 * HALF, :] * scale,
                projected[pairs + pair, at : at + 3 * HALF, :],
                projected[2 * pairs + pair, at : at + 3 * HALF, :],
                bias[block],
                lambda weights: weights,
            )


def attend(riding, normed, bias, pieces, made, ready):
    rows, width = normed.shape
    tok = rows - 2 * HALF
    layout = tuple(place for _, place in pieces)
    arrays = [array for array, _ in pieces]
    per = made.shape[0] // GROUPS
    return pl.pallas_call(
        functools.partial(attend_kernel, layout, ready, riding),
        out_shape=jax.ShapeDtypeStruct((tok, width), BF16),
        in_specs=[VMEM_SPEC, VMEM_SPEC] + [ANY] * (len(arrays) + 1),
        out_specs=VMEM_SPEC,
        scratch_shapes=[
            pltpu.VMEM((GROUPS, 2, 2, per * width // BANDS, LANES), BF16),
            pltpu.VMEM(made.shape, BF16),
            pltpu.SemaphoreType.DMA((len(arrays),)),
            pltpu.SemaphoreType.DMA((len(ready),)),
        ],
        compiler_params=params(),
        cost_estimate=SMALL,
        name="attend",
    )(normed, bias, *arrays, made)


def picked_rows(place, ids, spots, rows, asked, arrived):
    tok = rows.shape[0]
    if spots is None:
        which = ids[...]
    else:
        for at in range(GROUPS):
            asked[pl.ds(spots[at] * SLOTS, SLOTS), :] = jnp.broadcast_to(
                arrived[at, 0:1, :].astype(F32), (SLOTS, LANES)
            )
        count = GROUPS * SLOTS
        lane = lax.broadcasted_iota(jnp.int32, (count, LANES), 1)
        slot = lax.broadcasted_iota(jnp.int32, (count, LANES), 0) % SLOTS
        mine = jnp.where(lane == place[0] * SLOTS + slot, asked[...], 0.0)
        which = jnp.sum(mine, axis=1, keepdims=True).astype(jnp.int32)
    here = lax.broadcasted_iota(jnp.int32, (which.shape[0], tok), 1)
    return dot((which == here).astype(BF16), rows).astype(BF16)


def chunked(values, depth):
    return jnp.concatenate([values[:, b * depth : (b + 1) * depth] for b in CHUNKS], axis=1)


def mix_kernel(layout, riding, states, gain, *refs):
    place, spots = here_at(riding), ring_spots(riding)
    attended, refs = refs[0], refs[1:]
    ids = None
    if not riding:
        ids, refs = refs[0], refs[1:]
    pieces = refs[: len(layout)]
    decoded, found, mixed, scratch, asked, notes, arrived, noted = refs[len(layout) :]
    width = states.shape[1]
    depth = width // BANDS
    start = 3 * width // GROUPS // LANES * depth
    copies = start_loads(spots, pieces, layout, scratch, arrived, slice(start, start + depth))
    reads = []
    if riding:
        for piece, (at, core) in zip(pieces, layout):
            if core == 0:
                end = piece.shape[-2]
                reads.append(
                    pltpu.make_async_copy(
                        piece.at[0, end - SLOTS : end, :], notes.at[at], noted.at[at]
                    )
                )
                reads[-1].start()
    inputs = own_first(attended[...], place[1], depth)
    for at in range(GROUPS):
        wait_group(copies, at)
    for at in range(0, GROUPS, 2):
        columns = slice(at * LANES, (at + 2) * LANES)
        weight = [lanes_of(scratch[at + n], depth, 0, 1) for n in range(2)]
        total = dot(inputs, jnp.concatenate(weight, axis=1))
        mixed[:, columns] = (states[:, columns].astype(F32) + total).astype(BF16)
    for read in reads:
        read.wait()
    rows = chunked(layer_norm(mixed[...], gain[...]), depth)
    decoded[...] = rows
    found[...] = picked_rows(place, ids, spots if riding else None, rows, asked, notes)


def mix(states, attended, gain, ids, pieces, layout, shards):
    tok, width = states.shape
    more = [] if ids is None else [ids]
    return pl.pallas_call(
        functools.partial(mix_kernel, layout, ids is None),
        out_shape=(
            jax.ShapeDtypeStruct((tok, width), BF16),
            jax.ShapeDtypeStruct((shards * SLOTS, width), BF16),
        ),
        in_specs=[VMEM_SPEC] * (3 + len(more)) + [ANY] * len(pieces),
        out_specs=(VMEM_SPEC, VMEM_SPEC),
        scratch_shapes=[
            pltpu.VMEM((tok, width), BF16),
            pltpu.VMEM((GROUPS, 2, 2, width // BANDS, LANES), BF16),
            pltpu.VMEM((GROUPS * SLOTS, LANES), F32),
            pltpu.VMEM((GROUPS, SLOTS, LANES), BF16),
            pltpu.SemaphoreType.DMA((len(pieces),)),
            pltpu.SemaphoreType.DMA((GROUPS,)),
        ],
        compiler_params=params(),
        cost_estimate=SMALL,
        name="mix",
    )(states, gain, attended, *more, *pieces)


def decode_kernel(layout, each, riding, queries, decoded, fetched, here, there, *refs):
    spots = ring_spots(riding)
    pieces = refs[: len(layout)]
    fields, scratch, table, arrived = refs[len(layout) :]
    points, width = queries.shape
    depth = width // BANDS
    per = 2 * width // GROUPS // LANES
    kept = scratch.shape[3]
    copies = start_loads(
        spots, pieces, layout, scratch, arrived, slice(0, kept), spots[GROUPS]
    )
    inputs = jnp.concatenate([decoded[...], fetched[...]], axis=0)
    for at in range(GROUPS):
        wait_group(copies, at)
        spot = spots[at]
        total = dot(inputs, lanes_of(scratch[spot], depth, 0, per)).astype(BF16)
        for group in range(per):
            table[spot * per + group] = total[:, group * LANES : (group + 1) * LANES]

    pairs = width // LANES
    scale = BF16(1.0 / math.sqrt(width // HEADS))
    times = jnp.concatenate([here[...], there[...]], axis=1)
    bias = jnp.where(times > 0, 0.0, NEG)
    both = jnp.concatenate([times, times], axis=0)
    rows = []
    for pair in range(pairs):
        rows.append(
            pair_attend(
                queries[:, pair * LANES : (pair + 1) * LANES] * scale,
                table[pair],
                table[pairs + pair],
                bias,
                lambda weights: weights * both,
            )
        )
    gridded = jnp.concatenate(rows, axis=1)
    start = per * depth
    halves = depth // LANES
    height = (kept - start) // halves
    padded = jnp.zeros((GROUPS * height, points), F32)
    for chunk, band in enumerate(CHUNKS):
        for half in range(halves):
            at = start + half * height
            weight = scratch[:, chunk // 2, chunk % 2, at : at + height, :]
            first = band * depth + half * LANES
            padded += dot_nt(
                weight.reshape(GROUPS * height, LANES), gridded[:, first : first + LANES]
            )
    parts = [padded[group * height : group * height + each] for group in range(GROUPS)]
    fields[...] = jnp.concatenate(parts, axis=0).astype(BF16)


def decode(riding, queries, decoded, fetched, here, there, pieces, layout, outputs):
    points, width = queries.shape
    height = pieces[0].shape[-2]
    rows = decoded.shape[0] + fetched.shape[0]
    return pl.pallas_call(
        functools.partial(decode_kernel, layout, outputs // GROUPS, riding),
        out_shape=jax.ShapeDtypeStruct((outputs, points), BF16),
        in_specs=[VMEM_SPEC] * 5 + [ANY] * len(pieces),
        out_specs=VMEM_SPEC,
        scratch_shapes=[
            pltpu.VMEM((GROUPS, 2, 2, height, LANES), BF16),
            pltpu.VMEM((2 * width // LANES, rows, LANES), BF16),
            pltpu.SemaphoreType.DMA((len(pieces),)),
        ],
        compiler_params=params(),
        cost_estimate=SMALL,
        name="decode",
    )(queries, decoded, fetched, here, there, *pieces)


def stacked(*weights):
    parts = []
    for weight in weights:
        for at in range(0, weight.shape[-1], LANES):
            parts.append(weight[..., at : at + LANES])
    return jnp.concatenate(parts, axis=-2)


def pair_x(block, gate=None):
    if gate is not None:
        block, _ = lax.optimization_barrier((block, gate))
    other = lax.ppermute(block, "band", [(i, i ^ 2) for i in range(BANDS)])
    low = lax.axis_index("band") < 2
    return jnp.stack([jnp.where(low, block, other), jnp.where(low, other, block)])


def pair_core(block):
    other = swap_core(block)
    low = lax.axis_index("band") % 2 == 0
    return jnp.stack([jnp.where(low, block, other), jnp.where(low, other, block)])


def carry(block):
    pairs = []
    for i in range(GROUPS):
        here, there = RING[i] * BANDS, RING[(i + 1) % GROUPS] * BANDS
        for x in range(2):
            pairs.append((here + 2 * x, there + 2 * x))
            pairs.append((there + 2 * x + 1, here + 2 * x + 1))
    return lax.ppermute(block, ("seq", "band"), pairs)


def swap_core(block):
    return lax.ppermute(block, "band", [(i, i ^ 1) for i in range(BANDS)])


def chain_step(chains, step, gate=None):
    if gate is not None:
        *chains, _ = lax.optimization_barrier((*chains, gate))
    chains = [carry(block) for block in chains]
    pieces = []
    for half, block in enumerate(chains):
        pieces.append((block, (step, half)))
        pieces.append((swap_core(block), (GROUPS - step, 1 - half)))
    return chains, pieces


def ring_step(block, step, gate=None):
    if gate is not None:
        block, _ = lax.optimization_barrier((block, gate))
    block = carry(block)
    return block, [(block, (step, None)), (swap_core(block), (GROUPS - step, None))]


def last_step(block, gate):
    half = lax.dynamic_index_in_dim(block, lax.axis_index("band") % 2, 0, keepdims=False)
    half = carry(half)
    handed, _ = lax.optimization_barrier((half, gate))
    return [(half, (GROUPS // 2, 0)), (swap_core(handed), (GROUPS // 2, 1))]


def whole_blocks(*weights):
    parts = []
    for weight, height in weights:
        weight = lax.all_gather(weight, "seq", axis=1, tiled=True)
        weight = lax.all_gather(weight, "band", axis=0, tiled=True)
        depth, columns = weight.shape[0] // BANDS, weight.shape[1] // GROUPS
        weight = weight.reshape(2, 2, depth, GROUPS, columns).transpose(3, 1, 0, 2, 4)
        if height:
            weight = jnp.pad(
                weight.swapaxes(-1, -2), ((0, 0),) * 3 + ((0, height - columns), (0, 0))
            )
        parts.append(weight)
    return stacked(*parts)


def local(
    tokens, ln_gain, w_qkv, w_out, dec_gain, w_kv, w_final, reach, grid_query, neighbours, counts
):
    states = tokens[0]
    tok, width = states.shape
    shards, bands = lax.axis_size("seq"), lax.axis_size("band")
    outputs = w_final.shape[1] * shards
    height = -(-outputs // GROUPS // 16) * 16
    riding = (shards, bands) == (GROUPS, BANDS)
    up = [(i, i + 1) for i in range(shards - 1)]
    down = [(i + 1, i) for i in range(shards - 1)]
    left = lax.ppermute(states[tok - HALF :], "seq", up)
    right = lax.ppermute(states[:HALF], "seq", down)
    slots = (neighbours.T, counts.reshape(1, -1))
    there, requested, *payload = tables(tok, *slots, shards, (w_qkv, w_out) if riding else ())
    normed, bias, here = prepare(
        tok * shards, riding, left, states, right, ln_gain.reshape(1, width),
        reach.reshape(1, tok), *slots,
    )
    if riding:
        mine = pair_x(payload[0])
        mine, _, _ = lax.optimization_barrier((mine, left, right))
        other = swap_core(mine)
        pieces = [(mine, (0, 0)), (other, (0, 1))]
        chains, more = chain_step([mine, other], 1)
        pieces += more
        final = jnp.pad(w_final.T, ((0, height - w_final.shape[1]), (0, 0)))
        second = pair_core(pair_x(stacked(w_kv, final), chains[0]))
        later = [(second, (0, None))]
        chains[1], _ = lax.optimization_barrier((chains[1], normed))
        chains, more = chain_step(chains, 2)
        pieces += more
        normed, _ = lax.optimization_barrier((normed, chains[1]))
        made = project(riding, normed, pieces[:6], None)
        chains, more = chain_step(chains, 3)
        pieces += more
        last, more = chain_step(chains[:1], 4, (chains[1], made))
        pieces += more
        second, *_ = lax.optimization_barrier((second, chains[1], made, pieces[7][0], pieces[9][0]))
        later = [(second, (0, None))]
        block, more = ring_step(second, 1)
        later += more
        attended = attend(riding, normed, bias, pieces[6:], made, (0, 1, 7))
        block, more = ring_step(block, 2, attended)
        later += more
        ids = None
    else:
        block = whole_blocks((w_qkv, 0), (w_out, 0))
        block = jnp.pad(block, ((0, 0),) * 3 + ((0, SLOTS), (0, 0)))
        pieces = [(block[at, half], (at, half)) for at in range(GROUPS) for half in range(2)]
        block = whole_blocks((w_kv, 0), (w_final, height))
        later = [(block[at], (at, None)) for at in range(GROUPS)]
        made = project(riding, normed, pieces[:6], None)
        attended = attend(riding, normed, bias, pieces[6:], made, tuple(range(3)))
        ids = lax.all_to_all(
            requested.reshape(shards, SLOTS).astype(jnp.int32), "seq", 0, 0, tiled=True
        ).reshape(shards * SLOTS, 1)
    layout = tuple(at for _, at in pieces)
    pieces = [piece for piece, _ in pieces]
    decoded, found = mix(
        states, attended, dec_gain.reshape(1, width), ids, pieces, layout, shards
    )
    fetched = lax.all_to_all(
        found.reshape(shards, SLOTS, width), "seq", split_axis=0, concat_axis=0, tiled=True
    )
    if riding:
        block, more = ring_step(block, 3, found)
        later += more + last_step(block, fetched)
    layout = tuple(at for _, at in later)
    pieces = [piece for piece, _ in later]
    fields = decode(
        riding, grid_query[0], decoded, fetched.reshape(shards * SLOTS, width), here, there,
        pieces, layout, outputs,
    )
    return fields[None]


def solution(mesh):
    return jax.shard_map(
        local,
        mesh=mesh,
        in_specs=(
            P("band", "seq", None),
            P(),
            P("band", "seq"),
            P("band", "seq"),
            P(),
            P("band", "seq"),
            P("band", "seq"),
            P("seq"),
            P("band", "seq", None),
            P("seq", None),
            P("seq"),
        ),
        out_specs=P("band", None, "seq"),
        check_vma=False,
    )
```

```python
import functools
import math

import jax
import jax.numpy as jnp
import numpy as np
from jax import lax
from jax.experimental import pallas as pl
from jax.experimental.pallas import tpu as pltpu
from jax.sharding import PartitionSpec as P

HEADS = 16
HALF = 128
C = 12
SLOTS = 16
EPSILON = 1e-05
NEG = -1e30
LANES = 128
GROUPS = 8
BANDS = 4
CHUNKS = (0, 2, 1, 3)
RING = (0, 2, 4, 6, 7, 5, 3, 1)
VMEM = 60 * 1024 * 1024
SMALL = pl.CostEstimate(flops=1000, bytes_accessed=1000, transcendentals=0)
F32 = jnp.float32
BF16 = jnp.bfloat16


def dot(a, b):
    return jnp.dot(a, b, preferred_element_type=F32)


def dot_nt(a, b):
    return lax.dot_general(a, b, (((1,), (1,)), ((), ())), preferred_element_type=F32)


def layer_norm(values, gain):
    values = values.astype(F32)
    centred = values - jnp.mean(values, axis=-1, keepdims=True)
    spread = jnp.mean(centred * centred, axis=-1, keepdims=True)
    return (centred * lax.rsqrt(spread + EPSILON) * gain).astype(BF16)


def here_at(riding):
    return lax.axis_index("seq"), (lax.axis_index("band") % 2 if riding else 0)


def ring_spots(riding):
    if not riding:
        return list(range(GROUPS)) + [0]
    seq, core = here_at(True)
    at_ring = jnp.where(seq % 2 == 0, seq // 2, GROUPS - 1 - seq // 2)
    turn = jnp.where(core == 0, GROUPS - 1, 1)
    spots = []
    for at in range(GROUPS):
        step = (at_ring + turn * at) % GROUPS
        spots.append(jnp.where(step < GROUPS // 2, 2 * step, 2 * GROUPS - 1 - 2 * step))
    return spots + [core]


def params(**more):
    return pltpu.CompilerParams(vmem_limit_bytes=VMEM, **more)


def full_spec(shape):
    return pl.BlockSpec(shape, lambda *_: (0,) * len(shape))


def own_first(rows, core, depth):
    parts = [rows[:, b * depth : (b + 1) * depth] for b in range(BANDS)]
    order = ((0, 1), (2, 3), (1, 0), (3, 2))
    return jnp.concatenate([jnp.where(core == 0, parts[a], parts[b]) for a, b in order], axis=1)


def as_column(row):
    return jnp.broadcast_to(row, (8, row.shape[1])).T[:, :1]


def prepare_kernel(
    total, riding, left, own, right, gain, reach, neighbours, counts, normed, bias, multiplicity
):
    place = here_at(riding)
    tok = own.shape[0]
    depth = own.shape[1] // BANDS
    for at, part in ((0, left), (HALF, own), (HALF + tok, right)):
        rows = layer_norm(part[...], gain[...])
        normed[at : at + part.shape[0], :] = own_first(rows, place[1], depth)

    first = place[0] * tok
    span = 3 * HALF
    row = lax.broadcasted_iota(jnp.int32, (HALF, span), 0)
    col = lax.broadcasted_iota(jnp.int32, (HALF, span), 1)
    away = jnp.abs(row + HALF - col)
    limit = as_column(reach[...])
    for block in range(tok // HALF):
        key = first + (block - 1) * HALF + col
        allowed = (away <= limit[block * HALF : (block + 1) * HALF, :]) & (key >= 0) & (key < total)
        bias[block] = jnp.where(allowed, 0.0, NEG)

    ids = neighbours[...].T
    used = as_column(counts[...])
    mesh = lax.broadcasted_iota(jnp.int32, multiplicity.shape, 1) + first
    here = jnp.zeros(multiplicity.shape, F32)
    for slot in range(ids.shape[1]):
        here += ((ids[:, slot : slot + 1] == mesh) & (slot < used)).astype(F32)
    multiplicity[...] = here


def prepare(total, riding, left, own, right, gain, reach, neighbours, counts):
    tok, width = own.shape
    operands = (left, own, right, gain, reach, neighbours, counts)
    outs = (
        jax.ShapeDtypeStruct((tok + 2 * HALF, width), BF16),
        jax.ShapeDtypeStruct((tok // HALF, HALF, 3 * HALF), F32),
        jax.ShapeDtypeStruct((neighbours.shape[1], tok), F32),
    )
    return pl.pallas_call(
        functools.partial(prepare_kernel, total, riding),
        out_shape=outs,
        in_specs=[pl.BlockSpec(memory_space=pltpu.VMEM)] * len(operands),
        out_specs=[pl.BlockSpec(memory_space=pltpu.VMEM)] * len(outs),
        compiler_params=params(),
        cost_estimate=SMALL,
        name="prepare",
    )(*operands)


def tables_kernel(tok, count, neighbours, counts, low, rank, tri, *refs):
    weights, (multiplicity, requested) = refs[:count], refs[count : count + 2]
    first = lax.axis_index("seq") * tok
    slots = neighbours.shape[0]
    ids = neighbours[...].T
    used = as_column(counts[...])
    start = low[...]
    elsewhere = start != first
    hits = []
    for slot in range(slots):
        which = ids[:, slot : slot + 1]
        hits.append(
            ((which >= start) & (which < start + tok) & (slot < used) & elsewhere).astype(F32)
        )
    running = dot(tri[...], sum(hits).astype(BF16))
    order = rank[...]
    asked = jnp.zeros(hits[0].shape, F32)
    there = jnp.zeros(hits[0].shape, F32)
    for slot in range(slots):
        mine = jnp.where(running == order, hits[slot], 0.0)
        there += mine
        offset = (ids[:, slot : slot + 1] - start).astype(F32)
        asked += jnp.where(mine > 0, offset, 0.0)
        running += hits[slot]
    multiplicity[...] = there
    asked = jnp.sum(asked, axis=0, keepdims=True)
    requested[...] = asked.astype(BF16)
    if weights:
        payload = refs[-1]
        at = 0
        for weight in weights:
            depth, columns = weight.shape
            for first in range(0, columns, LANES):
                payload[at : at + depth, :] = weight[:, first : first + LANES]
                at += depth
        payload[at:, :] = jnp.broadcast_to(asked, (SLOTS, LANES)).astype(BF16)


def tables(tok, neighbours, counts, shards, weights):
    points = neighbours.shape[1]
    remote = shards * SLOTS
    column = np.arange(remote)
    low = (column // SLOTS * tok).astype(np.int32)[None]
    rank = (column % SLOTS).astype(np.float32)[None]
    tri = np.tril(np.ones((points, points), np.float32), -1).astype(BF16)
    operands = (neighbours, counts, low, rank, tri) + weights
    outs = (
        jax.ShapeDtypeStruct((points, remote), F32),
        jax.ShapeDtypeStruct((1, remote), BF16),
    )
    if weights:
        rows = sum(weight.shape[0] * weight.shape[1] // LANES for weight in weights) + SLOTS
        outs += (jax.ShapeDtypeStruct((rows, LANES), BF16),)
    return pl.pallas_call(
        functools.partial(tables_kernel, tok, len(weights)),
        out_shape=outs,
        in_specs=[pl.BlockSpec(memory_space=pltpu.VMEM)] * len(operands),
        out_specs=[pl.BlockSpec(memory_space=pltpu.VMEM)] * len(outs),
        compiler_params=params(),
        cost_estimate=SMALL,
        name="tables",
    )(*operands)


def pair_attend(queries, keys, values, bias, weights_of):
    rows = queries.shape[0]
    lane = lax.broadcasted_iota(jnp.int32, (rows, LANES), 1)
    first = lane < LANES // 2
    zero = jnp.zeros_like(queries)
    both = jnp.concatenate(
        [jnp.where(first, queries, zero), jnp.where(first, zero, queries)], axis=0
    )
    scores = dot_nt(both, keys)
    scores = scores + jnp.concatenate([bias, bias], axis=0)
    top = jnp.max(scores, axis=-1, keepdims=True)
    weights = weights_of(jnp.exp(scores - top)).astype(BF16)
    summed = dot(weights, jnp.concatenate([values, jnp.ones_like(values)], axis=1))
    share = summed[:, :LANES] / summed[:, LANES:]
    return jnp.where(first, share[:rows], share[rows:]).astype(BF16)


def start_loads(spots, pieces, layout, scratch, arrived, rows, core=None):
    copies = {}
    for n, (piece, (at, half)) in enumerate(zip(pieces, layout)):
        place = scratch.at[spots[at]]
        if half is None:
            copy = pltpu.make_async_copy(piece.at[:, :, rows, :], place, arrived.at[n])
        else:
            to = half if core is None else (1 - core if half else core)
            copy = pltpu.make_async_copy(piece.at[:, rows, :], place.at[to], arrived.at[n])
        copy.start()
        copies.setdefault(at, []).append(copy)
    return copies


def wait_group(copies, at):
    for copy in copies.get(at, ()):
        copy.wait()


def lanes_of(block, depth, start, count):
    rows = block.shape[0] * block.shape[1] * depth if block.ndim == 4 else block.shape[0] * depth
    columns = [
        block[..., start + g * depth : start + (g + 1) * depth, :].reshape(rows, LANES)
        for g in range(count)
    ]
    return columns[0] if count == 1 else jnp.concatenate(columns, axis=1)


SMEM = pl.BlockSpec(memory_space=pltpu.SMEM)
VMEM_SPEC = pl.BlockSpec(memory_space=pltpu.VMEM)
ANY = pl.BlockSpec(memory_space=pl.ANY)


def projection(normed, weight, depth, per):
    return dot(normed, lanes_of(weight[...], depth, 0, per)).astype(BF16)


def project_kernel(layout, riding, normed, *refs):
    spots = ring_spots(riding)
    pieces = refs[: len(layout)]
    out, scratch, made, arrived, sent = refs[-5:]
    per = made.shape[1]
    depth = normed.shape[1] // BANDS
    copies = start_loads(spots, pieces, layout, scratch, arrived, slice(0, per * depth))
    writes = []
    for n, at in enumerate(copies):
        wait_group(copies, at)
        total = projection(normed[...], scratch.at[spots[at]], depth, per)
        for group in range(per):
            made[n, group] = total[:, group * LANES : (group + 1) * LANES]
        writes.append(
            pltpu.make_async_copy(made.at[n], out.at[pl.ds(spots[at] * per, per)], sent.at[n])
        )
        writes[-1].start()
    for write in writes:
        write.wait()


def project(riding, normed, pieces, before):
    rows, width = normed.shape
    layout = tuple(place for _, place in pieces)
    arrays = [array for array, _ in pieces]
    per = 3 * width // LANES // GROUPS
    count = len({at for at, _ in layout})
    more = [] if before is None else [before]
    return pl.pallas_call(
        functools.partial(project_kernel, layout, riding),
        out_shape=jax.ShapeDtypeStruct((GROUPS * per, rows, LANES), BF16),
        in_specs=[VMEM_SPEC] + [ANY] * (len(arrays) + len(more)),
        out_specs=ANY,
        scratch_shapes=[
            pltpu.VMEM((GROUPS, 2, 2, per * width // BANDS, LANES), BF16),
            pltpu.VMEM((count, per, rows, LANES), BF16),
            pltpu.SemaphoreType.DMA((len(arrays),)),
            pltpu.SemaphoreType.DMA((count,)),
        ],
        input_output_aliases={1 + len(arrays): 0} if more else {},
        compiler_params=params(),
        cost_estimate=SMALL,
        name="project",
    )(normed, *arrays, *more)


def attend_kernel(layout, ready, riding, normed, bias, *refs):
    spots = ring_spots(riding)
    pieces = refs[: len(layout)]
    made, attended, scratch, projected, arrived, loaded = refs[len(layout) :]
    width = normed.shape[1]
    depth = width // BANDS
    per = projected.shape[0] // GROUPS
    copies = start_loads(spots, pieces, layout, scratch, arrived, slice(0, per * depth))
    reads = []
    for n, at in enumerate(ready):
        place = pl.ds(spots[at] * per, per)
        reads.append(pltpu.make_async_copy(made.at[place], projected.at[place], loaded.at[n]))
        reads[-1].start()
    for at in copies:
        wait_group(copies, at)
        total = projection(normed[...], scratch.at[spots[at]], depth, per)
        for group in range(per):
            projected[spots[at] * per + group] = total[:, group * LANES : (group + 1) * LANES]
    for read in reads:
        read.wait()
    pairs = width // LANES
    scale = BF16(1.0 / math.sqrt(width // HEADS))
    for pair in range(pairs):
        for block in range(bias.shape[0]):
            at = block * HALF
            attended[at : at + HALF, pair * LANES : (pair + 1) * LANES] = pair_attend(
                projected[pair, at + HALF : at + 2 * HALF, :] * scale,
                projected[pairs + pair, at : at + 3 * HALF, :],
                projected[2 * pairs + pair, at : at + 3 * HALF, :],
                bias[block],
                lambda weights: weights,
            )


def attend(riding, normed, bias, pieces, made, ready):
    rows, width = normed.shape
    tok = rows - 2 * HALF
    layout = tuple(place for _, place in pieces)
    arrays = [array for array, _ in pieces]
    per = made.shape[0] // GROUPS
    return pl.pallas_call(
        functools.partial(attend_kernel, layout, ready, riding),
        out_shape=jax.ShapeDtypeStruct((tok, width), BF16),
        in_specs=[VMEM_SPEC, VMEM_SPEC] + [ANY] * (len(arrays) + 1),
        out_specs=VMEM_SPEC,
        scratch_shapes=[
            pltpu.VMEM((GROUPS, 2, 2, per * width // BANDS, LANES), BF16),
            pltpu.VMEM(made.shape, BF16),
            pltpu.SemaphoreType.DMA((len(arrays),)),
            pltpu.SemaphoreType.DMA((len(ready),)),
        ],
        compiler_params=params(),
        cost_estimate=SMALL,
        name="attend",
    )(normed, bias, *arrays, made)


def picked_rows(place, ids, spots, rows, asked, arrived):
    tok = rows.shape[0]
    if spots is None:
        which = ids[...]
    else:
        for at in range(GROUPS):
            asked[pl.ds(spots[at] * SLOTS, SLOTS), :] = jnp.broadcast_to(
                arrived[at, 0:1, :].astype(F32), (SLOTS, LANES)
            )
        count = GROUPS * SLOTS
        lane = lax.broadcasted_iota(jnp.int32, (count, LANES), 1)
        slot = lax.broadcasted_iota(jnp.int32, (count, LANES), 0) % SLOTS
        mine = jnp.where(lane == place[0] * SLOTS + slot, asked[...], 0.0)
        which = jnp.sum(mine, axis=1, keepdims=True).astype(jnp.int32)
    here = lax.broadcasted_iota(jnp.int32, (which.shape[0], tok), 1)
    return dot((which == here).astype(BF16), rows).astype(BF16)


def chunked(values, depth):
    return jnp.concatenate([values[:, b * depth : (b + 1) * depth] for b in CHUNKS], axis=1)


def mix_kernel(layout, riding, states, gain, *refs):
    place, spots = here_at(riding), ring_spots(riding)
    attended, refs = refs[0], refs[1:]
    ids = None
    if not riding:
        ids, refs = refs[0], refs[1:]
    pieces = refs[: len(layout)]
    decoded, found, mixed, scratch, asked, notes, arrived, noted = refs[len(layout) :]
    width = states.shape[1]
    depth = width // BANDS
    start = 3 * width // GROUPS // LANES * depth
    copies = start_loads(spots, pieces, layout, scratch, arrived, slice(start, start + depth))
    reads = []
    if riding:
        for piece, (at, core) in zip(pieces, layout):
            if core == 0:
                end = piece.shape[-2]
                reads.append(
                    pltpu.make_async_copy(
                        piece.at[0, end - SLOTS : end, :], notes.at[at], noted.at[at]
                    )
                )
                reads[-1].start()
    inputs = own_first(attended[...], place[1], depth)
    for at in range(GROUPS):
        wait_group(copies, at)
    for at in range(0, GROUPS, 2):
        columns = slice(at * LANES, (at + 2) * LANES)
        weight = [lanes_of(scratch[at + n], depth, 0, 1) for n in range(2)]
        total = dot(inputs, jnp.concatenate(weight, axis=1))
        mixed[:, columns] = (states[:, columns].astype(F32) + total).astype(BF16)
    for read in reads:
        read.wait()
    rows = chunked(layer_norm(mixed[...], gain[...]), depth)
    decoded[...] = rows
    found[...] = picked_rows(place, ids, spots if riding else None, rows, asked, notes)


def mix(states, attended, gain, ids, pieces, layout, shards):
    tok, width = states.shape
    more = [] if ids is None else [ids]
    return pl.pallas_call(
        functools.partial(mix_kernel, layout, ids is None),
        out_shape=(
            jax.ShapeDtypeStruct((tok, width), BF16),
            jax.ShapeDtypeStruct((shards * SLOTS, width), BF16),
        ),
        in_specs=[VMEM_SPEC] * (3 + len(more)) + [ANY] * len(pieces),
        out_specs=(VMEM_SPEC, VMEM_SPEC),
        scratch_shapes=[
            pltpu.VMEM((tok, width), BF16),
            pltpu.VMEM((GROUPS, 2, 2, width // BANDS, LANES), BF16),
            pltpu.VMEM((GROUPS * SLOTS, LANES), F32),
            pltpu.VMEM((GROUPS, SLOTS, LANES), BF16),
            pltpu.SemaphoreType.DMA((len(pieces),)),
            pltpu.SemaphoreType.DMA((GROUPS,)),
        ],
        compiler_params=params(),
        cost_estimate=SMALL,
        name="mix",
    )(states, gain, attended, *more, *pieces)


def decode_kernel(layout, each, riding, queries, decoded, fetched, here, there, *refs):
    spots = ring_spots(riding)
    pieces = refs[: len(layout)]
    fields, scratch, table, arrived = refs[len(layout) :]
    points, width = queries.shape
    depth = width // BANDS
    per = 2 * width // GROUPS // LANES
    kept = scratch.shape[3]
    copies = start_loads(
        spots, pieces, layout, scratch, arrived, slice(0, kept), spots[GROUPS]
    )
    inputs = jnp.concatenate([decoded[...], fetched[...]], axis=0)
    for at in range(GROUPS):
        wait_group(copies, at)
        spot = spots[at]
        total = dot(inputs, lanes_of(scratch[spot], depth, 0, per)).astype(BF16)
        for group in range(per):
            table[spot * per + group] = total[:, group * LANES : (group + 1) * LANES]

    pairs = width // LANES
    scale = BF16(1.0 / math.sqrt(width // HEADS))
    times = jnp.concatenate([here[...], there[...]], axis=1)
    bias = jnp.where(times > 0, 0.0, NEG)
    both = jnp.concatenate([times, times], axis=0)
    rows = []
    for pair in range(pairs):
        rows.append(
            pair_attend(
                queries[:, pair * LANES : (pair + 1) * LANES] * scale,
                table[pair],
                table[pairs + pair],
                bias,
                lambda weights: weights * both,
            )
        )
    gridded = jnp.concatenate(rows, axis=1)
    start = per * depth
    halves = depth // LANES
    height = (kept - start) // halves
    padded = jnp.zeros((GROUPS * height, points), F32)
    for chunk, band in enumerate(CHUNKS):
        for half in range(halves):
            at = start + half * height
            weight = scratch[:, chunk // 2, chunk % 2, at : at + height, :]
            first = band * depth + half * LANES
            padded += dot_nt(
                weight.reshape(GROUPS * height, LANES), gridded[:, first : first + LANES]
            )
    parts = [padded[group * height : group * height + each] for group in range(GROUPS)]
    fields[...] = jnp.concatenate(parts, axis=0).astype(BF16)


def decode(riding, queries, decoded, fetched, here, there, pieces, layout, outputs):
    points, width = queries.shape
    height = pieces[0].shape[-2]
    rows = decoded.shape[0] + fetched.shape[0]
    return pl.pallas_call(
        functools.partial(decode_kernel, layout, outputs // GROUPS, riding),
        out_shape=jax.ShapeDtypeStruct((outputs, points), BF16),
        in_specs=[VMEM_SPEC] * 5 + [ANY] * len(pieces),
        out_specs=VMEM_SPEC,
        scratch_shapes=[
            pltpu.VMEM((GROUPS, 2, 2, height, LANES), BF16),
            pltpu.VMEM((2 * width // LANES, rows, LANES), BF16),
            pltpu.SemaphoreType.DMA((len(pieces),)),
        ],
        compiler_params=params(),
        cost_estimate=SMALL,
        name="decode",
    )(queries, decoded, fetched, here, there, *pieces)


def stacked(*weights):
    parts = []
    for weight in weights:
        for at in range(0, weight.shape[-1], LANES):
            parts.append(weight[..., at : at + LANES])
    return jnp.concatenate(parts, axis=-2)


def pair_x(block, gate=None):
    if gate is not None:
        block, _ = lax.optimization_barrier((block, gate))
    other = lax.ppermute(block, "band", [(i, i ^ 2) for i in range(BANDS)])
    low = lax.axis_index("band") < 2
    return jnp.stack([jnp.where(low, block, other), jnp.where(low, other, block)])


def pair_core(block):
    other = swap_core(block)
    low = lax.axis_index("band") % 2 == 0
    return jnp.stack([jnp.where(low, block, other), jnp.where(low, other, block)])


def carry(block):
    pairs = []
    for i in range(GROUPS):
        here, there = RING[i] * BANDS, RING[(i + 1) % GROUPS] * BANDS
        for x in range(2):
            pairs.append((here + 2 * x, there + 2 * x))
            pairs.append((there + 2 * x + 1, here + 2 * x + 1))
    return lax.ppermute(block, ("seq", "band"), pairs)


def swap_core(block):
    return lax.ppermute(block, "band", [(i, i ^ 1) for i in range(BANDS)])


def chain_step(chains, step, gate=None):
    if gate is not None:
        *chains, _ = lax.optimization_barrier((*chains, gate))
    chains = [carry(block) for block in chains]
    pieces = []
    for half, block in enumerate(chains):
        pieces.append((block, (step, half)))
        pieces.append((swap_core(block), (GROUPS - step, 1 - half)))
    return chains, pieces


def ring_step(block, step, gate=None):
    if gate is not None:
        block, _ = lax.optimization_barrier((block, gate))
    block = carry(block)
    return block, [(block, (step, None)), (swap_core(block), (GROUPS - step, None))]


def last_step(block):
    half = lax.dynamic_index_in_dim(block, lax.axis_index("band") % 2, 0, keepdims=False)
    half = carry(half)
    return [(half, (GROUPS // 2, 0)), (swap_core(half), (GROUPS // 2, 1))]


def whole_blocks(*weights):
    parts = []
    for weight, height in weights:
        weight = lax.all_gather(weight, "seq", axis=1, tiled=True)
        weight = lax.all_gather(weight, "band", axis=0, tiled=True)
        depth, columns = weight.shape[0] // BANDS, weight.shape[1] // GROUPS
        weight = weight.reshape(2, 2, depth, GROUPS, columns).transpose(3, 1, 0, 2, 4)
        if height:
            weight = jnp.pad(
                weight.swapaxes(-1, -2), ((0, 0),) * 3 + ((0, height - columns), (0, 0))
            )
        parts.append(weight)
    return stacked(*parts)


def local(
    tokens, ln_gain, w_qkv, w_out, dec_gain, w_kv, w_final, reach, grid_query, neighbours, counts
):
    states = tokens[0]
    tok, width = states.shape
    shards, bands = lax.axis_size("seq"), lax.axis_size("band")
    outputs = w_final.shape[1] * shards
    height = -(-outputs // GROUPS // 16) * 16
    riding = (shards, bands) == (GROUPS, BANDS)
    up = [(i, i + 1) for i in range(shards - 1)]
    down = [(i + 1, i) for i in range(shards - 1)]
    left = lax.ppermute(states[tok - HALF :], "seq", up)
    right = lax.ppermute(states[:HALF], "seq", down)
    slots = (neighbours.T, counts.reshape(1, -1))
    there, requested, *payload = tables(tok, *slots, shards, (w_qkv, w_out) if riding else ())
    normed, bias, here = prepare(
        tok * shards, riding, left, states, right, ln_gain.reshape(1, width),
        reach.reshape(1, tok), *slots,
    )
    if riding:
        mine = pair_x(payload[0])
        mine, _, _ = lax.optimization_barrier((mine, left, right))
        other = swap_core(mine)
        pieces = [(mine, (0, 0)), (other, (0, 1))]
        chains, more = chain_step([mine, other], 1)
        pieces += more
        final = jnp.pad(w_final.T, ((0, height - w_final.shape[1]), (0, 0)))
        second = pair_core(pair_x(stacked(w_kv, final), chains[0]))
        later = [(second, (0, None))]
        chains[1], _ = lax.optimization_barrier((chains[1], normed))
        chains, more = chain_step(chains, 2)
        pieces += more
        normed, _ = lax.optimization_barrier((normed, chains[1]))
        made = project(riding, normed, pieces[:6], None)
        chains, more = chain_step(chains, 3)
        pieces += more
        last, more = chain_step(chains[:1], 4, (chains[1], made))
        pieces += more
        second, *_ = lax.optimization_barrier((second, chains[1], made, pieces[7][0], pieces[9][0]))
        later = [(second, (0, None))]
        block, more = ring_step(second, 1)
        later += more
        block, more = ring_step(block, 2, [pieces[n][0] for n in (11, 13, 15)])
        later += more
        attended = attend(riding, normed, bias, pieces[6:], made, (0, 1, 7))
        block, more = ring_step(block, 3, attended)
        later += more
        ids = None
    else:
        block = whole_blocks((w_qkv, 0), (w_out, 0))
        block = jnp.pad(block, ((0, 0),) * 3 + ((0, SLOTS), (0, 0)))
        pieces = [(block[at, half], (at, half)) for at in range(GROUPS) for half in range(2)]
        block = whole_blocks((w_kv, 0), (w_final, height))
        later = [(block[at], (at, None)) for at in range(GROUPS)]
        made = project(riding, normed, pieces[:6], None)
        attended = attend(riding, normed, bias, pieces[6:], made, tuple(range(3)))
        ids = lax.all_to_all(
            requested.reshape(shards, SLOTS).astype(jnp.int32), "seq", 0, 0, tiled=True
        ).reshape(shards * SLOTS, 1)
    layout = tuple(at for _, at in pieces)
    pieces = [piece for piece, _ in pieces]
    decoded, found = mix(
        states, attended, dec_gain.reshape(1, width), ids, pieces, layout, shards
    )
    fetched = lax.all_to_all(
        found.reshape(shards, SLOTS, width), "seq", split_axis=0, concat_axis=0, tiled=True
    )
    if riding:
        block, _ = lax.optimization_barrier((block, found))
        later += last_step(block)
    layout = tuple(at for _, at in later)
    pieces = [piece for piece, _ in later]
    fields = decode(
        riding, grid_query[0], decoded, fetched.reshape(shards * SLOTS, width), here, there,
        pieces, layout, outputs,
    )
    return fields[None]


def solution(mesh):
    return jax.shard_map(
        local,
        mesh=mesh,
        in_specs=(
            P("band", "seq", None),
            P(),
            P("band", "seq"),
            P("band", "seq"),
            P(),
            P("band", "seq"),
            P("band", "seq"),
            P("seq"),
            P("band", "seq", None),
            P("seq", None),
            P("seq"),
        ),
        out_specs=P("band", None, "seq"),
        check_vma=False,
    )
```

```python
import functools
import math

import jax
import jax.numpy as jnp
import numpy as np
from jax import lax
from jax.experimental import pallas as pl
from jax.experimental.pallas import tpu as pltpu
from jax.sharding import PartitionSpec as P

HEADS = 16
HALF = 128
C = 12
SLOTS = 16
EPSILON = 1e-05
NEG = -1e30
LANES = 128
GROUPS = 8
BANDS = 4
CHUNKS = (0, 2, 1, 3)
RING = (0, 2, 4, 6, 7, 5, 3, 1)
VMEM = 60 * 1024 * 1024
SMALL = pl.CostEstimate(flops=1000, bytes_accessed=1000, transcendentals=0)
F32 = jnp.float32
BF16 = jnp.bfloat16


def dot(a, b):
    return jnp.dot(a, b, preferred_element_type=F32)


def dot_nt(a, b):
    return lax.dot_general(a, b, (((1,), (1,)), ((), ())), preferred_element_type=F32)


def layer_norm(values, gain):
    values = values.astype(F32)
    centred = values - jnp.mean(values, axis=-1, keepdims=True)
    spread = jnp.mean(centred * centred, axis=-1, keepdims=True)
    return (centred * lax.rsqrt(spread + EPSILON) * gain).astype(BF16)


def here_at(riding):
    return lax.axis_index("seq"), (lax.axis_index("band") % 2 if riding else 0)


def ring_spots(riding):
    if not riding:
        return list(range(GROUPS)) + [0]
    seq, core = here_at(True)
    at_ring = jnp.where(seq % 2 == 0, seq // 2, GROUPS - 1 - seq // 2)
    turn = jnp.where(core == 0, GROUPS - 1, 1)
    spots = []
    for at in range(GROUPS):
        step = (at_ring + turn * at) % GROUPS
        spots.append(jnp.where(step < GROUPS // 2, 2 * step, 2 * GROUPS - 1 - 2 * step))
    return spots + [core]


def params(**more):
    return pltpu.CompilerParams(vmem_limit_bytes=VMEM, **more)


def full_spec(shape):
    return pl.BlockSpec(shape, lambda *_: (0,) * len(shape))


def own_first(rows, core, depth):
    parts = [rows[:, b * depth : (b + 1) * depth] for b in range(BANDS)]
    order = ((0, 1), (2, 3), (1, 0), (3, 2))
    return jnp.concatenate([jnp.where(core == 0, parts[a], parts[b]) for a, b in order], axis=1)


def as_column(row):
    return jnp.broadcast_to(row, (8, row.shape[1])).T[:, :1]


def prepare_kernel(
    total, riding, left, own, right, gain, reach, neighbours, counts, normed, bias, multiplicity
):
    place = here_at(riding)
    tok = own.shape[0]
    depth = own.shape[1] // BANDS
    for at, part in ((0, left), (HALF, own), (HALF + tok, right)):
        rows = layer_norm(part[...], gain[...])
        normed[at : at + part.shape[0], :] = own_first(rows, place[1], depth)

    first = place[0] * tok
    span = 3 * HALF
    row = lax.broadcasted_iota(jnp.int32, (HALF, span), 0)
    col = lax.broadcasted_iota(jnp.int32, (HALF, span), 1)
    away = jnp.abs(row + HALF - col)
    limit = as_column(reach[...])
    for block in range(tok // HALF):
        key = first + (block - 1) * HALF + col
        allowed = (away <= limit[block * HALF : (block + 1) * HALF, :]) & (key >= 0) & (key < total)
        bias[block] = jnp.where(allowed, 0.0, NEG)

    ids = neighbours[...].T
    used = as_column(counts[...])
    mesh = lax.broadcasted_iota(jnp.int32, multiplicity.shape, 1) + first
    here = jnp.zeros(multiplicity.shape, F32)
    for slot in range(ids.shape[1]):
        here += ((ids[:, slot : slot + 1] == mesh) & (slot < used)).astype(F32)
    multiplicity[...] = here


def prepare(total, riding, left, own, right, gain, reach, neighbours, counts):
    tok, width = own.shape
    operands = (left, own, right, gain, reach, neighbours, counts)
    outs = (
        jax.ShapeDtypeStruct((tok + 2 * HALF, width), BF16),
        jax.ShapeDtypeStruct((tok // HALF, HALF, 3 * HALF), F32),
        jax.ShapeDtypeStruct((neighbours.shape[1], tok), F32),
    )
    return pl.pallas_call(
        functools.partial(prepare_kernel, total, riding),
        out_shape=outs,
        in_specs=[pl.BlockSpec(memory_space=pltpu.VMEM)] * len(operands),
        out_specs=[pl.BlockSpec(memory_space=pltpu.VMEM)] * len(outs),
        compiler_params=params(),
        cost_estimate=SMALL,
        name="prepare",
    )(*operands)


def tables_kernel(tok, count, neighbours, counts, low, rank, tri, *refs):
    weights, (multiplicity, requested) = refs[:count], refs[count : count + 2]
    first = lax.axis_index("seq") * tok
    slots = neighbours.shape[0]
    ids = neighbours[...].T
    used = as_column(counts[...])
    start = low[...]
    elsewhere = start != first
    hits = []
    for slot in range(slots):
        which = ids[:, slot : slot + 1]
        hits.append(
            ((which >= start) & (which < start + tok) & (slot < used) & elsewhere).astype(F32)
        )
    running = dot(tri[...], sum(hits).astype(BF16))
    order = rank[...]
    asked = jnp.zeros(hits[0].shape, F32)
    there = jnp.zeros(hits[0].shape, F32)
    for slot in range(slots):
        mine = jnp.where(running == order, hits[slot], 0.0)
        there += mine
        offset = (ids[:, slot : slot + 1] - start).astype(F32)
        asked += jnp.where(mine > 0, offset, 0.0)
        running += hits[slot]
    multiplicity[...] = there
    asked = jnp.sum(asked, axis=0, keepdims=True)
    requested[...] = asked.astype(BF16)
    if weights:
        payload = refs[-1]
        at = 0
        for weight in weights:
            depth, columns = weight.shape
            for first in range(0, columns, LANES):
                payload[at : at + depth, :] = weight[:, first : first + LANES]
                at += depth
        payload[at:, :] = jnp.broadcast_to(asked, (SLOTS, LANES)).astype(BF16)


def tables(tok, neighbours, counts, shards, weights):
    points = neighbours.shape[1]
    remote = shards * SLOTS
    column = np.arange(remote)
    low = (column // SLOTS * tok).astype(np.int32)[None]
    rank = (column % SLOTS).astype(np.float32)[None]
    tri = np.tril(np.ones((points, points), np.float32), -1).astype(BF16)
    operands = (neighbours, counts, low, rank, tri) + weights
    outs = (
        jax.ShapeDtypeStruct((points, remote), F32),
        jax.ShapeDtypeStruct((1, remote), BF16),
    )
    if weights:
        rows = sum(weight.shape[0] * weight.shape[1] // LANES for weight in weights) + SLOTS
        outs += (jax.ShapeDtypeStruct((rows, LANES), BF16),)
    return pl.pallas_call(
        functools.partial(tables_kernel, tok, len(weights)),
        out_shape=outs,
        in_specs=[pl.BlockSpec(memory_space=pltpu.VMEM)] * len(operands),
        out_specs=[pl.BlockSpec(memory_space=pltpu.VMEM)] * len(outs),
        compiler_params=params(),
        cost_estimate=SMALL,
        name="tables",
    )(*operands)


def pair_attend(queries, keys, values, bias, weights_of):
    rows = queries.shape[0]
    lane = lax.broadcasted_iota(jnp.int32, (rows, LANES), 1)
    first = lane < LANES // 2
    zero = jnp.zeros_like(queries)
    both = jnp.concatenate(
        [jnp.where(first, queries, zero), jnp.where(first, zero, queries)], axis=0
    )
    scores = dot_nt(both, keys)
    scores = scores + jnp.concatenate([bias, bias], axis=0)
    top = jnp.max(scores, axis=-1, keepdims=True)
    weights = weights_of(jnp.exp(scores - top)).astype(BF16)
    summed = dot(weights, jnp.concatenate([values, jnp.ones_like(values)], axis=1))
    share = summed[:, :LANES] / summed[:, LANES:]
    return jnp.where(first, share[:rows], share[rows:]).astype(BF16)


def start_loads(spots, pieces, layout, scratch, arrived, rows, core=None):
    copies = {}
    for n, (piece, (at, half)) in enumerate(zip(pieces, layout)):
        place = scratch.at[spots[at]]
        if half is None:
            copy = pltpu.make_async_copy(piece.at[:, :, rows, :], place, arrived.at[n])
        else:
            to = half if core is None else (1 - core if half else core)
            copy = pltpu.make_async_copy(piece.at[:, rows, :], place.at[to], arrived.at[n])
        copy.start()
        copies.setdefault(at, []).append(copy)
    return copies


def wait_group(copies, at):
    for copy in copies.get(at, ()):
        copy.wait()


def lanes_of(block, depth, start, count):
    rows = block.shape[0] * block.shape[1] * depth if block.ndim == 4 else block.shape[0] * depth
    columns = [
        block[..., start + g * depth : start + (g + 1) * depth, :].reshape(rows, LANES)
        for g in range(count)
    ]
    return columns[0] if count == 1 else jnp.concatenate(columns, axis=1)


SMEM = pl.BlockSpec(memory_space=pltpu.SMEM)
VMEM_SPEC = pl.BlockSpec(memory_space=pltpu.VMEM)
ANY = pl.BlockSpec(memory_space=pl.ANY)


def projection(normed, weight, depth, per):
    return dot(normed, lanes_of(weight[...], depth, 0, per)).astype(BF16)


def project_kernel(layout, riding, normed, *refs):
    spots = ring_spots(riding)
    pieces = refs[: len(layout)]
    out, scratch, made, arrived, sent = refs[-5:]
    per = made.shape[1]
    depth = normed.shape[1] // BANDS
    copies = start_loads(spots, pieces, layout, scratch, arrived, slice(0, per * depth))
    writes = []
    for n, at in enumerate(copies):
        wait_group(copies, at)
        total = projection(normed[...], scratch.at[spots[at]], depth, per)
        for group in range(per):
            made[n, group] = total[:, group * LANES : (group + 1) * LANES]
        writes.append(
            pltpu.make_async_copy(made.at[n], out.at[pl.ds(spots[at] * per, per)], sent.at[n])
        )
        writes[-1].start()
    for write in writes:
        write.wait()


def project(riding, normed, pieces, before):
    rows, width = normed.shape
    layout = tuple(place for _, place in pieces)
    arrays = [array for array, _ in pieces]
    per = 3 * width // LANES // GROUPS
    count = len({at for at, _ in layout})
    more = [] if before is None else [before]
    return pl.pallas_call(
        functools.partial(project_kernel, layout, riding),
        out_shape=jax.ShapeDtypeStruct((GROUPS * per, rows, LANES), BF16),
        in_specs=[VMEM_SPEC] + [ANY] * (len(arrays) + len(more)),
        out_specs=ANY,
        scratch_shapes=[
            pltpu.VMEM((GROUPS, 2, 2, per * width // BANDS, LANES), BF16),
            pltpu.VMEM((count, per, rows, LANES), BF16),
            pltpu.SemaphoreType.DMA((len(arrays),)),
            pltpu.SemaphoreType.DMA((count,)),
        ],
        input_output_aliases={1 + len(arrays): 0} if more else {},
        compiler_params=params(),
        cost_estimate=SMALL,
        name="project",
    )(normed, *arrays, *more)


def attend_kernel(layout, ready, riding, normed, bias, *refs):
    spots = ring_spots(riding)
    pieces = refs[: len(layout)]
    made, attended, scratch, projected, arrived, loaded = refs[len(layout) :]
    width = normed.shape[1]
    depth = width // BANDS
    per = projected.shape[0] // GROUPS
    copies = start_loads(spots, pieces, layout, scratch, arrived, slice(0, per * depth))
    reads = []
    for n, at in enumerate(ready):
        place = pl.ds(spots[at] * per, per)
        reads.append(pltpu.make_async_copy(made.at[place], projected.at[place], loaded.at[n]))
        reads[-1].start()
    for at in copies:
        wait_group(copies, at)
        total = projection(normed[...], scratch.at[spots[at]], depth, per)
        for group in range(per):
            projected[spots[at] * per + group] = total[:, group * LANES : (group + 1) * LANES]
    for read in reads:
        read.wait()
    pairs = width // LANES
    scale = BF16(1.0 / math.sqrt(width // HEADS))
    for pair in range(pairs):
        for block in range(bias.shape[0]):
            at = block * HALF
            attended[at : at + HALF, pair * LANES : (pair + 1) * LANES] = pair_attend(
                projected[pair, at + HALF : at + 2 * HALF, :] * scale,
                projected[pairs + pair, at : at + 3 * HALF, :],
                projected[2 * pairs + pair, at : at + 3 * HALF, :],
                bias[block],
                lambda weights: weights,
            )


def attend(riding, normed, bias, pieces, made, ready):
    rows, width = normed.shape
    tok = rows - 2 * HALF
    layout = tuple(place for _, place in pieces)
    arrays = [array for array, _ in pieces]
    per = made.shape[0] // GROUPS
    return pl.pallas_call(
        functools.partial(attend_kernel, layout, ready, riding),
        out_shape=jax.ShapeDtypeStruct((tok, width), BF16),
        in_specs=[VMEM_SPEC, VMEM_SPEC] + [ANY] * (len(arrays) + 1),
        out_specs=VMEM_SPEC,
        scratch_shapes=[
            pltpu.VMEM((GROUPS, 2, 2, per * width // BANDS, LANES), BF16),
            pltpu.VMEM(made.shape, BF16),
            pltpu.SemaphoreType.DMA((len(arrays),)),
            pltpu.SemaphoreType.DMA((len(ready),)),
        ],
        compiler_params=params(),
        cost_estimate=SMALL,
        name="attend",
    )(normed, bias, *arrays, made)


def picked_rows(place, ids, spots, rows, asked, arrived):
    tok = rows.shape[0]
    if spots is None:
        which = ids[...]
    else:
        for at in range(GROUPS):
            asked[pl.ds(spots[at] * SLOTS, SLOTS), :] = jnp.broadcast_to(
                arrived[at, 0:1, :].astype(F32), (SLOTS, LANES)
            )
        count = GROUPS * SLOTS
        lane = lax.broadcasted_iota(jnp.int32, (count, LANES), 1)
        slot = lax.broadcasted_iota(jnp.int32, (count, LANES), 0) % SLOTS
        mine = jnp.where(lane == place[0] * SLOTS + slot, asked[...], 0.0)
        which = jnp.sum(mine, axis=1, keepdims=True).astype(jnp.int32)
    here = lax.broadcasted_iota(jnp.int32, (which.shape[0], tok), 1)
    return dot((which == here).astype(BF16), rows).astype(BF16)


def chunked(values, depth):
    return jnp.concatenate([values[:, b * depth : (b + 1) * depth] for b in CHUNKS], axis=1)


def mix_kernel(layout, riding, states, gain, *refs):
    place, spots = here_at(riding), ring_spots(riding)
    attended, refs = refs[0], refs[1:]
    ids = None
    if not riding:
        ids, refs = refs[0], refs[1:]
    pieces = refs[: len(layout)]
    decoded, found, mixed, scratch, asked, notes, arrived, noted = refs[len(layout) :]
    width = states.shape[1]
    depth = width // BANDS
    start = 3 * width // GROUPS // LANES * depth
    copies = start_loads(spots, pieces, layout, scratch, arrived, slice(start, start + depth))
    reads = []
    if riding:
        for piece, (at, core) in zip(pieces, layout):
            if core == 0:
                end = piece.shape[-2]
                reads.append(
                    pltpu.make_async_copy(
                        piece.at[0, end - SLOTS : end, :], notes.at[at], noted.at[at]
                    )
                )
                reads[-1].start()
    inputs = own_first(attended[...], place[1], depth)
    for at in range(GROUPS):
        wait_group(copies, at)
    for at in range(0, GROUPS, 2):
        columns = slice(at * LANES, (at + 2) * LANES)
        weight = [lanes_of(scratch[at + n], depth, 0, 1) for n in range(2)]
        total = dot(inputs, jnp.concatenate(weight, axis=1))
        mixed[:, columns] = (states[:, columns].astype(F32) + total).astype(BF16)
    for read in reads:
        read.wait()
    rows = chunked(layer_norm(mixed[...], gain[...]), depth)
    decoded[...] = rows
    found[...] = picked_rows(place, ids, spots if riding else None, rows, asked, notes)


def mix(states, attended, gain, ids, pieces, layout, shards):
    tok, width = states.shape
    more = [] if ids is None else [ids]
    return pl.pallas_call(
        functools.partial(mix_kernel, layout, ids is None),
        out_shape=(
            jax.ShapeDtypeStruct((tok, width), BF16),
            jax.ShapeDtypeStruct((shards * SLOTS, width), BF16),
        ),
        in_specs=[VMEM_SPEC] * (3 + len(more)) + [ANY] * len(pieces),
        out_specs=(VMEM_SPEC, VMEM_SPEC),
        scratch_shapes=[
            pltpu.VMEM((tok, width), BF16),
            pltpu.VMEM((GROUPS, 2, 2, width // BANDS, LANES), BF16),
            pltpu.VMEM((GROUPS * SLOTS, LANES), F32),
            pltpu.VMEM((GROUPS, SLOTS, LANES), BF16),
            pltpu.SemaphoreType.DMA((len(pieces),)),
            pltpu.SemaphoreType.DMA((GROUPS,)),
        ],
        compiler_params=params(),
        cost_estimate=SMALL,
        name="mix",
    )(states, gain, attended, *more, *pieces)


def decode_kernel(layout, each, riding, queries, decoded, fetched, here, there, *refs):
    spots = ring_spots(riding)
    pieces = refs[: len(layout)]
    fields, scratch, table, arrived = refs[len(layout) :]
    points, width = queries.shape
    depth = width // BANDS
    per = 2 * width // GROUPS // LANES
    kept = scratch.shape[3]
    copies = start_loads(
        spots, pieces, layout, scratch, arrived, slice(0, kept), spots[GROUPS]
    )
    inputs = jnp.concatenate([decoded[...], fetched[...]], axis=0)
    for at in range(GROUPS):
        wait_group(copies, at)
        spot = spots[at]
        total = dot(inputs, lanes_of(scratch[spot], depth, 0, per)).astype(BF16)
        for group in range(per):
            table[spot * per + group] = total[:, group * LANES : (group + 1) * LANES]

    pairs = width // LANES
    scale = BF16(1.0 / math.sqrt(width // HEADS))
    times = jnp.concatenate([here[...], there[...]], axis=1)
    bias = jnp.where(times > 0, 0.0, NEG)
    both = jnp.concatenate([times, times], axis=0)
    rows = []
    for pair in range(pairs):
        rows.append(
            pair_attend(
                queries[:, pair * LANES : (pair + 1) * LANES] * scale,
                table[pair],
                table[pairs + pair],
                bias,
                lambda weights: weights * both,
            )
        )
    gridded = jnp.concatenate(rows, axis=1)
    start = per * depth
    halves = depth // LANES
    height = (kept - start) // halves
    padded = jnp.zeros((GROUPS * height, points), F32)
    for chunk, band in enumerate(CHUNKS):
        for half in range(halves):
            at = start + half * height
            weight = scratch[:, chunk // 2, chunk % 2, at : at + height, :]
            first = band * depth + half * LANES
            padded += dot_nt(
                weight.reshape(GROUPS * height, LANES), gridded[:, first : first + LANES]
            )
    parts = [padded[group * height : group * height + each] for group in range(GROUPS)]
    fields[...] = jnp.concatenate(parts, axis=0).astype(BF16)


def decode(riding, queries, decoded, fetched, here, there, pieces, layout, outputs):
    points, width = queries.shape
    height = pieces[0].shape[-2]
    rows = decoded.shape[0] + fetched.shape[0]
    return pl.pallas_call(
        functools.partial(decode_kernel, layout, outputs // GROUPS, riding),
        out_shape=jax.ShapeDtypeStruct((outputs, points), BF16),
        in_specs=[VMEM_SPEC] * 5 + [ANY] * len(pieces),
        out_specs=VMEM_SPEC,
        scratch_shapes=[
            pltpu.VMEM((GROUPS, 2, 2, height, LANES), BF16),
            pltpu.VMEM((2 * width // LANES, rows, LANES), BF16),
            pltpu.SemaphoreType.DMA((len(pieces),)),
        ],
        compiler_params=params(),
        cost_estimate=SMALL,
        name="decode",
    )(queries, decoded, fetched, here, there, *pieces)


def stacked(*weights):
    parts = []
    for weight in weights:
        for at in range(0, weight.shape[-1], LANES):
            parts.append(weight[..., at : at + LANES])
    return jnp.concatenate(parts, axis=-2)


def pair_x(block, gate=None):
    if gate is not None:
        block, _ = lax.optimization_barrier((block, gate))
    other = lax.ppermute(block, "band", [(i, i ^ 2) for i in range(BANDS)])
    low = lax.axis_index("band") < 2
    return jnp.stack([jnp.where(low, block, other), jnp.where(low, other, block)])


def pair_core(block):
    other = swap_core(block)
    low = lax.axis_index("band") % 2 == 0
    return jnp.stack([jnp.where(low, block, other), jnp.where(low, other, block)])


def carry(block):
    pairs = []
    for i in range(GROUPS):
        here, there = RING[i] * BANDS, RING[(i + 1) % GROUPS] * BANDS
        for x in range(2):
            pairs.append((here + 2 * x, there + 2 * x))
            pairs.append((there + 2 * x + 1, here + 2 * x + 1))
    return lax.ppermute(block, ("seq", "band"), pairs)


def swap_core(block):
    return lax.ppermute(block, "band", [(i, i ^ 1) for i in range(BANDS)])


def chain_step(chains, step, gate=None):
    if gate is not None:
        *chains, _ = lax.optimization_barrier((*chains, gate))
    chains = [carry(block) for block in chains]
    pieces = []
    for half, block in enumerate(chains):
        pieces.append((block, (step, half)))
        pieces.append((swap_core(block), (GROUPS - step, 1 - half)))
    return chains, pieces


def ring_step(block, step, gate=None):
    if gate is not None:
        block, _ = lax.optimization_barrier((block, gate))
    block = carry(block)
    return block, [(block, (step, None)), (swap_core(block), (GROUPS - step, None))]


def last_step(block):
    half = lax.dynamic_index_in_dim(block, lax.axis_index("band") % 2, 0, keepdims=False)
    half = carry(half)
    return [(half, (GROUPS // 2, 0)), (swap_core(half), (GROUPS // 2, 1))]


def whole_blocks(*weights):
    parts = []
    for weight, height in weights:
        weight = lax.all_gather(weight, "seq", axis=1, tiled=True)
        weight = lax.all_gather(weight, "band", axis=0, tiled=True)
        depth, columns = weight.shape[0] // BANDS, weight.shape[1] // GROUPS
        weight = weight.reshape(2, 2, depth, GROUPS, columns).transpose(3, 1, 0, 2, 4)
        if height:
            weight = jnp.pad(
                weight.swapaxes(-1, -2), ((0, 0),) * 3 + ((0, height - columns), (0, 0))
            )
        parts.append(weight)
    return stacked(*parts)


def local(
    tokens, ln_gain, w_qkv, w_out, dec_gain, w_kv, w_final, reach, grid_query, neighbours, counts
):
    states = tokens[0]
    tok, width = states.shape
    shards, bands = lax.axis_size("seq"), lax.axis_size("band")
    outputs = w_final.shape[1] * shards
    height = -(-outputs // GROUPS // 16) * 16
    riding = (shards, bands) == (GROUPS, BANDS)
    up = [(i, i + 1) for i in range(shards - 1)]
    down = [(i + 1, i) for i in range(shards - 1)]
    left = lax.ppermute(states[tok - HALF :], "seq", up)
    right = lax.ppermute(states[:HALF], "seq", down)
    slots = (neighbours.T, counts.reshape(1, -1))
    there, requested, *payload = tables(tok, *slots, shards, (w_qkv, w_out) if riding else ())
    normed, bias, here = prepare(
        tok * shards, riding, left, states, right, ln_gain.reshape(1, width),
        reach.reshape(1, tok), *slots,
    )
    if riding:
        mine = pair_x(payload[0])
        mine, _, _ = lax.optimization_barrier((mine, left, right))
        other = swap_core(mine)
        pieces = [(mine, (0, 0)), (other, (0, 1))]
        chains, more = chain_step([mine, other], 1)
        pieces += more
        final = jnp.pad(w_final.T, ((0, height - w_final.shape[1]), (0, 0)))
        second = pair_core(pair_x(stacked(w_kv, final), chains[0]))
        later = [(second, (0, None))]
        chains[1], _ = lax.optimization_barrier((chains[1], normed))
        chains, more = chain_step(chains, 2)
        pieces += more
        normed, _ = lax.optimization_barrier((normed, chains[1]))
        made = project(riding, normed, pieces[:6], None)
        chains, more = chain_step(chains, 3)
        pieces += more
        last, more = chain_step(chains[:1], 4, (chains[1], made))
        pieces += more
        second, *_ = lax.optimization_barrier((second, chains[1], made, pieces[7][0], pieces[9][0]))
        later = [(second, (0, None))]
        block, more = ring_step(second, 1)
        later += more
        block, more = ring_step(block, 2, [pieces[n][0] for n in (11, 13, 15)])
        later += more
        attended = attend(riding, normed, bias, pieces[6:], made, (0, 1, 7))
        block, _ = lax.optimization_barrier((block, attended))
        block = carry(block)
        ids = None
    else:
        block = whole_blocks((w_qkv, 0), (w_out, 0))
        block = jnp.pad(block, ((0, 0),) * 3 + ((0, SLOTS), (0, 0)))
        pieces = [(block[at, half], (at, half)) for at in range(GROUPS) for half in range(2)]
        block = whole_blocks((w_kv, 0), (w_final, height))
        later = [(block[at], (at, None)) for at in range(GROUPS)]
        made = project(riding, normed, pieces[:6], None)
        attended = attend(riding, normed, bias, pieces[6:], made, tuple(range(3)))
        ids = lax.all_to_all(
            requested.reshape(shards, SLOTS).astype(jnp.int32), "seq", 0, 0, tiled=True
        ).reshape(shards * SLOTS, 1)
    layout = tuple(at for _, at in pieces)
    pieces = [piece for piece, _ in pieces]
    decoded, found = mix(
        states, attended, dec_gain.reshape(1, width), ids, pieces, layout, shards
    )
    fetched = lax.all_to_all(
        found.reshape(shards, SLOTS, width), "seq", split_axis=0, concat_axis=0, tiled=True
    )
    if riding:
        handed, _ = lax.optimization_barrier((block, fetched))
        later += [(block, (3, None)), (swap_core(handed), (GROUPS - 3, None))]
        block, _ = lax.optimization_barrier((block, found))
        later += last_step(block)
    layout = tuple(at for _, at in later)
    pieces = [piece for piece, _ in later]
    fields = decode(
        riding, grid_query[0], decoded, fetched.reshape(shards * SLOTS, width), here, there,
        pieces, layout, outputs,
    )
    return fields[None]


def solution(mesh):
    return jax.shard_map(
        local,
        mesh=mesh,
        in_specs=(
            P("band", "seq", None),
            P(),
            P("band", "seq"),
            P("band", "seq"),
            P(),
            P("band", "seq"),
            P("band", "seq"),
            P("seq"),
            P("band", "seq", None),
            P("seq", None),
            P("seq"),
        ),
        out_specs=P("band", None, "seq"),
        check_vma=False,
    )
```

```python
import functools
import math

import jax
import jax.numpy as jnp
import numpy as np
from jax import lax
from jax.experimental import pallas as pl
from jax.experimental.pallas import tpu as pltpu
from jax.sharding import PartitionSpec as P

HEADS = 16
HALF = 128
C = 12
SLOTS = 16
EPSILON = 1e-05
NEG = -1e30
LANES = 128
GROUPS = 8
BANDS = 4
CHUNKS = (0, 2, 1, 3)
RING = (0, 2, 4, 6, 7, 5, 3, 1)
VMEM = 60 * 1024 * 1024
SMALL = pl.CostEstimate(flops=1000, bytes_accessed=1000, transcendentals=0)
F32 = jnp.float32
BF16 = jnp.bfloat16


def dot(a, b):
    return jnp.dot(a, b, preferred_element_type=F32)


def dot_nt(a, b):
    return lax.dot_general(a, b, (((1,), (1,)), ((), ())), preferred_element_type=F32)


def layer_norm(values, gain):
    values = values.astype(F32)
    centred = values - jnp.mean(values, axis=-1, keepdims=True)
    spread = jnp.mean(centred * centred, axis=-1, keepdims=True)
    return (centred * lax.rsqrt(spread + EPSILON) * gain).astype(BF16)


def here_at(riding):
    return lax.axis_index("seq"), (lax.axis_index("band") % 2 if riding else 0)


def ring_spots(riding):
    if not riding:
        return list(range(GROUPS)) + [0]
    seq, core = here_at(True)
    at_ring = jnp.where(seq % 2 == 0, seq // 2, GROUPS - 1 - seq // 2)
    turn = jnp.where(core == 0, GROUPS - 1, 1)
    spots = []
    for at in range(GROUPS):
        step = (at_ring + turn * at) % GROUPS
        spots.append(jnp.where(step < GROUPS // 2, 2 * step, 2 * GROUPS - 1 - 2 * step))
    return spots + [core]


def params(**more):
    return pltpu.CompilerParams(vmem_limit_bytes=VMEM, **more)


def full_spec(shape):
    return pl.BlockSpec(shape, lambda *_: (0,) * len(shape))


def own_first(rows, core, depth):
    parts = [rows[:, b * depth : (b + 1) * depth] for b in range(BANDS)]
    order = ((0, 1), (2, 3), (1, 0), (3, 2))
    return jnp.concatenate([jnp.where(core == 0, parts[a], parts[b]) for a, b in order], axis=1)


def as_column(row):
    return jnp.broadcast_to(row, (8, row.shape[1])).T[:, :1]


def prepare_kernel(
    total, riding, left, own, right, gain, reach, neighbours, counts, normed, bias, multiplicity
):
    place = here_at(riding)
    tok = own.shape[0]
    depth = own.shape[1] // BANDS
    for at, part in ((0, left), (HALF, own), (HALF + tok, right)):
        rows = layer_norm(part[...], gain[...])
        normed[at : at + part.shape[0], :] = own_first(rows, place[1], depth)

    first = place[0] * tok
    span = 3 * HALF
    row = lax.broadcasted_iota(jnp.int32, (HALF, span), 0)
    col = lax.broadcasted_iota(jnp.int32, (HALF, span), 1)
    away = jnp.abs(row + HALF - col)
    limit = as_column(reach[...])
    for block in range(tok // HALF):
        key = first + (block - 1) * HALF + col
        allowed = (away <= limit[block * HALF : (block + 1) * HALF, :]) & (key >= 0) & (key < total)
        bias[block] = jnp.where(allowed, 0.0, NEG)

    ids = neighbours[...].T
    used = as_column(counts[...])
    mesh = lax.broadcasted_iota(jnp.int32, multiplicity.shape, 1) + first
    here = jnp.zeros(multiplicity.shape, F32)
    for slot in range(ids.shape[1]):
        here += ((ids[:, slot : slot + 1] == mesh) & (slot < used)).astype(F32)
    multiplicity[...] = here


def prepare(total, riding, left, own, right, gain, reach, neighbours, counts):
    tok, width = own.shape
    operands = (left, own, right, gain, reach, neighbours, counts)
    outs = (
        jax.ShapeDtypeStruct((tok + 2 * HALF, width), BF16),
        jax.ShapeDtypeStruct((tok // HALF, HALF, 3 * HALF), F32),
        jax.ShapeDtypeStruct((neighbours.shape[1], tok), F32),
    )
    return pl.pallas_call(
        functools.partial(prepare_kernel, total, riding),
        out_shape=outs,
        in_specs=[pl.BlockSpec(memory_space=pltpu.VMEM)] * len(operands),
        out_specs=[pl.BlockSpec(memory_space=pltpu.VMEM)] * len(outs),
        compiler_params=params(),
        cost_estimate=SMALL,
        name="prepare",
    )(*operands)


def tables_kernel(tok, count, neighbours, counts, low, rank, tri, *refs):
    weights, (multiplicity, requested) = refs[:count], refs[count : count + 2]
    first = lax.axis_index("seq") * tok
    slots = neighbours.shape[0]
    ids = neighbours[...].T
    used = as_column(counts[...])
    start = low[...]
    elsewhere = start != first
    hits = []
    for slot in range(slots):
        which = ids[:, slot : slot + 1]
        hits.append(
            ((which >= start) & (which < start + tok) & (slot < used) & elsewhere).astype(F32)
        )
    running = dot(tri[...], sum(hits).astype(BF16))
    order = rank[...]
    asked = jnp.zeros(hits[0].shape, F32)
    there = jnp.zeros(hits[0].shape, F32)
    for slot in range(slots):
        mine = jnp.where(running == order, hits[slot], 0.0)
        there += mine
        offset = (ids[:, slot : slot + 1] - start).astype(F32)
        asked += jnp.where(mine > 0, offset, 0.0)
        running += hits[slot]
    multiplicity[...] = there
    asked = jnp.sum(asked, axis=0, keepdims=True)
    requested[...] = asked.astype(BF16)
    if weights:
        payload = refs[-1]
        at = 0
        for weight in weights:
            depth, columns = weight.shape
            for first in range(0, columns, LANES):
                payload[at : at + depth, :] = weight[:, first : first + LANES]
                at += depth
        payload[at:, :] = jnp.broadcast_to(asked, (SLOTS, LANES)).astype(BF16)


def tables(tok, neighbours, counts, shards, weights):
    points = neighbours.shape[1]
    remote = shards * SLOTS
    column = np.arange(remote)
    low = (column // SLOTS * tok).astype(np.int32)[None]
    rank = (column % SLOTS).astype(np.float32)[None]
    tri = np.tril(np.ones((points, points), np.float32), -1).astype(BF16)
    operands = (neighbours, counts, low, rank, tri) + weights
    outs = (
        jax.ShapeDtypeStruct((points, remote), F32),
        jax.ShapeDtypeStruct((1, remote), BF16),
    )
    if weights:
        rows = sum(weight.shape[0] * weight.shape[1] // LANES for weight in weights) + SLOTS
        outs += (jax.ShapeDtypeStruct((rows, LANES), BF16),)
    return pl.pallas_call(
        functools.partial(tables_kernel, tok, len(weights)),
        out_shape=outs,
        in_specs=[pl.BlockSpec(memory_space=pltpu.VMEM)] * len(operands),
        out_specs=[pl.BlockSpec(memory_space=pltpu.VMEM)] * len(outs),
        compiler_params=params(),
        cost_estimate=SMALL,
        name="tables",
    )(*operands)


def pair_attend(queries, keys, values, bias, weights_of):
    rows = queries.shape[0]
    lane = lax.broadcasted_iota(jnp.int32, (rows, LANES), 1)
    first = lane < LANES // 2
    zero = jnp.zeros_like(queries)
    both = jnp.concatenate(
        [jnp.where(first, queries, zero), jnp.where(first, zero, queries)], axis=0
    )
    scores = dot_nt(both, keys)
    scores = scores + jnp.concatenate([bias, bias], axis=0)
    top = jnp.max(scores, axis=-1, keepdims=True)
    weights = weights_of(jnp.exp(scores - top)).astype(BF16)
    summed = dot(weights, jnp.concatenate([values, jnp.ones_like(values)], axis=1))
    share = summed[:, :LANES] / summed[:, LANES:]
    return jnp.where(first, share[:rows], share[rows:]).astype(BF16)


def start_loads(spots, pieces, layout, scratch, arrived, rows, core=None):
    copies = {}
    for n, (piece, (at, half)) in enumerate(zip(pieces, layout)):
        place = scratch.at[spots[at]]
        if half is None:
            copy = pltpu.make_async_copy(piece.at[:, :, rows, :], place, arrived.at[n])
        else:
            to = half if core is None else (1 - core if half else core)
            copy = pltpu.make_async_copy(piece.at[:, rows, :], place.at[to], arrived.at[n])
        copy.start()
        copies.setdefault(at, []).append(copy)
    return copies


def wait_group(copies, at):
    for copy in copies.get(at, ()):
        copy.wait()


def lanes_of(block, depth, start, count):
    rows = block.shape[0] * block.shape[1] * depth if block.ndim == 4 else block.shape[0] * depth
    columns = [
        block[..., start + g * depth : start + (g + 1) * depth, :].reshape(rows, LANES)
        for g in range(count)
    ]
    return columns[0] if count == 1 else jnp.concatenate(columns, axis=1)


SMEM = pl.BlockSpec(memory_space=pltpu.SMEM)
VMEM_SPEC = pl.BlockSpec(memory_space=pltpu.VMEM)
ANY = pl.BlockSpec(memory_space=pl.ANY)


def projection(normed, weight, depth, per):
    return dot(normed, lanes_of(weight[...], depth, 0, per)).astype(BF16)


def project_kernel(layout, riding, normed, *refs):
    spots = ring_spots(riding)
    pieces = refs[: len(layout)]
    out, scratch, made, arrived, sent = refs[-5:]
    per = made.shape[1]
    depth = normed.shape[1] // BANDS
    copies = start_loads(spots, pieces, layout, scratch, arrived, slice(0, per * depth))
    writes = []
    for n, at in enumerate(copies):
        wait_group(copies, at)
        total = projection(normed[...], scratch.at[spots[at]], depth, per)
        for group in range(per):
            made[n, group] = total[:, group * LANES : (group + 1) * LANES]
        writes.append(
            pltpu.make_async_copy(made.at[n], out.at[pl.ds(spots[at] * per, per)], sent.at[n])
        )
        writes[-1].start()
    for write in writes:
        write.wait()


def project(riding, normed, pieces, before):
    rows, width = normed.shape
    layout = tuple(place for _, place in pieces)
    arrays = [array for array, _ in pieces]
    per = 3 * width // LANES // GROUPS
    count = len({at for at, _ in layout})
    more = [] if before is None else [before]
    return pl.pallas_call(
        functools.partial(project_kernel, layout, riding),
        out_shape=jax.ShapeDtypeStruct((GROUPS * per, rows, LANES), BF16),
        in_specs=[VMEM_SPEC] + [ANY] * (len(arrays) + len(more)),
        out_specs=ANY,
        scratch_shapes=[
            pltpu.VMEM((GROUPS, 2, 2, per * width // BANDS, LANES), BF16),
            pltpu.VMEM((count, per, rows, LANES), BF16),
            pltpu.SemaphoreType.DMA((len(arrays),)),
            pltpu.SemaphoreType.DMA((count,)),
        ],
        input_output_aliases={1 + len(arrays): 0} if more else {},
        compiler_params=params(),
        cost_estimate=SMALL,
        name="project",
    )(normed, *arrays, *more)


def attend_kernel(layout, ready, riding, normed, bias, *refs):
    spots = ring_spots(riding)
    pieces = refs[: len(layout)]
    made, attended, scratch, projected, arrived, loaded = refs[len(layout) :]
    width = normed.shape[1]
    depth = width // BANDS
    per = projected.shape[0] // GROUPS
    copies = start_loads(spots, pieces, layout, scratch, arrived, slice(0, per * depth))
    reads = []
    for n, at in enumerate(ready):
        place = pl.ds(spots[at] * per, per)
        reads.append(pltpu.make_async_copy(made.at[place], projected.at[place], loaded.at[n]))
        reads[-1].start()
    for at in copies:
        wait_group(copies, at)
        total = projection(normed[...], scratch.at[spots[at]], depth, per)
        for group in range(per):
            projected[spots[at] * per + group] = total[:, group * LANES : (group + 1) * LANES]
    for read in reads:
        read.wait()
    pairs = width // LANES
    scale = BF16(1.0 / math.sqrt(width // HEADS))
    for pair in range(pairs):
        for block in range(bias.shape[0]):
            at = block * HALF
            attended[at : at + HALF, pair * LANES : (pair + 1) * LANES] = pair_attend(
                projected[pair, at + HALF : at + 2 * HALF, :] * scale,
                projected[pairs + pair, at : at + 3 * HALF, :],
                projected[2 * pairs + pair, at : at + 3 * HALF, :],
                bias[block],
                lambda weights: weights,
            )


def attend(riding, normed, bias, pieces, made, ready):
    rows, width = normed.shape
    tok = rows - 2 * HALF
    layout = tuple(place for _, place in pieces)
    arrays = [array for array, _ in pieces]
    per = made.shape[0] // GROUPS
    return pl.pallas_call(
        functools.partial(attend_kernel, layout, ready, riding),
        out_shape=jax.ShapeDtypeStruct((tok, width), BF16),
        in_specs=[VMEM_SPEC, VMEM_SPEC] + [ANY] * (len(arrays) + 1),
        out_specs=VMEM_SPEC,
        scratch_shapes=[
            pltpu.VMEM((GROUPS, 2, 2, per * width // BANDS, LANES), BF16),
            pltpu.VMEM(made.shape, BF16),
            pltpu.SemaphoreType.DMA((len(arrays),)),
            pltpu.SemaphoreType.DMA((len(ready),)),
        ],
        compiler_params=params(),
        cost_estimate=SMALL,
        name="attend",
    )(normed, bias, *arrays, made)


def picked_rows(place, ids, spots, rows, asked, arrived):
    tok = rows.shape[0]
    if spots is None:
        which = ids[...]
    else:
        for at in range(GROUPS):
            asked[pl.ds(spots[at] * SLOTS, SLOTS), :] = jnp.broadcast_to(
                arrived[at, 0:1, :].astype(F32), (SLOTS, LANES)
            )
        count = GROUPS * SLOTS
        lane = lax.broadcasted_iota(jnp.int32, (count, LANES), 1)
        slot = lax.broadcasted_iota(jnp.int32, (count, LANES), 0) % SLOTS
        mine = jnp.where(lane == place[0] * SLOTS + slot, asked[...], 0.0)
        which = jnp.sum(mine, axis=1, keepdims=True).astype(jnp.int32)
    here = lax.broadcasted_iota(jnp.int32, (which.shape[0], tok), 1)
    return dot((which == here).astype(BF16), rows).astype(BF16)


def chunked(values, depth):
    return jnp.concatenate([values[:, b * depth : (b + 1) * depth] for b in CHUNKS], axis=1)


def mix_kernel(layout, riding, states, gain, *refs):
    place, spots = here_at(riding), ring_spots(riding)
    attended, refs = refs[0], refs[1:]
    ids = None
    if not riding:
        ids, refs = refs[0], refs[1:]
    pieces = refs[: len(layout)]
    decoded, found, mixed, scratch, asked, notes, arrived, noted = refs[len(layout) :]
    width = states.shape[1]
    depth = width // BANDS
    start = 3 * width // GROUPS // LANES * depth
    copies = start_loads(spots, pieces, layout, scratch, arrived, slice(start, start + depth))
    reads = []
    if riding:
        for piece, (at, core) in zip(pieces, layout):
            if core == 0:
                end = piece.shape[-2]
                reads.append(
                    pltpu.make_async_copy(
                        piece.at[0, end - SLOTS : end, :], notes.at[at], noted.at[at]
                    )
                )
                reads[-1].start()
    inputs = own_first(attended[...], place[1], depth)
    for at in range(GROUPS):
        wait_group(copies, at)
    for at in range(0, GROUPS, 2):
        columns = slice(at * LANES, (at + 2) * LANES)
        weight = [lanes_of(scratch[at + n], depth, 0, 1) for n in range(2)]
        total = dot(inputs, jnp.concatenate(weight, axis=1))
        mixed[:, columns] = (states[:, columns].astype(F32) + total).astype(BF16)
    for read in reads:
        read.wait()
    rows = chunked(layer_norm(mixed[...], gain[...]), depth)
    decoded[...] = rows
    found[...] = picked_rows(place, ids, spots if riding else None, rows, asked, notes)


def mix(states, attended, gain, ids, pieces, layout, shards):
    tok, width = states.shape
    more = [] if ids is None else [ids]
    return pl.pallas_call(
        functools.partial(mix_kernel, layout, ids is None),
        out_shape=(
            jax.ShapeDtypeStruct((tok, width), BF16),
            jax.ShapeDtypeStruct((shards * SLOTS, width), BF16),
        ),
        in_specs=[VMEM_SPEC] * (3 + len(more)) + [ANY] * len(pieces),
        out_specs=(VMEM_SPEC, VMEM_SPEC),
        scratch_shapes=[
            pltpu.VMEM((tok, width), BF16),
            pltpu.VMEM((GROUPS, 2, 2, width // BANDS, LANES), BF16),
            pltpu.VMEM((GROUPS * SLOTS, LANES), F32),
            pltpu.VMEM((GROUPS, SLOTS, LANES), BF16),
            pltpu.SemaphoreType.DMA((len(pieces),)),
            pltpu.SemaphoreType.DMA((GROUPS,)),
        ],
        compiler_params=params(),
        cost_estimate=SMALL,
        name="mix",
    )(states, gain, attended, *more, *pieces)


def decode_kernel(layout, each, riding, queries, decoded, fetched, here, there, *refs):
    spots = ring_spots(riding)
    pieces = refs[: len(layout)]
    fields, scratch, table, arrived = refs[len(layout) :]
    points, width = queries.shape
    depth = width // BANDS
    per = 2 * width // GROUPS // LANES
    kept = scratch.shape[3]
    copies = start_loads(
        spots, pieces, layout, scratch, arrived, slice(0, kept), spots[GROUPS]
    )
    inputs = jnp.concatenate([decoded[...], fetched[...]], axis=0)
    for at in range(GROUPS):
        wait_group(copies, at)
        spot = spots[at]
        total = dot(inputs, lanes_of(scratch[spot], depth, 0, per)).astype(BF16)
        for group in range(per):
            table[spot * per + group] = total[:, group * LANES : (group + 1) * LANES]

    pairs = width // LANES
    scale = BF16(1.0 / math.sqrt(width // HEADS))
    times = jnp.concatenate([here[...], there[...]], axis=1)
    bias = jnp.where(times > 0, 0.0, NEG)
    both = jnp.concatenate([times, times], axis=0)
    rows = []
    for pair in range(pairs):
        rows.append(
            pair_attend(
                queries[:, pair * LANES : (pair + 1) * LANES] * scale,
                table[pair],
                table[pairs + pair],
                bias,
                lambda weights: weights * both,
            )
        )
    gridded = jnp.concatenate(rows, axis=1)
    start = per * depth
    halves = depth // LANES
    height = (kept - start) // halves
    padded = jnp.zeros((GROUPS * height, points), F32)
    for chunk, band in enumerate(CHUNKS):
        for half in range(halves):
            at = start + half * height
            weight = scratch[:, chunk // 2, chunk % 2, at : at + height, :]
            first = band * depth + half * LANES
            padded += dot_nt(
                weight.reshape(GROUPS * height, LANES), gridded[:, first : first + LANES]
            )
    parts = [padded[group * height : group * height + each] for group in range(GROUPS)]
    fields[...] = jnp.concatenate(parts, axis=0).astype(BF16)


def decode(riding, queries, decoded, fetched, here, there, pieces, layout, outputs):
    points, width = queries.shape
    height = pieces[0].shape[-2]
    rows = decoded.shape[0] + fetched.shape[0]
    return pl.pallas_call(
        functools.partial(decode_kernel, layout, outputs // GROUPS, riding),
        out_shape=jax.ShapeDtypeStruct((outputs, points), BF16),
        in_specs=[VMEM_SPEC] * 5 + [ANY] * len(pieces),
        out_specs=VMEM_SPEC,
        scratch_shapes=[
            pltpu.VMEM((GROUPS, 2, 2, height, LANES), BF16),
            pltpu.VMEM((2 * width // LANES, rows, LANES), BF16),
            pltpu.SemaphoreType.DMA((len(pieces),)),
        ],
        compiler_params=params(),
        cost_estimate=SMALL,
        name="decode",
    )(queries, decoded, fetched, here, there, *pieces)


def stacked(*weights):
    parts = []
    for weight in weights:
        for at in range(0, weight.shape[-1], LANES):
            parts.append(weight[..., at : at + LANES])
    return jnp.concatenate(parts, axis=-2)


def pair_x(block, gate=None):
    if gate is not None:
        block, _ = lax.optimization_barrier((block, gate))
    other = lax.ppermute(block, "band", [(i, i ^ 2) for i in range(BANDS)])
    low = lax.axis_index("band") < 2
    return jnp.stack([jnp.where(low, block, other), jnp.where(low, other, block)])


def pair_core(block):
    other = swap_core(block)
    low = lax.axis_index("band") % 2 == 0
    return jnp.stack([jnp.where(low, block, other), jnp.where(low, other, block)])


def carry(block):
    pairs = []
    for i in range(GROUPS):
        here, there = RING[i] * BANDS, RING[(i + 1) % GROUPS] * BANDS
        for x in range(2):
            pairs.append((here + 2 * x, there + 2 * x))
            pairs.append((there + 2 * x + 1, here + 2 * x + 1))
    return lax.ppermute(block, ("seq", "band"), pairs)


def swap_core(block):
    return lax.ppermute(block, "band", [(i, i ^ 1) for i in range(BANDS)])


def chain_step(chains, step, gate=None):
    if gate is not None:
        *chains, _ = lax.optimization_barrier((*chains, gate))
    chains = [carry(block) for block in chains]
    pieces = []
    for half, block in enumerate(chains):
        pieces.append((block, (step, half)))
        pieces.append((swap_core(block), (GROUPS - step, 1 - half)))
    return chains, pieces


def ring_step(block, step, gate=None):
    if gate is not None:
        block, _ = lax.optimization_barrier((block, gate))
    block = carry(block)
    return block, [(block, (step, None)), (swap_core(block), (GROUPS - step, None))]


def last_step(block, gate):
    half = lax.dynamic_index_in_dim(block, lax.axis_index("band") % 2, 0, keepdims=False)
    half = carry(half)
    handed, _ = lax.optimization_barrier((half, gate))
    return [(half, (GROUPS // 2, 0)), (swap_core(handed), (GROUPS // 2, 1))]


def whole_blocks(*weights):
    parts = []
    for weight, height in weights:
        weight = lax.all_gather(weight, "seq", axis=1, tiled=True)
        weight = lax.all_gather(weight, "band", axis=0, tiled=True)
        depth, columns = weight.shape[0] // BANDS, weight.shape[1] // GROUPS
        weight = weight.reshape(2, 2, depth, GROUPS, columns).transpose(3, 1, 0, 2, 4)
        if height:
            weight = jnp.pad(
                weight.swapaxes(-1, -2), ((0, 0),) * 3 + ((0, height - columns), (0, 0))
            )
        parts.append(weight)
    return stacked(*parts)


def local(
    tokens, ln_gain, w_qkv, w_out, dec_gain, w_kv, w_final, reach, grid_query, neighbours, counts
):
    states = tokens[0]
    tok, width = states.shape
    shards, bands = lax.axis_size("seq"), lax.axis_size("band")
    outputs = w_final.shape[1] * shards
    height = -(-outputs // GROUPS // 16) * 16
    riding = (shards, bands) == (GROUPS, BANDS)
    up = [(i, i + 1) for i in range(shards - 1)]
    down = [(i + 1, i) for i in range(shards - 1)]
    left = lax.ppermute(states[tok - HALF :], "seq", up)
    right = lax.ppermute(states[:HALF], "seq", down)
    slots = (neighbours.T, counts.reshape(1, -1))
    there, requested, *payload = tables(tok, *slots, shards, (w_qkv, w_out) if riding else ())
    normed, bias, here = prepare(
        tok * shards, riding, left, states, right, ln_gain.reshape(1, width),
        reach.reshape(1, tok), *slots,
    )
    if riding:
        mine = pair_x(payload[0])
        mine, _, _ = lax.optimization_barrier((mine, left, right))
        other = swap_core(mine)
        pieces = [(mine, (0, 0)), (other, (0, 1))]
        chains, more = chain_step([mine, other], 1)
        pieces += more
        final = jnp.pad(w_final.T, ((0, height - w_final.shape[1]), (0, 0)))
        second = pair_core(pair_x(stacked(w_kv, final), chains[0]))
        later = [(second, (0, None))]
        chains[1], _ = lax.optimization_barrier((chains[1], normed))
        chains, more = chain_step(chains, 2)
        pieces += more
        normed, _ = lax.optimization_barrier((normed, chains[1]))
        made = project(riding, normed, pieces[:6], None)
        chains, more = chain_step(chains, 3)
        pieces += more
        last, more = chain_step(chains[:1], 4, (chains[1], made))
        pieces += more
        second, *_ = lax.optimization_barrier((second, chains[1], made, pieces[7][0], pieces[9][0]))
        later = [(second, (0, None))]
        block, more = ring_step(second, 1)
        later += more
        block, more = ring_step(block, 2, [pieces[n][0] for n in (11, 13, 15)])
        later += more
        attended = attend(riding, normed, bias, pieces[6:], made, (0, 1, 7))
        block, more = ring_step(block, 3, attended)
        later += more
        ids = None
    else:
        block = whole_blocks((w_qkv, 0), (w_out, 0))
        block = jnp.pad(block, ((0, 0),) * 3 + ((0, SLOTS), (0, 0)))
        pieces = [(block[at, half], (at, half)) for at in range(GROUPS) for half in range(2)]
        block = whole_blocks((w_kv, 0), (w_final, height))
        later = [(block[at], (at, None)) for at in range(GROUPS)]
        made = project(riding, normed, pieces[:6], None)
        attended = attend(riding, normed, bias, pieces[6:], made, tuple(range(3)))
        ids = lax.all_to_all(
            requested.reshape(shards, SLOTS).astype(jnp.int32), "seq", 0, 0, tiled=True
        ).reshape(shards * SLOTS, 1)
    layout = tuple(at for _, at in pieces)
    pieces = [piece for piece, _ in pieces]
    decoded, found = mix(
        states, attended, dec_gain.reshape(1, width), ids, pieces, layout, shards
    )
    fetched = lax.all_to_all(
        found.reshape(shards, SLOTS, width), "seq", split_axis=0, concat_axis=0, tiled=True
    )
    if riding:
        block, _ = lax.optimization_barrier((block, found))
        later += last_step(block, fetched)
    layout = tuple(at for _, at in later)
    pieces = [piece for piece, _ in later]
    fields = decode(
        riding, grid_query[0], decoded, fetched.reshape(shards * SLOTS, width), here, there,
        pieces, layout, outputs,
    )
    return fields[None]


def solution(mesh):
    return jax.shard_map(
        local,
        mesh=mesh,
        in_specs=(
            P("band", "seq", None),
            P(),
            P("band", "seq"),
            P("band", "seq"),
            P(),
            P("band", "seq"),
            P("band", "seq"),
            P("seq"),
            P("band", "seq", None),
            P("seq", None),
            P("seq"),
        ),
        out_specs=P("band", None, "seq"),
        check_vma=False,
    )
```

```python
import functools
import math

import jax
import jax.numpy as jnp
import numpy as np
from jax import lax
from jax.experimental import pallas as pl
from jax.experimental.pallas import tpu as pltpu
from jax.sharding import PartitionSpec as P

HEADS = 16
HALF = 128
C = 12
SLOTS = 16
EPSILON = 1e-05
NEG = -1e30
LANES = 128
GROUPS = 8
BANDS = 4
CHUNKS = (0, 2, 1, 3)
RING = (0, 2, 4, 6, 7, 5, 3, 1)
VMEM = 60 * 1024 * 1024
SMALL = pl.CostEstimate(flops=1000, bytes_accessed=1000, transcendentals=0)
F32 = jnp.float32
BF16 = jnp.bfloat16


def dot(a, b):
    return jnp.dot(a, b, preferred_element_type=F32)


def dot_nt(a, b):
    return lax.dot_general(a, b, (((1,), (1,)), ((), ())), preferred_element_type=F32)


def layer_norm(values, gain):
    values = values.astype(F32)
    centred = values - jnp.mean(values, axis=-1, keepdims=True)
    spread = jnp.mean(centred * centred, axis=-1, keepdims=True)
    return (centred * lax.rsqrt(spread + EPSILON) * gain).astype(BF16)


def here_at(riding):
    return lax.axis_index("seq"), (lax.axis_index("band") % 2 if riding else 0)


def ring_spots(riding):
    if not riding:
        return list(range(GROUPS)) + [0]
    seq, core = here_at(True)
    at_ring = jnp.where(seq % 2 == 0, seq // 2, GROUPS - 1 - seq // 2)
    turn = jnp.where(core == 0, GROUPS - 1, 1)
    spots = []
    for at in range(GROUPS):
        step = (at_ring + turn * at) % GROUPS
        spots.append(jnp.where(step < GROUPS // 2, 2 * step, 2 * GROUPS - 1 - 2 * step))
    return spots + [core]


def params(**more):
    return pltpu.CompilerParams(vmem_limit_bytes=VMEM, **more)


def full_spec(shape):
    return pl.BlockSpec(shape, lambda *_: (0,) * len(shape))


def own_first(rows, core, depth):
    parts = [rows[:, b * depth : (b + 1) * depth] for b in range(BANDS)]
    order = ((0, 1), (2, 3), (1, 0), (3, 2))
    return jnp.concatenate([jnp.where(core == 0, parts[a], parts[b]) for a, b in order], axis=1)


def as_column(row):
    return jnp.broadcast_to(row, (8, row.shape[1])).T[:, :1]


def prepare_kernel(
    total, riding, left, own, right, gain, reach, neighbours, counts, normed, bias, multiplicity
):
    place = here_at(riding)
    tok = own.shape[0]
    depth = own.shape[1] // BANDS
    for at, part in ((0, left), (HALF, own), (HALF + tok, right)):
        rows = layer_norm(part[...], gain[...])
        normed[at : at + part.shape[0], :] = own_first(rows, place[1], depth)

    first = place[0] * tok
    span = 3 * HALF
    row = lax.broadcasted_iota(jnp.int32, (HALF, span), 0)
    col = lax.broadcasted_iota(jnp.int32, (HALF, span), 1)
    away = jnp.abs(row + HALF - col)
    limit = as_column(reach[...])
    for block in range(tok // HALF):
        key = first + (block - 1) * HALF + col
        allowed = (away <= limit[block * HALF : (block + 1) * HALF, :]) & (key >= 0) & (key < total)
        bias[block] = jnp.where(allowed, 0.0, NEG)

    ids = neighbours[...].T
    used = as_column(counts[...])
    mesh = lax.broadcasted_iota(jnp.int32, multiplicity.shape, 1) + first
    here = jnp.zeros(multiplicity.shape, F32)
    for slot in range(ids.shape[1]):
        here += ((ids[:, slot : slot + 1] == mesh) & (slot < used)).astype(F32)
    multiplicity[...] = here


def prepare(total, riding, left, own, right, gain, reach, neighbours, counts):
    tok, width = own.shape
    operands = (left, own, right, gain, reach, neighbours, counts)
    outs = (
        jax.ShapeDtypeStruct((tok + 2 * HALF, width), BF16),
        jax.ShapeDtypeStruct((tok // HALF, HALF, 3 * HALF), F32),
        jax.ShapeDtypeStruct((neighbours.shape[1], tok), F32),
    )
    return pl.pallas_call(
        functools.partial(prepare_kernel, total, riding),
        out_shape=outs,
        in_specs=[pl.BlockSpec(memory_space=pltpu.VMEM)] * len(operands),
        out_specs=[pl.BlockSpec(memory_space=pltpu.VMEM)] * len(outs),
        compiler_params=params(),
        cost_estimate=SMALL,
        name="prepare",
    )(*operands)


def tables_kernel(tok, count, neighbours, counts, low, rank, tri, *refs):
    weights, (multiplicity, requested) = refs[:count], refs[count : count + 2]
    first = lax.axis_index("seq") * tok
    slots = neighbours.shape[0]
    ids = neighbours[...].T
    used = as_column(counts[...])
    start = low[...]
    elsewhere = start != first
    hits = []
    for slot in range(slots):
        which = ids[:, slot : slot + 1]
        hits.append(
            ((which >= start) & (which < start + tok) & (slot < used) & elsewhere).astype(F32)
        )
    running = dot(tri[...], sum(hits).astype(BF16))
    order = rank[...]
    asked = jnp.zeros(hits[0].shape, F32)
    there = jnp.zeros(hits[0].shape, F32)
    for slot in range(slots):
        mine = jnp.where(running == order, hits[slot], 0.0)
        there += mine
        offset = (ids[:, slot : slot + 1] - start).astype(F32)
        asked += jnp.where(mine > 0, offset, 0.0)
        running += hits[slot]
    multiplicity[...] = there
    asked = jnp.sum(asked, axis=0, keepdims=True)
    requested[...] = asked.astype(BF16)
    if weights:
        payload = refs[-1]
        at = 0
        for weight in weights:
            depth, columns = weight.shape
            for first in range(0, columns, LANES):
                payload[at : at + depth, :] = weight[:, first : first + LANES]
                at += depth
        payload[at:, :] = jnp.broadcast_to(asked, (SLOTS, LANES)).astype(BF16)


def tables(tok, neighbours, counts, shards, weights):
    points = neighbours.shape[1]
    remote = shards * SLOTS
    column = np.arange(remote)
    low = (column // SLOTS * tok).astype(np.int32)[None]
    rank = (column % SLOTS).astype(np.float32)[None]
    tri = np.tril(np.ones((points, points), np.float32), -1).astype(BF16)
    operands = (neighbours, counts, low, rank, tri) + weights
    outs = (
        jax.ShapeDtypeStruct((points, remote), F32),
        jax.ShapeDtypeStruct((1, remote), BF16),
    )
    if weights:
        rows = sum(weight.shape[0] * weight.shape[1] // LANES for weight in weights) + SLOTS
        outs += (jax.ShapeDtypeStruct((rows, LANES), BF16),)
    return pl.pallas_call(
        functools.partial(tables_kernel, tok, len(weights)),
        out_shape=outs,
        in_specs=[pl.BlockSpec(memory_space=pltpu.VMEM)] * len(operands),
        out_specs=[pl.BlockSpec(memory_space=pltpu.VMEM)] * len(outs),
        compiler_params=params(),
        cost_estimate=SMALL,
        name="tables",
    )(*operands)


def pair_attend(queries, keys, values, bias, weights_of):
    rows = queries.shape[0]
    lane = lax.broadcasted_iota(jnp.int32, (rows, LANES), 1)
    first = lane < LANES // 2
    zero = jnp.zeros_like(queries)
    both = jnp.concatenate(
        [jnp.where(first, queries, zero), jnp.where(first, zero, queries)], axis=0
    )
    scores = dot_nt(both, keys)
    scores = scores + jnp.concatenate([bias, bias], axis=0)
    top = jnp.max(scores, axis=-1, keepdims=True)
    weights = weights_of(jnp.exp(scores - top)).astype(BF16)
    summed = dot(weights, jnp.concatenate([values, jnp.ones_like(values)], axis=1))
    share = summed[:, :LANES] / summed[:, LANES:]
    return jnp.where(first, share[:rows], share[rows:]).astype(BF16)


def start_loads(spots, pieces, layout, scratch, arrived, rows, core=None):
    copies = {}
    for n, (piece, (at, half)) in enumerate(zip(pieces, layout)):
        place = scratch.at[spots[at]]
        if half is None:
            copy = pltpu.make_async_copy(piece.at[:, :, rows, :], place, arrived.at[n])
        else:
            to = half if core is None else (1 - core if half else core)
            copy = pltpu.make_async_copy(piece.at[:, rows, :], place.at[to], arrived.at[n])
        copy.start()
        copies.setdefault(at, []).append(copy)
    return copies


def wait_group(copies, at):
    for copy in copies.get(at, ()):
        copy.wait()


def lanes_of(block, depth, start, count):
    rows = block.shape[0] * block.shape[1] * depth if block.ndim == 4 else block.shape[0] * depth
    columns = [
        block[..., start + g * depth : start + (g + 1) * depth, :].reshape(rows, LANES)
        for g in range(count)
    ]
    return columns[0] if count == 1 else jnp.concatenate(columns, axis=1)


SMEM = pl.BlockSpec(memory_space=pltpu.SMEM)
VMEM_SPEC = pl.BlockSpec(memory_space=pltpu.VMEM)
ANY = pl.BlockSpec(memory_space=pl.ANY)


def projection(normed, weight, depth, per):
    return dot(normed, lanes_of(weight[...], depth, 0, per)).astype(BF16)


def project_kernel(layout, riding, normed, *refs):
    spots = ring_spots(riding)
    pieces = refs[: len(layout)]
    out, scratch, made, arrived, sent = refs[-5:]
    per = made.shape[1]
    depth = normed.shape[1] // BANDS
    copies = start_loads(spots, pieces, layout, scratch, arrived, slice(0, per * depth))
    writes = []
    for n, at in enumerate(copies):
        wait_group(copies, at)
        total = projection(normed[...], scratch.at[spots[at]], depth, per)
        for group in range(per):
            made[n, group] = total[:, group * LANES : (group + 1) * LANES]
        writes.append(
            pltpu.make_async_copy(made.at[n], out.at[pl.ds(spots[at] * per, per)], sent.at[n])
        )
        writes[-1].start()
    for write in writes:
        write.wait()


def project(riding, normed, pieces, before):
    rows, width = normed.shape
    layout = tuple(place for _, place in pieces)
    arrays = [array for array, _ in pieces]
    per = 3 * width // LANES // GROUPS
    count = len({at for at, _ in layout})
    more = [] if before is None else [before]
    return pl.pallas_call(
        functools.partial(project_kernel, layout, riding),
        out_shape=jax.ShapeDtypeStruct((GROUPS * per, rows, LANES), BF16),
        in_specs=[VMEM_SPEC] + [ANY] * (len(arrays) + len(more)),
        out_specs=ANY,
        scratch_shapes=[
            pltpu.VMEM((GROUPS, 2, 2, per * width // BANDS, LANES), BF16),
            pltpu.VMEM((count, per, rows, LANES), BF16),
            pltpu.SemaphoreType.DMA((len(arrays),)),
            pltpu.SemaphoreType.DMA((count,)),
        ],
        input_output_aliases={1 + len(arrays): 0} if more else {},
        compiler_params=params(),
        cost_estimate=SMALL,
        name="project",
    )(normed, *arrays, *more)


def attend_kernel(layout, ready, riding, normed, bias, *refs):
    spots = ring_spots(riding)
    pieces = refs[: len(layout)]
    made, attended, scratch, projected, arrived, loaded = refs[len(layout) :]
    width = normed.shape[1]
    depth = width // BANDS
    per = projected.shape[0] // GROUPS
    copies = start_loads(spots, pieces, layout, scratch, arrived, slice(0, per * depth))
    reads = []
    for n, at in enumerate(ready):
        place = pl.ds(spots[at] * per, per)
        reads.append(pltpu.make_async_copy(made.at[place], projected.at[place], loaded.at[n]))
        reads[-1].start()
    for at in copies:
        wait_group(copies, at)
        total = projection(normed[...], scratch.at[spots[at]], depth, per)
        for group in range(per):
            projected[spots[at] * per + group] = total[:, group * LANES : (group + 1) * LANES]
    for read in reads:
        read.wait()
    pairs = width // LANES
    scale = BF16(1.0 / math.sqrt(width // HEADS))
    for pair in range(pairs):
        for block in range(bias.shape[0]):
            at = block * HALF
            attended[at : at + HALF, pair * LANES : (pair + 1) * LANES] = pair_attend(
                projected[pair, at + HALF : at + 2 * HALF, :] * scale,
                projected[pairs + pair, at : at + 3 * HALF, :],
                projected[2 * pairs + pair, at : at + 3 * HALF, :],
                bias[block],
                lambda weights: weights,
            )


def attend(riding, normed, bias, pieces, made, ready):
    rows, width = normed.shape
    tok = rows - 2 * HALF
    layout = tuple(place for _, place in pieces)
    arrays = [array for array, _ in pieces]
    per = made.shape[0] // GROUPS
    return pl.pallas_call(
        functools.partial(attend_kernel, layout, ready, riding),
        out_shape=jax.ShapeDtypeStruct((tok, width), BF16),
        in_specs=[VMEM_SPEC, VMEM_SPEC] + [ANY] * (len(arrays) + 1),
        out_specs=VMEM_SPEC,
        scratch_shapes=[
            pltpu.VMEM((GROUPS, 2, 2, per * width // BANDS, LANES), BF16),
            pltpu.VMEM(made.shape, BF16),
            pltpu.SemaphoreType.DMA((len(arrays),)),
            pltpu.SemaphoreType.DMA((len(ready),)),
        ],
        compiler_params=params(),
        cost_estimate=SMALL,
        name="attend",
    )(normed, bias, *arrays, made)


def picked_rows(place, ids, spots, rows, asked, arrived):
    tok = rows.shape[0]
    if spots is None:
        which = ids[...]
    else:
        for at in range(GROUPS):
            asked[pl.ds(spots[at] * SLOTS, SLOTS), :] = jnp.broadcast_to(
                arrived[at, 0:1, :].astype(F32), (SLOTS, LANES)
            )
        count = GROUPS * SLOTS
        lane = lax.broadcasted_iota(jnp.int32, (count, LANES), 1)
        slot = lax.broadcasted_iota(jnp.int32, (count, LANES), 0) % SLOTS
        mine = jnp.where(lane == place[0] * SLOTS + slot, asked[...], 0.0)
        which = jnp.sum(mine, axis=1, keepdims=True).astype(jnp.int32)
    here = lax.broadcasted_iota(jnp.int32, (which.shape[0], tok), 1)
    return dot((which == here).astype(BF16), rows).astype(BF16)


def chunked(values, depth):
    return jnp.concatenate([values[:, b * depth : (b + 1) * depth] for b in CHUNKS], axis=1)


def mix_kernel(layout, riding, states, gain, *refs):
    place, spots = here_at(riding), ring_spots(riding)
    attended, refs = refs[0], refs[1:]
    ids = None
    if not riding:
        ids, refs = refs[0], refs[1:]
    pieces = refs[: len(layout)]
    decoded, found, mixed, scratch, asked, notes, arrived, noted = refs[len(layout) :]
    width = states.shape[1]
    depth = width // BANDS
    start = 3 * width // GROUPS // LANES * depth
    copies = start_loads(spots, pieces, layout, scratch, arrived, slice(start, start + depth))
    reads = []
    if riding:
        for piece, (at, core) in zip(pieces, layout):
            if core == 0:
                end = piece.shape[-2]
                reads.append(
                    pltpu.make_async_copy(
                        piece.at[0, end - SLOTS : end, :], notes.at[at], noted.at[at]
                    )
                )
                reads[-1].start()
    inputs = own_first(attended[...], place[1], depth)
    for at in range(GROUPS):
        wait_group(copies, at)
    for at in range(0, GROUPS, 2):
        columns = slice(at * LANES, (at + 2) * LANES)
        weight = [lanes_of(scratch[at + n], depth, 0, 1) for n in range(2)]
        total = dot(inputs, jnp.concatenate(weight, axis=1))
        mixed[:, columns] = (states[:, columns].astype(F32) + total).astype(BF16)
    for read in reads:
        read.wait()
    rows = chunked(layer_norm(mixed[...], gain[...]), depth)
    decoded[...] = rows
    found[...] = picked_rows(place, ids, spots if riding else None, rows, asked, notes)


def mix(states, attended, gain, ids, pieces, layout, shards):
    tok, width = states.shape
    more = [] if ids is None else [ids]
    return pl.pallas_call(
        functools.partial(mix_kernel, layout, ids is None),
        out_shape=(
            jax.ShapeDtypeStruct((tok, width), BF16),
            jax.ShapeDtypeStruct((shards * SLOTS, width), BF16),
        ),
        in_specs=[VMEM_SPEC] * (3 + len(more)) + [ANY] * len(pieces),
        out_specs=(VMEM_SPEC, VMEM_SPEC),
        scratch_shapes=[
            pltpu.VMEM((tok, width), BF16),
            pltpu.VMEM((GROUPS, 2, 2, width // BANDS, LANES), BF16),
            pltpu.VMEM((GROUPS * SLOTS, LANES), F32),
            pltpu.VMEM((GROUPS, SLOTS, LANES), BF16),
            pltpu.SemaphoreType.DMA((len(pieces),)),
            pltpu.SemaphoreType.DMA((GROUPS,)),
        ],
        compiler_params=params(),
        cost_estimate=SMALL,
        name="mix",
    )(states, gain, attended, *more, *pieces)


def decode_kernel(layout, each, riding, queries, decoded, fetched, here, there, *refs):
    spots = ring_spots(riding)
    pieces = refs[: len(layout)]
    fields, scratch, table, arrived = refs[len(layout) :]
    points, width = queries.shape
    depth = width // BANDS
    per = 2 * width // GROUPS // LANES
    kept = scratch.shape[3]
    copies = start_loads(
        spots, pieces, layout, scratch, arrived, slice(0, kept), spots[GROUPS]
    )
    inputs = jnp.concatenate([decoded[...], fetched[...]], axis=0)
    for at in range(GROUPS):
        wait_group(copies, at)
        spot = spots[at]
        total = dot(inputs, lanes_of(scratch[spot], depth, 0, per)).astype(BF16)
        for group in range(per):
            table[spot * per + group] = total[:, group * LANES : (group + 1) * LANES]

    pairs = width // LANES
    scale = BF16(1.0 / math.sqrt(width // HEADS))
    times = jnp.concatenate([here[...], there[...]], axis=1)
    bias = jnp.where(times > 0, 0.0, NEG)
    both = jnp.concatenate([times, times], axis=0)
    rows = []
    for pair in range(pairs):
        rows.append(
            pair_attend(
                queries[:, pair * LANES : (pair + 1) * LANES] * scale,
                table[pair],
                table[pairs + pair],
                bias,
                lambda weights: weights * both,
            )
        )
    gridded = jnp.concatenate(rows, axis=1)
    start = per * depth
    halves = depth // LANES
    height = (kept - start) // halves
    padded = jnp.zeros((GROUPS * height, points), F32)
    for chunk, band in enumerate(CHUNKS):
        for half in range(halves):
            at = start + half * height
            weight = scratch[:, chunk // 2, chunk % 2, at : at + height, :]
            first = band * depth + half * LANES
            padded += dot_nt(
                weight.reshape(GROUPS * height, LANES), gridded[:, first : first + LANES]
            )
    parts = [padded[group * height : group * height + each] for group in range(GROUPS)]
    fields[...] = jnp.concatenate(parts, axis=0).astype(BF16)


def decode(riding, queries, decoded, fetched, here, there, pieces, layout, outputs):
    points, width = queries.shape
    height = pieces[0].shape[-2]
    rows = decoded.shape[0] + fetched.shape[0]
    return pl.pallas_call(
        functools.partial(decode_kernel, layout, outputs // GROUPS, riding),
        out_shape=jax.ShapeDtypeStruct((outputs, points), BF16),
        in_specs=[VMEM_SPEC] * 5 + [ANY] * len(pieces),
        out_specs=VMEM_SPEC,
        scratch_shapes=[
            pltpu.VMEM((GROUPS, 2, 2, height, LANES), BF16),
            pltpu.VMEM((2 * width // LANES, rows, LANES), BF16),
            pltpu.SemaphoreType.DMA((len(pieces),)),
        ],
        compiler_params=params(),
        cost_estimate=SMALL,
        name="decode",
    )(queries, decoded, fetched, here, there, *pieces)


def stacked(*weights):
    parts = []
    for weight in weights:
        for at in range(0, weight.shape[-1], LANES):
            parts.append(weight[..., at : at + LANES])
    return jnp.concatenate(parts, axis=-2)


def pair_x(block, gate=None):
    if gate is not None:
        block, _ = lax.optimization_barrier((block, gate))
    other = lax.ppermute(block, "band", [(i, i ^ 2) for i in range(BANDS)])
    low = lax.axis_index("band") < 2
    return jnp.stack([jnp.where(low, block, other), jnp.where(low, other, block)])


def pair_core(block):
    other = swap_core(block)
    low = lax.axis_index("band") % 2 == 0
    return jnp.stack([jnp.where(low, block, other), jnp.where(low, other, block)])


def carry(block):
    pairs = []
    for i in range(GROUPS):
        here, there = RING[i] * BANDS, RING[(i + 1) % GROUPS] * BANDS
        for x in range(2):
            pairs.append((here + 2 * x, there + 2 * x))
            pairs.append((there + 2 * x + 1, here + 2 * x + 1))
    return lax.ppermute(block, ("seq", "band"), pairs)


def swap_core(block):
    return lax.ppermute(block, "band", [(i, i ^ 1) for i in range(BANDS)])


def chain_step(chains, step, gate=None):
    if gate is not None:
        *chains, _ = lax.optimization_barrier((*chains, gate))
    chains = [carry(block) for block in chains]
    pieces = []
    for half, block in enumerate(chains):
        pieces.append((block, (step, half)))
        pieces.append((swap_core(block), (GROUPS - step, 1 - half)))
    return chains, pieces


def ring_step(block, step, gate=None):
    if gate is not None:
        block, _ = lax.optimization_barrier((block, gate))
    block = carry(block)
    return block, [(block, (step, None)), (swap_core(block), (GROUPS - step, None))]


def last_step(block, gate):
    half = lax.dynamic_index_in_dim(block, lax.axis_index("band") % 2, 0, keepdims=False)
    half = carry(half)
    handed, _ = lax.optimization_barrier((half, gate))
    return [(half, (GROUPS // 2, 0)), (swap_core(handed), (GROUPS // 2, 1))]


def whole_blocks(*weights):
    parts = []
    for weight, height in weights:
        weight = lax.all_gather(weight, "seq", axis=1, tiled=True)
        weight = lax.all_gather(weight, "band", axis=0, tiled=True)
        depth, columns = weight.shape[0] // BANDS, weight.shape[1] // GROUPS
        weight = weight.reshape(2, 2, depth, GROUPS, columns).transpose(3, 1, 0, 2, 4)
        if height:
            weight = jnp.pad(
                weight.swapaxes(-1, -2), ((0, 0),) * 3 + ((0, height - columns), (0, 0))
            )
        parts.append(weight)
    return stacked(*parts)


def local(
    tokens, ln_gain, w_qkv, w_out, dec_gain, w_kv, w_final, reach, grid_query, neighbours, counts
):
    states = tokens[0]
    tok, width = states.shape
    shards, bands = lax.axis_size("seq"), lax.axis_size("band")
    outputs = w_final.shape[1] * shards
    height = -(-outputs // GROUPS // 16) * 16
    riding = (shards, bands) == (GROUPS, BANDS)
    up = [(i, i + 1) for i in range(shards - 1)]
    down = [(i + 1, i) for i in range(shards - 1)]
    left = lax.ppermute(states[tok - HALF :], "seq", up)
    right = lax.ppermute(states[:HALF], "seq", down)
    slots = (neighbours.T, counts.reshape(1, -1))
    there, requested, *payload = tables(tok, *slots, shards, (w_qkv, w_out) if riding else ())
    normed, bias, here = prepare(
        tok * shards, riding, left, states, right, ln_gain.reshape(1, width),
        reach.reshape(1, tok), *slots,
    )
    if riding:
        mine = pair_x(payload[0])
        mine, _, _ = lax.optimization_barrier((mine, left, right))
        other = swap_core(mine)
        pieces = [(mine, (0, 0)), (other, (0, 1))]
        chains, more = chain_step([mine, other], 1)
        pieces += more
        final = jnp.pad(w_final.T, ((0, height - w_final.shape[1]), (0, 0)))
        second = pair_core(pair_x(stacked(w_kv, final), chains[0]))
        later = [(second, (0, None))]
        chains[1], _ = lax.optimization_barrier((chains[1], normed))
        chains, more = chain_step(chains, 2)
        pieces += more
        normed, _ = lax.optimization_barrier((normed, chains[1]))
        made = project(riding, normed, pieces[:6], None)
        chains, more = chain_step(chains, 3)
        pieces += more
        end, _, _ = lax.optimization_barrier((chains[0], chains[1], made))
        end = carry(end)
        second, *_ = lax.optimization_barrier((second, chains[1], made, pieces[7][0], pieces[9][0]))
        later = [(second, (0, None))]
        block, more = ring_step(second, 1)
        later += more
        made = project(riding, normed, pieces[6:10], made)
        handed, _ = lax.optimization_barrier((end, made))
        pieces += [(end, (GROUPS // 2, 0)), (swap_core(handed), (GROUPS // 2, 1))]
        block, more = ring_step(block, 2, [pieces[n][0] for n in (11, 13, 15)])
        later += more
        attended = attend(riding, normed, bias, pieces[10:], made, (0, 1, 7, 2, 6))
        block, more = ring_step(block, 3, attended)
        later += more
        ids = None
    else:
        block = whole_blocks((w_qkv, 0), (w_out, 0))
        block = jnp.pad(block, ((0, 0),) * 3 + ((0, SLOTS), (0, 0)))
        pieces = [(block[at, half], (at, half)) for at in range(GROUPS) for half in range(2)]
        block = whole_blocks((w_kv, 0), (w_final, height))
        later = [(block[at], (at, None)) for at in range(GROUPS)]
        made = project(riding, normed, pieces[:6], None)
        attended = attend(riding, normed, bias, pieces[6:], made, tuple(range(3)))
        ids = lax.all_to_all(
            requested.reshape(shards, SLOTS).astype(jnp.int32), "seq", 0, 0, tiled=True
        ).reshape(shards * SLOTS, 1)
    layout = tuple(at for _, at in pieces)
    pieces = [piece for piece, _ in pieces]
    decoded, found = mix(
        states, attended, dec_gain.reshape(1, width), ids, pieces, layout, shards
    )
    fetched = lax.all_to_all(
        found.reshape(shards, SLOTS, width), "seq", split_axis=0, concat_axis=0, tiled=True
    )
    if riding:
        block, _ = lax.optimization_barrier((block, found))
        later += last_step(block, fetched)
    layout = tuple(at for _, at in later)
    pieces = [piece for piece, _ in later]
    fields = decode(
        riding, grid_query[0], decoded, fetched.reshape(shards * SLOTS, width), here, there,
        pieces, layout, outputs,
    )
    return fields[None]


def solution(mesh):
    return jax.shard_map(
        local,
        mesh=mesh,
        in_specs=(
            P("band", "seq", None),
            P(),
            P("band", "seq"),
            P("band", "seq"),
            P(),
            P("band", "seq"),
            P("band", "seq"),
            P("seq"),
            P("band", "seq", None),
            P("seq", None),
            P("seq"),
        ),
        out_specs=P("band", None, "seq"),
        check_vma=False,
    )
```

```python
import functools
import math

import jax
import jax.numpy as jnp
import numpy as np
from jax import lax
from jax.experimental import pallas as pl
from jax.experimental.pallas import tpu as pltpu
from jax.sharding import PartitionSpec as P

HEADS = 16
HALF = 128
C = 12
SLOTS = 16
EPSILON = 1e-05
NEG = -1e30
LANES = 128
GROUPS = 8
BANDS = 4
CHUNKS = (0, 2, 1, 3)
RING = (0, 2, 4, 6, 7, 5, 3, 1)
VMEM = 60 * 1024 * 1024
SMALL = pl.CostEstimate(flops=1000, bytes_accessed=1000, transcendentals=0)
F32 = jnp.float32
BF16 = jnp.bfloat16


def dot(a, b):
    return jnp.dot(a, b, preferred_element_type=F32)


def dot_nt(a, b):
    return lax.dot_general(a, b, (((1,), (1,)), ((), ())), preferred_element_type=F32)


def layer_norm(values, gain):
    values = values.astype(F32)
    centred = values - jnp.mean(values, axis=-1, keepdims=True)
    spread = jnp.mean(centred * centred, axis=-1, keepdims=True)
    return (centred * lax.rsqrt(spread + EPSILON) * gain).astype(BF16)


def here_at(riding):
    return lax.axis_index("seq"), (lax.axis_index("band") % 2 if riding else 0)


def ring_spots(riding):
    if not riding:
        return list(range(GROUPS)) + [0]
    seq, core = here_at(True)
    at_ring = jnp.where(seq % 2 == 0, seq // 2, GROUPS - 1 - seq // 2)
    turn = jnp.where(core == 0, GROUPS - 1, 1)
    spots = []
    for at in range(GROUPS):
        step = (at_ring + turn * at) % GROUPS
        spots.append(jnp.where(step < GROUPS // 2, 2 * step, 2 * GROUPS - 1 - 2 * step))
    return spots + [core]


def params(**more):
    return pltpu.CompilerParams(vmem_limit_bytes=VMEM, **more)


def full_spec(shape):
    return pl.BlockSpec(shape, lambda *_: (0,) * len(shape))


def own_first(rows, core, depth):
    parts = [rows[:, b * depth : (b + 1) * depth] for b in range(BANDS)]
    order = ((0, 1), (2, 3), (1, 0), (3, 2))
    return jnp.concatenate([jnp.where(core == 0, parts[a], parts[b]) for a, b in order], axis=1)


def as_column(row):
    return jnp.broadcast_to(row, (8, row.shape[1])).T[:, :1]


def prepare_kernel(
    total, riding, left, own, right, gain, reach, neighbours, counts, normed, bias, multiplicity
):
    place = here_at(riding)
    tok = own.shape[0]
    depth = own.shape[1] // BANDS
    for at, part in ((0, left), (HALF, own), (HALF + tok, right)):
        rows = layer_norm(part[...], gain[...])
        normed[at : at + part.shape[0], :] = own_first(rows, place[1], depth)

    first = place[0] * tok
    span = 3 * HALF
    row = lax.broadcasted_iota(jnp.int32, (HALF, span), 0)
    col = lax.broadcasted_iota(jnp.int32, (HALF, span), 1)
    away = jnp.abs(row + HALF - col)
    limit = as_column(reach[...])
    for block in range(tok // HALF):
        key = first + (block - 1) * HALF + col
        allowed = (away <= limit[block * HALF : (block + 1) * HALF, :]) & (key >= 0) & (key < total)
        bias[block] = jnp.where(allowed, 0.0, NEG)

    ids = neighbours[...].T
    used = as_column(counts[...])
    mesh = lax.broadcasted_iota(jnp.int32, multiplicity.shape, 1) + first
    here = jnp.zeros(multiplicity.shape, F32)
    for slot in range(ids.shape[1]):
        here += ((ids[:, slot : slot + 1] == mesh) & (slot < used)).astype(F32)
    multiplicity[...] = here


def prepare(total, riding, left, own, right, gain, reach, neighbours, counts):
    tok, width = own.shape
    operands = (left, own, right, gain, reach, neighbours, counts)
    outs = (
        jax.ShapeDtypeStruct((tok + 2 * HALF, width), BF16),
        jax.ShapeDtypeStruct((tok // HALF, HALF, 3 * HALF), F32),
        jax.ShapeDtypeStruct((neighbours.shape[1], tok), F32),
    )
    return pl.pallas_call(
        functools.partial(prepare_kernel, total, riding),
        out_shape=outs,
        in_specs=[pl.BlockSpec(memory_space=pltpu.VMEM)] * len(operands),
        out_specs=[pl.BlockSpec(memory_space=pltpu.VMEM)] * len(outs),
        compiler_params=params(),
        cost_estimate=SMALL,
        name="prepare",
    )(*operands)


def tables_kernel(tok, count, neighbours, counts, low, rank, tri, *refs):
    weights, (multiplicity, requested) = refs[:count], refs[count : count + 2]
    first = lax.axis_index("seq") * tok
    slots = neighbours.shape[0]
    ids = neighbours[...].T
    used = as_column(counts[...])
    start = low[...]
    elsewhere = start != first
    hits = []
    for slot in range(slots):
        which = ids[:, slot : slot + 1]
        hits.append(
            ((which >= start) & (which < start + tok) & (slot < used) & elsewhere).astype(F32)
        )
    running = dot(tri[...], sum(hits).astype(BF16))
    order = rank[...]
    asked = jnp.zeros(hits[0].shape, F32)
    there = jnp.zeros(hits[0].shape, F32)
    for slot in range(slots):
        mine = jnp.where(running == order, hits[slot], 0.0)
        there += mine
        offset = (ids[:, slot : slot + 1] - start).astype(F32)
        asked += jnp.where(mine > 0, offset, 0.0)
        running += hits[slot]
    multiplicity[...] = there
    asked = jnp.sum(asked, axis=0, keepdims=True)
    requested[...] = asked.astype(BF16)
    if weights:
        payload = refs[-1]
        at = 0
        for weight in weights:
            depth, columns = weight.shape
            for first in range(0, columns, LANES):
                payload[at : at + depth, :] = weight[:, first : first + LANES]
                at += depth
        payload[at:, :] = jnp.broadcast_to(asked, (SLOTS, LANES)).astype(BF16)


def tables(tok, neighbours, counts, shards, weights):
    points = neighbours.shape[1]
    remote = shards * SLOTS
    column = np.arange(remote)
    low = (column // SLOTS * tok).astype(np.int32)[None]
    rank = (column % SLOTS).astype(np.float32)[None]
    tri = np.tril(np.ones((points, points), np.float32), -1).astype(BF16)
    operands = (neighbours, counts, low, rank, tri) + weights
    outs = (
        jax.ShapeDtypeStruct((points, remote), F32),
        jax.ShapeDtypeStruct((1, remote), BF16),
    )
    if weights:
        rows = sum(weight.shape[0] * weight.shape[1] // LANES for weight in weights) + SLOTS
        outs += (jax.ShapeDtypeStruct((rows, LANES), BF16),)
    return pl.pallas_call(
        functools.partial(tables_kernel, tok, len(weights)),
        out_shape=outs,
        in_specs=[pl.BlockSpec(memory_space=pltpu.VMEM)] * len(operands),
        out_specs=[pl.BlockSpec(memory_space=pltpu.VMEM)] * len(outs),
        compiler_params=params(),
        cost_estimate=SMALL,
        name="tables",
    )(*operands)


def pair_attend(queries, keys, values, bias, weights_of):
    rows = queries.shape[0]
    lane = lax.broadcasted_iota(jnp.int32, (rows, LANES), 1)
    first = lane < LANES // 2
    zero = jnp.zeros_like(queries)
    both = jnp.concatenate(
        [jnp.where(first, queries, zero), jnp.where(first, zero, queries)], axis=0
    )
    scores = dot_nt(both, keys)
    scores = scores + jnp.concatenate([bias, bias], axis=0)
    top = jnp.max(scores, axis=-1, keepdims=True)
    weights = weights_of(jnp.exp(scores - top)).astype(BF16)
    summed = dot(weights, jnp.concatenate([values, jnp.ones_like(values)], axis=1))
    share = summed[:, :LANES] / summed[:, LANES:]
    return jnp.where(first, share[:rows], share[rows:]).astype(BF16)


def start_loads(spots, pieces, layout, scratch, arrived, rows, core=None):
    copies = {}
    for n, (piece, (at, half)) in enumerate(zip(pieces, layout)):
        place = scratch.at[spots[at]]
        if half is None:
            copy = pltpu.make_async_copy(piece.at[:, :, rows, :], place, arrived.at[n])
        else:
            to = half if core is None else (1 - core if half else core)
            copy = pltpu.make_async_copy(piece.at[:, rows, :], place.at[to], arrived.at[n])
        copy.start()
        copies.setdefault(at, []).append(copy)
    return copies


def wait_group(copies, at):
    for copy in copies.get(at, ()):
        copy.wait()


def lanes_of(block, depth, start, count):
    rows = block.shape[0] * block.shape[1] * depth if block.ndim == 4 else block.shape[0] * depth
    columns = [
        block[..., start + g * depth : start + (g + 1) * depth, :].reshape(rows, LANES)
        for g in range(count)
    ]
    return columns[0] if count == 1 else jnp.concatenate(columns, axis=1)


SMEM = pl.BlockSpec(memory_space=pltpu.SMEM)
VMEM_SPEC = pl.BlockSpec(memory_space=pltpu.VMEM)
ANY = pl.BlockSpec(memory_space=pl.ANY)


def projection(normed, weight, depth, per):
    return dot(normed, lanes_of(weight[...], depth, 0, per)).astype(BF16)


def project_kernel(layout, riding, normed, *refs):
    spots = ring_spots(riding)
    pieces = refs[: len(layout)]
    out, scratch, made, arrived, sent = refs[-5:]
    per = made.shape[1]
    depth = normed.shape[1] // BANDS
    copies = start_loads(spots, pieces, layout, scratch, arrived, slice(0, per * depth))
    writes = []
    for n, at in enumerate(copies):
        wait_group(copies, at)
        total = projection(normed[...], scratch.at[spots[at]], depth, per)
        for group in range(per):
            made[n, group] = total[:, group * LANES : (group + 1) * LANES]
        writes.append(
            pltpu.make_async_copy(made.at[n], out.at[pl.ds(spots[at] * per, per)], sent.at[n])
        )
        writes[-1].start()
    for write in writes:
        write.wait()


def project(riding, normed, pieces, before):
    rows, width = normed.shape
    layout = tuple(place for _, place in pieces)
    arrays = [array for array, _ in pieces]
    per = 3 * width // LANES // GROUPS
    count = len({at for at, _ in layout})
    more = [] if before is None else [before]
    return pl.pallas_call(
        functools.partial(project_kernel, layout, riding),
        out_shape=jax.ShapeDtypeStruct((GROUPS * per, rows, LANES), BF16),
        in_specs=[VMEM_SPEC] + [ANY] * (len(arrays) + len(more)),
        out_specs=ANY,
        scratch_shapes=[
            pltpu.VMEM((GROUPS, 2, 2, per * width // BANDS, LANES), BF16),
            pltpu.VMEM((count, per, rows, LANES), BF16),
            pltpu.SemaphoreType.DMA((len(arrays),)),
            pltpu.SemaphoreType.DMA((count,)),
        ],
        input_output_aliases={1 + len(arrays): 0} if more else {},
        compiler_params=params(),
        cost_estimate=SMALL,
        name="project",
    )(normed, *arrays, *more)


def attend_kernel(layout, ready, riding, normed, bias, *refs):
    spots = ring_spots(riding)
    pieces = refs[: len(layout)]
    made, attended, scratch, projected, arrived, loaded = refs[len(layout) :]
    width = normed.shape[1]
    depth = width // BANDS
    per = projected.shape[0] // GROUPS
    copies = start_loads(spots, pieces, layout, scratch, arrived, slice(0, per * depth))
    reads = []
    for n, at in enumerate(ready):
        place = pl.ds(spots[at] * per, per)
        reads.append(pltpu.make_async_copy(made.at[place], projected.at[place], loaded.at[n]))
        reads[-1].start()
    for at in copies:
        wait_group(copies, at)
        total = projection(normed[...], scratch.at[spots[at]], depth, per)
        for group in range(per):
            projected[spots[at] * per + group] = total[:, group * LANES : (group + 1) * LANES]
    for read in reads:
        read.wait()
    pairs = width // LANES
    scale = BF16(1.0 / math.sqrt(width // HEADS))
    for pair in range(pairs):
        for block in range(bias.shape[0]):
            at = block * HALF
            attended[at : at + HALF, pair * LANES : (pair + 1) * LANES] = pair_attend(
                projected[pair, at + HALF : at + 2 * HALF, :] * scale,
                projected[pairs + pair, at : at + 3 * HALF, :],
                projected[2 * pairs + pair, at : at + 3 * HALF, :],
                bias[block],
                lambda weights: weights,
            )


def attend(riding, normed, bias, pieces, made, ready):
    rows, width = normed.shape
    tok = rows - 2 * HALF
    layout = tuple(place for _, place in pieces)
    arrays = [array for array, _ in pieces]
    per = made.shape[0] // GROUPS
    return pl.pallas_call(
        functools.partial(attend_kernel, layout, ready, riding),
        out_shape=jax.ShapeDtypeStruct((tok, width), BF16),
        in_specs=[VMEM_SPEC, VMEM_SPEC] + [ANY] * (len(arrays) + 1),
        out_specs=VMEM_SPEC,
        scratch_shapes=[
            pltpu.VMEM((GROUPS, 2, 2, per * width // BANDS, LANES), BF16),
            pltpu.VMEM(made.shape, BF16),
            pltpu.SemaphoreType.DMA((len(arrays),)),
            pltpu.SemaphoreType.DMA((len(ready),)),
        ],
        compiler_params=params(),
        cost_estimate=SMALL,
        name="attend",
    )(normed, bias, *arrays, made)


def picked_rows(place, ids, spots, rows, asked, arrived):
    tok = rows.shape[0]
    if spots is None:
        which = ids[...]
    else:
        for at in range(GROUPS):
            asked[pl.ds(spots[at] * SLOTS, SLOTS), :] = jnp.broadcast_to(
                arrived[at, 0:1, :].astype(F32), (SLOTS, LANES)
            )
        count = GROUPS * SLOTS
        lane = lax.broadcasted_iota(jnp.int32, (count, LANES), 1)
        slot = lax.broadcasted_iota(jnp.int32, (count, LANES), 0) % SLOTS
        mine = jnp.where(lane == place[0] * SLOTS + slot, asked[...], 0.0)
        which = jnp.sum(mine, axis=1, keepdims=True).astype(jnp.int32)
    here = lax.broadcasted_iota(jnp.int32, (which.shape[0], tok), 1)
    return dot((which == here).astype(BF16), rows).astype(BF16)


def chunked(values, depth):
    return jnp.concatenate([values[:, b * depth : (b + 1) * depth] for b in CHUNKS], axis=1)


def mix_kernel(layout, riding, states, gain, *refs):
    place, spots = here_at(riding), ring_spots(riding)
    attended, refs = refs[0], refs[1:]
    ids = None
    if not riding:
        ids, refs = refs[0], refs[1:]
    pieces = refs[: len(layout)]
    decoded, found, mixed, scratch, asked, notes, arrived, noted = refs[len(layout) :]
    width = states.shape[1]
    depth = width // BANDS
    start = 3 * width // GROUPS // LANES * depth
    copies = start_loads(spots, pieces, layout, scratch, arrived, slice(start, start + depth))
    reads = []
    if riding:
        for piece, (at, core) in zip(pieces, layout):
            if core == 0:
                end = piece.shape[-2]
                reads.append(
                    pltpu.make_async_copy(
                        piece.at[0, end - SLOTS : end, :], notes.at[at], noted.at[at]
                    )
                )
                reads[-1].start()
    inputs = own_first(attended[...], place[1], depth)
    for at in range(GROUPS):
        wait_group(copies, at)
    for at in range(0, GROUPS, 2):
        columns = slice(at * LANES, (at + 2) * LANES)
        weight = [lanes_of(scratch[at + n], depth, 0, 1) for n in range(2)]
        total = dot(inputs, jnp.concatenate(weight, axis=1))
        mixed[:, columns] = (states[:, columns].astype(F32) + total).astype(BF16)
    for read in reads:
        read.wait()
    rows = chunked(layer_norm(mixed[...], gain[...]), depth)
    decoded[...] = rows
    found[...] = picked_rows(place, ids, spots if riding else None, rows, asked, notes)


def mix(states, attended, gain, ids, pieces, layout, shards):
    tok, width = states.shape
    more = [] if ids is None else [ids]
    return pl.pallas_call(
        functools.partial(mix_kernel, layout, ids is None),
        out_shape=(
            jax.ShapeDtypeStruct((tok, width), BF16),
            jax.ShapeDtypeStruct((shards * SLOTS, width), BF16),
        ),
        in_specs=[VMEM_SPEC] * (3 + len(more)) + [ANY] * len(pieces),
        out_specs=(VMEM_SPEC, VMEM_SPEC),
        scratch_shapes=[
            pltpu.VMEM((tok, width), BF16),
            pltpu.VMEM((GROUPS, 2, 2, width // BANDS, LANES), BF16),
            pltpu.VMEM((GROUPS * SLOTS, LANES), F32),
            pltpu.VMEM((GROUPS, SLOTS, LANES), BF16),
            pltpu.SemaphoreType.DMA((len(pieces),)),
            pltpu.SemaphoreType.DMA((GROUPS,)),
        ],
        compiler_params=params(),
        cost_estimate=SMALL,
        name="mix",
    )(states, gain, attended, *more, *pieces)


def decode_kernel(layout, each, riding, queries, decoded, fetched, here, there, *refs):
    spots = ring_spots(riding)
    pieces = refs[: len(layout)]
    fields, scratch, table, arrived = refs[len(layout) :]
    points, width = queries.shape
    depth = width // BANDS
    per = 2 * width // GROUPS // LANES
    kept = scratch.shape[3]
    copies = start_loads(
        spots, pieces, layout, scratch, arrived, slice(0, kept), spots[GROUPS]
    )
    inputs = jnp.concatenate([decoded[...], fetched[...]], axis=0)
    for at in range(GROUPS):
        wait_group(copies, at)
        spot = spots[at]
        total = dot(inputs, lanes_of(scratch[spot], depth, 0, per)).astype(BF16)
        for group in range(per):
            table[spot * per + group] = total[:, group * LANES : (group + 1) * LANES]

    pairs = width // LANES
    scale = BF16(1.0 / math.sqrt(width // HEADS))
    times = jnp.concatenate([here[...], there[...]], axis=1)
    bias = jnp.where(times > 0, 0.0, NEG)
    both = jnp.concatenate([times, times], axis=0)
    rows = []
    for pair in range(pairs):
        rows.append(
            pair_attend(
                queries[:, pair * LANES : (pair + 1) * LANES] * scale,
                table[pair],
                table[pairs + pair],
                bias,
                lambda weights: weights * both,
            )
        )
    gridded = jnp.concatenate(rows, axis=1)
    start = per * depth
    halves = depth // LANES
    height = (kept - start) // halves
    padded = jnp.zeros((GROUPS * height, points), F32)
    for chunk, band in enumerate(CHUNKS):
        for half in range(halves):
            at = start + half * height
            weight = scratch[:, chunk // 2, chunk % 2, at : at + height, :]
            first = band * depth + half * LANES
            padded += dot_nt(
                weight.reshape(GROUPS * height, LANES), gridded[:, first : first + LANES]
            )
    parts = [padded[group * height : group * height + each] for group in range(GROUPS)]
    fields[...] = jnp.concatenate(parts, axis=0).astype(BF16)


def decode(riding, queries, decoded, fetched, here, there, pieces, layout, outputs):
    points, width = queries.shape
    height = pieces[0].shape[-2]
    rows = decoded.shape[0] + fetched.shape[0]
    return pl.pallas_call(
        functools.partial(decode_kernel, layout, outputs // GROUPS, riding),
        out_shape=jax.ShapeDtypeStruct((outputs, points), BF16),
        in_specs=[VMEM_SPEC] * 5 + [ANY] * len(pieces),
        out_specs=VMEM_SPEC,
        scratch_shapes=[
            pltpu.VMEM((GROUPS, 2, 2, height, LANES), BF16),
            pltpu.VMEM((2 * width // LANES, rows, LANES), BF16),
            pltpu.SemaphoreType.DMA((len(pieces),)),
        ],
        compiler_params=params(),
        cost_estimate=SMALL,
        name="decode",
    )(queries, decoded, fetched, here, there, *pieces)


def stacked(*weights):
    parts = []
    for weight in weights:
        for at in range(0, weight.shape[-1], LANES):
            parts.append(weight[..., at : at + LANES])
    return jnp.concatenate(parts, axis=-2)


def pair_x(block, gate=None):
    if gate is not None:
        block, _ = lax.optimization_barrier((block, gate))
    other = lax.ppermute(block, "band", [(i, i ^ 2) for i in range(BANDS)])
    low = lax.axis_index("band") < 2
    return jnp.stack([jnp.where(low, block, other), jnp.where(low, other, block)])


def pair_core(block):
    other = swap_core(block)
    low = lax.axis_index("band") % 2 == 0
    return jnp.stack([jnp.where(low, block, other), jnp.where(low, other, block)])


def carry(block):
    pairs = []
    for i in range(GROUPS):
        here, there = RING[i] * BANDS, RING[(i + 1) % GROUPS] * BANDS
        for x in range(2):
            pairs.append((here + 2 * x, there + 2 * x))
            pairs.append((there + 2 * x + 1, here + 2 * x + 1))
    return lax.ppermute(block, ("seq", "band"), pairs)


def swap_core(block):
    return lax.ppermute(block, "band", [(i, i ^ 1) for i in range(BANDS)])


def chain_step(chains, step, gate=None):
    if gate is not None:
        *chains, _ = lax.optimization_barrier((*chains, gate))
    chains = [carry(block) for block in chains]
    pieces = []
    for half, block in enumerate(chains):
        pieces.append((block, (step, half)))
        pieces.append((swap_core(block), (GROUPS - step, 1 - half)))
    return chains, pieces


def ring_step(block, step, gate=None):
    if gate is not None:
        block, _ = lax.optimization_barrier((block, gate))
    block = carry(block)
    return block, [(block, (step, None)), (swap_core(block), (GROUPS - step, None))]


def last_step(block):
    half = lax.dynamic_index_in_dim(block, lax.axis_index("band") % 2, 0, keepdims=False)
    half = carry(half)
    return [(half, (GROUPS // 2, 0)), (swap_core(half), (GROUPS // 2, 1))]


def whole_blocks(*weights):
    parts = []
    for weight, height in weights:
        weight = lax.all_gather(weight, "seq", axis=1, tiled=True)
        weight = lax.all_gather(weight, "band", axis=0, tiled=True)
        depth, columns = weight.shape[0] // BANDS, weight.shape[1] // GROUPS
        weight = weight.reshape(2, 2, depth, GROUPS, columns).transpose(3, 1, 0, 2, 4)
        if height:
            weight = jnp.pad(
                weight.swapaxes(-1, -2), ((0, 0),) * 3 + ((0, height - columns), (0, 0))
            )
        parts.append(weight)
    return stacked(*parts)


def local(
    tokens, ln_gain, w_qkv, w_out, dec_gain, w_kv, w_final, reach, grid_query, neighbours, counts
):
    states = tokens[0]
    tok, width = states.shape
    shards, bands = lax.axis_size("seq"), lax.axis_size("band")
    outputs = w_final.shape[1] * shards
    height = -(-outputs // GROUPS // 16) * 16
    riding = (shards, bands) == (GROUPS, BANDS)
    up = [(i, i + 1) for i in range(shards - 1)]
    down = [(i + 1, i) for i in range(shards - 1)]
    left = lax.ppermute(states[tok - HALF :], "seq", up)
    right = lax.ppermute(states[:HALF], "seq", down)
    slots = (neighbours.T, counts.reshape(1, -1))
    there, requested, *payload = tables(tok, *slots, shards, (w_qkv, w_out) if riding else ())
    normed, bias, here = prepare(
        tok * shards, riding, left, states, right, ln_gain.reshape(1, width),
        reach.reshape(1, tok), *slots,
    )
    if riding:
        mine = pair_x(payload[0])
        mine, _, _ = lax.optimization_barrier((mine, left, right))
        other = swap_core(mine)
        pieces = [(mine, (0, 0)), (other, (0, 1))]
        chains, more = chain_step([mine, other], 1)
        pieces += more
        final = jnp.pad(w_final.T, ((0, height - w_final.shape[1]), (0, 0)))
        second = pair_core(pair_x(stacked(w_kv, final), chains[0]))
        later = [(second, (0, None))]
        chains[1], _ = lax.optimization_barrier((chains[1], normed))
        chains, more = chain_step(chains, 2)
        pieces += more
        normed, _ = lax.optimization_barrier((normed, chains[1]))
        made = project(riding, normed, pieces[:6], None)
        chains, more = chain_step(chains, 3)
        pieces += more
        end, _, _ = lax.optimization_barrier((chains[0], chains[1], made))
        end = carry(end)
        second, *_ = lax.optimization_barrier((second, chains[1], made, pieces[7][0], pieces[9][0]))
        later = [(second, (0, None))]
        block, more = ring_step(second, 1)
        later += more
        made = project(riding, normed, pieces[6:10], made)
        handed, _ = lax.optimization_barrier((end, made))
        pieces += [(end, (GROUPS // 2, 0)), (swap_core(handed), (GROUPS // 2, 1))]
        block, more = ring_step(block, 2, [pieces[n][0] for n in (11, 13, 15)])
        later += more
        attended = attend(riding, normed, bias, pieces[10:], made, (0, 1, 7, 2, 6))
        block, more = ring_step(block, 3, attended)
        later += more
        ids = None
    else:
        block = whole_blocks((w_qkv, 0), (w_out, 0))
        block = jnp.pad(block, ((0, 0),) * 3 + ((0, SLOTS), (0, 0)))
        pieces = [(block[at, half], (at, half)) for at in range(GROUPS) for half in range(2)]
        block = whole_blocks((w_kv, 0), (w_final, height))
        later = [(block[at], (at, None)) for at in range(GROUPS)]
        made = project(riding, normed, pieces[:6], None)
        attended = attend(riding, normed, bias, pieces[6:], made, tuple(range(3)))
        ids = lax.all_to_all(
            requested.reshape(shards, SLOTS).astype(jnp.int32), "seq", 0, 0, tiled=True
        ).reshape(shards * SLOTS, 1)
    layout = tuple(at for _, at in pieces)
    pieces = [piece for piece, _ in pieces]
    decoded, found = mix(
        states, attended, dec_gain.reshape(1, width), ids, pieces, layout, shards
    )
    fetched = lax.all_to_all(
        found.reshape(shards, SLOTS, width), "seq", split_axis=0, concat_axis=0, tiled=True
    )
    if riding:
        block, _ = lax.optimization_barrier((block, found))
        later += last_step(block)
    layout = tuple(at for _, at in later)
    pieces = [piece for piece, _ in later]
    fields = decode(
        riding, grid_query[0], decoded, fetched.reshape(shards * SLOTS, width), here, there,
        pieces, layout, outputs,
    )
    return fields[None]


def solution(mesh):
    return jax.shard_map(
        local,
        mesh=mesh,
        in_specs=(
            P("band", "seq", None),
            P(),
            P("band", "seq"),
            P("band", "seq"),
            P(),
            P("band", "seq"),
            P("band", "seq"),
            P("seq"),
            P("band", "seq", None),
            P("seq", None),
            P("seq"),
        ),
        out_specs=P("band", None, "seq"),
        check_vma=False,
    )
```

```python
import functools
import math

import jax
import jax.numpy as jnp
import numpy as np
from jax import lax
from jax.experimental import pallas as pl
from jax.experimental.pallas import tpu as pltpu
from jax.sharding import PartitionSpec as P

HEADS = 16
HALF = 128
C = 12
SLOTS = 16
EPSILON = 1e-05
NEG = -1e30
LANES = 128
GROUPS = 8
BANDS = 4
CHUNKS = (0, 2, 1, 3)
RING = (0, 2, 4, 6, 7, 5, 3, 1)
VMEM = 62 * 1024 * 1024
SMALL = pl.CostEstimate(flops=1000, bytes_accessed=1000, transcendentals=0)
F32 = jnp.float32
BF16 = jnp.bfloat16


def dot(a, b):
    return jnp.dot(a, b, preferred_element_type=F32)


def dot_nt(a, b):
    return lax.dot_general(a, b, (((1,), (1,)), ((), ())), preferred_element_type=F32)


def layer_norm(values, gain):
    values = values.astype(F32)
    centred = values - jnp.mean(values, axis=-1, keepdims=True)
    spread = jnp.mean(centred * centred, axis=-1, keepdims=True)
    return (centred * lax.rsqrt(spread + EPSILON) * gain).astype(BF16)


def here_at(riding):
    return lax.axis_index("seq"), (lax.axis_index("band") % 2 if riding else 0)


def ring_spots(riding):
    if not riding:
        return list(range(GROUPS)) + [0]
    seq, core = here_at(True)
    at_ring = jnp.where(seq % 2 == 0, seq // 2, GROUPS - 1 - seq // 2)
    turn = jnp.where(core == 0, GROUPS - 1, 1)
    spots = []
    for at in range(GROUPS):
        step = (at_ring + turn * at) % GROUPS
        spots.append(jnp.where(step < GROUPS // 2, 2 * step, 2 * GROUPS - 1 - 2 * step))
    return spots + [core]


def params(**more):
    return pltpu.CompilerParams(vmem_limit_bytes=VMEM, **more)


def full_spec(shape):
    return pl.BlockSpec(shape, lambda *_: (0,) * len(shape))


def own_first(rows, core, depth):
    parts = [rows[:, b * depth : (b + 1) * depth] for b in range(BANDS)]
    order = ((0, 1), (2, 3), (1, 0), (3, 2))
    return jnp.concatenate([jnp.where(core == 0, parts[a], parts[b]) for a, b in order], axis=1)


def as_column(row):
    return jnp.broadcast_to(row, (8, row.shape[1])).T[:, :1]


def prepare_kernel(
    total, riding, left, own, right, gain, reach, neighbours, counts, normed, bias, multiplicity
):
    place = here_at(riding)
    tok = own.shape[0]
    depth = own.shape[1] // BANDS
    for at, part in ((0, left), (HALF, own), (HALF + tok, right)):
        rows = layer_norm(part[...], gain[...])
        normed[at : at + part.shape[0], :] = own_first(rows, place[1], depth)

    first = place[0] * tok
    span = 3 * HALF
    row = lax.broadcasted_iota(jnp.int32, (HALF, span), 0)
    col = lax.broadcasted_iota(jnp.int32, (HALF, span), 1)
    away = jnp.abs(row + HALF - col)
    limit = as_column(reach[...])
    for block in range(tok // HALF):
        key = first + (block - 1) * HALF + col
        allowed = (away <= limit[block * HALF : (block + 1) * HALF, :]) & (key >= 0) & (key < total)
        bias[block] = jnp.where(allowed, 0.0, NEG)

    ids = neighbours[...].T
    used = as_column(counts[...])
    mesh = lax.broadcasted_iota(jnp.int32, multiplicity.shape, 1) + first
    here = jnp.zeros(multiplicity.shape, F32)
    for slot in range(ids.shape[1]):
        here += ((ids[:, slot : slot + 1] == mesh) & (slot < used)).astype(F32)
    multiplicity[...] = here


def prepare(total, riding, left, own, right, gain, reach, neighbours, counts):
    tok, width = own.shape
    operands = (left, own, right, gain, reach, neighbours, counts)
    outs = (
        jax.ShapeDtypeStruct((tok + 2 * HALF, width), BF16),
        jax.ShapeDtypeStruct((tok // HALF, HALF, 3 * HALF), F32),
        jax.ShapeDtypeStruct((neighbours.shape[1], tok), F32),
    )
    return pl.pallas_call(
        functools.partial(prepare_kernel, total, riding),
        out_shape=outs,
        in_specs=[pl.BlockSpec(memory_space=pltpu.VMEM)] * len(operands),
        out_specs=[pl.BlockSpec(memory_space=pltpu.VMEM)] * len(outs),
        compiler_params=params(),
        cost_estimate=SMALL,
        name="prepare",
    )(*operands)


def tables_kernel(tok, count, neighbours, counts, low, rank, tri, *refs):
    weights, (multiplicity, requested) = refs[:count], refs[count : count + 2]
    first = lax.axis_index("seq") * tok
    slots = neighbours.shape[0]
    ids = neighbours[...].T
    used = as_column(counts[...])
    start = low[...]
    elsewhere = start != first
    hits = []
    for slot in range(slots):
        which = ids[:, slot : slot + 1]
        hits.append(
            ((which >= start) & (which < start + tok) & (slot < used) & elsewhere).astype(F32)
        )
    running = dot(tri[...], sum(hits).astype(BF16))
    order = rank[...]
    asked = jnp.zeros(hits[0].shape, F32)
    there = jnp.zeros(hits[0].shape, F32)
    for slot in range(slots):
        mine = jnp.where(running == order, hits[slot], 0.0)
        there += mine
        offset = (ids[:, slot : slot + 1] - start).astype(F32)
        asked += jnp.where(mine > 0, offset, 0.0)
        running += hits[slot]
    multiplicity[...] = there
    asked = jnp.sum(asked, axis=0, keepdims=True)
    requested[...] = asked.astype(BF16)
    if weights:
        payload = refs[-1]
        at = 0
        for weight in weights:
            depth, columns = weight.shape
            for first in range(0, columns, LANES):
                payload[at : at + depth, :] = weight[:, first : first + LANES]
                at += depth
        payload[at:, :] = jnp.broadcast_to(asked, (SLOTS, LANES)).astype(BF16)


def tables(tok, neighbours, counts, shards, weights):
    points = neighbours.shape[1]
    remote = shards * SLOTS
    column = np.arange(remote)
    low = (column // SLOTS * tok).astype(np.int32)[None]
    rank = (column % SLOTS).astype(np.float32)[None]
    tri = np.tril(np.ones((points, points), np.float32), -1).astype(BF16)
    operands = (neighbours, counts, low, rank, tri) + weights
    outs = (
        jax.ShapeDtypeStruct((points, remote), F32),
        jax.ShapeDtypeStruct((1, remote), BF16),
    )
    if weights:
        rows = sum(weight.shape[0] * weight.shape[1] // LANES for weight in weights) + SLOTS
        outs += (jax.ShapeDtypeStruct((rows, LANES), BF16),)
    return pl.pallas_call(
        functools.partial(tables_kernel, tok, len(weights)),
        out_shape=outs,
        in_specs=[pl.BlockSpec(memory_space=pltpu.VMEM)] * len(operands),
        out_specs=[pl.BlockSpec(memory_space=pltpu.VMEM)] * len(outs),
        compiler_params=params(),
        cost_estimate=SMALL,
        name="tables",
    )(*operands)


def pair_attend(queries, keys, values, bias, weights_of):
    rows = queries.shape[0]
    lane = lax.broadcasted_iota(jnp.int32, (rows, LANES), 1)
    first = lane < LANES // 2
    zero = jnp.zeros_like(queries)
    both = jnp.concatenate(
        [jnp.where(first, queries, zero), jnp.where(first, zero, queries)], axis=0
    )
    scores = dot_nt(both, keys)
    scores = scores + jnp.concatenate([bias, bias], axis=0)
    top = jnp.max(scores, axis=-1, keepdims=True)
    weights = weights_of(jnp.exp(scores - top)).astype(BF16)
    summed = dot(weights, jnp.concatenate([values, jnp.ones_like(values)], axis=1))
    share = summed[:, :LANES] / summed[:, LANES:]
    return jnp.where(first, share[:rows], share[rows:]).astype(BF16)


def start_loads(spots, pieces, layout, scratch, arrived, rows, core=None):
    copies = {}
    for n, (piece, (at, half)) in enumerate(zip(pieces, layout)):
        place = scratch.at[spots[at]]
        if half is None:
            copy = pltpu.make_async_copy(piece.at[:, :, rows, :], place, arrived.at[n])
        else:
            to = half if core is None else (1 - core if half else core)
            copy = pltpu.make_async_copy(piece.at[:, rows, :], place.at[to], arrived.at[n])
        copy.start()
        copies.setdefault(at, []).append(copy)
    return copies


def wait_group(copies, at):
    for copy in copies.get(at, ()):
        copy.wait()


def lanes_of(block, depth, start, count):
    rows = block.shape[0] * block.shape[1] * depth if block.ndim == 4 else block.shape[0] * depth
    columns = [
        block[..., start + g * depth : start + (g + 1) * depth, :].reshape(rows, LANES)
        for g in range(count)
    ]
    return columns[0] if count == 1 else jnp.concatenate(columns, axis=1)


SMEM = pl.BlockSpec(memory_space=pltpu.SMEM)
VMEM_SPEC = pl.BlockSpec(memory_space=pltpu.VMEM)
ANY = pl.BlockSpec(memory_space=pl.ANY)


def projection(normed, weight, depth, per):
    return dot(normed, lanes_of(weight[...], depth, 0, per)).astype(BF16)


def project_kernel(layout, riding, normed, *refs):
    spots = ring_spots(riding)
    pieces = refs[: len(layout)]
    out, scratch, made, arrived, sent = refs[-5:]
    per = made.shape[1]
    depth = normed.shape[1] // BANDS
    copies = start_loads(spots, pieces, layout, scratch, arrived, slice(0, per * depth))
    writes = []
    for n, at in enumerate(copies):
        wait_group(copies, at)
        total = projection(normed[...], scratch.at[spots[at]], depth, per)
        for group in range(per):
            made[n, group] = total[:, group * LANES : (group + 1) * LANES]
        writes.append(
            pltpu.make_async_copy(made.at[n], out.at[pl.ds(spots[at] * per, per)], sent.at[n])
        )
        writes[-1].start()
    for write in writes:
        write.wait()


def project(riding, normed, pieces, before):
    rows, width = normed.shape
    layout = tuple(place for _, place in pieces)
    arrays = [array for array, _ in pieces]
    per = 3 * width // LANES // GROUPS
    count = len({at for at, _ in layout})
    more = [] if before is None else [before]
    return pl.pallas_call(
        functools.partial(project_kernel, layout, riding),
        out_shape=jax.ShapeDtypeStruct((GROUPS * per, rows, LANES), BF16),
        in_specs=[VMEM_SPEC] + [ANY] * (len(arrays) + len(more)),
        out_specs=ANY,
        scratch_shapes=[
            pltpu.VMEM((GROUPS, 2, 2, per * width // BANDS, LANES), BF16),
            pltpu.VMEM((count, per, rows, LANES), BF16),
            pltpu.SemaphoreType.DMA((len(arrays),)),
            pltpu.SemaphoreType.DMA((count,)),
        ],
        input_output_aliases={1 + len(arrays): 0} if more else {},
        compiler_params=params(),
        cost_estimate=SMALL,
        name="project",
    )(normed, *arrays, *more)


def attend_kernel(layout, ready, riding, normed, bias, *refs):
    spots = ring_spots(riding)
    pieces = refs[: len(layout)]
    made, attended, scratch, projected, arrived, loaded = refs[len(layout) :]
    width = normed.shape[1]
    depth = width // BANDS
    per = projected.shape[0] // GROUPS
    copies = start_loads(spots, pieces, layout, scratch, arrived, slice(0, per * depth))
    reads = []
    for n, at in enumerate(ready):
        place = pl.ds(spots[at] * per, per)
        reads.append(pltpu.make_async_copy(made.at[place], projected.at[place], loaded.at[n]))
        reads[-1].start()
    for at in copies:
        wait_group(copies, at)
        total = projection(normed[...], scratch.at[spots[at]], depth, per)
        for group in range(per):
            projected[spots[at] * per + group] = total[:, group * LANES : (group + 1) * LANES]
    for read in reads:
        read.wait()
    pairs = width // LANES
    scale = BF16(1.0 / math.sqrt(width // HEADS))
    for pair in range(pairs):
        for block in range(bias.shape[0]):
            at = block * HALF
            attended[at : at + HALF, pair * LANES : (pair + 1) * LANES] = pair_attend(
                projected[pair, at + HALF : at + 2 * HALF, :] * scale,
                projected[pairs + pair, at : at + 3 * HALF, :],
                projected[2 * pairs + pair, at : at + 3 * HALF, :],
                bias[block],
                lambda weights: weights,
            )


def attend(riding, normed, bias, pieces, made, ready):
    rows, width = normed.shape
    tok = rows - 2 * HALF
    layout = tuple(place for _, place in pieces)
    arrays = [array for array, _ in pieces]
    per = made.shape[0] // GROUPS
    return pl.pallas_call(
        functools.partial(attend_kernel, layout, ready, riding),
        out_shape=jax.ShapeDtypeStruct((tok, width), BF16),
        in_specs=[VMEM_SPEC, VMEM_SPEC] + [ANY] * (len(arrays) + 1),
        out_specs=VMEM_SPEC,
        scratch_shapes=[
            pltpu.VMEM((GROUPS, 2, 2, per * width // BANDS, LANES), BF16),
            pltpu.VMEM(made.shape, BF16),
            pltpu.SemaphoreType.DMA((len(arrays),)),
            pltpu.SemaphoreType.DMA((len(ready),)),
        ],
        compiler_params=params(),
        cost_estimate=SMALL,
        name="attend",
    )(normed, bias, *arrays, made)


def picked_rows(place, ids, spots, rows, asked, arrived):
    tok = rows.shape[0]
    if spots is None:
        which = ids[...]
    else:
        for at in range(GROUPS):
            asked[pl.ds(spots[at] * SLOTS, SLOTS), :] = jnp.broadcast_to(
                arrived[at, 0:1, :].astype(F32), (SLOTS, LANES)
            )
        count = GROUPS * SLOTS
        lane = lax.broadcasted_iota(jnp.int32, (count, LANES), 1)
        slot = lax.broadcasted_iota(jnp.int32, (count, LANES), 0) % SLOTS
        mine = jnp.where(lane == place[0] * SLOTS + slot, asked[...], 0.0)
        which = jnp.sum(mine, axis=1, keepdims=True).astype(jnp.int32)
    here = lax.broadcasted_iota(jnp.int32, (which.shape[0], tok), 1)
    return dot((which == here).astype(BF16), rows).astype(BF16)


def chunked(values, depth):
    return jnp.concatenate([values[:, b * depth : (b + 1) * depth] for b in CHUNKS], axis=1)


def mix_kernel(layout, riding, states, gain, *refs):
    place, spots = here_at(riding), ring_spots(riding)
    attended, refs = refs[0], refs[1:]
    ids = None
    if not riding:
        ids, refs = refs[0], refs[1:]
    pieces = refs[: len(layout)]
    decoded, found, mixed, scratch, asked, notes, arrived, noted = refs[len(layout) :]
    width = states.shape[1]
    depth = width // BANDS
    start = 3 * width // GROUPS // LANES * depth
    copies = start_loads(spots, pieces, layout, scratch, arrived, slice(start, start + depth))
    reads = []
    if riding:
        for piece, (at, core) in zip(pieces, layout):
            if core == 0:
                end = piece.shape[-2]
                reads.append(
                    pltpu.make_async_copy(
                        piece.at[0, end - SLOTS : end, :], notes.at[at], noted.at[at]
                    )
                )
                reads[-1].start()
    inputs = own_first(attended[...], place[1], depth)
    for at in range(GROUPS):
        wait_group(copies, at)
    for at in range(0, GROUPS, 2):
        columns = slice(at * LANES, (at + 2) * LANES)
        weight = [lanes_of(scratch[at + n], depth, 0, 1) for n in range(2)]
        total = dot(inputs, jnp.concatenate(weight, axis=1))
        mixed[:, columns] = (states[:, columns].astype(F32) + total).astype(BF16)
    for read in reads:
        read.wait()
    rows = chunked(layer_norm(mixed[...], gain[...]), depth)
    decoded[...] = rows
    found[...] = picked_rows(place, ids, spots if riding else None, rows, asked, notes)


def mix(states, attended, gain, ids, pieces, layout, shards):
    tok, width = states.shape
    more = [] if ids is None else [ids]
    return pl.pallas_call(
        functools.partial(mix_kernel, layout, ids is None),
        out_shape=(
            jax.ShapeDtypeStruct((tok, width), BF16),
            jax.ShapeDtypeStruct((shards * SLOTS, width), BF16),
        ),
        in_specs=[VMEM_SPEC] * (3 + len(more)) + [ANY] * len(pieces),
        out_specs=(VMEM_SPEC, VMEM_SPEC),
        scratch_shapes=[
            pltpu.VMEM((tok, width), BF16),
            pltpu.VMEM((GROUPS, 2, 2, width // BANDS, LANES), BF16),
            pltpu.VMEM((GROUPS * SLOTS, LANES), F32),
            pltpu.VMEM((GROUPS, SLOTS, LANES), BF16),
            pltpu.SemaphoreType.DMA((len(pieces),)),
            pltpu.SemaphoreType.DMA((GROUPS,)),
        ],
        compiler_params=params(),
        cost_estimate=SMALL,
        name="mix",
    )(states, gain, attended, *more, *pieces)


def decode_kernel(layout, each, riding, queries, decoded, fetched, here, there, *refs):
    spots = ring_spots(riding)
    pieces = refs[: len(layout)]
    fields, scratch, table, arrived = refs[len(layout) :]
    points, width = queries.shape
    depth = width // BANDS
    per = 2 * width // GROUPS // LANES
    kept = scratch.shape[3]
    copies = start_loads(
        spots, pieces, layout, scratch, arrived, slice(0, kept), spots[GROUPS]
    )
    inputs = jnp.concatenate([decoded[...], fetched[...]], axis=0)
    for at in range(GROUPS):
        wait_group(copies, at)
        spot = spots[at]
        total = dot(inputs, lanes_of(scratch[spot], depth, 0, per)).astype(BF16)
        for group in range(per):
            table[spot * per + group] = total[:, group * LANES : (group + 1) * LANES]

    pairs = width // LANES
    scale = BF16(1.0 / math.sqrt(width // HEADS))
    times = jnp.concatenate([here[...], there[...]], axis=1)
    bias = jnp.where(times > 0, 0.0, NEG)
    both = jnp.concatenate([times, times], axis=0)
    rows = []
    for pair in range(pairs):
        rows.append(
            pair_attend(
                queries[:, pair * LANES : (pair + 1) * LANES] * scale,
                table[pair],
                table[pairs + pair],
                bias,
                lambda weights: weights * both,
            )
        )
    gridded = jnp.concatenate(rows, axis=1)
    start = per * depth
    halves = depth // LANES
    height = (kept - start) // halves
    padded = jnp.zeros((GROUPS * height, points), F32)
    for chunk, band in enumerate(CHUNKS):
        for half in range(halves):
            at = start + half * height
            weight = scratch[:, chunk // 2, chunk % 2, at : at + height, :]
            first = band * depth + half * LANES
            padded += dot_nt(
                weight.reshape(GROUPS * height, LANES), gridded[:, first : first + LANES]
            )
    parts = [padded[group * height : group * height + each] for group in range(GROUPS)]
    fields[...] = jnp.concatenate(parts, axis=0).astype(BF16)


def decode(riding, queries, decoded, fetched, here, there, pieces, layout, outputs):
    points, width = queries.shape
    height = pieces[0].shape[-2]
    rows = decoded.shape[0] + fetched.shape[0]
    return pl.pallas_call(
        functools.partial(decode_kernel, layout, outputs // GROUPS, riding),
        out_shape=jax.ShapeDtypeStruct((outputs, points), BF16),
        in_specs=[VMEM_SPEC] * 5 + [ANY] * len(pieces),
        out_specs=VMEM_SPEC,
        scratch_shapes=[
            pltpu.VMEM((GROUPS, 2, 2, height, LANES), BF16),
            pltpu.VMEM((2 * width // LANES, rows, LANES), BF16),
            pltpu.SemaphoreType.DMA((len(pieces),)),
        ],
        compiler_params=params(),
        cost_estimate=SMALL,
        name="decode",
    )(queries, decoded, fetched, here, there, *pieces)


def stacked(*weights):
    parts = []
    for weight in weights:
        for at in range(0, weight.shape[-1], LANES):
            parts.append(weight[..., at : at + LANES])
    return jnp.concatenate(parts, axis=-2)


def pair_x(block, gate=None):
    if gate is not None:
        block, _ = lax.optimization_barrier((block, gate))
    other = lax.ppermute(block, "band", [(i, i ^ 2) for i in range(BANDS)])
    low = lax.axis_index("band") < 2
    return jnp.stack([jnp.where(low, block, other), jnp.where(low, other, block)])


def pair_core(block):
    other = swap_core(block)
    low = lax.axis_index("band") % 2 == 0
    return jnp.stack([jnp.where(low, block, other), jnp.where(low, other, block)])


def carry(block):
    pairs = []
    for i in range(GROUPS):
        here, there = RING[i] * BANDS, RING[(i + 1) % GROUPS] * BANDS
        for x in range(2):
            pairs.append((here + 2 * x, there + 2 * x))
            pairs.append((there + 2 * x + 1, here + 2 * x + 1))
    return lax.ppermute(block, ("seq", "band"), pairs)


def swap_core(block):
    return lax.ppermute(block, "band", [(i, i ^ 1) for i in range(BANDS)])


def chain_step(chains, step, gate=None):
    if gate is not None:
        *chains, _ = lax.optimization_barrier((*chains, gate))
    chains = [carry(block) for block in chains]
    pieces = []
    for half, block in enumerate(chains):
        pieces.append((block, (step, half)))
        pieces.append((swap_core(block), (GROUPS - step, 1 - half)))
    return chains, pieces


def ring_step(block, step, gate=None):
    if gate is not None:
        block, _ = lax.optimization_barrier((block, gate))
    block = carry(block)
    return block, [(block, (step, None)), (swap_core(block), (GROUPS - step, None))]


def last_step(block, gate):
    half = lax.dynamic_index_in_dim(block, lax.axis_index("band") % 2, 0, keepdims=False)
    half = carry(half)
    handed, _ = lax.optimization_barrier((half, gate))
    return [(half, (GROUPS // 2, 0)), (swap_core(handed), (GROUPS // 2, 1))]


def whole_blocks(*weights):
    parts = []
    for weight, height in weights:
        weight = lax.all_gather(weight, "seq", axis=1, tiled=True)
        weight = lax.all_gather(weight, "band", axis=0, tiled=True)
        depth, columns = weight.shape[0] // BANDS, weight.shape[1] // GROUPS
        weight = weight.reshape(2, 2, depth, GROUPS, columns).transpose(3, 1, 0, 2, 4)
        if height:
            weight = jnp.pad(
                weight.swapaxes(-1, -2), ((0, 0),) * 3 + ((0, height - columns), (0, 0))
            )
        parts.append(weight)
    return stacked(*parts)


def local(
    tokens, ln_gain, w_qkv, w_out, dec_gain, w_kv, w_final, reach, grid_query, neighbours, counts
):
    states = tokens[0]
    tok, width = states.shape
    shards, bands = lax.axis_size("seq"), lax.axis_size("band")
    outputs = w_final.shape[1] * shards
    height = -(-outputs // GROUPS // 16) * 16
    riding = (shards, bands) == (GROUPS, BANDS)
    up = [(i, i + 1) for i in range(shards - 1)]
    down = [(i + 1, i) for i in range(shards - 1)]
    left = lax.ppermute(states[tok - HALF :], "seq", up)
    right = lax.ppermute(states[:HALF], "seq", down)
    slots = (neighbours.T, counts.reshape(1, -1))
    there, requested, *payload = tables(tok, *slots, shards, (w_qkv, w_out) if riding else ())
    normed, bias, here = prepare(
        tok * shards, riding, left, states, right, ln_gain.reshape(1, width),
        reach.reshape(1, tok), *slots,
    )
    if riding:
        mine = pair_x(payload[0])
        mine, _, _ = lax.optimization_barrier((mine, left, right))
        other = swap_core(mine)
        pieces = [(mine, (0, 0)), (other, (0, 1))]
        chains, more = chain_step([mine, other], 1)
        pieces += more
        final = jnp.pad(w_final.T, ((0, height - w_final.shape[1]), (0, 0)))
        second = pair_core(pair_x(stacked(w_kv, final), chains[0]))
        later = [(second, (0, None))]
        chains[1], _ = lax.optimization_barrier((chains[1], normed))
        chains, more = chain_step(chains, 2)
        pieces += more
        normed, _ = lax.optimization_barrier((normed, chains[1]))
        made = project(riding, normed, pieces[:6], None)
        chains, more = chain_step(chains, 3)
        pieces += more
        end, _, _ = lax.optimization_barrier((chains[0], chains[1], made))
        end = carry(end)
        second, *_ = lax.optimization_barrier((second, chains[1], made, pieces[7][0], pieces[9][0]))
        later = [(second, (0, None))]
        block, more = ring_step(second, 1)
        later += more
        made = project(riding, normed, pieces[6:10], made)
        handed, _ = lax.optimization_barrier((end, made))
        pieces += [(end, (GROUPS // 2, 0)), (swap_core(handed), (GROUPS // 2, 1))]
        block, more = ring_step(block, 2, [pieces[n][0] for n in (11, 13, 15)])
        later += more
        attended = attend(riding, normed, bias, pieces[10:], made, (0, 1, 7, 2, 6))
        block, more = ring_step(block, 3, attended)
        later += more
        ids = None
    else:
        block = whole_blocks((w_qkv, 0), (w_out, 0))
        block = jnp.pad(block, ((0, 0),) * 3 + ((0, SLOTS), (0, 0)))
        pieces = [(block[at, half], (at, half)) for at in range(GROUPS) for half in range(2)]
        block = whole_blocks((w_kv, 0), (w_final, height))
        later = [(block[at], (at, None)) for at in range(GROUPS)]
        made = project(riding, normed, pieces[:6], None)
        attended = attend(riding, normed, bias, pieces[6:], made, tuple(range(3)))
        ids = lax.all_to_all(
            requested.reshape(shards, SLOTS).astype(jnp.int32), "seq", 0, 0, tiled=True
        ).reshape(shards * SLOTS, 1)
    layout = tuple(at for _, at in pieces)
    pieces = [piece for piece, _ in pieces]
    decoded, found = mix(
        states, attended, dec_gain.reshape(1, width), ids, pieces, layout, shards
    )
    fetched = lax.all_to_all(
        found.reshape(shards, SLOTS, width), "seq", split_axis=0, concat_axis=0, tiled=True
    )
    if riding:
        block, _ = lax.optimization_barrier((block, found))
        later += last_step(block, fetched)
    layout = tuple(at for _, at in later)
    pieces = [piece for piece, _ in later]
    fields = decode(
        riding, grid_query[0], decoded, fetched.reshape(shards * SLOTS, width), here, there,
        pieces, layout, outputs,
    )
    return fields[None]


def solution(mesh):
    return jax.shard_map(
        local,
        mesh=mesh,
        in_specs=(
            P("band", "seq", None),
            P(),
            P("band", "seq"),
            P("band", "seq"),
            P(),
            P("band", "seq"),
            P("band", "seq"),
            P("seq"),
            P("band", "seq", None),
            P("seq", None),
            P("seq"),
        ),
        out_specs=P("band", None, "seq"),
        check_vma=False,
    )
```
